32 devices in a mesh: wide: 4 (over y, x), rows: 4 (over z), cols: 2 (over core).
Axes of the slice: x: 2, y: 2, z: 4, core: 2. Of those that a mesh axis runs over, the one named last changes fastest.
Arguments:
- latent: bfloat16 [16, 4, 64, 32], P('wide', None, 'rows', 'cols'), may hold values from -6 to 6
- pred_grad: bfloat16 [16, 8, 64, 32], P('wide', None, 'rows', 'cols'), may hold values from -6 to 6
- timesteps: int32 [16], P('wide'), may hold values from 0 to 999
- labels: int32 [16], P('wide'), may hold values from 0 to 1000
- offsets: int32 [16], P('wide'), may hold values from 0 to 1
- counts: int32 [4], P('wide'), may hold values from 1 to 4, as said below
- patch_weight: bfloat16 [16, 384], replicated, may hold values from -1.5 to 1.5
- time_in: bfloat16 [256, 384], replicated, may hold values from -0.375 to 0.375
- time_out: bfloat16 [384, 384], replicated, may hold values from -0.3125 to 0.3125
- label_table: bfloat16 [1001, 384], replicated, may hold values from -6 to 6
- modulation: bfloat16 [2, 384, 2304], replicated, may hold values from -0.3125 to 0.3125
- qkv_weight: bfloat16 [2, 384, 1152], replicated, may hold values from -0.3125 to 0.3125
- proj_weight: bfloat16 [2, 384, 384], replicated, may hold values from -2.5 to 2.5
- up_weight: bfloat16 [2, 384, 1536], replicated, may hold values from -0.3125 to 0.3125
- down_weight: bfloat16 [2, 1536, 384], replicated, may hold values from -0.15625 to 0.15625
- final_mod: bfloat16 [384, 768], replicated, may hold values from -0.3125 to 0.3125
- final_weight: bfloat16 [384, 32], replicated, may hold values from -0.3125 to 0.3125
Outputs:
- prediction: bfloat16 [16, 8, 64, 32], P('wide', None, 'rows', 'cols')
- latent_grad: float32 [16, 4, 64, 32], P('wide', None, 'rows', 'cols')
- grad_patch: float32 [16, 384], replicated
- grad_time_in: float32 [256, 384], replicated
- grad_time_out: float32 [384, 384], replicated
- grad_table: float32 [1001, 384], replicated
- grad_modulation: float32 [2, 384, 2304], P(None, ('rows', 'cols'))
- grad_qkv: float32 [2, 384, 1152], P(None, ('rows', 'cols'))
- grad_proj: float32 [2, 384, 384], P(None, ('rows', 'cols'))
- grad_up: float32 [2, 384, 1536], P(None, ('rows', 'cols'))
- grad_down: float32 [2, 1536, 384], P(None, ('rows', 'cols'))
- grad_final_mod: float32 [384, 768], replicated
- grad_final: float32 [384, 32], replicated
The draws below stay inside these ranges and needn't reach their ends.
Inputs may be any that keep to these rules, and one draw needn't show every extreme that they name: Index w of wide holds live samples in its slots 0 to counts[w] - 1 and empty ones after; some index has all 4 slots filled. `labels`: label 1000 is the unconditional class.
All inputs are finite; a program needn't handle non-finite values.
Results may differ from the reference program's by a relative error of at most 0.02.
Values may be sent and summed in bfloat16 or wider, within the bound.
No kernel may reach another device: no remote copies, remote signals or barrier semaphores. Data moves between devices by JAX's collectives and lax.ppermute only.
A program may use at most 128 MiB of HBM per device.

```python
import math
import jax
import jax.numpy as jnp
from jax import lax

D = 384
HEADS = 6
HEAD_DIM = 64
FF = 1536
FREQ = 256
CLASSES = 1000
LAT_CH = 4
OUT_CH = 8
LAYERS = 2
SLOTS = 4
SAMPLES = 16
LAT_H = 64
LAT_W = 32
KEYS = 512
N_WIDE = 4


def draw_counts(key, part):
    key = jax.random.fold_in(key, 11)
    first_key, second_key, third_key = jax.random.split(key, 3)
    filled = jax.random.randint(first_key, (N_WIDE,), 1, SLOTS + 1)
    lowest_at = jax.random.randint(second_key, (), 0, N_WIDE)
    highest_at = jax.random.randint(third_key, (), 0, N_WIDE)
    position = jnp.arange(N_WIDE)
    filled = jnp.where(position == lowest_at, 1, filled)
    filled = jnp.where(position == highest_at, SLOTS, filled)
    return filled.astype(jnp.int32)


def set_ends(array, stream_key, low, top_value):
    extent = array.shape
    spot = [jax.random.randint(jax.random.fold_in(stream_key, axis), (), 0, extent[axis]) for axis in range(len(extent))]
    array = array.at[tuple(spot)].set(low)
    longest = extent.index(max(extent))
    spot[longest] = (spot[longest] + 1) % extent[longest]
    return array.at[tuple(spot)].set(top_value)


def shard_levels(own_key, extent, shards, smallest, top_value):
    level = 1.0
    for dim, shards_of in shards:
        draws = jax.random.uniform(jax.random.fold_in(jax.random.fold_in(own_key, 6), dim), (shards_of,), jnp.float32, smallest / len(shards), top_value / len(shards))
        level = level * jnp.repeat(jnp.exp(draws), extent[dim] // shards_of).reshape((-1,) + (1,) * (len(extent) - 1 - dim))
    return level


def bell_draw(stream_key, shape, deviation, most, cuts=(), held_as=jnp.bfloat16):
    gain = shard_levels(stream_key, shape, cuts, -0.22, 0.18) if cuts else 1.0
    drawn = jax.random.normal(stream_key, shape, jnp.float32) * deviation * gain
    return jnp.minimum(jnp.maximum(drawn, -most), most).astype(held_as)


def setup_inputs(seed: int = 0) -> dict:
    arg_keys = jax.random.split(jax.random.key(seed), 18)
    return {
        "latent": bell_draw(arg_keys[0], (SAMPLES, LAT_CH, LAT_H, LAT_W), 1.0, 6.0, ((0, 4), (2, 4), (3, 2))),
        "pred_grad": bell_draw(arg_keys[1], (SAMPLES, OUT_CH, LAT_H, LAT_W), 1.0, 6.0, ((0, 4), (2, 4), (3, 2))),
        "timesteps": set_ends(jax.random.randint(arg_keys[2], (SAMPLES,), 0, 1000), jax.random.fold_in(arg_keys[2], 1), 0, 999).astype(jnp.int32),
        "labels": set_ends(jax.random.randint(arg_keys[3], (SAMPLES,), 0, CLASSES + 1), jax.random.fold_in(arg_keys[3], 1), 0, CLASSES).astype(jnp.int32),
        "offsets": set_ends(jax.random.randint(arg_keys[4], (SAMPLES,), 0, 2), jax.random.fold_in(arg_keys[4], 1), 0, 1).astype(jnp.int32),
        "counts": draw_counts(jax.random.fold_in(arg_keys[17], 71), 0),
        "patch_weight": bell_draw(arg_keys[6], (4 * LAT_CH, D), (4 * LAT_CH) ** -0.5, 1.5),
        "time_in": bell_draw(arg_keys[7], (FREQ, D), FREQ ** -0.5, 0.375),
        "time_out": bell_draw(arg_keys[8], (D, D), D ** -0.5, 0.3125),
        "label_table": bell_draw(arg_keys[9], (CLASSES + 1, D), 1.0, 6.0),
        "modulation": bell_draw(arg_keys[10], (LAYERS, D, 6 * D), D ** -0.5, 0.3125),
        "qkv_weight": bell_draw(arg_keys[11], (LAYERS, D, 3 * D), D ** -0.5, 0.3125),
        "proj_weight": bell_draw(arg_keys[12], (LAYERS, D, D), (max(2, 8 * D // KEYS)) ** -0.5, 2.5),
        "up_weight": bell_draw(arg_keys[13], (LAYERS, D, FF), D ** -0.5, 0.3125),
        "down_weight": bell_draw(arg_keys[14], (LAYERS, FF, D), FF ** -0.5, 0.15625),
        "final_mod": bell_draw(arg_keys[15], (D, 2 * D), D ** -0.5, 0.3125),
        "final_weight": bell_draw(arg_keys[16], (D, 4 * OUT_CH), D ** -0.5, 0.3125),
    }


HIGH = lax.Precision.HIGHEST
EPS = 1e-06

@jax.custom_vjp
def low(v):
    return lax.optimization_barrier(v.astype(jnp.bfloat16)).astype(jnp.float32)

@jax.custom_vjp
def low_back(v):
    return v

def low_keep(v):
    return (low(v), None)

def low_pass(kept, grad):
    return (grad,)

def back_keep(v):
    return (v, None)

def back_low(kept, grad):
    return (low(grad),)
low.defvjp(low_keep, low_pass)
low_back.defvjp(back_keep, back_low)

def matmul(first_op, second_op):
    return jnp.matmul(first_op, second_op, precision=HIGH)

def layer_norm(states):
    centred = states - lax.optimization_barrier(jnp.mean(states, axis=-1, keepdims=True))
    inverse = lax.rsqrt(lax.optimization_barrier(jnp.mean(centred * centred, axis=-1, keepdims=True)) + EPS)
    return centred * inverse

def timestep_features(timesteps, feature_count):
    half_count = feature_count // 2
    freqs = jnp.exp(-math.log(10000.0) * jnp.arange(half_count, dtype=jnp.float32) / half_count)
    angles = timesteps.astype(jnp.float32)[:, None] * freqs[None, :]
    return jnp.concatenate([jnp.cos(angles), jnp.sin(angles)], axis=-1)

def position_table(row_start, col_start, row_count, col_count, model_width):
    quarter = model_width // 4
    omega = jnp.exp(-math.log(10000.0) * jnp.arange(quarter, dtype=jnp.float32) / quarter)
    row_angle = (row_start + jnp.arange(row_count, dtype=jnp.float32))[:, None] * omega[None, :]
    col_angle = (col_start + jnp.arange(col_count, dtype=jnp.float32))[:, None] * omega[None, :]
    row_part = jnp.concatenate([jnp.sin(row_angle), jnp.cos(row_angle)], axis=-1)
    col_part = jnp.concatenate([jnp.sin(col_angle), jnp.cos(col_angle)], axis=-1)
    half_width = model_width // 2
    table = jnp.concatenate([jnp.broadcast_to(row_part[:, None, :], (row_count, col_count, half_width)), jnp.broadcast_to(col_part[None, :, :], (row_count, col_count, half_width))], axis=-1)
    return table.reshape(row_count * col_count, model_width)

def patchify(images):
    batch_size, channel_count, row_count, col_count = images.shape
    blocks = images.reshape(batch_size, channel_count, row_count // 2, 2, col_count // 2, 2)
    blocks = blocks.transpose(0, 2, 4, 3, 5, 1)
    return blocks.reshape(batch_size, row_count // 2 * (col_count // 2), 4 * channel_count)

def unpatchify(tokens, row_count, col_count):
    batch_size = tokens.shape[0]
    channel_count = tokens.shape[2] // 4
    blocks = tokens.reshape(batch_size, row_count // 2, col_count // 2, 2, 2, channel_count)
    blocks = blocks.transpose(0, 5, 1, 3, 2, 4)
    return blocks.reshape(batch_size, channel_count, row_count, col_count)

def take_rows(image, start):
    return lax.dynamic_slice_in_dim(image, start, LAT_H, 1)

def place_rows(canvas, image, start):
    return lax.dynamic_update_slice_in_dim(canvas, image, start, 1)

def attend(triple):
    sample_queries, sample_keys, sample_values = triple
    scores = low_back(jnp.einsum('phd,khd->hpk', sample_queries, sample_keys, precision=HIGH) * HEAD_DIM ** (-0.5))
    attention = jax.nn.softmax(scores, axis=-1)
    return jnp.einsum('hpk,khd->phd', low(attention), sample_values, precision=HIGH)

def block(states, shared, mod_matrix, qkv_matrix, proj_matrix, up_matrix, down_matrix):
    batch_size, tok_count, model_width = states.shape
    mod_values = matmul(shared, mod_matrix)[:, None, :]
    shift_attn, scale_attn, gate_attn, shift_mlp, scale_mlp, gate_mlp = jnp.split(mod_values, 6, axis=-1)
    inner_a = low(layer_norm(states) * (1.0 + scale_attn) + shift_attn)
    projected = low_back(low(matmul(inner_a, qkv_matrix)))
    heads_shape = (batch_size, tok_count, HEADS, HEAD_DIM)
    queries = projected[..., :model_width].reshape(heads_shape)
    keys_all = projected[..., model_width:2 * model_width].reshape(heads_shape)
    values_all = projected[..., 2 * model_width:].reshape(heads_shape)
    attended = lax.map(jax.checkpoint(attend), (queries, keys_all, values_all))
    attended = low_back(low(attended.reshape(batch_size, tok_count, model_width)))
    middle = states + gate_attn * low_back(matmul(attended, proj_matrix))
    inner_m = low(layer_norm(middle) * (1.0 + scale_mlp) + shift_mlp)
    hidden = low_back(matmul(inner_m, up_matrix))
    activated = low(jax.nn.gelu(hidden, approximate=True))
    return middle + gate_mlp * low_back(matmul(activated, down_matrix))

def reference(latent, pred_grad, timesteps, labels, offsets, counts, patch_weight, time_in, time_out, label_table, modulation, qkv_weight, proj_weight, up_weight, down_weight, final_mod, final_weight):
    sample_index = jnp.arange(SAMPLES)
    live = (sample_index % SLOTS < counts[sample_index // SLOTS]).astype(jnp.float32)
    starts = offsets.astype(jnp.int32)
    features = low(timestep_features(timesteps, FREQ))
    positions = position_table(0.0, 0.0, LAT_H // 2, LAT_W // 2, D)
    floats = tuple((member.astype(jnp.float32) for member in (latent, patch_weight, time_in, time_out, label_table, modulation, qkv_weight, proj_weight, up_weight, down_weight, final_mod, final_weight)))

    def forward(latent_f, patch_f, time_in_f, time_out_f, table_f, mod_f, qkv_f, proj_f, up_f, down_f, final_mod_f, final_f):
        time_hidden = matmul(features, time_in_f)
        condition = matmul(low(jax.nn.silu(time_hidden)), time_out_f) + jnp.take(table_f, labels, axis=0)
        shared = low(jax.nn.silu(condition))

        def group_forward(pieces):
            latent_g, starts_g, live_g, shared_g = pieces
            padded = jnp.pad(latent_g, ((0, 0), (0, 0), (0, 1), (0, 0)))
            windows = jax.vmap(take_rows)(padded, starts_g)
            states = low_back(matmul(patchify(windows), patch_f)) + positions[None]
            for layer in range(LAYERS):
                states = block(states, shared_g, mod_f[layer], qkv_f[layer], proj_f[layer], up_f[layer], down_f[layer])
            final_values = matmul(shared_g, final_mod_f)[:, None, :]
            final_shift, final_scale = jnp.split(final_values, 2, axis=-1)
            inner_f = low(layer_norm(states) * (1.0 + final_scale) + final_shift)
            out_tokens = low_back(matmul(inner_f, final_f))
            images = unpatchify(out_tokens, LAT_H, LAT_W)
            canvas = jnp.zeros((SLOTS, OUT_CH, LAT_H + 1, LAT_W), jnp.float32)
            placed = jax.vmap(place_rows)(canvas, images, starts_g)
            return placed[:, :, :LAT_H, :] * live_g[:, None, None, None]
        grouped = (latent_f.reshape(N_WIDE, SLOTS, LAT_CH, LAT_H, LAT_W), starts.reshape(N_WIDE, SLOTS), live.reshape(N_WIDE, SLOTS), shared.reshape(N_WIDE, SLOTS, D))
        predicted = lax.map(jax.checkpoint(group_forward), grouped)
        return predicted.reshape(SAMPLES, OUT_CH, LAT_H, LAT_W)
    pred_full, pullback = jax.vjp(forward, *floats)
    grads = pullback(pred_grad.astype(jnp.float32))
    return (pred_full.astype(jnp.bfloat16), grads[0], grads[1], grads[2], grads[3], grads[4], grads[5], grads[6], grads[7], grads[8], grads[9], grads[10], grads[11])
```

```python
from functools import partial
import math

import jax
import jax.numpy as jnp
import numpy as np
from jax import lax
from jax.experimental import pallas as pl
from jax.experimental.pallas import tpu as pltpu
from jax.sharding import PartitionSpec as P

HEADS = 6
HEAD_DIM = 64
PAIRS = HEADS // 2
LANES = 2 * HEAD_DIM
EPS = 1e-06
F32 = jnp.float32
BF16 = jnp.bfloat16
ROWS = 24
ROW_F, ROW_SHARED, ROW_ACT, ROW_COND, ROW_HID, ROW_FEAT = 12, 14, 15, 16, 17, 18

VM = pl.BlockSpec(memory_space=pltpu.VMEM)
SM = pl.BlockSpec(memory_space=pltpu.SMEM)
HB = pl.BlockSpec(memory_space=pl.ANY)


def dot(a, b):
    return jnp.dot(a, b, preferred_element_type=F32)


def dot_nt(a, b):
    return lax.dot_general(a, b, (((1,), (1,)), ((), ())), preferred_element_type=F32)


def dot_tn(a, b):
    return lax.dot_general(a, b, (((0,), (0,)), ((), ())), preferred_element_type=F32)


def sds(shape, dtype):
    return jax.ShapeDtypeStruct(shape, dtype)


def layer_norm(states):
    centred = states - jnp.mean(states, axis=-1, keepdims=True)
    inverse = lax.rsqrt(jnp.mean(centred * centred, axis=-1, keepdims=True) + EPS)
    return centred * inverse, inverse


def norm_back(grad, normed, inverse):
    mean_grad = jnp.mean(grad, axis=-1, keepdims=True)
    mean_cross = jnp.mean(grad * normed, axis=-1, keepdims=True)
    return inverse * (grad - mean_grad - normed * mean_cross)


def token_sum(values):
    return jnp.sum(values, axis=0, keepdims=True)


def head_masks(dtype):
    lane = lax.broadcasted_iota(jnp.int32, (1, LANES), 1)
    first = (lane < HEAD_DIM).astype(F32)
    return first.astype(dtype), (1.0 - first).astype(dtype)


def unit_place(zz, ww, cc):
    x, y = ww % 2, ww // 2
    return (x * 8 + y * 4 + zz) if cc == 0 else (y * 8 + x * 4 + zz)


def fetch(copies):
    for copy in copies:
        copy.start()


def kernel_call(kernel, args, specs, outs, scratch=(), flops=0, touched=0):
    return pl.pallas_call(
        kernel,
        in_specs=list(specs),
        out_specs=[VM] * len(outs),
        out_shape=list(outs),
        scratch_shapes=list(scratch),
        compiler_params=pltpu.CompilerParams(vmem_limit_bytes=56 * 1024 * 1024),
        cost_estimate=pl.CostEstimate(flops=flops, bytes_accessed=touched, transcendentals=0),
    )(*args)


def cond_kernel(feat, trow, time_in, time_out, modulation, final_mod, mods, cond):
    width = trow.shape[-1]
    count = time_in.shape[0]
    rows = jnp.broadcast_to(feat[...], (8, width))
    hidden = dot(rows[:, :count].astype(BF16), time_in[...])
    act = (hidden * jax.nn.sigmoid(hidden)).astype(BF16)
    condition = dot(act, time_out[...]) + trow[...]
    shared = (condition * jax.nn.sigmoid(condition)).astype(BF16)
    for layer in range(2):
        values = dot(shared, modulation[layer])
        for k in range(6):
            mods[layer, k : k + 1, :] = values[0:1, k * width : (k + 1) * width]
    values = dot(shared, final_mod[...])
    for k in range(2):
        mods[2, k : k + 1, :] = values[0:1, k * width : (k + 1) * width]
    cond[0:1, :] = shared[0:1].astype(F32)
    cond[1:2, :] = act[0:1].astype(F32)
    cond[2:3, :] = condition[0:1]
    cond[3:4, :] = hidden[0:1]
    cond[4:5, :] = feat[...]


def qkv_forward(state, mods, layer, weight, q, kv):
    width = state.shape[-1]
    normed, _ = layer_norm(state)
    inner = (normed * (1.0 + mods[layer, 1:2]) + mods[layer, 0:1]).astype(BF16)
    projected = dot(inner, weight).astype(BF16)
    q[...] = projected[:, :width]
    kv[...] = projected[:, width:]


def attend_forward(q, kv, kvp, probs, attended):
    width = q.shape[-1]
    masks = head_masks(BF16)
    for p in range(PAIRS):
        at = slice(p * LANES, (p + 1) * LANES)
        av = slice(width + p * LANES, width + (p + 1) * LANES)
        qp = q[:, at] * BF16(HEAD_DIM**-0.5)
        k0, k1, v0, v1 = kv[:, at], kvp[:, at], kv[:, av], kvp[:, av]
        total = None
        for h in range(2):
            qh = qp * masks[h]
            s0, s1 = dot_nt(qh, k0), dot_nt(qh, k1)
            peak = jnp.maximum(
                jnp.max(s0, axis=-1, keepdims=True), jnp.max(s1, axis=-1, keepdims=True)
            )
            e0, e1 = jnp.exp(s0 - peak), jnp.exp(s1 - peak)
            scale = 1.0 / (
                jnp.sum(e0, axis=-1, keepdims=True) + jnp.sum(e1, axis=-1, keepdims=True)
            )
            p0, p1 = (e0 * scale).astype(BF16), (e1 * scale).astype(BF16)
            probs[2 * p + h, 0] = p0
            probs[2 * p + h, 1] = p1
            part = dot(p0, v0 * masks[h]) + dot(p1, v1 * masks[h])
            total = part if total is None else total + part
        attended[:, at] = total.astype(BF16)


def mlp_forward(state, mods, layer, attended, proj, up, down, attn_out, gp, act):
    attn = dot(attended, proj)
    attn_out[...] = attn.astype(BF16)
    middle = state + mods[layer, 2:3] * attn
    normed, _ = layer_norm(middle)
    inner = (normed * (1.0 + mods[layer, 4:5]) + mods[layer, 3:4]).astype(BF16)
    width = middle.shape[-1]
    branch = None
    for i in range(up.shape[-1] // width):
        at = slice(i * width, (i + 1) * width)
        hidden = dot(inner, up[:, at])
        square = hidden * hidden
        root = math.sqrt(2.0 / math.pi)
        bent = jnp.tanh(root * hidden * (1.0 + 0.044715 * square))
        half = 0.5 * (1.0 + bent)
        activated = (hidden * half).astype(BF16)
        act[:, at] = activated
        slope = half + 0.5 * hidden * (1.0 - bent * bent) * (root * (1.0 + 3 * 0.044715 * square))
        gp[:, at] = slope.astype(BF16)
        part = dot(activated, down[at, :])
        branch = part if branch is None else branch + part
    return middle, branch


def mlp_backward(grad, middle, branch, mods, layer, gp, act, up, down, units, rows, first):
    width = middle.shape[-1]
    normed, inverse = layer_norm(middle)
    scale = 1.0 + mods[layer, 4:5]
    inner_t = (normed * scale + mods[layer, 3:4]).astype(BF16).T
    branch_grad = (mods[layer, 5:6] * grad).astype(BF16)
    inner_grad = None
    pieces = up.shape[-1] // width
    block = width // 8
    for i in range(pieces):
        at = slice(i * width, (i + 1) * width)
        act_grad = dot_nt(branch_grad, down[at, :])
        hidden_grad = (act_grad * gp[:, at].astype(F32)).astype(BF16)
        part = dot_nt(hidden_grad, up[:, at])
        inner_grad = part if inner_grad is None else inner_grad + part
        grad_up = dot(inner_t, hidden_grad).astype(BF16)
        for b in range(8):
            units[b % 2, unit_place(b // 2, i, b % 2), 0:block] = grad_up[b * block : (b + 1) * block]
        grad_down = dot_tn(act[:, at], branch_grad).astype(BF16)
        for cc in range(2):
            for j in range(4):
                start = (cc * 4 + j) * block
                units[cc, unit_place(i, j, cc), block : 2 * block] = grad_down[start : start + block]
    rows[first : first + 1, :] = token_sum(inner_grad)
    rows[first + 1 : first + 2, :] = token_sum(inner_grad * normed)
    rows[first + 2 : first + 3, :] = token_sum(grad * branch.astype(F32))
    return grad + norm_back(inner_grad * scale, normed, inverse)


def qkv_backward(state, middle_grad, dq, dkv, dkvr, mods, layer, weight, gproj, units, at_row, rows):
    width = state.shape[-1]
    block = width // 8
    normed, inverse = layer_norm(state)
    scale = 1.0 + mods[layer, 1:2]
    inner_t = (normed * scale + mods[layer, 0:1]).astype(BF16).T
    dkv_sum = (dkv[...].astype(F32) + dkvr[...].astype(F32)).astype(BF16)
    pieces = (dq[...], dkv_sum[:, :width], dkv_sum[:, width:])
    inner_grad = None
    for i, piece in enumerate(pieces):
        part = dot_nt(piece, weight[:, i * width : (i + 1) * width])
        inner_grad = part if inner_grad is None else inner_grad + part
        grad_piece = dot(inner_t, piece).astype(BF16)
        for b in range(8):
            place = unit_place(b // 2, i, b % 2)
            units[b % 2, place, at_row : at_row + block] = grad_piece[b * block : (b + 1) * block]
    for b in range(8):
        place = unit_place(b // 2, 3, b % 2)
        units[b % 2, place, at_row : at_row + block] = gproj[b * block : (b + 1) * block, :]
    rows[0:1, :] = token_sum(inner_grad)
    rows[1:2, :] = token_sum(inner_grad * normed)
    return middle_grad + norm_back(inner_grad * scale, normed, inverse)


def embed_kernel(scal, tiles, pos, mods, pw, qkv_hbm, state, patches, q, kv, qkv, sem):
    copy = pltpu.make_async_copy(qkv_hbm.at[0], qkv, sem.at[0])
    copy.start()
    z, offset = scal[0], scal[3]
    count = tiles.shape[0]
    even = jnp.concatenate([tiles[z ^ t, 0] for t in range(count)], axis=0).astype(F32)
    odd = jnp.concatenate([tiles[z ^ t, 1] for t in range(count)], axis=0).astype(F32)
    step = pos.shape[0] // 32
    later = jnp.concatenate([even[step:], jnp.zeros((step, even.shape[1]), F32)], axis=0)
    first = jnp.where(offset == 1, odd, even).astype(BF16)
    second = jnp.where(offset == 1, later, odd).astype(BF16)
    patches[0] = first
    patches[1] = second
    values = dot(first, pw[0]) + dot(second, pw[1]) + pos[...]
    state[...] = values
    copy.wait()
    qkv_forward(values, mods, 0, qkv[...], q, kv)


def block_kernel(
    state, q, kv, kvp, mods, proj_hbm, up_hbm, down_hbm, qkv_hbm,
    probs, attended, attn_out, middle, gp, act, branch, state1, q1, kv1,
    proj, up, down, qkv, sem,
):
    copies = [
        pltpu.make_async_copy(proj_hbm.at[0], proj, sem.at[0]),
        pltpu.make_async_copy(up_hbm.at[0], up, sem.at[1]),
        pltpu.make_async_copy(down_hbm.at[0], down, sem.at[2]),
        pltpu.make_async_copy(qkv_hbm.at[1], qkv, sem.at[3]),
    ]
    fetch(copies)
    attend_forward(q, kv, kvp, probs, attended)
    for copy in copies[:3]:
        copy.wait()
    mid, out = mlp_forward(
        state[...], mods, 0, attended[...], proj[...], up, down, attn_out, gp, act
    )
    middle[...] = mid
    branch[...] = out.astype(BF16)
    new = mid + mods[0, 5:6] * out
    state1[...] = new
    copies[3].wait()
    qkv_forward(new, mods, 1, qkv[...], q1, kv1)


def turn_kernel(
    scal, state, q, kv, kvp, mods, patches, fw, fwt, proj_hbm, up_hbm, down_hbm,
    probs, attended, attn_out, middle_grad, pred, units, rows, gfinal,
    proj, up, down, gp, act, sem,
):
    copies = [
        pltpu.make_async_copy(proj_hbm.at[1], proj, sem.at[0]),
        pltpu.make_async_copy(up_hbm.at[1], up, sem.at[1]),
        pltpu.make_async_copy(down_hbm.at[1], down, sem.at[2]),
    ]
    fetch(copies)
    offset, live = scal[3], scal[4].astype(F32)
    attend_forward(q, kv, kvp, probs, attended)
    for copy in copies:
        copy.wait()
    middle, branch = mlp_forward(
        state[...], mods, 1, attended[...], proj[...], up, down, attn_out, gp, act
    )
    last = middle + mods[1, 5:6] * branch
    normed, inverse = layer_norm(last)
    scale = 1.0 + mods[2, 1:2]
    inner = (normed * scale + mods[2, 0:1]).astype(BF16)
    upper, lower = dot(inner, fw[0]) * live, dot(inner, fw[1]) * live
    step = upper.shape[0] // 32
    moved = jnp.concatenate([jnp.zeros((step, lower.shape[1]), F32), lower[:-step]], axis=0)
    pred[0] = jnp.where(offset == 1, moved, upper).astype(BF16)
    pred[1] = jnp.where(offset == 1, upper, lower).astype(BF16)
    inner_grad = (dot(patches[0], fwt[0]) + dot(patches[1], fwt[1])) * live
    gfinal[0] = dot_tn(patches[0], inner) * live
    gfinal[1] = dot_tn(patches[1], inner) * live
    rows[3:4, :] = token_sum(inner_grad)
    rows[4:5, :] = token_sum(inner_grad * normed)
    grad = norm_back(inner_grad * scale, normed, inverse)
    middle_grad[...] = mlp_backward(
        grad, middle, branch, mods, 1, gp, act, up, down, units, rows, 0
    )


def attend_back_kernel(
    layer, q, kv, kvp, probs, attended, attn_out, middle_grad, mods, proj_hbm,
    dq, dkv, dkvs, gproj, rows,
    proj, sem,
):
    copy = pltpu.make_async_copy(proj_hbm.at[layer], proj, sem.at[0])
    copy.start()
    width = q.shape[-1]
    grad = middle_grad[...]
    rows[0:1, :] = token_sum(grad * attn_out[...].astype(F32))
    attn_grad = (mods[layer, 2:3] * grad).astype(BF16)
    copy.wait()
    attended_grad = dot_nt(attn_grad, proj[...]).astype(BF16)
    gproj[...] = dot_tn(attended[...], attn_grad).astype(BF16)
    masks = head_masks(BF16)
    for p in range(PAIRS):
        at = slice(p * LANES, (p + 1) * LANES)
        av = slice(width + p * LANES, width + (p + 1) * LANES)
        qp = q[:, at] * BF16(HEAD_DIM**-0.5)
        dop = attended_grad[:, at]
        ks, vs = (kv[:, at], kvp[:, at]), (kv[:, av], kvp[:, av])
        total = None
        parts = [None] * 4
        for h in range(2):
            doh = dop * masks[h]
            qh = qp * masks[h]
            ps = [probs[2 * p + h, i] for i in range(2)]
            dps = [dot_nt(doh, vs[i]) for i in range(2)]
            pfs = [ps[i].astype(F32) for i in range(2)]
            inner = sum(jnp.sum(dps[i] * pfs[i], axis=-1, keepdims=True) for i in range(2))
            for i in range(2):
                ds = (pfs[i] * (dps[i] - inner)).astype(BF16)
                part = dot(ds, ks[i] * masks[h])
                total = part if total is None else total + part
                dk, dv = dot_tn(ds, qh), dot_tn(ps[i], doh)
                parts[2 * i] = dk if h == 0 else parts[2 * i] + dk
                parts[2 * i + 1] = dv if h == 0 else parts[2 * i + 1] + dv
        dq[:, at] = (total * HEAD_DIM**-0.5).astype(BF16)
        dkv[:, at] = parts[0].astype(BF16)
        dkv[:, av] = parts[1].astype(BF16)
        dkvs[:, at] = parts[2].astype(BF16)
        dkvs[:, av] = parts[3].astype(BF16)


def middle_kernel(
    state1, middle_grad1, dq, dkv, dkvr, gproj, middle, branch, gp, act, mods,
    qkv_hbm, up_hbm, down_hbm,
    middle_grad, units, rows,
    qkv, up, down, sem,
):
    copies = [
        pltpu.make_async_copy(qkv_hbm.at[1], qkv, sem.at[0]),
        pltpu.make_async_copy(up_hbm.at[0], up, sem.at[1]),
        pltpu.make_async_copy(down_hbm.at[0], down, sem.at[2]),
    ]
    fetch(copies)
    width = state1.shape[-1]
    copies[0].wait()
    grad = qkv_backward(
        state1[...], middle_grad1[...], dq, dkv, dkvr, mods, 1, qkv, gproj, units, width // 4, rows
    )
    copies[1].wait()
    copies[2].wait()
    middle_grad[...] = mlp_backward(
        grad, middle[...], branch[...], mods, 0, gp, act, up, down, units, rows, 2
    )


def last_kernel(
    scal, state0, middle_grad, dq, dkv, dkvr, gproj, mods, patches, pw, cond,
    rows_turn, rows_a1, rows_mid, rows_a0, gfinal, qkv_hbm,
    units, lgrad, table,
    qkv, rows, sem,
):
    copy = pltpu.make_async_copy(qkv_hbm.at[0], qkv, sem.at[0])
    copy.start()
    offset = scal[3]
    copy.wait()
    grad = qkv_backward(
        state0[...], middle_grad[...], dq, dkv, dkvr, mods, 0, qkv, gproj, units, 0, rows
    )
    embed_grad = grad.astype(BF16)
    gp0, gp1 = dot_tn(patches[0], embed_grad), dot_tn(patches[1], embed_grad)
    chans = pw.shape[1] - gfinal.shape[1] // 3 * 2
    upper, lower = dot_nt(embed_grad, pw[0])[:, :chans], dot_nt(embed_grad, pw[1])[:, :chans]
    step = upper.shape[0] // 32
    moved = jnp.concatenate([jnp.zeros((step, chans), F32), lower[:-step]], axis=0)
    lgrad[0] = jnp.where(offset == 1, moved, upper)
    lgrad[1] = jnp.where(offset == 1, upper, lower)
    table[...] = jnp.zeros_like(table)
    table[0:2, :] = rows[0:2, :]
    table[2:3, :] = rows_a0[0:1, :]
    table[3:6, :] = rows_mid[2:5, :]
    table[6:8, :] = rows_mid[0:2, :]
    table[8:9, :] = rows_a1[0:1, :]
    table[9:12, :] = rows_turn[0:3, :]
    table[12:14, :] = rows_turn[3:5, :]
    table[14:19, :] = 0.5 * cond[0:5, :]
    table[ROWS : ROWS + chans, :] = gp0[:chans]
    table[ROWS + chans : ROWS + 2 * chans, :] = gp1[:chans]
    outs = gfinal.shape[1] - chans
    base = ROWS + 2 * chans
    table[base : base + outs, :] = gfinal[0, chans:, :]
    table[base + outs : base + 2 * outs, :] = gfinal[1, chans:, :]


def silu_slope(values):
    sigmoid = jax.nn.sigmoid(values)
    return sigmoid * (1.0 + values * (1.0 - sigmoid))


def sums_kernel(
    scal, rows, sums, modulation, final_mod, time_out,
    g_time_in, g_time_out, g_table, g_mod, g_final_mod, g_patch, g_final,
    shared_t,
):
    width = rows.shape[-1]
    mods = [
        jnp.concatenate([rows[6 * layer + k] for k in range(6)], axis=-1).astype(BF16)
        for layer in range(2)
    ]
    fmods = jnp.concatenate([rows[ROW_F], rows[ROW_F + 1]], axis=-1).astype(BF16)
    shared_grad = dot_nt(fmods, final_mod[...])
    for layer in range(2):
        shared_grad += dot_nt(mods[layer], modulation[layer])
    cond_grad = shared_grad * silu_slope(rows[ROW_COND])
    cond_low = cond_grad.astype(BF16)
    time_grad = dot_nt(cond_low, time_out[...]) * silu_slope(rows[ROW_HID])
    feats = rows[ROW_FEAT]
    count = g_time_in.shape[0]
    g_time_in[...] = dot(feats[:, :count].T.astype(BF16), time_grad.astype(BF16))
    g_time_out[...] = dot(rows[ROW_ACT].T.astype(BF16), cond_low)
    shared_t[...] = rows[ROW_SHARED].T
    label = (feats[:, count : count + 1] * 32.0 + feats[:, count + 1 : count + 2]).astype(jnp.int32)
    classes = g_table.shape[0]
    padded = (classes + 127) // 128 * 128
    lane = lax.broadcasted_iota(jnp.int32, (feats.shape[0], padded), 1)
    hot = (lane == label).astype(F32).T
    cond_rest = (cond_grad - cond_low.astype(F32)).astype(BF16)
    hot_low = hot[:classes].astype(BF16)
    g_table[...] = dot(hot_low, cond_low) + dot(hot_low, cond_rest)
    block = g_mod.shape[1]
    start = pl.multiple_of((scal[0] * 2 + scal[1]) * block, 8)
    own = shared_t[pl.ds(start, block), :].astype(BF16)
    for layer in range(2):
        g_mod[layer] = dot(own, mods[layer])
    g_final_mod[...] = dot(shared_t[...].astype(BF16), fmods)
    patch = g_patch.shape[0]
    g_patch[...] = sums[:patch, :]
    g_final[...] = sums[patch:, :].T


def spread_kernel(scal, *refs):
    ins, (g_qkv, g_proj, g_up, g_down) = refs[:12], refs[12:]
    width = g_proj.shape[-1]
    block = g_proj.shape[1]
    spot = scal[2] % 4

    def place_mlp(layer, piece, unit):
        cols = pl.ds(pl.multiple_of(unit * width, 128), width)
        g_up[layer, :, cols] = piece[0:block].astype(F32)
        g_down[layer, pl.ds(pl.multiple_of(unit * block, 8), block), :] = piece[
            block : 2 * block
        ].astype(F32)

    def place_attn(layer, piece, unit):
        @pl.when(unit < 3)
        def _():
            cols = pl.ds(pl.multiple_of(unit * width, 128), width)
            g_qkv[layer, :, cols] = piece.astype(F32)

        @pl.when(unit == 3)
        def _():
            g_proj[layer] = piece.astype(F32)

    for k in range(4):
        unit = spot ^ k
        place_mlp(1, ins[k][...], unit)
        both = ins[4 + k]
        place_mlp(0, both[0 : 2 * block], unit)
        place_attn(1, both[2 * block :], unit)
        place_attn(0, ins[8 + k][...], unit)


def swap(value, axis, bit):
    count = lax.axis_size(axis)
    return lax.ppermute(value, axis, [(i, i ^ bit) for i in range(count)])


def swap_wide_by_core(value, bits):
    wide, cores = lax.axis_size("wide"), lax.axis_size("cols")
    pairs = [
        (w * cores + c, (w ^ bits[c % 2]) * cores + c) for w in range(wide) for c in range(cores)
    ]
    return lax.ppermute(value, ("wide", "cols"), pairs)


def pick(value, index):
    return lax.dynamic_index_in_dim(value, index, 0, keepdims=False)


def to_rows(tiles, z):
    count = tiles.shape[0]
    return [pick(tiles, z)] + [swap(pick(tiles, z ^ k), "rows", k) for k in range(1, count)]


def rest_sum(value):
    bit = 4
    while bit < lax.axis_size("wide"):
        value = (value.astype(F32) + swap(value, "wide", bit).astype(F32)).astype(value.dtype)
        bit *= 2
    return value


def add(*values):
    total = values[0].astype(F32)
    for value in values[1:]:
        total = total + value.astype(F32)
    return total.astype(values[0].dtype)


def reduce_units(units, z, c, w):
    x, y = w % 2, (w // 2) % 2
    held = add(pick(units, c), swap(pick(units, 1 - c), "cols", 1))
    for bits, mine in (((1, 2), jnp.where(c == 0, x, y)), ((2, 1), jnp.where(c == 0, y, x))):
        half = held.shape[0] // 2
        keep = lax.dynamic_slice_in_dim(held, mine * half, half, 0)
        send = lax.dynamic_slice_in_dim(held, (1 - mine) * half, half, 0)
        held = add(keep, swap_wide_by_core(send, bits))
    unit = rest_sum(add(*to_rows(held, z)))
    return [unit] + [swap(unit, "wide", k) for k in range(1, 4)]


def gather_rows(table, z):
    table = (table + swap(table, "cols", 1)).astype(BF16)
    wide = [table] + [swap(table, "wide", k) for k in range(1, 4)]
    rows = jnp.stack([t[:ROWS] for t in wide])
    sums = add(*[t[ROWS:] for t in wide])
    bit = 4
    while bit < lax.axis_size("wide"):
        rows = jnp.concatenate([rows, swap(rows, "wide", bit)])
        bit *= 2
    sums = rest_sum(sums)
    count, width = rows.shape[0], rows.shape[-1]
    packed = jnp.concatenate([rows.reshape(count * ROWS, width), sums])
    every = [packed] + [swap(packed, "rows", k) for k in range(1, lax.axis_size("rows"))]
    rows = jnp.concatenate([e[: count * ROWS].reshape(count, ROWS, width) for e in every])
    sums = sum(e[count * ROWS :].astype(F32) for e in every)
    return rows.transpose(1, 0, 2).astype(F32), sums


def position_tables(row_count, col_count, cores, width):
    quarter = width // 4
    omega = np.exp(-math.log(10000.0) * np.arange(quarter) / quarter)
    row_angle = np.arange(row_count)[:, None] * omega[None, :]
    col_angle = np.arange(col_count * cores)[:, None] * omega[None, :]
    row_part = np.concatenate([np.sin(row_angle), np.cos(row_angle)], axis=-1)
    col_part = np.concatenate([np.sin(col_angle), np.cos(col_angle)], axis=-1)
    col_part = col_part.reshape(cores, 1, col_count, width // 2)
    table = np.concatenate(
        [
            np.broadcast_to(row_part[None, :, None, :], (cores, row_count, col_count, width // 2)),
            np.broadcast_to(col_part, (cores, row_count, col_count, width // 2)),
        ],
        axis=-1,
    )
    return table.reshape(cores, row_count * col_count, width).astype(np.float32)


def shards(
    latent, pred_grad, timesteps, labels, offsets, counts, patch_weight, time_in, time_out,
    label_table, modulation, qkv_weight, proj_weight, up_weight, down_weight, final_mod, final_weight,
):
    slots, lat_ch, tile_h, tile_w = latent.shape
    out_ch = pred_grad.shape[1]
    width = patch_weight.shape[1]
    ff = up_weight.shape[2]
    n_rows, n_cols = lax.axis_size("rows"), lax.axis_size("cols")
    z, c, w = lax.axis_index("rows"), lax.axis_index("cols"), lax.axis_index("wide")
    hp, wp = tile_h // 2, tile_w // 2
    tile_tok = hp * wp
    tokens = n_rows * tile_tok
    channels = lat_ch + out_ch
    lat_lanes, out_lanes = 2 * lat_ch, 2 * out_ch
    lanes = lat_lanes + out_lanes

    offset = pick(offsets, z)
    label = pick(labels, z)
    live = (z < counts[0]).astype(jnp.int32)
    scal = jnp.stack([z, c, w, offset, live, z, z, z]).astype(jnp.int32)

    def by_parity(image):
        ch = image.shape[1]
        blocks = image.reshape(slots, ch, hp, 2, wp, 2).transpose(0, 3, 2, 4, 5, 1)
        return blocks.reshape(slots, 2, tile_tok, 2 * ch)

    tiles = jnp.concatenate([by_parity(latent), by_parity(pred_grad)], axis=-1)
    tiles = jnp.stack(to_rows(tiles, z))

    half = time_in.shape[0] // 2
    freqs = np.exp(-math.log(10000.0) * np.arange(half, dtype=np.float32) / np.float32(half))
    angles = pick(timesteps, z).astype(F32) * jnp.asarray(freqs.astype(np.float32))
    feats = jnp.concatenate([jnp.cos(angles), jnp.sin(angles)]).astype(BF16).astype(F32)
    marks = jnp.stack([label // 32, label % 32]).astype(F32)
    feat_row = jnp.concatenate([feats, marks, jnp.zeros((width - 2 * half - 2,), F32)])[None]
    table_row = lax.dynamic_slice(label_table, (label, 0), (1, width)).astype(F32)

    mods, cond = kernel_call(
        cond_kernel,
        (feat_row, table_row, time_in, time_out, modulation, final_mod),
        [VM] * 6,
        [sds((3, 8, width), F32), sds((8, width), F32)],
        flops=2 * 8 * width * (14 * width + 3 * width),
        touched=2 * width * width * 17,
    )

    pos = pick(jnp.asarray(position_tables(n_rows * hp, wp, n_cols, width)), c)
    pad_patch = jnp.pad(
        patch_weight.reshape(2, lat_lanes, width), ((0, 0), (0, out_lanes), (0, 0))
    )
    fw = final_weight.reshape(width, 2, out_lanes).transpose(1, 0, 2)
    pad_final = jnp.pad(fw.transpose(0, 2, 1), ((0, 0), (lat_lanes, 0), (0, 0)))

    tok = (tokens, width)
    weight_scratch = {
        "qkv": pltpu.VMEM((width, 3 * width), BF16),
        "proj": pltpu.VMEM((width, width), BF16),
        "up": pltpu.VMEM((width, ff), BF16),
        "down": pltpu.VMEM((ff, width), BF16),
    }

    def sems(n):
        return pltpu.SemaphoreType.DMA((n,))

    unit_flop = 2 * tokens * width * width
    state0, patches, q0, kv0 = kernel_call(
        embed_kernel,
        (scal, tiles, pos, mods, pad_patch, qkv_weight),
        [SM, VM, VM, VM, VM, HB],
        [sds(tok, F32), sds((2, tokens, lanes), BF16), sds(tok, BF16), sds((tokens, 2 * width), BF16)],
        [weight_scratch["qkv"], sems(1)],
        flops=3 * unit_flop,
        touched=6 * width * width,
    )
    kv0p = swap(kv0, "cols", 1)
    probs_shape = sds((HEADS, 2, tokens, tokens), BF16)
    probs0, attended0, attn_out0, middle0, gp0, act0, branch0, state1, q1, kv1 = kernel_call(
        block_kernel,
        (state0, q0, kv0, kv0p, mods, proj_weight, up_weight, down_weight, qkv_weight),
        [VM] * 5 + [HB] * 4,
        [
            probs_shape, sds(tok, BF16), sds(tok, BF16), sds(tok, F32), sds((tokens, ff), BF16),
            sds((tokens, ff), BF16), sds(tok, BF16), sds(tok, F32), sds(tok, BF16),
            sds((tokens, 2 * width), BF16),
        ],
        [weight_scratch[k] for k in ("proj", "up", "down", "qkv")] + [sems(4)],
        flops=14 * unit_flop,
        touched=24 * width * width,
    )
    kv1p = swap(kv1, "cols", 1)
    block = width // 8
    probs1, attended1, attn_out1, mgrad1, pred, units1, rows_turn, gfinal = kernel_call(
        turn_kernel,
        (scal, state1, q1, kv1, kv1p, mods, patches, fw, pad_final, proj_weight, up_weight, down_weight),
        [SM] + [VM] * 8 + [HB] * 3,
        [
            probs_shape, sds(tok, BF16), sds(tok, BF16), sds(tok, F32),
            sds((2, tokens, out_lanes), BF16), sds((2, 16, 2 * block, width), BF16),
            sds((8, width), F32), sds((2, lanes, width), F32),
        ],
        [weight_scratch[k] for k in ("proj", "up", "down")]
        + [pltpu.VMEM((tokens, ff), BF16), pltpu.VMEM((tokens, ff), BF16), sems(3)],
        flops=28 * unit_flop,
        touched=24 * width * width,
    )
    held1 = reduce_units(units1, z, c, w)

    def attend_back(layer, q, kv, kvp, probs, attended, attn_out, mgrad):
        return kernel_call(
            partial(attend_back_kernel, layer),
            (q, kv, kvp, probs, attended, attn_out, mgrad, mods, proj_weight),
            [VM] * 8 + [HB],
            [
                sds(tok, BF16), sds((tokens, 2 * width), BF16), sds((tokens, 2 * width), BF16),
                sds((width, width), BF16), sds((8, width), F32),
            ],
            [weight_scratch["proj"], sems(1)],
            flops=12 * unit_flop,
            touched=12 * width * width,
        )

    dq1, dkv1, dkvs1, gproj1, rows_a1 = attend_back(
        1, q1, kv1, kv1p, probs1, attended1, attn_out1, mgrad1
    )
    dkvr1 = swap(dkvs1, "cols", 1)
    mgrad0, units2, rows_mid = kernel_call(
        middle_kernel,
        (
            state1, mgrad1, dq1, dkv1, dkvr1, gproj1, middle0, branch0, gp0, act0, mods,
            qkv_weight, up_weight, down_weight,
        ),
        [VM] * 11 + [HB] * 3,
        [sds(tok, F32), sds((2, 16, 3 * block, width), BF16), sds((8, width), F32)],
        [weight_scratch[k] for k in ("qkv", "up", "down")] + [sems(3)],
        flops=22 * unit_flop,
        touched=24 * width * width,
    )
    held2 = reduce_units(units2, z, c, w)
    dq0, dkv0, dkvs0, gproj0, rows_a0 = attend_back(
        0, q0, kv0, kv0p, probs0, attended0, attn_out0, mgrad0
    )
    dkvr0 = swap(dkvs0, "cols", 1)
    units3, lgrad, table = kernel_call(
        last_kernel,
        (
            scal, state0, mgrad0, dq0, dkv0, dkvr0, gproj0, mods, patches, pad_patch, cond,
            rows_turn, rows_a1, rows_mid, rows_a0, gfinal, qkv_weight,
        ),
        [SM] + [VM] * 15 + [HB],
        [
            sds((2, 16, block, width), BF16), sds((2, tokens, lat_lanes), F32),
            sds((ROWS + 2 * lanes, width), F32),
        ],
        [weight_scratch["qkv"], pltpu.VMEM((8, width), F32), sems(1)],
        flops=7 * unit_flop,
        touched=10 * width * width,
    )
    held3 = reduce_units(units3, z, c, w)

    def from_parity(tokens_out, ch):
        tiles_out = tokens_out.reshape(2, n_rows, tile_tok, 2 * ch).transpose(1, 0, 2, 3)
        arrived = jnp.stack(to_rows(tiles_out, z))
        ordered = jnp.stack([pick(arrived, z ^ s) for s in range(slots)])
        blocks = ordered.reshape(slots, 2, hp, wp, 2, ch).transpose(0, 5, 2, 1, 3, 4)
        return blocks.reshape(slots, ch, tile_h, tile_w)

    prediction = from_parity(pred, out_ch)
    latent_grad = from_parity(lgrad, lat_ch)
    rows, sums = gather_rows(table, z)
    classes = label_table.shape[0]
    g_time_in, g_time_out, g_table, g_mod, g_final_mod, g_patch, g_final = kernel_call(
        sums_kernel,
        (scal, rows, sums, modulation, final_mod, time_out),
        [SM] + [VM] * 5,
        [
            sds(time_in.shape, F32), sds(time_out.shape, F32), sds((classes, width), F32),
            sds((2, block, 6 * width), F32), sds(final_mod.shape, F32), sds(patch_weight.shape, F32),
            sds(final_weight.shape, F32),
        ],
        [pltpu.VMEM((width, rows.shape[1]), F32)],
        flops=2 * 16 * width * width * 30,
        touched=8 * width * width * 8,
    )
    g_qkv, g_proj, g_up, g_down = kernel_call(
        spread_kernel,
        (scal, *held1, *held2, *held3),
        [SM] + [VM] * 12,
        [
            sds((2, block, 3 * width), F32), sds((2, block, width), F32), sds((2, block, ff), F32),
            sds((2, ff // 8, width), F32),
        ],
        touched=width * width * 18,
    )
    return (
        prediction, latent_grad, g_patch, g_time_in, g_time_out, g_table, g_mod, g_qkv, g_proj,
        g_up, g_down, g_final_mod, g_final,
    )


def solution(mesh):
    tiled, split = P("wide", None, "rows", "cols"), P(None, ("rows", "cols"), None)
    return jax.shard_map(
        shards,
        mesh=mesh,
        in_specs=(tiled, tiled, P("wide"), P("wide"), P("wide"), P("wide")) + (P(),) * 11,
        out_specs=(tiled, tiled, P(), P(), P(), P(), split, split, split, split, split, P(), P()),
        check_vma=False,
    )
```

```python
from functools import partial
import math

import jax
import jax.numpy as jnp
import numpy as np
from jax import lax
from jax.experimental import pallas as pl
from jax.experimental.pallas import tpu as pltpu
from jax.sharding import PartitionSpec as P

HEADS = 6
HEAD_DIM = 64
PAIRS = HEADS // 2
LANES = 2 * HEAD_DIM
EPS = 1e-06
F32 = jnp.float32
BF16 = jnp.bfloat16
ROWS = 24
ROW_F, ROW_SHARED, ROW_ACT, ROW_COND, ROW_HID, ROW_FEAT = 12, 14, 15, 16, 17, 18

def dot(a, b):
    return jnp.dot(a, b, preferred_element_type=F32)


def dot_nt(a, b):
    return lax.dot_general(a, b, (((1,), (1,)), ((), ())), preferred_element_type=F32)


def dot_tn(a, b):
    return lax.dot_general(a, b, (((0,), (0,)), ((), ())), preferred_element_type=F32)


def sds(shape, dtype):
    return jax.ShapeDtypeStruct(shape, dtype)


def layer_norm(states):
    centred = states - jnp.mean(states, axis=-1, keepdims=True)
    inverse = lax.rsqrt(jnp.mean(centred * centred, axis=-1, keepdims=True) + EPS)
    return centred * inverse, inverse


def norm_back(grad, normed, inverse):
    mean_grad = jnp.mean(grad, axis=-1, keepdims=True)
    mean_cross = jnp.mean(grad * normed, axis=-1, keepdims=True)
    return inverse * (grad - mean_grad - normed * mean_cross)


def token_sum(values):
    return jnp.sum(values, axis=0, keepdims=True)


def head_masks(dtype):
    lane = lax.broadcasted_iota(jnp.int32, (1, LANES), 1)
    first = (lane < HEAD_DIM).astype(F32)
    return first.astype(dtype), (1.0 - first).astype(dtype)


def unit_place(zz, ww, cc):
    x, y = ww % 2, ww // 2
    return (x * 8 + y * 4 + zz) if cc == 0 else (y * 8 + x * 4 + zz)


def kernel_call(body, ins, outs, scratch=(), us=1.0, after=None):
    spaces = {"v": pltpu.VMEM, "p": pltpu.VMEM, "s": pltpu.SMEM, "h": pltpu.HBM}
    specs, arrays = [], []
    for kind, array in ins:
        specs.append(pl.BlockSpec(memory_space=spaces[kind]))
        if kind in "ph":
            array = pltpu.with_memory_space_constraint(array, spaces[kind])
        arrays.append(array)
    if after is not None:
        specs.append(pl.BlockSpec(memory_space=pl.ANY))
        arrays.append(after)

    def kernel(*refs):
        body(*refs[: len(ins)], *refs[len(arrays) :])

    return pl.pallas_call(
        kernel,
        in_specs=specs,
        out_specs=[pl.BlockSpec(memory_space=pltpu.VMEM)] * len(outs),
        out_shape=[sds(o[0], o[1]) if len(o) > 2 else pltpu.VMEM(o[0], o[1]) for o in outs],
        scratch_shapes=list(scratch),
        compiler_params=pltpu.CompilerParams(vmem_limit_bytes=24 * 1024 * 1024),
        cost_estimate=pl.CostEstimate(
            flops=int(us * 1.5e9), bytes_accessed=int(us * 1e6), transcendentals=0
        ),
    )(*arrays)


def one_hot(shape, test):
    first = lax.broadcasted_iota(jnp.int32, shape, 0)
    second = lax.broadcasted_iota(jnp.int32, shape, 1)
    return test(first, second).astype(F32).astype(BF16)


def places():
    return lax.axis_index("rows"), lax.axis_index("cols"), lax.axis_index("wide")


def wide_bits():
    _, c, w = places()
    x, y = lax.rem(w, 2), lax.rem(lax.div(w, 2), 2)
    return jnp.where(c == 0, x, y), jnp.where(c == 0, y, x)


def rows_at(index, count):
    return pl.ds(pl.multiple_of(index * count, 16), count)


def tiles_body(latent, pred_grad, *tiles):
    z, _, _ = places()
    _, lat_ch, height, wide = latent.shape
    out_ch = pred_grad.shape[1]
    chans, tok = lat_ch + out_ch, height * wide // 4
    half = wide // 2
    lanes = 2 * chans
    spread = [one_hot((tok, wide), lambda t, v: v == 2 * (t % half) + u) for u in range(2)]
    inside = [
        one_hot((tok, chans * height), lambda t, v: v % height == 2 * (t // half) + par).astype(F32)
        for par in range(2)
    ]

    def lane_of(channel, u):
        return jnp.where(
            channel < lat_ch, u * lat_ch + channel, 2 * lat_ch + u * out_ch + channel - lat_ch
        )

    fold = [
        one_hot((chans * height, lanes), lambda v, lane: lane == lane_of(v // height, u))
        for u in range(2)
    ]
    for k, tile in enumerate(tiles):
        image = jnp.concatenate(
            [
                latent[z ^ k].reshape(lat_ch * height, wide),
                pred_grad[z ^ k].reshape(out_ch * height, wide),
            ],
            axis=0,
        )
        wide_rows = [dot_nt(spread[u], image) for u in range(2)]
        for par in range(2):
            tile[par] = sum(
                dot((wide_rows[u] * inside[par]).astype(BF16), fold[u]) for u in range(2)
            ).astype(BF16)


def packed_tile(parities, lanes, order):
    tok = parities[0].shape[0]
    across = tok // order
    total = order * 2 * lanes
    block = 0.0
    for par in range(2):
        copy = one_hot((lanes, total), lambda a, b: b % (2 * lanes) == par * lanes + a)
        block = block + dot(parities[par].astype(BF16), copy)
    own = one_hot((tok, total), lambda t, b: b // (2 * lanes) == t // across).astype(F32)
    gather = one_hot((across, tok), lambda j, t: t % across == j)
    return dot(gather, (block * own).astype(BF16))


def unpacked_tile(block, chans, height, wide):
    lanes = 2 * chans
    half = wide // 2
    image = 0.0
    for u in range(2):
        chosen = one_hot(
            (chans * height, block.shape[1]),
            lambda v, b: b
            == (v % height) // 2 * 2 * lanes + v % 2 * lanes + u * chans + v // height,
        )
        column = dot_nt(chosen, block).astype(BF16)
        image = image + dot(column, one_hot((half, wide), lambda j, v: v == 2 * j + u))
    return image


def by_parity(first, second, offset):
    step = first.shape[0] // 32
    moved = jnp.concatenate([jnp.zeros((step, second.shape[1]), F32), second[:-step]], axis=0)
    return jnp.where(offset == 1, moved, first), jnp.where(offset == 1, first, second)


def cond_body(
    timesteps, labels, freqs, label_table, time_in, final_weight, positions, *rest,
):
    sources, (mods, cond, final_copy, pos), held = rest[:7], rest[7:11], rest[11:18]
    sem = rest[18]
    final_copy[...] = final_weight[...]
    sources, held = sources + (positions.at[lax.axis_index("cols")],), held + (pos,)
    copies = [
        pltpu.make_async_copy(source, target, sem.at[i])
        for i, (source, target) in enumerate(zip(sources, held))
    ]
    for copy in copies:
        copy.start()
    time_out, modulation, final_mod = held[:3]
    z, _, _ = places()
    label = labels[z]
    count, width = time_in.shape
    angles = jnp.full((8, count // 2), timesteps[z].astype(F32)) * freqs[...]
    feats = jnp.concatenate([jnp.cos(angles), jnp.sin(angles)], axis=-1).astype(BF16)
    hidden = dot(feats, time_in[...])
    act = (hidden * jax.nn.sigmoid(hidden)).astype(BF16)
    chosen = one_hot((8, label_table.shape[0]), lambda a, b: b == label)
    copies[0].wait()
    condition = dot(act, time_out[...]) + dot(chosen, label_table[...])
    shared = (condition * jax.nn.sigmoid(condition)).astype(BF16)
    mods[...] = jnp.zeros_like(mods)
    copies[1].wait()
    for layer in range(2):
        values = dot(shared, modulation[layer])
        for k in range(6):
            mods[layer, k : k + 1, :] = values[0:1, k * width : (k + 1) * width]
    copies[2].wait()
    values = dot(shared, final_mod[...])
    for k in range(2):
        mods[2, k : k + 1, :] = values[0:1, k * width : (k + 1) * width]
    lane = lax.broadcasted_iota(jnp.int32, (1, width - count), 1)
    marks = jnp.where(
        lane == 0, lax.div(label, 32), jnp.where(lane == 1, lax.rem(label, 32), 0)
    ).astype(F32)
    cond[...] = jnp.zeros_like(cond)
    cond[0:1, :] = shared[0:1].astype(F32)
    cond[1:2, :] = act[0:1].astype(F32)
    cond[2:3, :] = condition[0:1]
    cond[3:4, :] = hidden[0:1]
    cond[4:5, :] = jnp.concatenate([feats[0:1].astype(F32), marks], axis=-1)
    for copy in copies[3:]:
        copy.wait()


def qkv_forward(state, mods, layer, weight):
    width = state.shape[-1]
    normed, _ = layer_norm(state)
    inner = (normed * (1.0 + mods[layer, 1:2]) + mods[layer, 0:1]).astype(BF16)
    projected = dot(inner, weight[layer]).astype(BF16)
    return projected[:, :width], projected[:, width:]


def attend_forward(q, kv, kvp, probs, attended):
    width = q.shape[-1]
    masks = head_masks(BF16)
    for p in range(PAIRS):
        at = slice(p * LANES, (p + 1) * LANES)
        av = slice(width + p * LANES, width + (p + 1) * LANES)
        qp = q[:, at] * BF16(HEAD_DIM**-0.5)
        k0, v0, k1, v1 = kv[:, at], kv[:, av], kvp[:, at], kvp[:, av]
        total = None
        for h in range(2):
            qh = qp * masks[h]
            s0, s1 = dot_nt(qh, k0), dot_nt(qh, k1)
            peak = jnp.maximum(
                jnp.max(s0, axis=-1, keepdims=True), jnp.max(s1, axis=-1, keepdims=True)
            )
            e0, e1 = jnp.exp(s0 - peak), jnp.exp(s1 - peak)
            scale = 1.0 / (
                jnp.sum(e0, axis=-1, keepdims=True) + jnp.sum(e1, axis=-1, keepdims=True)
            )
            p0, p1 = (e0 * scale).astype(BF16), (e1 * scale).astype(BF16)
            probs[2 * p + h, 0] = p0
            probs[2 * p + h, 1] = p1
            part = dot(p0, v0 * masks[h]) + dot(p1, v1 * masks[h])
            total = part if total is None else total + part
        attended[:, at] = total.astype(BF16)


def mlp_forward(middle, mods, layer, up, down, gp, act):
    normed, _ = layer_norm(middle)
    inner = (normed * (1.0 + mods[layer, 4:5]) + mods[layer, 3:4]).astype(BF16)
    width = middle.shape[-1]
    branch = None
    for i in range(up.shape[-1] // width):
        at = slice(i * width, (i + 1) * width)
        hidden = dot(inner, up[layer, :, at])
        square = hidden * hidden
        root = math.sqrt(2.0 / math.pi)
        bent = jnp.tanh(root * hidden * (1.0 + 0.044715 * square))
        half = 0.5 * (1.0 + bent)
        activated = (hidden * half).astype(BF16)
        act[:, at] = activated
        slope = half + 0.5 * hidden * (1.0 - bent * bent) * (root * (1.0 + 3 * 0.044715 * square))
        gp[:, at] = slope.astype(BF16)
        part = dot(activated, down[layer, at, :])
        branch = part if branch is None else branch + part
    return branch


def put_units(keep, send, pair, place, size, at_row):
    first = lax.axis_index("cols") == 0
    block = pair[0].shape[0]
    own = jnp.where(first, place[0], place[1]) * size + at_row
    other = jnp.where(first, place[1], place[0]) * size + at_row
    keep[pl.ds(pl.multiple_of(own, 16), block), :] = jnp.where(first, pair[0], pair[1])
    send[pl.ds(pl.multiple_of(other, 16), block), :] = jnp.where(first, pair[1], pair[0])


def mlp_backward(grad, middle, branch, mods, layer, gp, act, up, down, keep, send, size, rows, first):
    width = middle.shape[-1]
    normed, inverse = layer_norm(middle)
    scale = 1.0 + mods[layer, 4:5]
    inner_t = (normed * scale + mods[layer, 3:4]).astype(BF16).T
    branch_grad = (mods[layer, 5:6] * grad).astype(BF16)
    inner_grad = None
    pieces = up.shape[-1] // width
    block = width // 8
    for i in range(pieces):
        at = slice(i * width, (i + 1) * width)
        act_grad = dot_nt(branch_grad, down[layer, at, :])
        hidden_grad = (act_grad * gp[:, at].astype(F32)).astype(BF16)
        part = dot_nt(hidden_grad, up[layer, :, at])
        inner_grad = part if inner_grad is None else inner_grad + part
        grad_up = dot(inner_t, hidden_grad).astype(BF16)
        for b in range(4):
            pair = [grad_up[(2 * b + cc) * block : (2 * b + cc + 1) * block] for cc in range(2)]
            put_units(keep, send, pair, [unit_place(b, i, cc) for cc in range(2)], size, 0)
        grad_down = dot_tn(act[:, at], branch_grad).astype(BF16)
        for j in range(4):
            pair = [grad_down[(4 * cc + j) * block : (4 * cc + j + 1) * block] for cc in range(2)]
            put_units(keep, send, pair, [unit_place(i, j, cc) for cc in range(2)], size, block)
    rows[first : first + 1, :] = token_sum(inner_grad)
    rows[first + 1 : first + 2, :] = token_sum(inner_grad * normed)
    rows[first + 2 : first + 3, :] = token_sum(grad * branch.astype(F32))
    return grad + norm_back(inner_grad * scale, normed, inverse)


def qkv_backward(
    state, middle_grad, dq, dkv, dkvr, mods, layer, weight, gproj, keep, send, size, at_row, flip, rows
):
    width = state.shape[-1]
    block = width // 8
    normed, inverse = layer_norm(state)
    scale = 1.0 + mods[layer, 1:2]
    inner_t = (normed * scale + mods[layer, 0:1]).astype(BF16).T
    dkv_sum = dkv[...] + dkvr[...]
    pieces = (dq[...], dkv_sum[:, :width], dkv_sum[:, width:])
    inner_grad = None

    def put(values, i):
        for b in range(4):
            pair = [values[(2 * b + cc) * block : (2 * b + cc + 1) * block] for cc in range(2)]
            place = [unit_place(b, i, cc ^ flip) for cc in range(2)]
            put_units(keep, send, pair, place, size, at_row)

    for i, piece in enumerate(pieces):
        part = dot_nt(piece, weight[layer, :, i * width : (i + 1) * width])
        inner_grad = part if inner_grad is None else inner_grad + part
        put(dot(inner_t, piece).astype(BF16), i)
    put(gproj[...], 3)
    rows[0:1, :] = token_sum(inner_grad)
    rows[1:2, :] = token_sum(inner_grad * normed)
    return middle_grad + norm_back(inner_grad * scale, normed, inverse)


def embed_body(
    offsets, t0, t1, t2, t3, pos, mods, patch_weight, qkv,
    state, q, kv, patches, tiles,
):
    z, _, _ = places()
    offset = offsets[z]
    for k, tile in enumerate((t0, t1, t2, t3)):
        tiles[k] = tile[...]
    count = tiles.shape[0]
    even = jnp.concatenate([tiles[z ^ t, 0] for t in range(count)], axis=0).astype(F32)
    odd = jnp.concatenate([tiles[z ^ t, 1] for t in range(count)], axis=0).astype(F32)
    step = even.shape[0] // 32
    later = jnp.concatenate([even[step:], jnp.zeros((step, even.shape[1]), F32)], axis=0)
    first = jnp.where(offset == 1, odd, even).astype(BF16)
    second = jnp.where(offset == 1, later, odd).astype(BF16)
    patches[0] = first
    patches[1] = second
    weight = patch_weight[...].astype(F32)
    lanes = weight.shape[0] // 2
    fill = jnp.zeros((even.shape[1] - lanes, weight.shape[1]), F32)
    upper = jnp.concatenate([weight[:lanes], fill], axis=0).astype(BF16)
    lower = jnp.concatenate([weight[lanes:], fill], axis=0).astype(BF16)
    values = dot(first, upper) + dot(second, lower) + pos[...]
    state[...] = values
    q[...], kv[...] = qkv_forward(values, mods, 0, qkv)


def block_body(
    state, q, kv, kvp, mods, proj, up, down, qkv,
    state1, q1, kv1, probs, attended, attn_out, middle, gp, act, branch,
):
    attend_forward(q, kv, kvp, probs, attended)
    m = mods
    attn = dot(attended[...], proj[0])
    attn_out[...] = attn.astype(BF16)
    mid = state[...] + m[0, 2:3] * attn
    middle[...] = mid
    out = mlp_forward(mid, m, 0, up, down, gp, act)
    branch[...] = out.astype(BF16)
    new = mid + m[0, 5:6] * out
    state1[...] = new
    q1[...], kv1[...] = qkv_forward(new, m, 1, qkv)


def turn_body(
    offsets, counts, state, q, kv, kvp, mods, patches, final_weight, proj, up, down,
    probs, attended, attn_out, middle_grad, keep, send, rows, gfinal, predt,
    gp, act, preds,
):
    z, _, _ = places()
    offset = offsets[z]
    live = (z < counts[0]).astype(F32)
    attend_forward(q, kv, kvp, probs, attended)
    m = mods
    attn = dot(attended[...], proj[1])
    attn_out[...] = attn.astype(BF16)
    middle = state[...] + m[1, 2:3] * attn
    branch = mlp_forward(middle, m, 1, up, down, gp, act)
    last = middle + m[1, 5:6] * branch
    normed, inverse = layer_norm(last)
    scale = 1.0 + m[2, 1:2]
    inner = (normed * scale + m[2, 0:1]).astype(BF16)
    weight = final_weight[...]
    lanes = weight.shape[1] // 2
    out = dot(inner, weight) * live
    preds[0], preds[1] = by_parity(out[:, :lanes], out[:, lanes:], offset)
    tok = preds.shape[1] // 4
    for k in range(4):
        cut = pl.ds(pl.multiple_of((z ^ k) * tok, 8), tok)
        predt[k] = packed_tile([preds[0, cut, :], preds[1, cut, :]], lanes, 8)
    across = weight.astype(F32).T
    chosen = patches
    fill = jnp.zeros((chosen.shape[2] - lanes, across.shape[1]), F32)
    upper = jnp.concatenate([fill, across[:lanes]], axis=0).astype(BF16)
    lower = jnp.concatenate([fill, across[lanes:]], axis=0).astype(BF16)
    inner_grad = (dot(chosen[0], upper) + dot(chosen[1], lower)) * live
    gfinal[0] = dot_tn(chosen[0], inner) * live
    gfinal[1] = dot_tn(chosen[1], inner) * live
    rows[...] = jnp.zeros_like(rows)
    rows[3:4, :] = token_sum(inner_grad)
    rows[4:5, :] = token_sum(inner_grad * normed)
    grad = norm_back(inner_grad * scale, normed, inverse)
    size = 2 * (weight.shape[0] // 8)
    middle_grad[...] = mlp_backward(
        grad, middle, branch, m, 1, gp, act, up, down, keep, send, size, rows, 0
    )


def attend_back_body(
    layer, q, kv, kvp, probs, attended, attn_out, middle_grad, mods, proj,
    dq, dkv, gproj, dkvs, rows,
):
    grad = middle_grad[...]
    attn_grad = (mods[layer, 2:3] * grad).astype(BF16)
    attended_grad = dot_nt(attn_grad, proj[layer]).astype(BF16)
    masks = head_masks(BF16)
    width = q.shape[-1]
    for p in range(PAIRS):
        at = slice(p * LANES, (p + 1) * LANES)
        av = slice(width + p * LANES, width + (p + 1) * LANES)
        qp = q[:, at] * BF16(HEAD_DIM**-0.5)
        dop = attended_grad[:, at]
        ks, vs = (kv[:, at], kvp[:, at]), (kv[:, av], kvp[:, av])
        total = None
        parts = [None] * 4
        for h in range(2):
            doh = dop * masks[h]
            qh = qp * masks[h]
            ps = [probs[2 * p + h, i] for i in range(2)]
            dps = [dot_nt(doh, vs[i]) for i in range(2)]
            pfs = [ps[i].astype(F32) for i in range(2)]
            inner = sum(jnp.sum(dps[i] * pfs[i], axis=-1, keepdims=True) for i in range(2))
            for i in range(2):
                ds = (pfs[i] * (dps[i] - inner)).astype(BF16)
                part = dot(ds, ks[i] * masks[h])
                total = part if total is None else total + part
                dk, dv = dot_tn(ds, qh), dot_tn(ps[i], doh)
                parts[2 * i] = dk if h == 0 else parts[2 * i] + dk
                parts[2 * i + 1] = dv if h == 0 else parts[2 * i + 1] + dv
        dq[:, at] = (total * HEAD_DIM**-0.5).astype(BF16)
        dkv[:, at] = parts[0].astype(BF16)
        dkv[:, av] = parts[1].astype(BF16)
        dkvs[:, at] = parts[2].astype(BF16)
        dkvs[:, av] = parts[3].astype(BF16)
    rows[...] = jnp.zeros_like(rows)
    rows[0:1, :] = token_sum(grad * attn_out[...].astype(F32))
    gproj[...] = dot_tn(attended[...], attn_grad).astype(BF16)


def middle_body(
    state1, middle_grad1, dq, dkv, dkvr, gproj, middle, branch, gp, act, mods, qkv, up, down,
    middle_grad, keep, send, rows,
):
    width = dq.shape[-1]
    size = 3 * (width // 8)
    rows[...] = jnp.zeros_like(rows)
    m = mods
    grad = qkv_backward(
        state1[...], middle_grad1[...], dq, dkv, dkvr, m, 1, qkv, gproj, keep, send, size,
        2 * (width // 8), 0, rows,
    )
    middle_grad[...] = mlp_backward(
        grad, middle[...], branch[...], m, 0, gp, act, up, down, keep, send, size,
        rows, 2,
    )


def last_body(
    offsets, state0, middle_grad, dq, dkv, dkvr, gproj, mods, patches, patch_weight, cond,
    rows_turn, rows_a1, rows_mid, rows_a0, gfinal, qkv,
    keep, send, lgradt, rows, lgrads, table,
):
    z, _, _ = places()
    offset = offsets[z]
    width = dq.shape[-1]
    block = width // 8
    grad = qkv_backward(
        state0[...], middle_grad[...], dq, dkv, dkvr, mods, 0, qkv, gproj, keep, send, block,
        0, 1, rows,
    )
    embed_grad = grad.astype(BF16)
    chosen = patches
    gp0, gp1 = dot_tn(chosen[0], embed_grad), dot_tn(chosen[1], embed_grad)
    chans = patch_weight.shape[0] // 2
    window = dot_nt(embed_grad, patch_weight[...])
    lgrads[0], lgrads[1] = by_parity(window[:, :chans], window[:, chans:], offset)
    tok = lgrads.shape[1] // 4
    for k in range(4):
        cut = pl.ds(pl.multiple_of((z ^ k) * tok, 8), tok)
        parts = [lgrads[0, cut, :], lgrads[1, cut, :]]
        leading = [part.astype(BF16).astype(F32) for part in parts]
        lgradt[k, :, 0:128] = packed_tile(leading, chans, 8)
        lgradt[k, :, 128:256] = packed_tile([a - b for a, b in zip(parts, leading)], chans, 8)
    table[...] = jnp.zeros_like(table)
    table[0:2, :] = rows[0:2, :]
    table[2:3, :] = rows_a0[0:1, :]
    table[3:6, :] = rows_mid[2:5, :]
    table[6:8, :] = rows_mid[0:2, :]
    table[8:9, :] = rows_a1[0:1, :]
    table[9:12, :] = rows_turn[0:3, :]
    table[12:14, :] = rows_turn[3:5, :]
    table[14:19, :] = 0.5 * cond[0:5, :]
    table[ROWS : ROWS + chans, :] = gp0[:chans]
    table[ROWS + chans : ROWS + 2 * chans, :] = gp1[:chans]
    final = gfinal
    outs = final.shape[1] - chans
    base = ROWS + 2 * chans
    table[base : base + outs, :] = final[0, chans:, :]
    table[base + outs : base + 2 * outs, :] = final[1, chans:, :]
    keep[16 * block :] = table[...].astype(BF16)
    send[16 * block :] = table[...].astype(BF16)


def split_body(keep, recv, keep_out, send_out, bit_at):
    half = keep.shape[0] // 2
    bit = wide_bits()[bit_at]
    keep_out[...] = keep[rows_at(bit, half)] + recv[rows_at(bit, half)]
    send_out[...] = keep[rows_at(1 - bit, half)] + recv[rows_at(1 - bit, half)]


def one_split_body(bit_at, keep, recv, keep_out, send_out):
    split_body(keep, recv, keep_out, send_out, bit_at)


def to_chips(held, recv, outs):
    z, _, _ = places()
    size = held.shape[0] // 4
    for k, out in enumerate(outs):
        out[...] = held[rows_at(z ^ k, size)] + recv[rows_at(z ^ k, size)]


def second_body(keep2, recv2, held1, recv1, keep2_out, send2_out, *units1):
    split_body(keep2, recv2, keep2_out, send2_out, 0)
    to_chips(held1, recv1, units1)


def third_body(keep2, recv2, keep3, recv3, u0, u1, u2, u3, keep2_out, keep3_out, table, unit1, send):
    half2 = keep2.shape[0] // 2
    size3 = keep3.shape[0] - 80
    half3 = size3 // 2
    bit = wide_bits()[1]
    keep2_out[...] = keep2[rows_at(bit, half2)] + recv2[rows_at(bit, half2)]
    send[0:half2] = keep2[rows_at(1 - bit, half2)] + recv2[rows_at(1 - bit, half2)]
    keep3_out[...] = keep3[rows_at(bit, half3)] + recv3[rows_at(bit, half3)]
    send[half2 : half2 + half3] = keep3[rows_at(1 - bit, half3)] + recv3[rows_at(1 - bit, half3)]
    rows = keep3[size3:] + recv3[size3:]
    table[...] = rows
    send[half2 + half3 :] = rows
    unit1[...] = (
        u0[...].astype(F32) + u1[...].astype(F32) + u2[...].astype(F32) + u3[...].astype(F32)
    ).astype(BF16)


def fourth_body(keep2, keep3, table, recv, z0, z1, z2, z3, keep3_out, pair_out, send):
    z, _, _ = places()
    size2, size3 = keep2.shape[0], keep3.shape[0]
    unit2, half3 = size2 // 4, size3 // 2
    for k, out in enumerate((z0, z1, z2, z3)):
        out[...] = keep2[rows_at(z ^ k, unit2)] + recv[rows_at(z ^ k, unit2)]
    bit = wide_bits()[0]

    def half(index):
        start = pl.multiple_of(index * half3, 16)
        return keep3[pl.ds(start, half3)] + recv[pl.ds(pl.multiple_of(start + size2, 16), half3)]

    keep3_out[...] = half(bit)
    send[0:half3] = half(1 - bit)
    mine = table[...].astype(F32)
    other = recv[size2 + size3 :].astype(F32)
    pair = jnp.concatenate(
        [mine[:ROWS], other[:ROWS], mine[ROWS : ROWS + 48] + other[ROWS : ROWS + 48]], axis=0
    ).astype(BF16)
    pair_out[...] = pair
    send[half3:] = pair


def fifth_body(keep3, pair, recv, predt, lgradt, z0, z1, z2, z3, four):
    z, c, w = places()
    size3 = keep3.shape[0]
    unit3 = size3 // 4
    first = jnp.where(c == 0, 2, 1)
    second = 3 - first
    spot = lax.rem(w, 4)
    mine, other = pair[...].astype(F32), recv[size3:].astype(F32)
    four[spot] = mine[:ROWS]
    four[spot ^ first] = mine[ROWS : 2 * ROWS]
    four[spot ^ second] = other[:ROWS]
    four[spot ^ first ^ second] = other[ROWS : 2 * ROWS]
    rows = jnp.concatenate([four[2 * c], four[2 * c + 1]], axis=0).astype(BF16)
    sums = (mine[2 * ROWS :] + other[2 * ROWS :]).astype(BF16)
    base = unit3 + 2 * ROWS
    for k, out in enumerate((z0, z1, z2, z3)):
        out[0:unit3] = keep3[rows_at(z ^ k, unit3)] + recv[rows_at(z ^ k, unit3)]
        out[unit3:base] = rows
        out[base : base + 48] = sums
        tile = jnp.concatenate([lgradt[k], predt[k]], axis=0)
        out[base + 48 : base + 64, 0:256] = tile.astype(BF16)
        out[base + 48 : base + 64, 256:384] = jnp.zeros((16, 128), BF16)


def sixth_body(*refs):
    twos, threes = refs[:4], refs[4:8]
    unit, half, sums, tiles = refs[8:]
    size2 = twos[0].shape[0]
    size3 = threes[0].shape[0] - 2 * ROWS - 64
    base = size3 + 2 * ROWS
    unit[0:size2] = sum(t[...].astype(F32) for t in twos).astype(BF16)
    unit[size2:] = sum(t[0:size3].astype(F32) for t in threes).astype(BF16)
    sums[...] = sum(t[base : base + 48].astype(F32) for t in threes)
    for k, t in enumerate(threes):
        half[2 * ROWS * k : 2 * ROWS * (k + 1)] = t[size3:base]
        tiles[k] = t[base + 48 :]


def silu_slope(values):
    sigmoid = jax.nn.sigmoid(values)
    return sigmoid * (1.0 + values * (1.0 - sigmoid))


def sums_body(
    own, other, sums, modulation, final_mod, time_out,
    g_time_in, g_time_out, g_table, g_mod, g_final_mod, g_patch, g_final,
    table, shared_t,
):
    z, c, _ = places()
    half = own.shape[0]
    parts = table.shape[0]
    for i in range(parts):
        at = slice(128 * i, 128 * (i + 1))
        table[i, 0:half] = own[:, at].astype(F32)
        table[i, half:] = other[:, at].astype(F32)
    samples = table.shape[1] // ROWS

    def rows(r):
        pieces = [table[i, pl.ds(r, samples, stride=ROWS), :] for i in range(parts)]
        return jnp.concatenate(pieces, axis=-1)

    mods = [
        jnp.concatenate([rows(6 * layer + k) for k in range(6)], axis=-1).astype(BF16)
        for layer in range(2)
    ]
    fmods = jnp.concatenate([rows(ROW_F), rows(ROW_F + 1)], axis=-1).astype(BF16)
    shared_t[...] = rows(ROW_SHARED).T
    block = g_mod.shape[1]
    start = pl.multiple_of((z * 2 + c) * block, 8)
    mine = shared_t[pl.ds(start, block), :].astype(BF16)
    for layer in range(2):
        g_mod[layer] = dot(mine, mods[layer])
    g_final_mod[...] = dot(shared_t[...].astype(BF16), fmods)
    patch = g_patch.shape[0]
    g_patch[...] = sums[:patch, :]
    g_final[...] = sums[patch:, :].T
    shared_grad = dot_nt(fmods, final_mod[...])
    for layer in range(2):
        shared_grad += dot_nt(mods[layer], modulation[layer])
    cond_grad = shared_grad * silu_slope(rows(ROW_COND))
    cond_low = cond_grad.astype(BF16)
    feats = rows(ROW_FEAT)
    count = g_time_in.shape[0]
    label = (feats[:, count : count + 1] * 32.0 + feats[:, count + 1 : count + 2]).astype(jnp.int32)
    classes = g_table.shape[0]
    padded = (classes + 127) // 128 * 128
    lane = lax.broadcasted_iota(jnp.int32, (samples, padded), 1)
    hot = (lane == label).astype(F32).T[:classes].astype(BF16)
    cond_rest = (cond_grad - cond_low.astype(F32)).astype(BF16)
    g_table[...] = dot(hot, cond_low) + dot(hot, cond_rest)
    g_time_out[...] = dot(rows(ROW_ACT).T.astype(BF16), cond_low)
    time_grad = dot_nt(cond_low, time_out[...]) * silu_slope(rows(ROW_HID))
    g_time_in[...] = dot(feats[:, :count].T.astype(BF16), time_grad.astype(BF16))


def spread_body(*refs):
    ones, others, tiles = refs[:4], refs[4:8], refs[8]
    g_qkv, g_proj, g_up, g_down, prediction, latent_grad = refs[9:]
    z, _, w = places()
    width = g_proj.shape[-1]
    block = g_proj.shape[1]
    spot = lax.rem(w, 4)

    def place_mlp(layer, piece, unit):
        cols = pl.ds(pl.multiple_of(unit * width, 128), width)
        g_up[layer, :, cols] = piece[0:block].astype(F32)
        down_rows = pl.ds(pl.multiple_of(unit * block, 8), block)
        g_down[layer, down_rows, :] = piece[block : 2 * block].astype(F32)

    def place_attn(layer, piece, unit):
        @pl.when(unit < 3)
        def _():
            cols = pl.ds(pl.multiple_of(unit * width, 128), width)
            g_qkv[layer, :, cols] = piece.astype(F32)

        @pl.when(unit == 3)
        def _():
            g_proj[layer] = piece.astype(F32)

    for k in range(4):
        unit = spot ^ k
        place_mlp(1, ones[k][...], unit)
        both = others[k]
        place_mlp(0, both[0 : 2 * block], unit)
        place_attn(1, both[2 * block : 3 * block], unit)
        place_attn(0, both[3 * block :], unit)
        _, out_ch, height, wide = prediction.shape
        lat_ch = latent_grad.shape[1]
        tile = tiles[k].astype(F32)
        image = unpacked_tile(tile[8:16, 0:256].astype(BF16), out_ch, height, wide)
        prediction[z ^ k] = image.astype(BF16).reshape(out_ch, height, wide)
        image = unpacked_tile(tile[0:8, 0:128].astype(BF16), lat_ch, height, wide)
        image = image + unpacked_tile(tile[0:8, 128:256].astype(BF16), lat_ch, height, wide)
        latent_grad[z ^ k] = image.reshape(lat_ch, height, wide)


def swap(value, axis, bit):
    count = lax.axis_size(axis)
    return lax.ppermute(value, axis, [(i, i ^ bit) for i in range(count)])


def swap_by_core(value, bits):
    wide, cores = lax.axis_size("wide"), lax.axis_size("cols")
    pairs = [
        (w * cores + c, (w ^ bits[c % 2]) * cores + c) for w in range(wide) for c in range(cores)
    ]
    return lax.ppermute(value, ("wide", "cols"), pairs)


FIRST, SECOND = (1, 2), (2, 1)


def rest_sum(value):
    bit = 4
    while bit < lax.axis_size("wide"):
        value = (value.astype(F32) + swap(value, "wide", bit).astype(F32)).astype(value.dtype)
        bit *= 2
    return value


def rest_gather(value):
    bit = 4
    while bit < lax.axis_size("wide"):
        value = jnp.concatenate([value, swap(value, "wide", bit)])
        bit *= 2
    return value


def position_tables(row_count, col_count, cores, width):
    quarter = width // 4
    omega = np.exp(-math.log(10000.0) * np.arange(quarter) / quarter)
    row_angle = np.arange(row_count)[:, None] * omega[None, :]
    col_angle = np.arange(col_count * cores)[:, None] * omega[None, :]
    row_part = np.concatenate([np.sin(row_angle), np.cos(row_angle)], axis=-1)
    col_part = np.concatenate([np.sin(col_angle), np.cos(col_angle)], axis=-1)
    col_part = col_part.reshape(cores, 1, col_count, width // 2)
    table = np.concatenate(
        [
            np.broadcast_to(row_part[None, :, None, :], (cores, row_count, col_count, width // 2)),
            np.broadcast_to(col_part, (cores, row_count, col_count, width // 2)),
        ],
        axis=-1,
    )
    return table.reshape(cores, row_count * col_count, width).astype(np.float32)


def shards(
    latent, pred_grad, timesteps, labels, offsets, counts, patch_weight, time_in, time_out,
    label_table, modulation, qkv_weight, proj_weight, up_weight, down_weight, final_mod, final_weight,
):
    slots, lat_ch, tile_h, tile_w = latent.shape
    out_ch = pred_grad.shape[1]
    width = patch_weight.shape[1]
    ff = up_weight.shape[2]
    n_rows, n_cols = lax.axis_size("rows"), lax.axis_size("cols")
    hp, wp = tile_h // 2, tile_w // 2
    tile_tok = hp * wp
    tokens = n_rows * tile_tok
    lanes = 2 * (lat_ch + out_ch)
    block = width // 8
    tok, wide_tok, double = (tokens, width), (tokens, ff), (tokens, 2 * width)

    tiles = kernel_call(
        tiles_body, [("v", latent), ("v", pred_grad)], [((2, tile_tok, lanes), BF16)] * n_rows, us=1
    )
    tiles = [tiles[0]] + [swap(tiles[k], "rows", k) for k in range(1, n_rows)]
    half = time_in.shape[0] // 2
    freqs = np.exp(-math.log(10000.0) * np.arange(half, dtype=np.float32) / np.float32(half))
    positions = jnp.asarray(position_tables(n_rows * hp, wp, n_cols, width))
    weights = (time_out, modulation, final_mod, qkv_weight, proj_weight, up_weight, down_weight)
    mods, cond, final_v, pos, time_out_v, modulation_v, final_mod_v, qkv, proj, up, down = kernel_call(
        cond_body,
        [("s", timesteps), ("s", labels), ("v", jnp.asarray(freqs.astype(np.float32))[None])]
        + [("v", label_table), ("v", time_in), ("v", final_weight), ("h", positions)]
        + [("h", weight) for weight in weights],
        [((3, 8, width), F32), ((8, width), F32), (final_weight.shape, BF16), (tok, F32)]
        + [(weight.shape, BF16) for weight in weights],
        [pltpu.SemaphoreType.DMA((len(weights) + 1,))],
        us=5,
    )
    probs_shape = (HEADS, 2, tokens, tokens)
    state0, q0, kv0, patches = kernel_call(
        embed_body,
        [("s", offsets)]
        + [("v", t) for t in tiles]
        + [("p", pos), ("p", mods), ("v", patch_weight), ("p", qkv)],
        [(tok, F32), (tok, BF16), (double, BF16), ((2, tokens, lanes), BF16)],
        [pltpu.VMEM((n_rows, 2, tile_tok, lanes), BF16)],
        us=2,
    )
    kv0p = swap(kv0, "cols", 1)
    state1, q1, kv1, probs0, attended0, attn_out0, middle0, gp0, act0, branch0 = kernel_call(
        block_body,
        [("p", state0), ("p", q0), ("p", kv0), ("v", kv0p)]
        + [("p", a) for a in (mods, proj, up, down, qkv)],
        [
            (tok, F32), (tok, BF16), (double, BF16), (probs_shape, BF16), (tok, BF16), (tok, BF16),
            (tok, F32), (wide_tok, BF16), (wide_tok, BF16), (tok, BF16),
        ],
        us=7,
    )
    kv1p = swap(kv1, "cols", 1)
    probs1, attended1, attn_out1, mgrad1, keep1, send1, rows_turn, gfinal, predt = kernel_call(
        turn_body,
        [("s", offsets), ("s", counts), ("p", state1), ("p", q1), ("p", kv1), ("v", kv1p)]
        + [("p", mods), ("p", patches), ("p", final_v), ("p", proj), ("p", up), ("p", down)],
        [
            (probs_shape, BF16), (tok, BF16), (tok, BF16), (tok, F32), ((16 * 2 * block, width), BF16),
            ((16 * 2 * block, width), BF16), ((8, width), F32), ((2, lanes, width), F32),
            ((4, wp, 4 * out_ch * hp), F32),
        ],
        [
            pltpu.VMEM(wide_tok, BF16), pltpu.VMEM(wide_tok, BF16),
            pltpu.VMEM((2, tokens, 2 * out_ch), F32),
        ],
        us=10,
    )
    recv1 = swap(send1, "cols", 1)

    def attend_back(layer, q, kv, kvp, *saved, after):
        return kernel_call(
            partial(attend_back_body, layer),
            [("p", q), ("p", kv), ("v", kvp)] + [("p", a) for a in saved + (mods, proj)],
            [
                (tok, BF16), (double, BF16), ((width, width), BF16), (double, BF16), ((8, width), F32),
            ],
            us=5,
            after=after,
        )

    dq1, dkv1, gproj1, dkvs1, rows_a1 = attend_back(
        1, q1, kv1, kv1p, probs1, attended1, attn_out1, mgrad1, after=None
    )
    dkvr1 = swap(dkvs1, "cols", 1)
    keep1, send1 = kernel_call(
        partial(one_split_body, 0),
        [("p", keep1), ("v", recv1)],
        [((8 * 2 * block, width), BF16)] * 2,
        us=0.5,
        after=rows_a1,
    )
    recv1 = swap_by_core(send1, FIRST)
    mgrad0, keep2, send2, rows_mid = kernel_call(
        middle_body,
        [("p", a) for a in (state1, mgrad1, dq1, dkv1)]
        + [("v", dkvr1)]
        + [("p", a) for a in (gproj1, middle0, branch0, gp0, act0, mods, qkv, up, down)],
        [
            (tok, F32), ((16 * 3 * block, width), BF16), ((16 * 3 * block, width), BF16),
            ((8, width), F32),
        ],
        us=6,
        after=keep1,
    )
    recv2 = swap(send2, "cols", 1)
    keep1, send1 = kernel_call(
        partial(one_split_body, 1),
        [("p", keep1), ("v", recv1)],
        [((4 * 2 * block, width), BF16)] * 2,
        us=0.5,
        after=rows_mid,
    )
    recv1 = swap_by_core(send1, SECOND)
    dq0, dkv0, gproj0, dkvs0, rows_a0 = attend_back(
        0, q0, kv0, kv0p, probs0, attended0, attn_out0, mgrad0, after=keep1
    )
    dkvr0 = swap(dkvs0, "cols", 1)
    keep2, send2, *units1 = kernel_call(
        second_body,
        [("p", keep2), ("v", recv2), ("p", keep1), ("v", recv1)],
        [((8 * 3 * block, width), BF16)] * 2 + [((2 * block, width), BF16)] * 4,
        us=1,
        after=rows_a0,
    )
    recv2 = swap_by_core(send2, FIRST)
    units1 = [units1[0]] + [swap(units1[k], "rows", k) for k in range(1, n_rows)]
    keep3, send3, lgradt = kernel_call(
        last_body,
        [("s", offsets), ("p", state0), ("p", mgrad0), ("p", dq0), ("p", dkv0), ("v", dkvr0)]
        + [("p", gproj0), ("p", mods), ("p", patches), ("v", patch_weight), ("p", cond)]
        + [("p", a) for a in (rows_turn, rows_a1, rows_mid, rows_a0, gfinal, qkv)],
        [
            ((16 * block + 80, width), BF16), ((16 * block + 80, width), BF16),
            ((4, wp, 4 * lat_ch * hp * 2), F32),
        ],
        [
            pltpu.VMEM((8, width), F32), pltpu.VMEM((2, tokens, 2 * lat_ch), F32),
            pltpu.VMEM((80, width), F32),
        ],
        us=3,
        after=keep2,
    )
    recv3 = swap(send3, "cols", 1)
    keep2, keep3, table, unit1, send = kernel_call(
        third_body,
        [("p", keep2), ("v", recv2), ("p", keep3), ("v", recv3), ("p", units1[0])]
        + [("v", u) for u in units1[1:]],
        [
            ((4 * 3 * block, width), BF16), ((8 * block, width), BF16), ((80, width), BF16),
            ((2 * block, width), BF16), ((4 * 3 * block + 8 * block + 80, width), BF16),
        ],
        us=1,
    )
    recv = swap_by_core(send, SECOND)
    unit1 = rest_sum(unit1)
    ones = [unit1] + [swap(unit1, "wide", k) for k in range(1, 4)]
    *twos, keep3, pair, send = kernel_call(
        fourth_body,
        [("p", keep2), ("p", keep3), ("p", table), ("v", recv)],
        [((3 * block, width), BF16)] * 4
        + [
            ((4 * block, width), BF16), ((2 * ROWS + 48, width), BF16),
            ((4 * block + 2 * ROWS + 48, width), BF16),
        ],
        us=1,
    )
    recv = swap_by_core(send, FIRST)
    twos = [twos[0]] + [swap(twos[k], "rows", k) for k in range(1, n_rows)]
    threes = kernel_call(
        fifth_body,
        [("p", keep3), ("p", pair), ("v", recv), ("p", predt), ("p", lgradt)],
        [((block + 2 * ROWS + 64, width), BF16)] * 4,
        [pltpu.VMEM((4, ROWS, width), F32)],
        us=1,
    )
    threes = [threes[0]] + [swap(threes[k], "rows", k) for k in range(1, n_rows)]
    unit, rows, sums, tiles = kernel_call(
        sixth_body,
        [("v", t) for t in twos + threes],
        [
            ((4 * block, width), BF16), ((4 * 2 * ROWS, width), BF16), ((48, width), F32),
            ((4, 16, width), BF16),
        ],
        us=1,
    )
    unit, sums = rest_sum(unit), rest_sum(sums)
    others = [unit] + [swap(unit, "wide", k) for k in range(1, 4)]
    rows_other = rest_gather(swap(rows, "cols", 1))
    rows = rest_gather(rows)
    classes = label_table.shape[0]
    g_time_in, g_time_out, g_table, g_mod, g_final_mod, g_patch, g_final = kernel_call(
        sums_body,
        [("v", rows), ("v", rows_other), ("v", sums)]
        + [("p", a) for a in (modulation_v, final_mod_v, time_out_v)],
        [
            (shape, F32, 0)
            for shape in (
                time_in.shape, time_out.shape, (classes, width), (2, block, 6 * width), final_mod.shape,
                patch_weight.shape, final_weight.shape,
            )
        ],
        [
            pltpu.VMEM((width // 128, 2 * rows.shape[0], 128), F32),
            pltpu.VMEM((width, 2 * rows.shape[0] // ROWS), F32),
        ],
        us=5,
    )
    g_qkv, g_proj, g_up, g_down, prediction, latent_grad = kernel_call(
        spread_body,
        [("v", a) for a in ones + others] + [("v", tiles)],
        [
            ((2, block, 3 * width), F32, 0), ((2, block, width), F32, 0), ((2, block, ff), F32, 0),
            ((2, ff // 8, width), F32, 0), ((slots, out_ch, tile_h, tile_w), BF16, 0),
            (latent.shape, F32, 0),
        ],
        us=2,
    )
    return (
        prediction, latent_grad, g_patch, g_time_in, g_time_out, g_table, g_mod, g_qkv, g_proj,
        g_up, g_down, g_final_mod, g_final,
    )


def solution(mesh):
    tiled, split = P("wide", None, "rows", "cols"), P(None, ("rows", "cols"), None)
    return jax.shard_map(
        shards,
        mesh=mesh,
        in_specs=(tiled, tiled, P("wide"), P("wide"), P("wide"), P("wide")) + (P(),) * 11,
        out_specs=(tiled, tiled, P(), P(), P(), P(), split, split, split, split, split, P(), P()),
        check_vma=False,
    )
```

```python
from functools import partial
import math

import jax
import jax.numpy as jnp
import numpy as np
from jax import lax
from jax.experimental import pallas as pl
from jax.experimental.pallas import tpu as pltpu
from jax.sharding import PartitionSpec as P

HEADS = 6
HEAD_DIM = 64
PAIRS = HEADS // 2
LANES = 2 * HEAD_DIM
EPS = 1e-06
F32 = jnp.float32
BF16 = jnp.bfloat16
ROWS = 12
ROW_SHARED, ROW_ACT, ROW_COND, ROW_HID, ROW_FEAT = 5, 6, 7, 8, 9
US = {
    "cond": 5, "embed": 2, "block": 6, "turn": 9, "back": 20, "middle": 4, "last": 4, "sums": 5, "spread": 2,
    "A1": 0.05, "A2": 0.05, "A2b": 0.05, "A3": 0.05, "A3b": 0.05, "A4": 30, "A4b": 0.05, "A5": 0.05, "A6": 0.05, "S1": 0.05, "U2": 0.05,
    "U1": 20,
}


def dot(a, b):
    return jnp.dot(a, b, preferred_element_type=F32)


def dot_nt(a, b):
    return lax.dot_general(a, b, (((1,), (1,)), ((), ())), preferred_element_type=F32)


def dot_tn(a, b):
    return lax.dot_general(a, b, (((0,), (0,)), ((), ())), preferred_element_type=F32)


def sds(shape, dtype):
    return jax.ShapeDtypeStruct(shape, dtype)


def layer_norm(states):
    centred = states - jnp.mean(states, axis=-1, keepdims=True)
    inverse = lax.rsqrt(jnp.mean(centred * centred, axis=-1, keepdims=True) + EPS)
    return centred * inverse, inverse


def norm_back(grad, normed, inverse):
    mean_grad = jnp.mean(grad, axis=-1, keepdims=True)
    mean_cross = jnp.mean(grad * normed, axis=-1, keepdims=True)
    return inverse * (grad - mean_grad - normed * mean_cross)


def token_sum(values):
    return jnp.sum(values, axis=0, keepdims=True)


def head_masks(dtype):
    lane = lax.broadcasted_iota(jnp.int32, (1, LANES), 1)
    first = (lane < HEAD_DIM).astype(F32)
    return first.astype(dtype), (1.0 - first).astype(dtype)


def unit_place(zz, ww, cc):
    x, y = ww % 2, ww // 2
    return (x * 8 + y * 4 + zz) if cc == 0 else (y * 8 + x * 4 + zz)


def kernel_call(body, ins, outs, scratch=(), us=1.0, after=None):
    spaces = {"v": pltpu.VMEM, "p": pltpu.VMEM, "s": pltpu.SMEM, "h": pltpu.HBM}
    specs, arrays = [], []
    for kind, array in ins:
        specs.append(pl.BlockSpec(memory_space=spaces[kind]))
        if kind in "ph":
            array = pltpu.with_memory_space_constraint(array, spaces[kind])
        arrays.append(array)
    if after is not None:
        specs.append(pl.BlockSpec(memory_space=pl.ANY))
        arrays.append(after)

    def kernel(*refs):
        body(*refs[: len(ins)], *refs[len(arrays) :])

    return pl.pallas_call(
        kernel,
        in_specs=specs,
        out_specs=[pl.BlockSpec(memory_space=pltpu.VMEM)] * len(outs),
        out_shape=[sds(o[0], o[1]) if len(o) > 2 else pltpu.VMEM(o[0], o[1]) for o in outs],
        scratch_shapes=list(scratch),
        compiler_params=pltpu.CompilerParams(vmem_limit_bytes=24 * 1024 * 1024),
        cost_estimate=pl.CostEstimate(
            flops=int(us * 1.5e9), bytes_accessed=int(us * 1e6), transcendentals=0
        ),
    )(*arrays)


def one_hot(shape, test):
    first = lax.broadcasted_iota(jnp.int32, shape, 0)
    second = lax.broadcasted_iota(jnp.int32, shape, 1)
    return test(first, second).astype(F32).astype(BF16)


def places():
    return lax.axis_index("rows"), lax.axis_index("cols"), lax.axis_index("wide")


def chip_place(zz, ww, cc):
    x, y = ww % 2, ww // 2
    return zz * 4 + ((2 * y + x) if cc == 0 else (2 * x + y))


def wide_bits():
    _, c, w = places()
    x, y = lax.rem(w, 2), lax.rem(lax.div(w, 2), 2)
    return jnp.where(c == 0, x, y), jnp.where(c == 0, y, x)


def rows_at(index, count):
    return pl.ds(pl.multiple_of(index * count, 16), count)


def tiles_body(latent, pred_grad, *tiles):
    z, _, _ = places()
    _, lat_ch, height, wide = latent.shape
    out_ch = pred_grad.shape[1]
    chans, tok = lat_ch + out_ch, height * wide // 4
    half = wide // 2
    lanes = 2 * chans
    spread = [one_hot((tok, wide), lambda t, v: v == 2 * (t % half) + u) for u in range(2)]
    inside = [
        one_hot((tok, chans * height), lambda t, v: v % height == 2 * (t // half) + par).astype(F32)
        for par in range(2)
    ]

    def lane_of(channel, u):
        return jnp.where(
            channel < lat_ch, u * lat_ch + channel, 2 * lat_ch + u * out_ch + channel - lat_ch
        )

    fold = [
        one_hot((chans * height, lanes), lambda v, lane: lane == lane_of(v // height, u))
        for u in range(2)
    ]
    for k, tile in enumerate(tiles):
        image = jnp.concatenate(
            [
                latent[z ^ k].reshape(lat_ch * height, wide),
                pred_grad[z ^ k].reshape(out_ch * height, wide),
            ],
            axis=0,
        )
        wide_rows = [dot_nt(spread[u], image) for u in range(2)]
        for par in range(2):
            tile[par] = sum(
                dot((wide_rows[u] * inside[par]).astype(BF16), fold[u]) for u in range(2)
            ).astype(BF16)


def packed_tile(parities, lanes, order):
    tok = parities[0].shape[0]
    across = tok // order
    total = order * 2 * lanes
    block = 0.0
    for par in range(2):
        copy = one_hot((lanes, total), lambda a, b: b % (2 * lanes) == par * lanes + a)
        block = block + dot(parities[par].astype(BF16), copy)
    own = one_hot((tok, total), lambda t, b: b // (2 * lanes) == t // across).astype(F32)
    gather = one_hot((across, tok), lambda j, t: t % across == j)
    return dot(gather, (block * own).astype(BF16))


def unpacked_tile(block, chans, height, wide):
    lanes = 2 * chans
    half = wide // 2
    image = 0.0
    for u in range(2):
        chosen = one_hot(
            (chans * height, block.shape[1]),
            lambda v, b: b
            == (v % height) // 2 * 2 * lanes + v % 2 * lanes + u * chans + v // height,
        )
        column = dot_nt(chosen, block).astype(BF16)
        image = image + dot(column, one_hot((half, wide), lambda j, v: v == 2 * j + u))
    return image


def by_parity(first, second, offset):
    step = first.shape[0] // 32
    moved = jnp.concatenate([jnp.zeros((step, second.shape[1]), F32), second[:-step]], axis=0)
    return jnp.where(offset == 1, moved, first), jnp.where(offset == 1, first, second)


def cond_body(
    timesteps, labels, freqs, label_table, time_in, final_weight, positions, *rest,
):
    sources, (mods, cond, final_copy, pos), held = rest[:7], rest[7:11], rest[11:18]
    sem = rest[18]
    final_copy[...] = final_weight[...]
    sources, held = sources + (positions.at[lax.axis_index("cols")],), held + (pos,)
    copies = [
        pltpu.make_async_copy(source, target, sem.at[i])
        for i, (source, target) in enumerate(zip(sources, held))
    ]
    for copy in copies:
        copy.start()
    time_out, modulation, final_mod = held[:3]
    z, _, _ = places()
    label = labels[z]
    count, width = time_in.shape
    angles = jnp.full((8, count // 2), timesteps[z].astype(F32)) * freqs[...]
    feats = jnp.concatenate([jnp.cos(angles), jnp.sin(angles)], axis=-1).astype(BF16)
    hidden = dot(feats, time_in[...])
    act = (hidden * jax.nn.sigmoid(hidden)).astype(BF16)
    chosen = one_hot((8, label_table.shape[0]), lambda a, b: b == label)
    copies[0].wait()
    condition = dot(act, time_out[...]) + dot(chosen, label_table[...])
    shared = (condition * jax.nn.sigmoid(condition)).astype(BF16)
    mods[...] = jnp.zeros_like(mods)
    copies[1].wait()
    for layer in range(2):
        values = dot(shared, modulation[layer])
        for k in range(6):
            mods[layer, k : k + 1, :] = values[0:1, k * width : (k + 1) * width]
    copies[2].wait()
    values = dot(shared, final_mod[...])
    for k in range(2):
        mods[2, k : k + 1, :] = values[0:1, k * width : (k + 1) * width]
    lane = lax.broadcasted_iota(jnp.int32, (1, width - count), 1)
    marks = jnp.where(
        lane == 0, lax.div(label, 32), jnp.where(lane == 1, lax.rem(label, 32), 0)
    ).astype(F32)
    cond[...] = jnp.zeros_like(cond)
    cond[0:1, :] = shared[0:1].astype(F32)
    cond[1:2, :] = act[0:1].astype(F32)
    cond[2:3, :] = condition[0:1]
    cond[3:4, :] = hidden[0:1]
    cond[4:5, :] = jnp.concatenate([feats[0:1].astype(F32), marks], axis=-1)
    for copy in copies[3:]:
        copy.wait()


def qkv_forward(state, mods, layer, weight):
    width = state.shape[-1]
    normed, _ = layer_norm(state)
    inner = (normed * (1.0 + mods[layer, 1:2]) + mods[layer, 0:1]).astype(BF16)
    projected = dot(inner, weight[layer]).astype(BF16)
    return projected[:, :width], projected[:, width:]


def attend_forward(q, kv, kvp, probs, attended):
    width = q.shape[-1]
    masks = head_masks(BF16)
    for p in range(PAIRS):
        at = slice(p * LANES, (p + 1) * LANES)
        av = slice(width + p * LANES, width + (p + 1) * LANES)
        qp = q[:, at] * BF16(HEAD_DIM**-0.5)
        k0, v0, k1, v1 = kv[:, at], kv[:, av], kvp[:, at], kvp[:, av]
        total = None
        for h in range(2):
            qh = qp * masks[h]
            s0, s1 = dot_nt(qh, k0), dot_nt(qh, k1)
            peak = jnp.maximum(
                jnp.max(s0, axis=-1, keepdims=True), jnp.max(s1, axis=-1, keepdims=True)
            )
            e0, e1 = jnp.exp(s0 - peak), jnp.exp(s1 - peak)
            scale = 1.0 / (
                jnp.sum(e0, axis=-1, keepdims=True) + jnp.sum(e1, axis=-1, keepdims=True)
            )
            p0, p1 = (e0 * scale).astype(BF16), (e1 * scale).astype(BF16)
            probs[2 * p + h, 0] = p0
            probs[2 * p + h, 1] = p1
            part = dot(p0, v0 * masks[h]) + dot(p1, v1 * masks[h])
            total = part if total is None else total + part
        attended[:, at] = total.astype(BF16)


def mlp_forward(middle, mods, layer, up, down, gp, act):
    normed, _ = layer_norm(middle)
    inner = (normed * (1.0 + mods[layer, 4:5]) + mods[layer, 3:4]).astype(BF16)
    width = middle.shape[-1]
    branch = None
    for i in range(up.shape[-1] // width):
        at = slice(i * width, (i + 1) * width)
        hidden = dot(inner, up[layer, :, at])
        square = hidden * hidden
        root = math.sqrt(2.0 / math.pi)
        bent = jnp.tanh(root * hidden * (1.0 + 0.044715 * square))
        half = 0.5 * (1.0 + bent)
        activated = (hidden * half).astype(BF16)
        act[:, at] = activated
        slope = half + 0.5 * hidden * (1.0 - bent * bent) * (root * (1.0 + 3 * 0.044715 * square))
        gp[:, at] = slope.astype(BF16)
        part = dot(activated, down[layer, at, :])
        branch = part if branch is None else branch + part
    return branch


def put_units(keep, send, pair, place, size, at_row):
    first = lax.axis_index("cols") == 0
    block = pair[0].shape[0]
    own = jnp.where(first, place[0], place[1]) * size + at_row
    other = jnp.where(first, place[1], place[0]) * size + at_row
    keep[pl.ds(pl.multiple_of(own, 16), block), :] = jnp.where(first, pair[0], pair[1])
    send[pl.ds(pl.multiple_of(other, 16), block), :] = jnp.where(first, pair[1], pair[0])


def mlp_backward(grad, middle, branch, mods, layer, gp, act, up, down, keep, send, size, rows, first):
    width = middle.shape[-1]
    normed, inverse = layer_norm(middle)
    scale = 1.0 + mods[layer, 4:5]
    inner_t = (normed * scale + mods[layer, 3:4]).astype(BF16).T
    branch_grad = (mods[layer, 5:6] * grad).astype(BF16)
    inner_grad = None
    pieces = up.shape[-1] // width
    block = width // 8
    for i in range(pieces):
        at = slice(i * width, (i + 1) * width)
        act_grad = dot_nt(branch_grad, down[layer, at, :])
        hidden_grad = (act_grad * gp[:, at].astype(F32)).astype(BF16)
        part = dot_nt(hidden_grad, up[layer, :, at])
        inner_grad = part if inner_grad is None else inner_grad + part
        grad_up = dot(inner_t, hidden_grad).astype(BF16)
        for b in range(4):
            pair = [grad_up[(2 * b + cc) * block : (2 * b + cc + 1) * block] for cc in range(2)]
            put_units(keep, send, pair, [unit_place(b, i, cc) for cc in range(2)], size, 0)
        grad_down = dot_tn(act[:, at], branch_grad).astype(BF16)
        for j in range(4):
            pair = [grad_down[(4 * cc + j) * block : (4 * cc + j + 1) * block] for cc in range(2)]
            put_units(keep, send, pair, [unit_place(i, j, cc) for cc in range(2)], size, block)
    rows[first : first + 1, :] = token_sum(inner_grad)
    rows[first + 1 : first + 2, :] = token_sum(inner_grad * normed)
    rows[first + 2 : first + 3, :] = token_sum(grad * branch.astype(F32))
    return grad + norm_back(inner_grad * scale, normed, inverse)


def qkv_backward(
    state, middle_grad, dq, dkv, dkvr, mods, layer, weight, gproj, keep, send, at_row, place_of, rows
):
    width = state.shape[-1]
    block = width // 8
    normed, inverse = layer_norm(state)
    scale = 1.0 + mods[layer, 1:2]
    inner_t = (normed * scale + mods[layer, 0:1]).astype(BF16).T
    dkv_sum = dkv[...] + dkvr[...]
    pieces = (dq[...], dkv_sum[:, :width], dkv_sum[:, width:])
    inner_grad = None

    def put(values, i):
        for b in range(4):
            pair = [values[(2 * b + cc) * block : (2 * b + cc + 1) * block] for cc in range(2)]
            place = [place_of(b, i, cc) for cc in range(2)]
            put_units(keep, send, pair, place, block, at_row)

    for i, piece in enumerate(pieces):
        part = dot_nt(piece, weight[layer, :, i * width : (i + 1) * width])
        inner_grad = part if inner_grad is None else inner_grad + part
        put(dot(inner_t, piece).astype(BF16), i)
    put(gproj[...], 3)
    rows[0:1, :] = token_sum(inner_grad)
    rows[1:2, :] = token_sum(inner_grad * normed)
    return middle_grad + norm_back(inner_grad * scale, normed, inverse)


def embed_body(
    offsets, t0, t1, t2, t3, pos, mods, patch_weight, qkv,
    state, q, kv, patches, tiles,
):
    z, _, _ = places()
    offset = offsets[z]
    for k, tile in enumerate((t0, t1, t2, t3)):
        tiles[k] = tile[...]
    count = tiles.shape[0]
    even = jnp.concatenate([tiles[z ^ t, 0] for t in range(count)], axis=0).astype(F32)
    odd = jnp.concatenate([tiles[z ^ t, 1] for t in range(count)], axis=0).astype(F32)
    step = even.shape[0] // 32
    later = jnp.concatenate([even[step:], jnp.zeros((step, even.shape[1]), F32)], axis=0)
    first = jnp.where(offset == 1, odd, even).astype(BF16)
    second = jnp.where(offset == 1, later, odd).astype(BF16)
    patches[0] = first
    patches[1] = second
    weight = patch_weight[...].astype(F32)
    lanes = weight.shape[0] // 2
    fill = jnp.zeros((even.shape[1] - lanes, weight.shape[1]), F32)
    upper = jnp.concatenate([weight[:lanes], fill], axis=0).astype(BF16)
    lower = jnp.concatenate([weight[lanes:], fill], axis=0).astype(BF16)
    values = dot(first, upper) + dot(second, lower) + pos[...]
    state[...] = values
    q[...], kv[...] = qkv_forward(values, mods, 0, qkv)


def block_body(
    state, q, kv, kvp, mods, proj, up, down, qkv,
    state1, q1, kv1, probs, attended, attn_out, middle, gp, act, branch,
):
    attend_forward(q, kv, kvp, probs, attended)
    m = mods
    attn = dot(attended[...], proj[0])
    attn_out[...] = attn.astype(BF16)
    mid = state[...] + m[0, 2:3] * attn
    middle[...] = mid
    out = mlp_forward(mid, m, 0, up, down, gp, act)
    branch[...] = out.astype(BF16)
    new = mid + m[0, 5:6] * out
    state1[...] = new
    q1[...], kv1[...] = qkv_forward(new, m, 1, qkv)


def turn_body(
    offsets, counts, state, q, kv, kvp, mods, cond, patches, final_weight, proj, up, down,
    probs, attended, attn_out, middle_grad, keep, send, preds,
    gp, act, table,
):
    z, _, _ = places()
    offset = offsets[z]
    live = (z < counts[0]).astype(F32)
    attend_forward(q, kv, kvp, probs, attended)
    m = mods
    attn = dot(attended[...], proj[1])
    attn_out[...] = attn.astype(BF16)
    middle = state[...] + m[1, 2:3] * attn
    branch = mlp_forward(middle, m, 1, up, down, gp, act)
    last = middle + m[1, 5:6] * branch
    normed, inverse = layer_norm(last)
    scale = 1.0 + m[2, 1:2]
    inner = (normed * scale + m[2, 0:1]).astype(BF16)
    weight = final_weight[...]
    lanes = weight.shape[1] // 2
    out = dot(inner, weight) * live
    preds[0], preds[1] = by_parity(out[:, :lanes], out[:, lanes:], offset)
    across = weight.astype(F32).T
    chosen = patches
    fill = jnp.zeros((chosen.shape[2] - lanes, across.shape[1]), F32)
    upper = jnp.concatenate([fill, across[:lanes]], axis=0).astype(BF16)
    lower = jnp.concatenate([fill, across[lanes:]], axis=0).astype(BF16)
    inner_grad = (dot(chosen[0], upper) + dot(chosen[1], lower)) * live
    table[...] = jnp.zeros_like(table)
    table[0:1, :] = token_sum(inner_grad)
    table[1:2, :] = token_sum(inner_grad * normed)
    table[5:10, :] = 0.5 * cond[0:5, :]
    skip = chosen.shape[2] - lanes
    for r in range(2):
        at = ROWS + r * lanes
        table[at : at + lanes, :] = (dot_tn(chosen[r], inner) * live)[skip:]
    grad = norm_back(inner_grad * scale, normed, inverse)
    size = 2 * (weight.shape[0] // 8)
    middle_grad[...] = mlp_backward(
        grad, middle, branch, m, 1, gp, act, up, down, keep, send, size, table, 2
    )
    base = 4 * weight.shape[0]
    keep[base:] = table[...].astype(BF16)
    send[base:] = table[...].astype(BF16)


def attend_back_body(
    layer, q, kv, kvp, probs, attended, attn_out, middle_grad, mods, proj,
    dq, dkv, gproj, dkvs, rows,
):
    grad = middle_grad[...]
    attn_grad = (mods[layer, 2:3] * grad).astype(BF16)
    attended_grad = dot_nt(attn_grad, proj[layer]).astype(BF16)
    masks = head_masks(BF16)
    width = q.shape[-1]
    for p in range(PAIRS):
        at = slice(p * LANES, (p + 1) * LANES)
        av = slice(width + p * LANES, width + (p + 1) * LANES)
        qp = q[:, at] * BF16(HEAD_DIM**-0.5)
        dop = attended_grad[:, at]
        ks, vs = (kv[:, at], kvp[:, at]), (kv[:, av], kvp[:, av])
        total = None
        parts = [None] * 4
        for h in range(2):
            doh = dop * masks[h]
            qh = qp * masks[h]
            ps = [probs[2 * p + h, i] for i in range(2)]
            dps = [dot_nt(doh, vs[i]) for i in range(2)]
            pfs = [ps[i].astype(F32) for i in range(2)]
            inner = sum(jnp.sum(dps[i] * pfs[i], axis=-1, keepdims=True) for i in range(2))
            for i in range(2):
                ds = (pfs[i] * (dps[i] - inner)).astype(BF16)
                part = dot(ds, ks[i] * masks[h])
                total = part if total is None else total + part
                dk, dv = dot_tn(ds, qh), dot_tn(ps[i], doh)
                parts[2 * i] = dk if h == 0 else parts[2 * i] + dk
                parts[2 * i + 1] = dv if h == 0 else parts[2 * i + 1] + dv
        dq[:, at] = (total * HEAD_DIM**-0.5).astype(BF16)
        dkv[:, at] = parts[0].astype(BF16)
        dkv[:, av] = parts[1].astype(BF16)
        dkvs[:, at] = parts[2].astype(BF16)
        dkvs[:, av] = parts[3].astype(BF16)
    rows[...] = jnp.zeros_like(rows)
    rows[0:1, :] = token_sum(grad * attn_out[...].astype(F32))
    gproj[...] = dot_tn(attended[...], attn_grad).astype(BF16)


def middle_body(
    state1, middle_grad1, dq, dkv, dkvr, gproj, middle, branch, gp, act, mods, qkv, up, down,
    middle_grad, keep, send, rows,
):
    width = dq.shape[-1]
    size = 2 * (width // 8)
    rows[...] = jnp.zeros_like(rows)
    m = mods
    grad = qkv_backward(
        state1[...], middle_grad1[...], dq, dkv, dkvr, m, 1, qkv, gproj, keep, send,
        16 * size, chip_place, rows,
    )
    middle_grad[...] = mlp_backward(
        grad, middle[...], branch[...], m, 0, gp, act, up, down, keep, send, size,
        rows, 2,
    )


def last_body(
    offsets, state0, middle_grad, dq, dkv, dkvr, gproj, mods, patches, patch_weight,
    rows_a1, rows_mid, rows_a0, qkv,
    keep, send, lgrads, rows, table,
):
    z, _, _ = places()
    offset = offsets[z]
    width = dq.shape[-1]
    block = width // 8
    grad = qkv_backward(
        state0[...], middle_grad[...], dq, dkv, dkvr, mods, 0, qkv, gproj, keep, send,
        0, lambda zz, ww, cc: unit_place(zz, ww, 1 - cc), rows,
    )
    embed_grad = grad.astype(BF16)
    chosen = patches
    gp0, gp1 = dot_tn(chosen[0], embed_grad), dot_tn(chosen[1], embed_grad)
    chans = patch_weight.shape[0] // 2
    window = dot_nt(embed_grad, patch_weight[...])
    lgrads[0], lgrads[1] = by_parity(window[:, :chans], window[:, chans:], offset)
    table[...] = jnp.zeros_like(table)
    table[0:2, :] = rows[0:2, :]
    table[2:3, :] = rows_a0[0:1, :]
    table[3:6, :] = rows_mid[2:5, :]
    table[6:8, :] = rows_mid[0:2, :]
    table[8:9, :] = rows_a1[0:1, :]
    table[ROWS : ROWS + chans, :] = gp0[:chans]
    table[ROWS + chans : ROWS + 2 * chans, :] = gp1[:chans]
    keep[16 * block :] = table[...].astype(BF16)
    send[16 * block :] = table[...].astype(BF16)


def second_body(keep, recv, keep_out, send_out):
    half = keep_out.shape[0]
    bit = wide_bits()[0]
    keep_out[...] = keep[rows_at(bit, half)] + recv[rows_at(bit, half)]
    send_out[...] = keep[rows_at(1 - bit, half)] + recv[rows_at(1 - bit, half)]


def beta_body(keep, recv, *chips):
    z, _, _ = places()
    size = chips[0].shape[0]
    base = keep.shape[0] - 4 * size
    for k, out in enumerate(chips):
        at = pl.ds(pl.multiple_of(base + (z ^ k) * size, 16), size)
        out[...] = keep[at] + recv[at]


def padded(*pieces):
    rows = jnp.concatenate(pieces, axis=0)
    fill = -rows.shape[0] % 16
    if fill:
        rows = jnp.concatenate([rows, jnp.zeros((fill, rows.shape[1]), F32)], axis=0)
    return rows.astype(BF16)


def paired(mine, other, sums):
    return padded(
        mine[:ROWS], other[:ROWS], mine[ROWS : ROWS + sums] + other[ROWS : ROWS + sums]
    )


def half_of_four(mine, other, sums, flip, four, total):
    _, c, w = places()
    first = jnp.where(c == flip, 1, 2)
    second = 3 - first
    spot = lax.rem(w, 4)
    four[spot] = mine[:ROWS]
    four[spot ^ first] = mine[ROWS : 2 * ROWS]
    four[spot ^ second] = other[:ROWS]
    four[spot ^ first ^ second] = other[ROWS : 2 * ROWS]
    at = slice(2 * ROWS, 2 * ROWS + sums)
    total[...] = mine[at] + other[at]
    half = sums // 2
    return padded(four[2 * c], four[2 * c + 1], total[pl.ds(pl.multiple_of(c * half, 8), half), :])


def first_body(keep, recv, keep_out, table, send):
    half = (keep.shape[0] - table.shape[0]) // 2
    bit = wide_bits()[0]
    keep_out[...] = keep[rows_at(bit, half)] + recv[rows_at(bit, half)]
    send[0:half] = keep[rows_at(1 - bit, half)] + recv[rows_at(1 - bit, half)]
    rows = keep[2 * half :] + recv[2 * half :]
    table[...] = rows
    send[half:] = rows


def first_pair_body(sums, keep, table, recv, keep_out, pair_out, send):
    size = keep.shape[0]
    half = size // 2
    bit = wide_bits()[1]
    keep_out[...] = keep[rows_at(bit, half)] + recv[rows_at(bit, half)]
    send[0:half] = keep[rows_at(1 - bit, half)] + recv[rows_at(1 - bit, half)]
    pair = paired(table[...].astype(F32), recv[size:].astype(F32), sums)
    pair_out[...] = pair
    send[half:] = pair


def first_chip_body(
    sums, keep, pair, recv, preds, lgrads, z0, z1, z2, z3, tiles, four, total
):
    z, _, _ = places()
    size = keep.shape[0]
    unit = size // 4
    rows = half_of_four(pair[...].astype(F32), recv[size:].astype(F32), sums, 0, four, total)
    for k, out in enumerate((z0, z1, z2, z3)):
        out[0:unit] = keep[rows_at(z ^ k, unit)] + recv[rows_at(z ^ k, unit)]
        out[unit:] = rows
    tok = preds.shape[1] // 4
    tiles[:, :, 256:] = jnp.zeros((4, 16, 128), BF16)
    for k in range(4):
        cut = pl.ds(pl.multiple_of((z ^ k) * tok, 8), tok)
        parts = [lgrads[0, cut, :], lgrads[1, cut, :]]
        leading = [part.astype(BF16).astype(F32) for part in parts]
        chans = lgrads.shape[2]
        latents = jnp.concatenate(
            [
                packed_tile(leading, chans, 8),
                packed_tile([a - b for a, b in zip(parts, leading)], chans, 8),
            ],
            axis=1,
        )
        predicted = packed_tile([preds[0, cut, :], preds[1, cut, :]], preds.shape[2], 8)
        tiles[k, :, 0:256] = jnp.concatenate([latents, predicted], axis=0).astype(BF16)


def chip_sum(parts, at):
    return sum(part[at].astype(F32) for part in parts)


def third_body(keep2, recv2, b0, b1, b2, b3, keep2_out, keepb, part, whole):
    half2, halfb = keep2.shape[0] // 2, keepb.shape[0]
    bit = wide_bits()[1]
    keep2_out[...] = keep2[rows_at(bit, half2)] + recv2[rows_at(bit, half2)]
    part[0:half2] = keep2[rows_at(1 - bit, half2)] + recv2[rows_at(1 - bit, half2)]
    whole[...] = chip_sum((b0, b1, b2, b3), slice(None)).astype(BF16)
    keepb[...] = whole[rows_at(bit, halfb)]
    part[half2:] = whole[rows_at(1 - bit, halfb)]


def third_send_body(keep3, recv3, part, keep3_out, table, send):
    size = part.shape[0]
    size3 = keep3.shape[0] - table.shape[0]
    half3 = size3 // 2
    bit = wide_bits()[1]
    send[0:size] = part[...]
    keep3_out[...] = keep3[rows_at(bit, half3)] + recv3[rows_at(bit, half3)]
    send[size : size + half3] = keep3[rows_at(1 - bit, half3)] + recv3[rows_at(1 - bit, half3)]
    rows = keep3[size3:] + recv3[size3:]
    table[...] = rows
    send[size + half3 :] = rows


def fourth_body(sums, keep2, keep3, keepb, table, recv, whole2, keep3_out, keepb_out, pair_out, send):
    size2, size3, sizeb = keep2.shape[0], keep3.shape[0], keepb.shape[0]
    half3, halfb = size3 // 2, sizeb // 2
    whole2[...] = keep2[...] + recv[0:size2]
    bit = wide_bits()[0]

    def half(held, index, size, base):
        start = pl.multiple_of(index * size, 16)
        return held[pl.ds(start, size)] + recv[pl.ds(pl.multiple_of(start + base, 16), size)]

    keep3_out[...] = half(keep3, bit, half3, size2 + sizeb)
    send[0:half3] = half(keep3, 1 - bit, half3, size2 + sizeb)
    keepb_out[...] = half(keepb, bit, halfb, size2)
    send[half3 : half3 + halfb] = half(keepb, 1 - bit, halfb, size2)
    pair = paired(table[...].astype(F32), recv[size2 + size3 + sizeb :].astype(F32), sums)
    pair_out[...] = pair
    send[half3 + halfb :] = pair


def fifth_body(sums, whole2, keep3, keepb, pair, recv, tiles, z0, z1, z2, z3, unitb, four, total):
    z, _, _ = places()
    unit2, size3, sizeb = whole2.shape[0] // 4, keep3.shape[0], keepb.shape[0]
    unit3 = size3 // 4
    other = recv[size3 + sizeb :].astype(F32)
    rows = half_of_four(pair[...].astype(F32), other, sums, 1, four, total)
    start = unit2 + unit3
    end = start + rows.shape[0]
    for k, out in enumerate((z0, z1, z2, z3)):
        out[0:unit2] = whole2[rows_at(z ^ k, unit2)]
        out[unit2:start] = keep3[rows_at(z ^ k, unit3)] + recv[rows_at(z ^ k, unit3)]
        out[start:end] = rows
        out[end:] = tiles[k]
    unitb[...] = keepb[...] + recv[size3 : size3 + sizeb]


def chip_rows(sums, parts, size, pack):
    rows = [part[size : size + 48 if sums > 8 else size + 32].astype(F32) for part in parts]
    total = sum(r[2 * ROWS : 2 * ROWS + sums] for r in rows)
    pack[...] = padded(*[r[: 2 * ROWS] for r in rows], total)


def unit1_body(sums, z0, z1, z2, z3, unit, pack):
    parts = (z0, z1, z2, z3)
    size = unit.shape[0]
    unit[...] = chip_sum(parts, slice(0, size)).astype(BF16)
    chip_rows(sums, parts, size, pack)


def unit2_body(sums, z0, z1, z2, z3, unitb, unit, pack, tiles):
    parts = (z0, z1, z2, z3)
    size = unit.shape[0] - unitb.shape[0]
    unit[0:size] = chip_sum(parts, slice(0, size)).astype(BF16)
    unit[size:] = unitb[...]
    chip_rows(sums, parts, size, pack)
    for k, part in enumerate(parts):
        tiles[k] = part[size + 32 :]


def silu_slope(values):
    sigmoid = jax.nn.sigmoid(values)
    return sigmoid * (1.0 + values * (1.0 - sigmoid))


def sums_body(
    pack_a, other_a, pack_b, other_b, modulation, final_mod, time_out,
    g_time_in, g_time_out, g_table, g_mod, g_final_mod, g_patch, g_final,
    table, shared_t, total,
):
    z, c, _ = places()
    parts = table.shape[1]
    half = table.shape[2] // 2
    for which, pair in enumerate(((pack_a, other_a), (pack_b, other_b))):
        for side, pack in enumerate(pair):
            for i in range(parts):
                at = slice(128 * i, 128 * (i + 1))
                table[which, i, half * side : half * (side + 1)] = pack[0:half, at].astype(F32)
    count = g_patch.shape[0] // 2
    for side, pack in enumerate((pack_b, other_b)):
        at = pl.ds(pl.multiple_of((c ^ side) * count, 8), count)
        g_patch[at, :] = pack[half : half + 16].astype(F32)[:count]
    count = total.shape[0] // 2
    for side, pack in enumerate((pack_a, other_a)):
        at = pl.ds(pl.multiple_of((c ^ side) * count, 8), count)
        total[at, :] = pack[half : half + count].astype(F32)
    g_final[...] = total[...].T
    samples = table.shape[2] // ROWS

    def rows(r, which=0):
        pieces = [table[which, i, pl.ds(r, samples, stride=ROWS), :] for i in range(parts)]
        return jnp.concatenate(pieces, axis=-1)

    low = [rows(k, 1) for k in range(6)]
    high = [rows(k, 1) for k in range(6, 9)] + [rows(k) for k in range(2, 5)]
    mods = [jnp.concatenate(pieces, axis=-1).astype(BF16) for pieces in (low, high)]
    fmods = jnp.concatenate([rows(0), rows(1)], axis=-1).astype(BF16)
    shared_t[...] = rows(ROW_SHARED).T
    block = g_mod.shape[1]
    start = pl.multiple_of((z * 2 + c) * block, 8)
    mine = shared_t[pl.ds(start, block), :].astype(BF16)
    for layer in range(2):
        g_mod[layer] = dot(mine, mods[layer])
    g_final_mod[...] = dot(shared_t[...].astype(BF16), fmods)
    shared_grad = dot_nt(fmods, final_mod[...])
    for layer in range(2):
        shared_grad += dot_nt(mods[layer], modulation[layer])
    cond_grad = shared_grad * silu_slope(rows(ROW_COND))
    cond_low = cond_grad.astype(BF16)
    feats = rows(ROW_FEAT)
    count = g_time_in.shape[0]
    label = (feats[:, count : count + 1] * 32.0 + feats[:, count + 1 : count + 2]).astype(jnp.int32)
    classes = g_table.shape[0]
    padded = (classes + 127) // 128 * 128
    lane = lax.broadcasted_iota(jnp.int32, (samples, padded), 1)
    hot = (lane == label).astype(F32).T[:classes].astype(BF16)
    cond_rest = (cond_grad - cond_low.astype(F32)).astype(BF16)
    g_table[...] = dot(hot, cond_low) + dot(hot, cond_rest)
    g_time_out[...] = dot(rows(ROW_ACT).T.astype(BF16), cond_low)
    time_grad = dot_nt(cond_low, time_out[...]) * silu_slope(rows(ROW_HID))
    g_time_in[...] = dot(feats[:, :count].T.astype(BF16), time_grad.astype(BF16))


def place_mlp(g_up, g_down, layer, piece, unit):
    block, width = g_up.shape[1], g_down.shape[2]
    cols = pl.ds(pl.multiple_of(unit * width, 128), width)
    g_up[layer, :, cols] = piece[0:block].astype(F32)
    down_rows = pl.ds(pl.multiple_of(unit * block, 8), block)
    g_down[layer, down_rows, :] = piece[block : 2 * block].astype(F32)


def place_attn(g_qkv, g_proj, layer, piece, unit):
    width = g_proj.shape[2]

    @pl.when(unit < 3)
    def _():
        cols = pl.ds(pl.multiple_of(unit * width, 128), width)
        g_qkv[layer, :, cols] = piece.astype(F32)

    @pl.when(unit == 3)
    def _():
        g_proj[layer] = piece.astype(F32)


def first_spread_body(*refs):
    ones, (g_up, g_down) = refs[:4], refs[4:]
    spot = lax.rem(lax.axis_index("wide"), 4)
    for k in range(4):
        place_mlp(g_up, g_down, 1, ones[k][...], spot ^ k)


def spread_body(*refs):
    twos, tiles, up, down = refs[:4], refs[4], refs[5], refs[6]
    g_qkv, g_proj, g_up, g_down, prediction, latent_grad = refs[7:]
    z, _, w = places()
    block = g_proj.shape[1]
    spot = lax.rem(w, 4)
    g_up[1] = up[1]
    g_down[1] = down[1]
    _, out_ch, height, wide = prediction.shape
    lat_ch = latent_grad.shape[1]
    for k in range(4):
        tile = tiles[k].astype(F32)
        image = unpacked_tile(tile[8:16, 0:256].astype(BF16), out_ch, height, wide)
        prediction[z ^ k] = image.astype(BF16).reshape(out_ch, height, wide)
        image = unpacked_tile(tile[0:8, 0:128].astype(BF16), lat_ch, height, wide)
        image = image + unpacked_tile(tile[0:8, 128:256].astype(BF16), lat_ch, height, wide)
        latent_grad[z ^ k] = image.reshape(lat_ch, height, wide)
    for k in range(4):
        unit = spot ^ k
        place_mlp(g_up, g_down, 0, twos[k][0 : 2 * block], unit)
        place_attn(g_qkv, g_proj, 0, twos[k][2 * block : 3 * block], unit)
        place_attn(g_qkv, g_proj, 1, twos[k][3 * block :], unit)


def swap(value, axis, bit):
    count = lax.axis_size(axis)
    return lax.ppermute(value, axis, [(i, i ^ bit) for i in range(count)])


def swap_by_core(value, bits):
    wide, cores = lax.axis_size("wide"), lax.axis_size("cols")
    pairs = [
        (w * cores + c, (w ^ bits[c % 2]) * cores + c) for w in range(wide) for c in range(cores)
    ]
    return lax.ppermute(value, ("wide", "cols"), pairs)


FIRST, SECOND = (1, 2), (2, 1)


def rest_sum(value):
    bit = 4
    while bit < lax.axis_size("wide"):
        value = (value.astype(F32) + swap(value, "wide", bit).astype(F32)).astype(value.dtype)
        bit *= 2
    return value


def rest_gather(value):
    bit = 4
    while bit < lax.axis_size("wide"):
        value = jnp.concatenate([value, swap(value, "wide", bit)])
        bit *= 2
    return value


def position_tables(row_count, col_count, cores, width):
    quarter = width // 4
    omega = np.exp(-math.log(10000.0) * np.arange(quarter) / quarter)
    row_angle = np.arange(row_count)[:, None] * omega[None, :]
    col_angle = np.arange(col_count * cores)[:, None] * omega[None, :]
    row_part = np.concatenate([np.sin(row_angle), np.cos(row_angle)], axis=-1)
    col_part = np.concatenate([np.sin(col_angle), np.cos(col_angle)], axis=-1)
    col_part = col_part.reshape(cores, 1, col_count, width // 2)
    table = np.concatenate(
        [
            np.broadcast_to(row_part[None, :, None, :], (cores, row_count, col_count, width // 2)),
            np.broadcast_to(col_part, (cores, row_count, col_count, width // 2)),
        ],
        axis=-1,
    )
    return table.reshape(cores, row_count * col_count, width).astype(np.float32)


def shards(
    latent, pred_grad, timesteps, labels, offsets, counts, patch_weight, time_in, time_out,
    label_table, modulation, qkv_weight, proj_weight, up_weight, down_weight, final_mod, final_weight,
):
    slots, lat_ch, tile_h, tile_w = latent.shape
    out_ch = pred_grad.shape[1]
    width = patch_weight.shape[1]
    ff = up_weight.shape[2]
    n_rows, n_cols = lax.axis_size("rows"), lax.axis_size("cols")
    hp, wp = tile_h // 2, tile_w // 2
    tile_tok = hp * wp
    tokens = n_rows * tile_tok
    lanes = 2 * (lat_ch + out_ch)
    block = width // 8
    tok, wide_tok, double = (tokens, width), (tokens, ff), (tokens, 2 * width)

    tiles = kernel_call(
        tiles_body, [("v", latent), ("v", pred_grad)], [((2, tile_tok, lanes), BF16)] * n_rows, us=1
    )

    def along_z(parts):
        return [parts[0]] + [swap(parts[k], "rows", k) for k in range(1, n_rows)]

    def along_wide(unit):
        unit = rest_sum(unit)
        return [unit] + [swap(unit, "wide", k) for k in range(1, 4)]

    def both_halves(pack):
        if lax.axis_size("wide") > 4:
            rows, sums = rest_gather(pack[: 8 * ROWS]), rest_sum(pack[8 * ROWS :])
            pack = jnp.concatenate([rows, sums])
        return pack, swap(pack, "cols", 1)

    tiles = along_z(tiles)
    half = time_in.shape[0] // 2
    freqs = np.exp(-math.log(10000.0) * np.arange(half, dtype=np.float32) / np.float32(half))
    positions = jnp.asarray(position_tables(n_rows * hp, wp, n_cols, width))
    weights = (time_out, modulation, final_mod, qkv_weight, proj_weight, up_weight, down_weight)
    mods, cond, final_v, pos, time_out_v, modulation_v, final_mod_v, qkv, proj, up, down = kernel_call(
        cond_body,
        [("s", timesteps), ("s", labels), ("v", jnp.asarray(freqs.astype(np.float32))[None])]
        + [("v", label_table), ("v", time_in), ("v", final_weight), ("h", positions)]
        + [("h", weight) for weight in weights],
        [((3, 8, width), F32), ((8, width), F32), (final_weight.shape, BF16), (tok, F32)]
        + [(weight.shape, BF16) for weight in weights],
        [pltpu.SemaphoreType.DMA((len(weights) + 1,))],
        us=US["cond"],
    )
    probs_shape = (HEADS, 2, tokens, tokens)
    state0, q0, kv0, patches = kernel_call(
        embed_body,
        [("s", offsets)]
        + [("v", t) for t in tiles]
        + [("p", pos), ("p", mods), ("v", patch_weight), ("p", qkv)],
        [(tok, F32), (tok, BF16), (double, BF16), ((2, tokens, lanes), BF16)],
        [pltpu.VMEM((n_rows, 2, tile_tok, lanes), BF16)],
        us=US["embed"],
    )
    kv0p = swap(kv0, "cols", 1)
    state1, q1, kv1, probs0, attended0, attn_out0, middle0, gp0, act0, branch0 = kernel_call(
        block_body,
        [("p", state0), ("p", q0), ("p", kv0), ("v", kv0p)]
        + [("p", a) for a in (mods, proj, up, down, qkv)],
        [
            (tok, F32), (tok, BF16), (double, BF16), (probs_shape, BF16), (tok, BF16), (tok, BF16),
            (tok, F32), (wide_tok, BF16), (wide_tok, BF16), (tok, BF16),
        ],
        us=US["block"],
    )
    kv1p = swap(kv1, "cols", 1)
    sums_a, sums_b = 4 * out_ch, 4 * lat_ch
    rows_1 = 16 * 2 * block + 48
    probs1, attended1, attn_out1, mgrad1, keep1, send1, preds = kernel_call(
        turn_body,
        [("s", offsets), ("s", counts), ("p", state1), ("p", q1), ("p", kv1), ("v", kv1p)]
        + [("p", a) for a in (mods, cond, patches, final_v, proj, up, down)],
        [
            (probs_shape, BF16), (tok, BF16), (tok, BF16), (tok, F32), ((rows_1, width), BF16),
            ((rows_1, width), BF16), ((2, tokens, 2 * out_ch), F32),
        ],
        [pltpu.VMEM(wide_tok, BF16), pltpu.VMEM(wide_tok, BF16), pltpu.VMEM((48, width), F32)],
        us=US["turn"],
    )
    recv1 = swap(send1, "cols", 1)

    def attend_back(layer, q, kv, kvp, *saved, after):
        return kernel_call(
            partial(attend_back_body, layer),
            [("p", q), ("p", kv), ("v", kvp)] + [("p", a) for a in saved + (mods, proj)],
            [
                (tok, BF16), (double, BF16), ((width, width), BF16), (double, BF16), ((8, width), F32),
            ],
            us=US["back"],
            after=after,
        )

    dq1, dkv1, gproj1, dkvs1, rows_a1 = attend_back(
        1, q1, kv1, kv1p, probs1, attended1, attn_out1, mgrad1, after=None
    )
    dkvr1 = swap(dkvs1, "cols", 1)
    keep1, table1, send1 = kernel_call(
        first_body,
        [("p", keep1), ("v", recv1)],
        [((8 * 2 * block, width), BF16), ((48, width), BF16), ((8 * 2 * block + 48, width), BF16)],
        us=US["A1"],
        after=rows_a1,
    )
    recv1 = swap_by_core(send1, FIRST)
    mgrad0, keep2, send2, rows_mid = kernel_call(
        middle_body,
        [("p", a) for a in (state1, mgrad1, dq1, dkv1)]
        + [("v", dkvr1)]
        + [("p", a) for a in (gproj1, middle0, branch0, gp0, act0, mods, qkv, up, down)],
        [
            (tok, F32), ((16 * 3 * block, width), BF16), ((16 * 3 * block, width), BF16),
            ((8, width), F32),
        ],
        us=US["middle"],
        after=table1,
    )
    recv2 = swap(send2, "cols", 1)
    dq0, dkv0, gproj0, dkvs0, rows_a0 = attend_back(
        0, q0, kv0, kv0p, probs0, attended0, attn_out0, mgrad0, after=None
    )
    dkvr0 = swap(dkvs0, "cols", 1)
    keep1, pair1, send1 = kernel_call(
        partial(first_pair_body, sums_a),
        [("p", keep1), ("p", table1), ("v", recv1)],
        [((4 * 2 * block, width), BF16), ((64, width), BF16), ((4 * 2 * block + 64, width), BF16)],
        us=US["A2"],
        after=rows_a0,
    )
    recv1 = swap_by_core(send1, SECOND)
    whole_2, whole_r = keep2, recv2
    keep2, send2 = kernel_call(
        second_body,
        [("p", whole_2), ("v", whole_r)],
        [((8 * 2 * block, width), BF16)] * 2,
        us=US["A3"],
        after=pair1,
    )
    recv2 = swap_by_core(send2, FIRST)
    betas = kernel_call(
        beta_body,
        [("p", whole_2), ("v", whole_r)],
        [((4 * block, width), BF16)] * 4,
        us=US["A3b"],
        after=keep2,
    )
    chips = betas[0]
    betas = along_z(betas)
    rows_3 = 16 * block + 32
    keep3, send3, lgrads = kernel_call(
        last_body,
        [("s", offsets), ("p", state0), ("p", mgrad0), ("p", dq0), ("p", dkv0), ("v", dkvr0)]
        + [("p", gproj0), ("p", mods), ("p", patches), ("v", patch_weight)]
        + [("p", a) for a in (rows_a1, rows_mid, rows_a0, qkv)],
        [((rows_3, width), BF16), ((rows_3, width), BF16), ((2, tokens, 2 * lat_ch), F32)],
        [pltpu.VMEM((8, width), F32), pltpu.VMEM((32, width), F32)],
        us=US["last"],
        after=chips,
    )
    recv3 = swap(send3, "cols", 1)
    *ones, tiles = kernel_call(
        partial(first_chip_body, sums_a),
        [("p", keep1), ("p", pair1), ("v", recv1), ("p", preds), ("p", lgrads)],
        [((2 * block + 48, width), BF16)] * 4 + [((4, 16, width), BF16)],
        [pltpu.VMEM((4, ROWS, width), F32), pltpu.VMEM((sums_a, width), F32)],
        us=US["A2b"],
    )
    ones = along_z(ones)
    keep2, keepb, part = kernel_call(
        third_body,
        [("p", keep2), ("v", recv2), ("p", betas[0])] + [("v", beta) for beta in betas[1:]],
        [((8 * block, width), BF16), ((2 * block, width), BF16), ((10 * block, width), BF16)],
        [pltpu.VMEM((4 * block, width), BF16)],
        us=US["A4"],
        after=tiles,
    )
    keep3, table3, send = kernel_call(
        third_send_body,
        [("p", keep3), ("v", recv3), ("p", part)],
        [((8 * block, width), BF16), ((32, width), BF16), ((18 * block + 32, width), BF16)],
        us=US["A4b"],
    )
    recv = swap_by_core(send, SECOND)
    whole2, keep3, keepb, pair3, send = kernel_call(
        partial(fourth_body, sums_b),
        [("p", keep2), ("p", keep3), ("p", keepb), ("p", table3), ("v", recv)],
        [
            ((8 * block, width), BF16), ((4 * block, width), BF16), ((block, width), BF16),
            ((48, width), BF16), ((5 * block + 48, width), BF16),
        ],
        us=US["A5"],
    )
    recv = swap_by_core(send, FIRST)
    pack = (8 * ROWS + 16, width)
    unit1, pack_a = kernel_call(
        partial(unit1_body, sums_a // 2),
        [("p", ones[0])] + [("v", one) for one in ones[1:]],
        [((2 * block, width), BF16), (pack, BF16)],
        us=US["U1"],
        after=pair3,
    )
    ones = along_wide(unit1)
    *twos, unitb = kernel_call(
        partial(fifth_body, sums_b),
        [("p", whole2), ("p", keep3), ("p", keepb), ("p", pair3), ("v", recv), ("p", tiles)],
        [((3 * block + 32 + 16, width), BF16)] * 4 + [((block, width), BF16)],
        [pltpu.VMEM((4, ROWS, width), F32), pltpu.VMEM((sums_b, width), F32)],
        us=US["A6"],
        after=pack_a,
    )
    chips = twos[0]
    twos = along_z(twos)
    packs = both_halves(pack_a)
    g_up, g_down = kernel_call(
        first_spread_body,
        [("p", ones[0])] + [("v", one) for one in ones[1:]],
        [((2, block, ff), F32), ((2, ff // 8, width), F32)],
        us=US["S1"],
        after=chips,
    )
    unit2, pack_b, tiles = kernel_call(
        partial(unit2_body, sums_b // 2),
        [("p", twos[0])] + [("v", two) for two in twos[1:]] + [("p", unitb)],
        [((4 * block, width), BF16), (pack, BF16), ((4, 16, width), BF16)],
        us=US["U2"],
        after=g_up,
    )
    twos = along_wide(unit2)
    packs = packs + both_halves(pack_b)
    samples = 2 * (packs[0].shape[0] - 16) // ROWS
    classes = label_table.shape[0]
    g_time_in, g_time_out, g_table, g_mod, g_final_mod, g_patch, g_final = kernel_call(
        sums_body,
        [("v", half) for half in packs]
        + [("p", a) for a in (modulation_v, final_mod_v, time_out_v)],
        [
            (shape, F32, 0)
            for shape in (
                time_in.shape, time_out.shape, (classes, width), (2, block, 6 * width), final_mod.shape,
                patch_weight.shape, final_weight.shape,
            )
        ],
        [
            pltpu.VMEM((2, width // 128, samples * ROWS, 128), F32),
            pltpu.VMEM((width, samples), F32), pltpu.VMEM((sums_a, width), F32),
        ],
        us=US["sums"],
    )
    g_qkv, g_proj, g_up, g_down, prediction, latent_grad = kernel_call(
        spread_body,
        [("v", a) for a in twos] + [("p", tiles), ("p", g_up), ("p", g_down)],
        [
            ((2, block, 3 * width), F32, 0), ((2, block, width), F32, 0), ((2, block, ff), F32, 0),
            ((2, ff // 8, width), F32, 0), ((slots, out_ch, tile_h, tile_w), BF16, 0),
            (latent.shape, F32, 0),
        ],
        us=US["spread"],
        after=g_patch,
    )
    return (
        prediction, latent_grad, g_patch, g_time_in, g_time_out, g_table, g_mod, g_qkv, g_proj,
        g_up, g_down, g_final_mod, g_final,
    )


def solution(mesh):
    tiled, split = P("wide", None, "rows", "cols"), P(None, ("rows", "cols"), None)
    return jax.shard_map(
        shards,
        mesh=mesh,
        in_specs=(tiled, tiled, P("wide"), P("wide"), P("wide"), P("wide")) + (P(),) * 11,
        out_specs=(tiled, tiled, P(), P(), P(), P(), split, split, split, split, split, P(), P()),
        check_vma=False,
    )
```

```python
from functools import partial
import math

import jax
import jax.numpy as jnp
import numpy as np
from jax import lax
from jax.experimental import pallas as pl
from jax.experimental.pallas import tpu as pltpu
from jax.sharding import PartitionSpec as P

HEADS = 6
HEAD_DIM = 64
PAIRS = HEADS // 2
LANES = 2 * HEAD_DIM
EPS = 1e-06
F32 = jnp.float32
BF16 = jnp.bfloat16
ROWS = 12
ROW_SHARED, ROW_ACT, ROW_COND, ROW_HID, ROW_FEAT = 5, 6, 7, 8, 9
US = {
    "cond": 5, "embed": 2, "block": 6, "turn": 9, "back": 20, "middle": 4, "last": 4, "early": 0.05, "pack": 0.05, "join": 0.05, "U12": 0.05, "F3": 0.05, "sums": 5, "spread": 0.05,
    "A1": 0.05, "A2": 0.05, "A2b": 0.05, "A3": 0.05, "A3b": 0.05, "A4": 30, "A4b": 0.05, "A5": 0.05, "A6": 0.05, "S1": 0.05, "U2": 3,
    "U1": 1,
}


def dot(a, b):
    return jnp.dot(a, b, preferred_element_type=F32)


def dot_nt(a, b):
    return lax.dot_general(a, b, (((1,), (1,)), ((), ())), preferred_element_type=F32)


def dot_tn(a, b):
    return lax.dot_general(a, b, (((0,), (0,)), ((), ())), preferred_element_type=F32)


def sds(shape, dtype):
    return jax.ShapeDtypeStruct(shape, dtype)


def layer_norm(states):
    centred = states - jnp.mean(states, axis=-1, keepdims=True)
    inverse = lax.rsqrt(jnp.mean(centred * centred, axis=-1, keepdims=True) + EPS)
    return centred * inverse, inverse


def norm_back(grad, normed, inverse):
    mean_grad = jnp.mean(grad, axis=-1, keepdims=True)
    mean_cross = jnp.mean(grad * normed, axis=-1, keepdims=True)
    return inverse * (grad - mean_grad - normed * mean_cross)


def token_sum(values):
    return jnp.sum(values, axis=0, keepdims=True)


def head_masks(dtype):
    lane = lax.broadcasted_iota(jnp.int32, (1, LANES), 1)
    first = (lane < HEAD_DIM).astype(F32)
    return first.astype(dtype), (1.0 - first).astype(dtype)


def unit_place(zz, ww, cc):
    x, y = ww % 2, ww // 2
    return (x * 8 + y * 4 + zz) if cc == 0 else (y * 8 + x * 4 + zz)


def kernel_call(body, ins, outs, scratch=(), us=1.0, after=None, aliases=()):
    spaces = {"v": pltpu.VMEM, "p": pltpu.VMEM, "s": pltpu.SMEM, "h": pltpu.HBM}
    specs, arrays = [], []
    for kind, array in ins:
        specs.append(pl.BlockSpec(memory_space=spaces[kind]))
        if kind in "ph":
            array = pltpu.with_memory_space_constraint(array, spaces[kind])
        arrays.append(array)
    if after is not None:
        specs.append(pl.BlockSpec(memory_space=pl.ANY))
        arrays.append(after)

    def kernel(*refs):
        body(*refs[: len(ins)], *refs[len(arrays) :])

    return pl.pallas_call(
        kernel,
        in_specs=specs,
        out_specs=[
            pl.BlockSpec(memory_space=pltpu.HBM if "hbm" in o[2:] else pltpu.VMEM) for o in outs
        ],
        out_shape=[
            pltpu.VMEM(o[0], o[1]) if len(o) < 3 else sds(o[0], o[1]) if o[2] == "any" else pltpu.HBM(o[0], o[1])
            for o in outs
        ],
        input_output_aliases=dict(aliases),
        scratch_shapes=list(scratch),
        compiler_params=pltpu.CompilerParams(vmem_limit_bytes=24 * 1024 * 1024),
        cost_estimate=pl.CostEstimate(
            flops=int(us * 1.5e9), bytes_accessed=int(us * 1e6), transcendentals=0
        ),
    )(*arrays)


def one_hot(shape, test):
    first = lax.broadcasted_iota(jnp.int32, shape, 0)
    second = lax.broadcasted_iota(jnp.int32, shape, 1)
    return test(first, second).astype(F32).astype(BF16)


def places():
    return lax.axis_index("rows"), lax.axis_index("cols"), lax.axis_index("wide")


def chip_place(zz, ww, cc):
    x, y = ww % 2, ww // 2
    return zz * 4 + ((2 * y + x) if cc == 0 else (2 * x + y))


def wide_bits():
    _, c, w = places()
    x, y = lax.rem(w, 2), lax.rem(lax.div(w, 2), 2)
    return jnp.where(c == 0, x, y), jnp.where(c == 0, y, x)


def rows_at(index, count):
    return pl.ds(pl.multiple_of(index * count, 16), count)


def tiles_body(latent_h, pred_h, *rest):
    tiles, (latent, pred_grad, sem) = rest[:-3], rest[-3:]
    copies = [
        pltpu.make_async_copy(latent_h, latent, sem.at[0]),
        pltpu.make_async_copy(pred_h, pred_grad, sem.at[1]),
    ]
    for copy in copies:
        copy.start()
    z, _, _ = places()
    _, lat_ch, height, wide = latent.shape
    out_ch = pred_grad.shape[1]
    chans, tok = lat_ch + out_ch, height * wide // 4
    half = wide // 2
    lanes = 2 * chans
    spread = [one_hot((tok, wide), lambda t, v: v == 2 * (t % half) + u) for u in range(2)]
    inside = [
        one_hot((tok, chans * height), lambda t, v: v % height == 2 * (t // half) + par).astype(F32)
        for par in range(2)
    ]

    def lane_of(channel, u):
        return jnp.where(
            channel < lat_ch, u * lat_ch + channel, 2 * lat_ch + u * out_ch + channel - lat_ch
        )

    fold = [
        one_hot((chans * height, lanes), lambda v, lane: lane == lane_of(v // height, u))
        for u in range(2)
    ]
    for copy in copies:
        copy.wait()
    for k, tile in enumerate(tiles):
        image = jnp.concatenate(
            [
                latent[z ^ k].reshape(lat_ch * height, wide),
                pred_grad[z ^ k].reshape(out_ch * height, wide),
            ],
            axis=0,
        )
        wide_rows = [dot_nt(spread[u], image) for u in range(2)]
        for par in range(2):
            tile[par] = sum(
                dot((wide_rows[u] * inside[par]).astype(BF16), fold[u]) for u in range(2)
            ).astype(BF16)


def packed_tile(parities, lanes, order):
    tok = parities[0].shape[0]
    across = tok // order
    total = order * 2 * lanes
    block = 0.0
    for par in range(2):
        copy = one_hot((lanes, total), lambda a, b: b % (2 * lanes) == par * lanes + a)
        block = block + dot(parities[par].astype(BF16), copy)
    own = one_hot((tok, total), lambda t, b: b // (2 * lanes) == t // across).astype(F32)
    gather = one_hot((across, tok), lambda j, t: t % across == j)
    return dot(gather, (block * own).astype(BF16))


def unpacked_tile(block, chans, height, wide):
    lanes = 2 * chans
    half = wide // 2
    image = 0.0
    for u in range(2):
        chosen = one_hot(
            (chans * height, block.shape[1]),
            lambda v, b: b
            == (v % height) // 2 * 2 * lanes + v % 2 * lanes + u * chans + v // height,
        )
        column = dot_nt(chosen, block).astype(BF16)
        image = image + dot(column, one_hot((half, wide), lambda j, v: v == 2 * j + u))
    return image


def by_parity(first, second, offset):
    step = first.shape[0] // 32
    moved = jnp.concatenate([jnp.zeros((step, second.shape[1]), F32), second[:-step]], axis=0)
    return jnp.where(offset == 1, moved, first), jnp.where(offset == 1, first, second)


def cond_body(
    timesteps, labels, freqs, label_table, time_in, final_weight, positions, *rest,
):
    sources, (mods, cond, final_copy, pos), held = rest[:7], rest[7:11], rest[11:18]
    sem = rest[18]
    final_copy[...] = final_weight[...]
    sources = sources[:3] + tuple(source.at[0] for source in sources[3:])
    sources += (positions.at[lax.axis_index("cols")],)
    held = held + (pos,)
    copies = [
        pltpu.make_async_copy(source, target, sem.at[i])
        for i, (source, target) in enumerate(zip(sources, held))
    ]
    for copy in copies:
        copy.start()
    time_out, modulation, final_mod = held[:3]
    z, _, _ = places()
    label = labels[z]
    count, width = time_in.shape
    angles = jnp.full((8, count // 2), timesteps[z].astype(F32)) * freqs[...]
    feats = jnp.concatenate([jnp.cos(angles), jnp.sin(angles)], axis=-1).astype(BF16)
    hidden = dot(feats, time_in[...])
    act = (hidden * jax.nn.sigmoid(hidden)).astype(BF16)
    chosen = one_hot((8, label_table.shape[0]), lambda a, b: b == label)
    copies[0].wait()
    condition = dot(act, time_out[...]) + dot(chosen, label_table[...])
    shared = (condition * jax.nn.sigmoid(condition)).astype(BF16)
    mods[...] = jnp.zeros_like(mods)
    copies[1].wait()
    for layer in range(2):
        values = dot(shared, modulation[layer])
        for k in range(6):
            mods[layer, k : k + 1, :] = values[0:1, k * width : (k + 1) * width]
    copies[2].wait()
    values = dot(shared, final_mod[...])
    for k in range(2):
        mods[2, k : k + 1, :] = values[0:1, k * width : (k + 1) * width]
    lane = lax.broadcasted_iota(jnp.int32, (1, width - count), 1)
    marks = jnp.where(
        lane == 0, lax.div(label, 32), jnp.where(lane == 1, lax.rem(label, 32), 0)
    ).astype(F32)
    cond[...] = jnp.zeros_like(cond)
    cond[0:1, :] = shared[0:1].astype(F32)
    cond[1:2, :] = act[0:1].astype(F32)
    cond[2:3, :] = condition[0:1]
    cond[3:4, :] = hidden[0:1]
    cond[4:5, :] = jnp.concatenate([feats[0:1].astype(F32), marks], axis=-1)
    for copy in copies[3:]:
        copy.wait()


def qkv_forward(state, mods, layer, weight):
    width = state.shape[-1]
    normed, _ = layer_norm(state)
    inner = (normed * (1.0 + mods[layer, 1:2]) + mods[layer, 0:1]).astype(BF16)
    projected = dot(inner, weight[...]).astype(BF16)
    return projected[:, :width], projected[:, width:]


def attend_forward(q, kv, kvp, probs, attended):
    width = q.shape[-1]
    masks = head_masks(BF16)
    for p in range(PAIRS):
        at = slice(p * LANES, (p + 1) * LANES)
        av = slice(width + p * LANES, width + (p + 1) * LANES)
        qp = q[:, at] * BF16(HEAD_DIM**-0.5)
        k0, v0, k1, v1 = kv[:, at], kv[:, av], kvp[:, at], kvp[:, av]
        total = None
        for h in range(2):
            qh = qp * masks[h]
            s0, s1 = dot_nt(qh, k0), dot_nt(qh, k1)
            peak = jnp.maximum(
                jnp.max(s0, axis=-1, keepdims=True), jnp.max(s1, axis=-1, keepdims=True)
            )
            e0, e1 = jnp.exp(s0 - peak), jnp.exp(s1 - peak)
            scale = 1.0 / (
                jnp.sum(e0, axis=-1, keepdims=True) + jnp.sum(e1, axis=-1, keepdims=True)
            )
            p0, p1 = (e0 * scale).astype(BF16), (e1 * scale).astype(BF16)
            probs[2 * p + h, 0] = p0
            probs[2 * p + h, 1] = p1
            part = dot(p0, v0 * masks[h]) + dot(p1, v1 * masks[h])
            total = part if total is None else total + part
        attended[:, at] = total.astype(BF16)


CHUNK = 768


def mlp_forward(middle, mods, layer, up, down, gp, act):
    normed, _ = layer_norm(middle)
    inner = (normed * (1.0 + mods[layer, 4:5]) + mods[layer, 3:4]).astype(BF16)
    branch = None
    for start in range(0, up.shape[1], CHUNK):
        at = slice(start, start + CHUNK)
        hidden = dot(inner, up[:, at])
        square = hidden * hidden
        root = math.sqrt(2.0 / math.pi)
        bent = jnp.tanh(root * hidden * (1.0 + 0.044715 * square))
        half = 0.5 * (1.0 + bent)
        activated = (hidden * half).astype(BF16)
        act[:, at] = activated
        slope = half + 0.5 * hidden * (1.0 - bent * bent) * (root * (1.0 + 3 * 0.044715 * square))
        gp[:, at] = slope.astype(BF16)
        part = dot(activated, down[at, :])
        branch = part if branch is None else branch + part
    return branch


def put_units(keep, send, pair, place, size, at_row):
    first = lax.axis_index("cols") == 0
    block = pair[0].shape[0]
    own = jnp.where(first, place[0], place[1]) * size + at_row
    other = jnp.where(first, place[1], place[0]) * size + at_row
    keep[pl.ds(pl.multiple_of(own, 16), block), :] = jnp.where(first, pair[0], pair[1])
    send[pl.ds(pl.multiple_of(other, 16), block), :] = jnp.where(first, pair[1], pair[0])


def mlp_backward(
    grad, middle, branch, mods, layer, gp, act, up, down, keep, send, size, flip, rows, first, low
):
    width = middle.shape[-1]
    normed, inverse = layer_norm(middle)
    scale = 1.0 + mods[layer, 4:5]
    inner_t = (normed * scale + mods[layer, 3:4]).astype(BF16).T
    branch_grad = (mods[layer, 5:6] * grad).astype(BF16)
    inner_grad = None
    for start in range(0, up.shape[1], CHUNK):
        at = slice(start, start + CHUNK)
        act_grad = dot_nt(branch_grad, down[at, :])
        hidden_grad = (act_grad * gp[:, at].astype(F32)).astype(BF16)
        low[:, at] = hidden_grad
        part = dot_nt(hidden_grad, up[:, at])
        inner_grad = part if inner_grad is None else inner_grad + part
    block = width // 8
    for i in range(up.shape[1] // width):
        at = slice(i * width, (i + 1) * width)
        grad_up = dot(inner_t, low[:, at]).astype(BF16)
        for b in range(4):
            pair = [grad_up[(2 * b + cc) * block : (2 * b + cc + 1) * block] for cc in range(2)]
            place = [unit_place(b, i, cc ^ flip) for cc in range(2)]
            put_units(keep, send, pair, place, size, 0)
        grad_down = dot_tn(act[:, at], branch_grad).astype(BF16)
        for j in range(4):
            pair = [grad_down[(4 * cc + j) * block : (4 * cc + j + 1) * block] for cc in range(2)]
            place = [unit_place(i, j, cc ^ flip) for cc in range(2)]
            put_units(keep, send, pair, place, size, block)
    rows[first : first + 1, :] = token_sum(inner_grad)
    rows[first + 1 : first + 2, :] = token_sum(inner_grad * normed)
    rows[first + 2 : first + 3, :] = token_sum(grad * branch.astype(F32))
    return grad + norm_back(inner_grad * scale, normed, inverse)


def qkv_backward(
    state, middle_grad, dq, dkv, dkvr, mods, layer, weight, gproj, keep, send, shares, rows
):
    width = state.shape[-1]
    block = width // 8
    normed, inverse = layer_norm(state)
    scale = 1.0 + mods[layer, 1:2]
    inner_t = (normed * scale + mods[layer, 0:1]).astype(BF16).T
    dkv_sum = dkv[...] + dkvr[...]
    pieces = (dq[...], dkv_sum[:, :width], dkv_sum[:, width:])
    inner_grad = None

    def put(values, i):
        for b in range(4):
            pair = [values[(2 * b + cc) * block : (2 * b + cc + 1) * block] for cc in range(2)]
            for start, end, place_of, size, at_row in shares:
                place = [place_of(b, i, cc) for cc in range(2)]
                put_units(keep, send, [part[start:end] for part in pair], place, size, at_row)

    for i, piece in enumerate(pieces):
        part = dot_nt(piece, weight[:, i * width : (i + 1) * width])
        inner_grad = part if inner_grad is None else inner_grad + part
        put(dot(inner_t, piece).astype(BF16), i)
    put(gproj[...], 3)
    rows[0:1, :] = token_sum(inner_grad)
    rows[1:2, :] = token_sum(inner_grad * normed)
    return middle_grad + norm_back(inner_grad * scale, normed, inverse)


def embed_body(
    offsets, t0, t1, t2, t3, pos, mods, patch_weight, qkv,
    state, q, kv, patches, tiles,
):
    z, _, _ = places()
    offset = offsets[z]
    for k, tile in enumerate((t0, t1, t2, t3)):
        tiles[k] = tile[...]
    count = tiles.shape[0]
    even = jnp.concatenate([tiles[z ^ t, 0] for t in range(count)], axis=0).astype(F32)
    odd = jnp.concatenate([tiles[z ^ t, 1] for t in range(count)], axis=0).astype(F32)
    step = even.shape[0] // 32
    later = jnp.concatenate([even[step:], jnp.zeros((step, even.shape[1]), F32)], axis=0)
    first = jnp.where(offset == 1, odd, even).astype(BF16)
    second = jnp.where(offset == 1, later, odd).astype(BF16)
    patches[0] = first
    patches[1] = second
    weight = patch_weight[...].astype(F32)
    lanes = weight.shape[0] // 2
    fill = jnp.zeros((even.shape[1] - lanes, weight.shape[1]), F32)
    upper = jnp.concatenate([weight[:lanes], fill], axis=0).astype(BF16)
    lower = jnp.concatenate([weight[lanes:], fill], axis=0).astype(BF16)
    values = dot(first, upper) + dot(second, lower) + pos[...]
    state[...] = values
    q[...], kv[...] = qkv_forward(values, mods, 0, qkv)


def block_body(
    state, q, kv, kvp, mods, proj, up, down, *rest,
):
    sources, rest = rest[:4], rest[4:]
    state1, q1, kv1, probs, attended, attn_out, middle, gp, act, branch = rest[:10]
    targets, sem = rest[10:14], rest[14]
    copies = [
        pltpu.make_async_copy(source.at[1], target, sem.at[i])
        for i, (source, target) in enumerate(zip(sources, targets))
    ]
    for copy in copies:
        copy.start()
    attend_forward(q, kv, kvp, probs, attended)
    m = mods
    attn = dot(attended[...], proj[...])
    attn_out[...] = attn.astype(BF16)
    mid = state[...] + m[0, 2:3] * attn
    middle[...] = mid
    out = mlp_forward(mid, m, 0, up, down, gp, act)
    branch[...] = out.astype(BF16)
    new = mid + m[0, 5:6] * out
    state1[...] = new
    copies[0].wait()
    q1[...], kv1[...] = qkv_forward(new, m, 1, targets[0])
    for copy in copies[1:]:
        copy.wait()


def turn_body(
    offsets, counts, state, q, kv, kvp, mods, cond, patches, final_weight, proj, up, down,
    probs, attended, attn_out, middle_grad, keep, send, preds,
    gp, act, table, low,
):
    z, _, _ = places()
    offset = offsets[z]
    live = (z < counts[0]).astype(F32)
    attend_forward(q, kv, kvp, probs, attended)
    m = mods
    attn = dot(attended[...], proj[...])
    attn_out[...] = attn.astype(BF16)
    middle = state[...] + m[1, 2:3] * attn
    branch = mlp_forward(middle, m, 1, up, down, gp, act)
    last = middle + m[1, 5:6] * branch
    normed, inverse = layer_norm(last)
    scale = 1.0 + m[2, 1:2]
    inner = (normed * scale + m[2, 0:1]).astype(BF16)
    weight = final_weight[...]
    lanes = weight.shape[1] // 2
    out = dot(inner, weight) * live
    preds[0], preds[1] = by_parity(out[:, :lanes], out[:, lanes:], offset)
    across = weight.astype(F32).T
    chosen = patches
    fill = jnp.zeros((chosen.shape[2] - lanes, across.shape[1]), F32)
    upper = jnp.concatenate([fill, across[:lanes]], axis=0).astype(BF16)
    lower = jnp.concatenate([fill, across[lanes:]], axis=0).astype(BF16)
    inner_grad = (dot(chosen[0], upper) + dot(chosen[1], lower)) * live
    table[...] = jnp.zeros_like(table)
    table[0:1, :] = token_sum(inner_grad)
    table[1:2, :] = token_sum(inner_grad * normed)
    table[5:10, :] = 0.5 * cond[0:5, :]
    skip = chosen.shape[2] - lanes
    for r in range(2):
        at = ROWS + r * lanes
        table[at : at + lanes, :] = (dot_tn(chosen[r], inner) * live)[skip:]
    grad = norm_back(inner_grad * scale, normed, inverse)
    size = 2 * (weight.shape[0] // 8)
    middle_grad[...] = mlp_backward(
        grad, middle, branch, m, 1, gp, act, up, down, keep, send, size, 0, table, 2, low
    )
    base = 4 * weight.shape[0]
    keep[base:] = table[...].astype(BF16)
    send[base:] = table[...].astype(BF16)


def attend_back_body(
    layer, q, kv, kvp, probs, attended, attn_out, middle_grad, mods, proj,
    dq, dkv, gproj, dkvs, rows,
):
    grad = middle_grad[...]
    attn_grad = (mods[layer, 2:3] * grad).astype(BF16)
    attended_grad = dot_nt(attn_grad, proj[...]).astype(BF16)
    masks = head_masks(BF16)
    width = q.shape[-1]
    for p in range(PAIRS):
        at = slice(p * LANES, (p + 1) * LANES)
        av = slice(width + p * LANES, width + (p + 1) * LANES)
        qp = q[:, at] * BF16(HEAD_DIM**-0.5)
        dop = attended_grad[:, at]
        ks, vs = (kv[:, at], kvp[:, at]), (kv[:, av], kvp[:, av])
        total = None
        parts = [[], [], [], []]
        q_t, do_t = qp.T, dop.T
        for h in range(2):
            doh = dop * masks[h]
            own = slice(h * HEAD_DIM, (h + 1) * HEAD_DIM)
            ps = [probs[2 * p + h, i] for i in range(2)]
            dps = [dot_nt(doh, vs[i]) for i in range(2)]
            pfs = [ps[i].astype(F32) for i in range(2)]
            inner = sum(jnp.sum(dps[i] * pfs[i], axis=-1, keepdims=True) for i in range(2))
            for i in range(2):
                ds = (pfs[i] * (dps[i] - inner)).astype(BF16)
                part = dot(ds, ks[i] * masks[h])
                total = part if total is None else total + part
                parts[2 * i].append(dot(q_t[own], ds))
                parts[2 * i + 1].append(dot(do_t[own], ps[i]))
        dq[:, at] = (total * HEAD_DIM**-0.5).astype(BF16)
        turned = [jnp.concatenate(part, axis=0).astype(BF16).T for part in parts]
        dkv[:, at] = turned[0]
        dkv[:, av] = turned[1]
        dkvs[:, at] = turned[2]
        dkvs[:, av] = turned[3]
    rows[...] = jnp.zeros_like(rows)
    rows[0:1, :] = token_sum(grad * attn_out[...].astype(F32))
    gproj[...] = dot_tn(attended[...], attn_grad).astype(BF16)


def middle_body(
    state1, middle_grad1, dq, dkv, dkvr, gproj, middle, branch, gp, act, mods, qkv, up, down,
    middle_grad, keep, send, rows, low,
):
    width = dq.shape[-1]
    block = width // 8
    size = 2 * block + 16
    rows[...] = jnp.zeros_like(rows)
    m = mods
    grad = qkv_backward(
        state1[...], middle_grad1[...], dq, dkv, dkvr, m, 1, qkv, gproj, keep, send,
        ((0, 16, unit_place, size, 2 * block), (16, block, chip_place, block - 16, 16 * size)), rows,
    )
    middle_grad[...] = mlp_backward(
        grad, middle[...], branch[...], m, 0, gp, act, up, down, keep, send, size, 0,
        rows, 2, low,
    )


def last_body(
    offsets, state0, middle_grad, dq, dkv, dkvr, gproj, mods, patches, patch_weight,
    rows_a1, rows_mid, rows_a0, qkv,
    keep, send, lgrads, rows, table,
):
    z, _, _ = places()
    offset = offsets[z]
    width = dq.shape[-1]
    block = width // 8
    grad = qkv_backward(
        state0[...], middle_grad[...], dq, dkv, dkvr, mods, 0, qkv, gproj, keep, send,
        ((0, block, lambda zz, ww, cc: unit_place(zz, ww, 1 - cc), block, 0),), rows,
    )
    embed_grad = grad.astype(BF16)
    chosen = patches
    gp0, gp1 = dot_tn(chosen[0], embed_grad), dot_tn(chosen[1], embed_grad)
    chans = patch_weight.shape[0] // 2
    window = dot_nt(embed_grad, patch_weight[...])
    lgrads[0], lgrads[1] = by_parity(window[:, :chans], window[:, chans:], offset)
    table[...] = jnp.zeros_like(table)
    table[0:2, :] = rows[0:2, :]
    table[2:3, :] = rows_a0[0:1, :]
    table[3:6, :] = rows_mid[2:5, :]
    table[6:8, :] = rows_mid[0:2, :]
    table[8:9, :] = rows_a1[0:1, :]
    table[ROWS : ROWS + chans, :] = gp0[:chans]
    table[ROWS + chans : ROWS + 2 * chans, :] = gp1[:chans]
    keep[16 * block :] = table[...].astype(BF16)
    send[16 * block :] = table[...].astype(BF16)


def second_body(keep, recv, keep_out, send_out):
    half = keep_out.shape[0]
    bit = wide_bits()[0]
    keep_out[...] = keep[rows_at(bit, half)] + recv[rows_at(bit, half)]
    send_out[...] = keep[rows_at(1 - bit, half)] + recv[rows_at(1 - bit, half)]


def beta_body(keep, recv, *chips):
    z, _, _ = places()
    size = chips[0].shape[0]
    base = keep.shape[0] - 4 * size
    for k, out in enumerate(chips):
        at = pl.ds(pl.multiple_of(base + (z ^ k) * size, 16), size)
        out[...] = keep[at] + recv[at]


def padded(*pieces):
    rows = jnp.concatenate(pieces, axis=0)
    fill = -rows.shape[0] % 16
    if fill:
        rows = jnp.concatenate([rows, jnp.zeros((fill, rows.shape[1]), F32)], axis=0)
    return rows.astype(BF16)


def paired(mine, other, sums):
    return padded(
        mine[:ROWS], other[:ROWS], mine[ROWS : ROWS + sums] + other[ROWS : ROWS + sums]
    )


def half_of_four(mine, other, sums, flip, four, total):
    _, c, w = places()
    first = jnp.where(c == flip, 1, 2)
    second = 3 - first
    spot = lax.rem(w, 4)
    four[spot] = mine[:ROWS]
    four[spot ^ first] = mine[ROWS : 2 * ROWS]
    four[spot ^ second] = other[:ROWS]
    four[spot ^ first ^ second] = other[ROWS : 2 * ROWS]
    at = slice(2 * ROWS, 2 * ROWS + sums)
    total[...] = mine[at] + other[at]
    half = sums // 2
    return padded(four[2 * c], four[2 * c + 1], total[pl.ds(pl.multiple_of(c * half, 8), half), :])


def first_body(keep, recv, keep_out, table, send):
    half = (keep.shape[0] - table.shape[0]) // 2
    bit = wide_bits()[0]
    keep_out[...] = keep[rows_at(bit, half)] + recv[rows_at(bit, half)]
    send[0:half] = keep[rows_at(1 - bit, half)] + recv[rows_at(1 - bit, half)]
    rows = keep[2 * half :] + recv[2 * half :]
    table[...] = rows
    send[half:] = rows


def first_pair_body(sums, keep, table, recv, keep_out, pair_out, send):
    size = keep.shape[0]
    half = size // 2
    bit = wide_bits()[1]
    keep_out[...] = keep[rows_at(bit, half)] + recv[rows_at(bit, half)]
    send[0:half] = keep[rows_at(1 - bit, half)] + recv[rows_at(1 - bit, half)]
    pair = paired(table[...].astype(F32), recv[size:].astype(F32), sums)
    pair_out[...] = pair
    send[half:] = pair


def first_chip_body(
    sums, keep, pair, recv, z0, z1, z2, z3, four, total
):
    z, _, _ = places()
    size = keep.shape[0]
    unit = size // 4
    rows = half_of_four(pair[...].astype(F32), recv[size:].astype(F32), sums, 0, four, total)
    for k, out in enumerate((z0, z1, z2, z3)):
        out[0:unit] = keep[rows_at(z ^ k, unit)] + recv[rows_at(z ^ k, unit)]
        out[unit:] = rows


def unit1_body(sums, o0, o1, o2, o3, unit, pack):
    ones = (o0, o1, o2, o3)
    unit[...] = chip_sum(ones, slice(0, unit.shape[0])).astype(BF16)
    chip_rows(sums, ones, unit.shape[0], pack)


def pack_body(preds, lgrads, tiles):
    z, _, _ = places()
    tok = preds.shape[1] // 4
    tiles[:, :, 256:] = jnp.zeros((4, 16, 128), BF16)
    for k in range(4):
        cut = pl.ds(pl.multiple_of((z ^ k) * tok, 8), tok)
        parts = [lgrads[0, cut, :], lgrads[1, cut, :]]
        leading = [part.astype(BF16).astype(F32) for part in parts]
        chans = lgrads.shape[2]
        latents = jnp.concatenate(
            [
                packed_tile(leading, chans, 8),
                packed_tile([a - b for a, b in zip(parts, leading)], chans, 8),
            ],
            axis=1,
        )
        predicted = packed_tile([preds[0, cut, :], preds[1, cut, :]], preds.shape[2], 8)
        tiles[k, :, 0:256] = jnp.concatenate([latents, predicted], axis=0).astype(BF16)


def chip_sum(parts, at):
    return sum(part[at].astype(F32) for part in parts)


def third_body(keep2, recv2, b0, b1, b2, b3, keep2_out, keepb, part, whole):
    half2, halfb = keep2.shape[0] // 2, keepb.shape[0]
    bit = wide_bits()[1]
    keep2_out[...] = keep2[rows_at(bit, half2)] + recv2[rows_at(bit, half2)]
    part[0:half2] = keep2[rows_at(1 - bit, half2)] + recv2[rows_at(1 - bit, half2)]
    whole[...] = chip_sum((b0, b1, b2, b3), slice(None)).astype(BF16)
    keepb[...] = whole[rows_at(bit, halfb)]
    part[half2:] = whole[rows_at(1 - bit, halfb)]


def third_send_body(keep3, recv3, part, keep3_out, table, send):
    size = part.shape[0]
    size3 = keep3.shape[0] - table.shape[0]
    half3 = size3 // 2
    bit = wide_bits()[1]
    send[0:size] = part[...]
    keep3_out[...] = keep3[rows_at(bit, half3)] + recv3[rows_at(bit, half3)]
    send[size : size + half3] = keep3[rows_at(1 - bit, half3)] + recv3[rows_at(1 - bit, half3)]
    rows = keep3[size3:] + recv3[size3:]
    table[...] = rows
    send[size + half3 :] = rows


def fourth_body(
    sums, keep2, keep3, keepb, table, recv, z0, z1, z2, z3, keep3_out, keepb_out, pair_out, send
):
    z, _, _ = places()
    size2, size3, sizeb = keep2.shape[0], keep3.shape[0], keepb.shape[0]
    half3, halfb = size3 // 2, sizeb // 2
    unit = size2 // 4
    for k, out in enumerate((z0, z1, z2, z3)):
        out[...] = keep2[rows_at(z ^ k, unit)] + recv[rows_at(z ^ k, unit)]
    bit = wide_bits()[0]

    def half(held, index, size, base):
        start = pl.multiple_of(index * size, 16)
        return held[pl.ds(start, size)] + recv[pl.ds(pl.multiple_of(start + base, 16), size)]

    keep3_out[...] = half(keep3, bit, half3, size2 + sizeb)
    send[0:half3] = half(keep3, 1 - bit, half3, size2 + sizeb)
    keepb_out[...] = half(keepb, bit, halfb, size2)
    send[half3 : half3 + halfb] = half(keepb, 1 - bit, halfb, size2)
    pair = paired(table[...].astype(F32), recv[size2 + size3 + sizeb :].astype(F32), sums)
    pair_out[...] = pair
    send[half3 + halfb :] = pair


def fifth_body(sums, keep3, keepb, pair, recv, tiles, z0, z1, z2, z3, unitb, four, total):
    z, _, _ = places()
    size3, sizeb = keep3.shape[0], keepb.shape[0]
    unit3 = size3 // 4
    other = recv[size3 + sizeb :].astype(F32)
    rows = half_of_four(pair[...].astype(F32), other, sums, 1, four, total)
    end = unit3 + rows.shape[0]
    for k, out in enumerate((z0, z1, z2, z3)):
        out[0:unit3] = keep3[rows_at(z ^ k, unit3)] + recv[rows_at(z ^ k, unit3)]
        out[unit3:end] = rows
        out[end:] = tiles[k]
    unitb[...] = keepb[...] + recv[size3 : size3 + sizeb]


def chip_rows(sums, parts, size, pack):
    rows = [part[size : size + 48 if sums > 8 else size + 32].astype(F32) for part in parts]
    total = sum(r[2 * ROWS : 2 * ROWS + sums] for r in rows)
    pack[...] = padded(*[r[: 2 * ROWS] for r in rows], total)


def unit12_body(unit1, t0, t1, t2, t3, unitb, unit):
    size, end2 = unit1.shape[0], t0.shape[0]
    unit[0:size] = unit1[...]
    unit[size : size + end2] = chip_sum((t0, t1, t2, t3), slice(None)).astype(BF16)
    unit[size + end2 :] = unitb[...]


def join_body(own2, near2, own3, send):
    size = own2.shape[0]
    send[0:size] = own2[...]
    send[size : 2 * size] = near2[...]
    send[2 * size :] = own3[...]


def unit3_body(sums, z0, z1, z2, z3, unit, pack, tiles):
    parts = (z0, z1, z2, z3)
    size = unit.shape[0]
    unit[...] = chip_sum(parts, slice(0, size)).astype(BF16)
    chip_rows(sums, parts, size, pack)
    for k, part in enumerate(parts):
        tiles[k] = part[size + 32 :]


def far_body(unit, recv, send):
    size = unit.shape[0]
    send[0:size] = unit[...]
    send[size:] = recv[recv.shape[0] - size :]


def silu_slope(values):
    sigmoid = jax.nn.sigmoid(values)
    return sigmoid * (1.0 + values * (1.0 - sigmoid))


def sample_table(table, pack, other):
    parts, half = table.shape[0], table.shape[1] // 2
    for side, held in enumerate((pack, other)):
        for i in range(parts):
            at = slice(128 * i, 128 * (i + 1))
            table[i, half * side : half * (side + 1)] = held[0:half, at].astype(F32)
    samples = table.shape[1] // ROWS

    def rows(r):
        return jnp.concatenate(
            [table[i, pl.ds(r, samples, stride=ROWS), :] for i in range(parts)], axis=-1
        )

    return rows


def join_sums(out, pack, other):
    c = lax.axis_index("cols")
    count = out.shape[0] // 2
    for side, held in enumerate((pack, other)):
        at = pl.ds(pl.multiple_of((c ^ side) * count, 8), count)
        out[at, :] = held[held.shape[0] - 16 :].astype(F32)[:count]


def early_sums_body(
    pack, other, final_mod,
    g_final_mod, g_final, shared_t, slopes, base, high, act_t, feat_t, hot, table,
):
    rows = sample_table(table, pack, other)
    join_sums(g_final, pack, other)
    fmods = jnp.concatenate([rows(0), rows(1)], axis=-1).astype(BF16)
    shared_t[...] = rows(ROW_SHARED).T
    g_final_mod[...] = dot(shared_t[...].astype(BF16), fmods)
    base[...] = dot_nt(fmods, final_mod[...])
    slopes[0] = silu_slope(rows(ROW_COND))
    slopes[1] = silu_slope(rows(ROW_HID))
    for k in range(3):
        high[k] = rows(2 + k)
    act_t[...] = rows(ROW_ACT).T.astype(BF16)
    feats = rows(ROW_FEAT)
    count = feat_t.shape[0]
    feat_t[...] = feats[:, :count].T.astype(BF16)
    label = (feats[:, count : count + 1] * 32.0 + feats[:, count + 1 : count + 2]).astype(jnp.int32)
    classes = hot.shape[0]
    lane = lax.broadcasted_iota(jnp.int32, (feats.shape[0], (classes + 127) // 128 * 128), 1)
    hot[...] = (lane == label).astype(F32).T[:classes].astype(BF16)


def sums_body(
    pack, other, modulation, time_out, shared_t, slopes, base, high, act_t, feat_t, hot, tiles,
    g_time_in, g_time_out, g_table, g_mod, g_patch, prediction, latent_grad, token,
    table, mod_v, table_v, time_out_v, time_in_v, sem,
):
    z, c, _ = places()
    token[...] = jnp.zeros_like(token)
    rows = sample_table(table, pack, other)
    mods = [
        jnp.concatenate([rows(k) for k in range(6)], axis=-1).astype(BF16),
        jnp.concatenate(
            [rows(k) for k in range(6, 9)] + [high[k] for k in range(3)], axis=-1
        ).astype(BF16),
    ]
    block = mod_v.shape[1]
    start = pl.multiple_of((z * 2 + c) * block, 8)
    mine = shared_t[pl.ds(start, block), :].astype(BF16)
    copies = []

    def leave(source, target):
        copies.append(pltpu.make_async_copy(source, target, sem.at[len(copies)]))
        copies[-1].start()

    for layer in range(2):
        mod_v[layer] = dot(mine, mods[layer])
    leave(mod_v, g_mod)
    shared_grad = base[...]
    for layer in range(2):
        shared_grad += dot_nt(mods[layer], modulation[layer])
    cond_grad = shared_grad * slopes[0]
    cond_low = cond_grad.astype(BF16)
    cond_rest = (cond_grad - cond_low.astype(F32)).astype(BF16)
    table_v[...] = dot(hot[...], cond_low) + dot(hot[...], cond_rest)
    leave(table_v, g_table)
    time_out_v[...] = dot(act_t[...], cond_low)
    leave(time_out_v, g_time_out)
    time_grad = dot_nt(cond_low, time_out[...]) * slopes[1]
    time_in_v[...] = dot(feat_t[...], time_grad.astype(BF16))
    leave(time_in_v, g_time_in)
    join_sums(g_patch, pack, other)
    _, out_ch, height, wide = prediction.shape
    lat_ch = latent_grad.shape[1]
    for k in range(4):
        tile = tiles[k].astype(F32)
        image = unpacked_tile(tile[8:16, 0:256].astype(BF16), out_ch, height, wide)
        prediction[z ^ k] = image.astype(BF16).reshape(out_ch, height, wide)
        image = unpacked_tile(tile[0:8, 0:128].astype(BF16), lat_ch, height, wide)
        image = image + unpacked_tile(tile[0:8, 128:256].astype(BF16), lat_ch, height, wide)
        latent_grad[z ^ k] = image.reshape(lat_ch, height, wide)
    for copy in copies:
        copy.wait()


def place_mlp(up, down, piece, unit):
    block, width = up.shape[0], down.shape[1]
    cols = pl.ds(pl.multiple_of(unit * width, 128), width)
    up[:, cols] = piece[0:block].astype(F32)
    down_rows = pl.ds(pl.multiple_of(unit * block, 8), block)
    down[down_rows, :] = piece[block : 2 * block].astype(F32)


def place_attn(g_qkv, g_proj, layer, piece, unit):
    width = g_proj.shape[2]

    @pl.when(unit < 3)
    def _():
        cols = pl.ds(pl.multiple_of(unit * width, 128), width)
        g_qkv[layer, :, cols] = piece.astype(F32)

    @pl.when(unit == 3)
    def _():
        g_proj[layer] = piece.astype(F32)


def spread_body(own2, near2, far, own3, near3, g_qkv, g_proj, g_up, g_down, up, down, sem):
    _, c, w = places()
    first = jnp.where(c == 0, 1, 2)
    spot = lax.rem(w, 4)
    spots = (spot, spot ^ first, spot ^ first ^ 3, spot ^ 3)
    size2, size3 = own2.shape[0], own3.shape[0]
    block = g_proj.shape[1]
    size = 2 * block
    twos = ((own2, 0), (near2, 0), (far, 0), (far, size2))
    threes = ((own3, 0), (near3, 0), (far, 2 * size2), (near3, size3))
    copies = []
    for layer, start in ((1, 0), (0, size)):
        for (ref, base), unit in zip(twos, spots):
            piece = ref[base + start : base + start + size]
            place_mlp(up.at[layer], down.at[layer], piece, unit)
        for source, target in ((up, g_up), (down, g_down)):
            copies.append(
                pltpu.make_async_copy(source.at[layer], target.at[layer], sem.at[len(copies)])
            )
            copies[-1].start()
    for (ref, base), unit in zip(twos, spots):
        place_attn(g_qkv, g_proj, 1, ref[base + 2 * size : base + size2], unit)
    for (ref, base), unit in zip(threes, spots):
        place_attn(g_qkv, g_proj, 0, ref[base : base + size3], unit)
    for copy in copies:
        copy.wait()


def swap(value, axis, bit):
    count = lax.axis_size(axis)
    return lax.ppermute(value, axis, [(i, i ^ bit) for i in range(count)])


def swap_by_core(value, bits):
    wide, cores = lax.axis_size("wide"), lax.axis_size("cols")
    pairs = [
        (w * cores + c, (w ^ bits[c % 2]) * cores + c) for w in range(wide) for c in range(cores)
    ]
    return lax.ppermute(value, ("wide", "cols"), pairs)


FIRST, SECOND = (1, 2), (2, 1)


def rest_sum(value):
    bit = 4
    while bit < lax.axis_size("wide"):
        value = (value.astype(F32) + swap(value, "wide", bit).astype(F32)).astype(value.dtype)
        bit *= 2
    return value


def rest_gather(value):
    bit = 4
    while bit < lax.axis_size("wide"):
        value = jnp.concatenate([value, swap(value, "wide", bit)])
        bit *= 2
    return value


def position_tables(row_count, col_count, cores, width):
    quarter = width // 4
    omega = np.exp(-math.log(10000.0) * np.arange(quarter) / quarter)
    row_angle = np.arange(row_count)[:, None] * omega[None, :]
    col_angle = np.arange(col_count * cores)[:, None] * omega[None, :]
    row_part = np.concatenate([np.sin(row_angle), np.cos(row_angle)], axis=-1)
    col_part = np.concatenate([np.sin(col_angle), np.cos(col_angle)], axis=-1)
    col_part = col_part.reshape(cores, 1, col_count, width // 2)
    table = np.concatenate(
        [
            np.broadcast_to(row_part[None, :, None, :], (cores, row_count, col_count, width // 2)),
            np.broadcast_to(col_part, (cores, row_count, col_count, width // 2)),
        ],
        axis=-1,
    )
    return table.reshape(cores, row_count * col_count, width).astype(np.float32)


def shards(
    latent, pred_grad, timesteps, labels, offsets, counts, patch_weight, time_in, time_out,
    label_table, modulation, qkv_weight, proj_weight, up_weight, down_weight, final_mod, final_weight,
):
    slots, lat_ch, tile_h, tile_w = latent.shape
    out_ch = pred_grad.shape[1]
    width = patch_weight.shape[1]
    ff = up_weight.shape[2]
    n_rows, n_cols = lax.axis_size("rows"), lax.axis_size("cols")
    hp, wp = tile_h // 2, tile_w // 2
    tile_tok = hp * wp
    tokens = n_rows * tile_tok
    lanes = 2 * (lat_ch + out_ch)
    block = width // 8
    tok, wide_tok, double = (tokens, width), (tokens, ff), (tokens, 2 * width)

    tiles = kernel_call(
        tiles_body,
        [("h", latent), ("h", pred_grad)],
        [((2, tile_tok, lanes), BF16)] * n_rows,
        [
            pltpu.VMEM(latent.shape, BF16), pltpu.VMEM(pred_grad.shape, BF16),
            pltpu.SemaphoreType.DMA((2,)),
        ],
        us=1,
    )

    def along_z(parts):
        return [parts[0]] + [swap(parts[k], "rows", k) for k in range(1, n_rows)]

    def both_halves(pack):
        if lax.axis_size("wide") > 4:
            rows, sums = rest_gather(pack[: 8 * ROWS]), rest_sum(pack[8 * ROWS :])
            pack = jnp.concatenate([rows, sums])
        return pack, swap(pack, "cols", 1)

    tiles = along_z(tiles)
    half = time_in.shape[0] // 2
    freqs = np.exp(-math.log(10000.0) * np.arange(half, dtype=np.float32) / np.float32(half))
    positions = jnp.asarray(position_tables(n_rows * hp, wp, n_cols, width))
    blocks = (qkv_weight, proj_weight, up_weight, down_weight)
    weights = (time_out, modulation, final_mod) + blocks
    held = [(weight.shape[1:], BF16) for weight in blocks]
    (
        mods, cond, final_v, pos, time_out_v, modulation_v, final_mod_v, qkv0, proj0, up0, down0,
    ) = kernel_call(
        cond_body,
        [("s", timesteps), ("s", labels), ("v", jnp.asarray(freqs.astype(np.float32))[None])]
        + [("v", label_table), ("v", time_in), ("v", final_weight), ("h", positions)]
        + [("h", weight) for weight in weights],
        [((3, 8, width), F32), ((8, width), F32), (final_weight.shape, BF16), (tok, F32)]
        + [(weight.shape, BF16) for weight in weights[:3]]
        + held,
        [pltpu.SemaphoreType.DMA((len(weights) + 1,))],
        us=US["cond"],
    )
    probs_shape = (HEADS, 2, tokens, tokens)
    state0, q0, kv0, patches = kernel_call(
        embed_body,
        [("s", offsets)]
        + [("v", t) for t in tiles]
        + [("p", pos), ("p", mods), ("v", patch_weight), ("p", qkv0)],
        [(tok, F32), (tok, BF16), (double, BF16), ((2, tokens, lanes), BF16)],
        [pltpu.VMEM((n_rows, 2, tile_tok, lanes), BF16)],
        us=US["embed"],
    )
    kv0p = swap(kv0, "cols", 1)
    (
        state1, q1, kv1, probs0, attended0, attn_out0, middle0, gp0, act0, branch0, qkv1, proj1, up1, down1,
    ) = kernel_call(
        block_body,
        [("p", state0), ("p", q0), ("p", kv0), ("v", kv0p)]
        + [("p", a) for a in (mods, proj0, up0, down0)]
        + [("h", weight) for weight in blocks],
        [
            (tok, F32), (tok, BF16), (double, BF16), (probs_shape, BF16), (tok, BF16), (tok, BF16),
            (tok, F32), (wide_tok, BF16), (wide_tok, BF16), (tok, BF16),
        ]
        + held,
        [pltpu.SemaphoreType.DMA((4,))],
        us=US["block"],
    )
    kv1p = swap(kv1, "cols", 1)
    sums_a, sums_b = 4 * out_ch, 4 * lat_ch
    rows_1 = 16 * 2 * block + 48
    probs1, attended1, attn_out1, mgrad1, keep1, send1, preds = kernel_call(
        turn_body,
        [("s", offsets), ("s", counts), ("p", state1), ("p", q1), ("p", kv1), ("v", kv1p)]
        + [("p", a) for a in (mods, cond, patches, final_v, proj1, up1, down1)],
        [
            (probs_shape, BF16), (tok, BF16), (tok, BF16), (tok, F32), ((rows_1, width), BF16),
            ((rows_1, width), BF16), ((2, tokens, 2 * out_ch), F32),
        ],
        [
            pltpu.VMEM(wide_tok, BF16), pltpu.VMEM(wide_tok, BF16), pltpu.VMEM((48, width), F32),
            pltpu.VMEM(wide_tok, BF16),
        ],
        us=US["turn"],
    )
    recv1 = swap(send1, "cols", 1)

    def attend_back(layer, q, kv, kvp, *saved, after):
        return kernel_call(
            partial(attend_back_body, layer),
            [("p", q), ("p", kv), ("v", kvp)] + [("p", a) for a in saved[:-1] + (mods, saved[-1])],
            [
                (tok, BF16), (double, BF16), ((width, width), BF16), (double, BF16), ((8, width), F32),
            ],
            us=US["back"],
            after=after,
        )

    dq1, dkv1, gproj1, dkvs1, rows_a1 = attend_back(
        1, q1, kv1, kv1p, probs1, attended1, attn_out1, mgrad1, proj1, after=None
    )
    dkvr1 = swap(dkvs1, "cols", 1)
    keep1, table1, send1 = kernel_call(
        first_body,
        [("p", keep1), ("v", recv1)],
        [((8 * 2 * block, width), BF16), ((48, width), BF16), ((8 * 2 * block + 48, width), BF16)],
        us=US["A1"],
        after=rows_a1,
    )
    recv1 = swap_by_core(send1, FIRST)
    mgrad0, keep2, send2, rows_mid = kernel_call(
        middle_body,
        [("p", a) for a in (state1, mgrad1, dq1, dkv1)]
        + [("v", dkvr1)]
        + [("p", a) for a in (gproj1, middle0, branch0, gp0, act0, mods, qkv1, up0, down0)],
        [
            (tok, F32), ((16 * 3 * block, width), BF16), ((16 * 3 * block, width), BF16),
            ((8, width), F32),
        ],
        [pltpu.VMEM(wide_tok, BF16)],
        us=US["middle"],
        after=table1,
    )
    recv2 = swap(send2, "cols", 1)
    dq0, dkv0, gproj0, dkvs0, rows_a0 = attend_back(
        0, q0, kv0, kv0p, probs0, attended0, attn_out0, mgrad0, proj0, after=None
    )
    dkvr0 = swap(dkvs0, "cols", 1)
    keep1, pair1, send1 = kernel_call(
        partial(first_pair_body, sums_a),
        [("p", keep1), ("p", table1), ("v", recv1)],
        [((4 * 2 * block, width), BF16), ((64, width), BF16), ((4 * 2 * block + 64, width), BF16)],
        us=US["A2"],
        after=rows_a0,
    )
    recv1 = swap_by_core(send1, SECOND)
    alpha, beta = 2 * block + 16, block - 16
    send_rows = 4 * alpha + 2 * beta + 8 * block + 32
    whole_2, whole_r = keep2, recv2
    keep2, send2 = kernel_call(
        second_body,
        [("p", whole_2), ("v", whole_r)],
        [((8 * alpha, width), BF16)] * 2,
        us=US["A3"],
        after=pair1,
    )
    recv2 = swap_by_core(send2, FIRST)
    betas = kernel_call(
        beta_body,
        [("p", whole_2), ("v", whole_r)],
        [((4 * beta, width), BF16)] * 4,
        us=US["A3b"],
        after=keep2,
    )
    chips = betas[0]
    betas = along_z(betas)
    rows_3 = 16 * block + 32
    keep3, send3, lgrads = kernel_call(
        last_body,
        [("s", offsets), ("p", state0), ("p", mgrad0), ("p", dq0), ("p", dkv0), ("v", dkvr0)]
        + [("p", gproj0), ("p", mods), ("p", patches), ("v", patch_weight)]
        + [("p", a) for a in (rows_a1, rows_mid, rows_a0, qkv0)],
        [((rows_3, width), BF16), ((rows_3, width), BF16), ((2, tokens, 2 * lat_ch), F32)],
        [pltpu.VMEM((8, width), F32), pltpu.VMEM((32, width), F32)],
        us=US["last"],
        after=chips,
    )
    recv3 = swap(send3, "cols", 1)
    (tiles,) = kernel_call(
        pack_body, [("p", preds), ("p", lgrads)], [((4, 16, width), BF16)], us=US["pack"]
    )
    ones = kernel_call(
        partial(first_chip_body, sums_a),
        [("p", keep1), ("p", pair1), ("v", recv1)],
        [((2 * block + 48, width), BF16)] * 4,
        [pltpu.VMEM((4, ROWS, width), F32), pltpu.VMEM((sums_a, width), F32)],
        us=US["A2b"],
        after=tiles,
    )
    chips = ones[0]
    ones = along_z(ones)
    keep2, keepb, part = kernel_call(
        third_body,
        [("p", keep2), ("v", recv2), ("p", betas[0])] + [("v", beta) for beta in betas[1:]],
        [
            ((4 * alpha, width), BF16), ((2 * beta, width), BF16),
            ((4 * alpha + 2 * beta, width), BF16),
        ],
        [pltpu.VMEM((4 * beta, width), BF16)],
        us=US["A4"],
        after=chips,
    )
    keep3, table3, send = kernel_call(
        third_send_body,
        [("p", keep3), ("v", recv3), ("p", part)],
        [((8 * block, width), BF16), ((32, width), BF16), ((send_rows, width), BF16)],
        us=US["A4b"],
    )
    recv = swap_by_core(send, SECOND)
    *twos, keep3, keepb, pair3, send = kernel_call(
        partial(fourth_body, sums_b),
        [("p", keep2), ("p", keep3), ("p", keepb), ("p", table3), ("v", recv)],
        [((alpha, width), BF16)] * 4
        + [
            ((4 * block, width), BF16), ((beta, width), BF16), ((48, width), BF16),
            ((4 * block + beta + 48, width), BF16),
        ],
        us=US["A5"],
    )
    recv = swap_by_core(send, FIRST)
    twos = along_z(twos)
    pack = (8 * ROWS + 16, width)
    unit1, pack_a = kernel_call(
        partial(unit1_body, sums_a // 2),
        [("p", ones[0])] + [("v", one) for one in ones[1:]],
        [((2 * block, width), BF16), (pack, BF16)],
        us=US["U1"],
        after=pair3,
    )
    packs = both_halves(pack_a)
    *threes, unitb = kernel_call(
        partial(fifth_body, sums_b),
        [("p", keep3), ("p", keepb), ("p", pair3), ("v", recv), ("p", tiles)],
        [((block + 32 + 16, width), BF16)] * 4 + [((beta, width), BF16)],
        [pltpu.VMEM((4, ROWS, width), F32), pltpu.VMEM((sums_b, width), F32)],
        us=US["A6"],
        after=pack_a,
    )
    threes = along_z(threes)
    (unit2,) = kernel_call(
        unit12_body,
        [("p", unit1), ("p", twos[0])] + [("v", two) for two in twos[1:]] + [("p", unitb)],
        [((2 * block + alpha + beta, width), BF16)],
        us=US["U12"],
    )
    unit2 = rest_sum(unit2)
    near2 = swap_by_core(unit2, FIRST)
    samples = 2 * (packs[0].shape[0] - 16) // ROWS
    classes = label_table.shape[0]
    feat_count = time_in.shape[0]
    g_final_mod, g_final, *early = kernel_call(
        early_sums_body,
        [("p", packs[0]), ("v", packs[1]), ("p", final_mod_v)],
        [
            (final_mod.shape, F32, "any"), ((sums_a, width), F32, "any"), ((width, samples), F32),
            ((2, samples, width), F32), ((samples, width), F32), ((3, samples, width), F32),
            ((width, samples), BF16), ((feat_count, samples), BF16), ((classes, samples), BF16),
        ],
        [pltpu.VMEM((width // 128, samples * ROWS, 128), F32)],
        us=US["early"],
        after=unit2,
    )
    unit3, pack_b, tiles = kernel_call(
        partial(unit3_body, sums_b // 2),
        [("p", threes[0])] + [("v", three) for three in threes[1:]],
        [((block, width), BF16), (pack, BF16), ((4, 16, width), BF16)],
        us=US["U2"],
        after=early[0],
    )
    unit3 = rest_sum(unit3)
    (send,) = kernel_call(
        join_body,
        [("p", unit2), ("v", near2), ("p", unit3)],
        [((2 * unit2.shape[0] + block, width), BF16)],
        us=US["join"],
    )
    far = swap_by_core(send, SECOND)
    packs = both_halves(pack_b)
    mod_shape = (2, block, 6 * width)
    g_time_in, g_time_out, g_table, g_mod, g_patch, prediction, latent_grad, token = kernel_call(
        sums_body,
        [("p", packs[0]), ("v", packs[1])]
        + [("p", a) for a in (modulation_v, time_out_v, *early, tiles)],
        [
            (time_in.shape, F32, "hbm"), (time_out.shape, F32, "hbm"), ((classes, width), F32, "hbm"),
            (mod_shape, F32, "hbm"), (patch_weight.shape, F32, "any"),
            ((slots, out_ch, tile_h, tile_w), BF16, "any"), (latent.shape, F32, "any"),
            ((8, 128), F32),
        ],
        [
            pltpu.VMEM((width // 128, samples * ROWS, 128), F32), pltpu.VMEM(mod_shape, F32),
            pltpu.VMEM((classes, width), F32), pltpu.VMEM(time_out.shape, F32),
            pltpu.VMEM(time_in.shape, F32), pltpu.SemaphoreType.DMA((4,)),
        ],
        us=US["sums"],
    )
    (send3,) = kernel_call(
        far_body,
        [("p", unit3), ("v", far)],
        [((2 * block, width), BF16)],
        us=US["F3"],
        after=token,
    )
    near3 = swap_by_core(send3, FIRST)
    up_shape, down_shape = (2, block, ff), (2, ff // 8, width)
    g_qkv, g_proj, g_up, g_down = kernel_call(
        spread_body,
        [("p", unit2), ("v", near2), ("v", far), ("p", unit3), ("v", near3)],
        [
            ((2, block, 3 * width), F32, "any"), ((2, block, width), F32, "any"),
            (up_shape, F32, "hbm"), (down_shape, F32, "hbm"),
        ],
        [pltpu.VMEM(up_shape, F32), pltpu.VMEM(down_shape, F32), pltpu.SemaphoreType.DMA((4,))],
        us=US["spread"],
    )
    return (
        prediction, latent_grad, g_patch, g_time_in, g_time_out, g_table, g_mod, g_qkv, g_proj,
        g_up, g_down, g_final_mod, g_final.T,
    )


def solution(mesh):
    tiled, split = P("wide", None, "rows", "cols"), P(None, ("rows", "cols"), None)
    return jax.shard_map(
        shards,
        mesh=mesh,
        in_specs=(tiled, tiled, P("wide"), P("wide"), P("wide"), P("wide")) + (P(),) * 11,
        out_specs=(tiled, tiled, P(), P(), P(), P(), split, split, split, split, split, P(), P()),
        check_vma=False,
    )
```

```python
from functools import partial
import math

import jax
import jax.numpy as jnp
import numpy as np
from jax import lax
from jax.experimental import pallas as pl
from jax.experimental.pallas import tpu as pltpu
from jax.sharding import PartitionSpec as P

HEADS = 6
HEAD_DIM = 64
PAIRS = HEADS // 2
LANES = 2 * HEAD_DIM
EPS = 1e-06
F32 = jnp.float32
BF16 = jnp.bfloat16
ROWS = 12
ROW_SHARED, ROW_ACT, ROW_COND, ROW_HID, ROW_FEAT = 5, 6, 7, 8, 9
US = {
    "cond": 5, "embed": 2, "block": 6, "turn": 9, "back": 20, "middle": 4, "last": 4, "early": 0.05, "pack": 0.05, "join": 0.05, "U12": 0.05, "F3": 0.05, "unpack": 0.05, "sums": 5, "spread": 0.05,
    "A1": 0.05, "A2": 0.05, "A2b": 0.05, "A3": 0.05, "A3b": 0.05, "A4": 30, "A4b": 0.05, "A5": 0.05, "A6": 0.05, "S1": 0.05, "U2": 3,
    "U1": 1,
}


def dot(a, b):
    return jnp.dot(a, b, preferred_element_type=F32)


def dot_nt(a, b):
    return lax.dot_general(a, b, (((1,), (1,)), ((), ())), preferred_element_type=F32)


def dot_tn(a, b):
    return lax.dot_general(a, b, (((0,), (0,)), ((), ())), preferred_element_type=F32)


def sds(shape, dtype):
    return jax.ShapeDtypeStruct(shape, dtype)


def layer_norm(states):
    centred = states - jnp.mean(states, axis=-1, keepdims=True)
    inverse = lax.rsqrt(jnp.mean(centred * centred, axis=-1, keepdims=True) + EPS)
    return centred * inverse, inverse


def norm_back(grad, normed, inverse):
    mean_grad = jnp.mean(grad, axis=-1, keepdims=True)
    mean_cross = jnp.mean(grad * normed, axis=-1, keepdims=True)
    return inverse * (grad - mean_grad - normed * mean_cross)


def token_sum(values):
    return jnp.sum(values, axis=0, keepdims=True)


def head_masks(dtype):
    lane = lax.broadcasted_iota(jnp.int32, (1, LANES), 1)
    first = (lane < HEAD_DIM).astype(F32)
    return first.astype(dtype), (1.0 - first).astype(dtype)


def unit_place(zz, ww, cc):
    x, y = ww % 2, ww // 2
    return (x * 8 + y * 4 + zz) if cc == 0 else (y * 8 + x * 4 + zz)


def kernel_call(body, ins, outs, scratch=(), us=1.0, after=None, aliases=()):
    spaces = {"v": pltpu.VMEM, "p": pltpu.VMEM, "s": pltpu.SMEM, "h": pltpu.HBM}
    specs, arrays = [], []
    for kind, array in ins:
        specs.append(pl.BlockSpec(memory_space=spaces[kind]))
        if kind in "ph":
            array = pltpu.with_memory_space_constraint(array, spaces[kind])
        arrays.append(array)
    if after is not None:
        specs.append(pl.BlockSpec(memory_space=pl.ANY))
        arrays.append(after)

    def kernel(*refs):
        body(*refs[: len(ins)], *refs[len(arrays) :])

    return pl.pallas_call(
        kernel,
        in_specs=specs,
        out_specs=[
            pl.BlockSpec(memory_space=pltpu.HBM if "hbm" in o[2:] else pltpu.VMEM) for o in outs
        ],
        out_shape=[
            pltpu.VMEM(o[0], o[1]) if len(o) < 3 else sds(o[0], o[1]) if o[2] == "any" else pltpu.HBM(o[0], o[1])
            for o in outs
        ],
        input_output_aliases=dict(aliases),
        scratch_shapes=list(scratch),
        compiler_params=pltpu.CompilerParams(vmem_limit_bytes=24 * 1024 * 1024),
        cost_estimate=pl.CostEstimate(
            flops=int(us * 1.5e9), bytes_accessed=int(us * 1e6), transcendentals=0
        ),
    )(*arrays)


def one_hot(shape, test):
    first = lax.broadcasted_iota(jnp.int32, shape, 0)
    second = lax.broadcasted_iota(jnp.int32, shape, 1)
    return test(first, second).astype(F32).astype(BF16)


def places():
    return lax.axis_index("rows"), lax.axis_index("cols"), lax.axis_index("wide")


def chip_place(zz, ww, cc):
    x, y = ww % 2, ww // 2
    return zz * 4 + ((2 * y + x) if cc == 0 else (2 * x + y))


def wide_bits():
    _, c, w = places()
    x, y = lax.rem(w, 2), lax.rem(lax.div(w, 2), 2)
    return jnp.where(c == 0, x, y), jnp.where(c == 0, y, x)


def rows_at(index, count):
    return pl.ds(pl.multiple_of(index * count, 16), count)


def tiles_body(latent_h, pred_h, *rest):
    tiles, (latent, pred_grad, sem) = rest[:-3], rest[-3:]
    copies = [
        pltpu.make_async_copy(latent_h, latent, sem.at[0]),
        pltpu.make_async_copy(pred_h, pred_grad, sem.at[1]),
    ]
    for copy in copies:
        copy.start()
    z, _, _ = places()
    _, lat_ch, height, wide = latent.shape
    out_ch = pred_grad.shape[1]
    chans, tok = lat_ch + out_ch, height * wide // 4
    half = wide // 2
    lanes = 2 * chans
    spread = [one_hot((tok, wide), lambda t, v: v == 2 * (t % half) + u) for u in range(2)]
    inside = [
        one_hot((tok, chans * height), lambda t, v: v % height == 2 * (t // half) + par).astype(F32)
        for par in range(2)
    ]

    def lane_of(channel, u):
        return jnp.where(
            channel < lat_ch, u * lat_ch + channel, 2 * lat_ch + u * out_ch + channel - lat_ch
        )

    fold = [
        one_hot((chans * height, lanes), lambda v, lane: lane == lane_of(v // height, u))
        for u in range(2)
    ]
    for copy in copies:
        copy.wait()
    for k, tile in enumerate(tiles):
        image = jnp.concatenate(
            [
                latent[z ^ k].reshape(lat_ch * height, wide),
                pred_grad[z ^ k].reshape(out_ch * height, wide),
            ],
            axis=0,
        )
        wide_rows = [dot_nt(spread[u], image) for u in range(2)]
        for par in range(2):
            tile[par] = sum(
                dot((wide_rows[u] * inside[par]).astype(BF16), fold[u]) for u in range(2)
            ).astype(BF16)


def packed_tile(parities, lanes, order):
    tok = parities[0].shape[0]
    across = tok // order
    total = order * 2 * lanes
    block = 0.0
    for par in range(2):
        copy = one_hot((lanes, total), lambda a, b: b % (2 * lanes) == par * lanes + a)
        block = block + dot(parities[par].astype(BF16), copy)
    own = one_hot((tok, total), lambda t, b: b // (2 * lanes) == t // across).astype(F32)
    gather = one_hot((across, tok), lambda j, t: t % across == j)
    return dot(gather, (block * own).astype(BF16))


def unpacked_tile(block, chans, height, wide):
    lanes = 2 * chans
    half = wide // 2
    image = 0.0
    for u in range(2):
        chosen = one_hot(
            (chans * height, block.shape[1]),
            lambda v, b: b
            == (v % height) // 2 * 2 * lanes + v % 2 * lanes + u * chans + v // height,
        )
        column = dot_nt(chosen, block).astype(BF16)
        image = image + dot(column, one_hot((half, wide), lambda j, v: v == 2 * j + u))
    return image


def by_parity(first, second, offset):
    step = first.shape[0] // 32
    moved = jnp.concatenate([jnp.zeros((step, second.shape[1]), F32), second[:-step]], axis=0)
    return jnp.where(offset == 1, moved, first), jnp.where(offset == 1, first, second)


def cond_body(
    timesteps, labels, freqs, label_table, time_in, final_weight, positions, *rest,
):
    sources, (mods, cond, final_copy, pos), held = rest[:7], rest[7:11], rest[11:18]
    sem = rest[18]
    final_copy[...] = final_weight[...]
    sources = sources[:3] + tuple(source.at[0] for source in sources[3:])
    sources += (positions.at[lax.axis_index("cols")],)
    held = held + (pos,)
    copies = [
        pltpu.make_async_copy(source, target, sem.at[i])
        for i, (source, target) in enumerate(zip(sources, held))
    ]
    for copy in copies:
        copy.start()
    time_out, modulation, final_mod = held[:3]
    z, _, _ = places()
    label = labels[z]
    count, width = time_in.shape
    angles = jnp.full((8, count // 2), timesteps[z].astype(F32)) * freqs[...]
    feats = jnp.concatenate([jnp.cos(angles), jnp.sin(angles)], axis=-1).astype(BF16)
    hidden = dot(feats, time_in[...])
    act = (hidden * jax.nn.sigmoid(hidden)).astype(BF16)
    chosen = one_hot((8, label_table.shape[0]), lambda a, b: b == label)
    copies[0].wait()
    condition = dot(act, time_out[...]) + dot(chosen, label_table[...])
    shared = (condition * jax.nn.sigmoid(condition)).astype(BF16)
    mods[...] = jnp.zeros_like(mods)
    copies[1].wait()
    for layer in range(2):
        values = dot(shared, modulation[layer])
        for k in range(6):
            mods[layer, k : k + 1, :] = values[0:1, k * width : (k + 1) * width]
    copies[2].wait()
    values = dot(shared, final_mod[...])
    for k in range(2):
        mods[2, k : k + 1, :] = values[0:1, k * width : (k + 1) * width]
    lane = lax.broadcasted_iota(jnp.int32, (1, width - count), 1)
    marks = jnp.where(
        lane == 0, lax.div(label, 32), jnp.where(lane == 1, lax.rem(label, 32), 0)
    ).astype(F32)
    cond[...] = jnp.zeros_like(cond)
    cond[0:1, :] = shared[0:1].astype(F32)
    cond[1:2, :] = act[0:1].astype(F32)
    cond[2:3, :] = condition[0:1]
    cond[3:4, :] = hidden[0:1]
    cond[4:5, :] = jnp.concatenate([feats[0:1].astype(F32), marks], axis=-1)
    for copy in copies[3:]:
        copy.wait()


def qkv_forward(state, mods, layer, weight):
    width = state.shape[-1]
    normed, _ = layer_norm(state)
    inner = (normed * (1.0 + mods[layer, 1:2]) + mods[layer, 0:1]).astype(BF16)
    projected = dot(inner, weight[...]).astype(BF16)
    return projected[:, :width], projected[:, width:]


def attend_forward(q, kv, kvp, probs, attended):
    width = q.shape[-1]
    masks = head_masks(BF16)
    for p in range(PAIRS):
        at = slice(p * LANES, (p + 1) * LANES)
        av = slice(width + p * LANES, width + (p + 1) * LANES)
        qp = q[:, at] * BF16(HEAD_DIM**-0.5)
        k0, v0, k1, v1 = kv[:, at], kv[:, av], kvp[:, at], kvp[:, av]
        total = None
        for h in range(2):
            qh = qp * masks[h]
            s0, s1 = dot_nt(qh, k0), dot_nt(qh, k1)
            peak = jnp.maximum(
                jnp.max(s0, axis=-1, keepdims=True), jnp.max(s1, axis=-1, keepdims=True)
            )
            e0, e1 = jnp.exp(s0 - peak), jnp.exp(s1 - peak)
            scale = 1.0 / (
                jnp.sum(e0, axis=-1, keepdims=True) + jnp.sum(e1, axis=-1, keepdims=True)
            )
            p0, p1 = (e0 * scale).astype(BF16), (e1 * scale).astype(BF16)
            probs[2 * p + h, 0] = p0
            probs[2 * p + h, 1] = p1
            part = dot(p0, v0 * masks[h]) + dot(p1, v1 * masks[h])
            total = part if total is None else total + part
        attended[:, at] = total.astype(BF16)


CHUNK = 768


def mlp_forward(middle, mods, layer, up, down, gp, act):
    normed, _ = layer_norm(middle)
    inner = (normed * (1.0 + mods[layer, 4:5]) + mods[layer, 3:4]).astype(BF16)
    branch = None
    for start in range(0, up.shape[1], CHUNK):
        at = slice(start, start + CHUNK)
        hidden = dot(inner, up[:, at])
        square = hidden * hidden
        root = math.sqrt(2.0 / math.pi)
        bent = jnp.tanh(root * hidden * (1.0 + 0.044715 * square))
        half = 0.5 * (1.0 + bent)
        activated = (hidden * half).astype(BF16)
        act[:, at] = activated
        slope = half + 0.5 * hidden * (1.0 - bent * bent) * (root * (1.0 + 3 * 0.044715 * square))
        gp[:, at] = slope.astype(BF16)
        part = dot(activated, down[at, :])
        branch = part if branch is None else branch + part
    return branch


def put_units(keep, send, pair, place, size, at_row):
    first = lax.axis_index("cols") == 0
    block = pair[0].shape[0]
    own = jnp.where(first, place[0], place[1]) * size + at_row
    other = jnp.where(first, place[1], place[0]) * size + at_row
    keep[pl.ds(pl.multiple_of(own, 16), block), :] = jnp.where(first, pair[0], pair[1])
    send[pl.ds(pl.multiple_of(other, 16), block), :] = jnp.where(first, pair[1], pair[0])


def mlp_backward(
    grad, middle, branch, mods, layer, gp, act, up, down, keep, send, size, flip, rows, first, low
):
    width = middle.shape[-1]
    normed, inverse = layer_norm(middle)
    scale = 1.0 + mods[layer, 4:5]
    inner_t = (normed * scale + mods[layer, 3:4]).astype(BF16).T
    branch_grad = (mods[layer, 5:6] * grad).astype(BF16)
    inner_grad = None
    for start in range(0, up.shape[1], CHUNK):
        at = slice(start, start + CHUNK)
        act_grad = dot_nt(branch_grad, down[at, :])
        hidden_grad = (act_grad * gp[:, at].astype(F32)).astype(BF16)
        low[:, at] = hidden_grad
        part = dot_nt(hidden_grad, up[:, at])
        inner_grad = part if inner_grad is None else inner_grad + part
    block = width // 8
    for i in range(up.shape[1] // width):
        at = slice(i * width, (i + 1) * width)
        grad_up = dot(inner_t, low[:, at]).astype(BF16)
        for b in range(4):
            pair = [grad_up[(2 * b + cc) * block : (2 * b + cc + 1) * block] for cc in range(2)]
            place = [unit_place(b, i, cc ^ flip) for cc in range(2)]
            put_units(keep, send, pair, place, size, 0)
        grad_down = dot_tn(act[:, at], branch_grad).astype(BF16)
        for j in range(4):
            pair = [grad_down[(4 * cc + j) * block : (4 * cc + j + 1) * block] for cc in range(2)]
            place = [unit_place(i, j, cc ^ flip) for cc in range(2)]
            put_units(keep, send, pair, place, size, block)
    rows[first : first + 1, :] = token_sum(inner_grad)
    rows[first + 1 : first + 2, :] = token_sum(inner_grad * normed)
    rows[first + 2 : first + 3, :] = token_sum(grad * branch.astype(F32))
    return grad + norm_back(inner_grad * scale, normed, inverse)


def qkv_backward(
    state, middle_grad, dq, dkv, dkvr, mods, layer, weight, gproj, keep, send, shares, rows
):
    width = state.shape[-1]
    block = width // 8
    normed, inverse = layer_norm(state)
    scale = 1.0 + mods[layer, 1:2]
    inner_t = (normed * scale + mods[layer, 0:1]).astype(BF16).T
    dkv_sum = dkv[...] + dkvr[...]
    pieces = (dq[...], dkv_sum[:, :width], dkv_sum[:, width:])
    inner_grad = None

    def put(values, i):
        for b in range(4):
            pair = [values[(2 * b + cc) * block : (2 * b + cc + 1) * block] for cc in range(2)]
            for start, end, place_of, size, at_row in shares:
                place = [place_of(b, i, cc) for cc in range(2)]
                put_units(keep, send, [part[start:end] for part in pair], place, size, at_row)

    for i, piece in enumerate(pieces):
        part = dot_nt(piece, weight[:, i * width : (i + 1) * width])
        inner_grad = part if inner_grad is None else inner_grad + part
        put(dot(inner_t, piece).astype(BF16), i)
    put(gproj[...], 3)
    rows[0:1, :] = token_sum(inner_grad)
    rows[1:2, :] = token_sum(inner_grad * normed)
    return middle_grad + norm_back(inner_grad * scale, normed, inverse)


def embed_body(
    offsets, t0, t1, t2, t3, pos, mods, patch_weight, qkv,
    state, q, kv, patches, tiles,
):
    z, _, _ = places()
    offset = offsets[z]
    for k, tile in enumerate((t0, t1, t2, t3)):
        tiles[k] = tile[...]
    count = tiles.shape[0]
    even = jnp.concatenate([tiles[z ^ t, 0] for t in range(count)], axis=0).astype(F32)
    odd = jnp.concatenate([tiles[z ^ t, 1] for t in range(count)], axis=0).astype(F32)
    step = even.shape[0] // 32
    later = jnp.concatenate([even[step:], jnp.zeros((step, even.shape[1]), F32)], axis=0)
    first = jnp.where(offset == 1, odd, even).astype(BF16)
    second = jnp.where(offset == 1, later, odd).astype(BF16)
    patches[0] = first
    patches[1] = second
    weight = patch_weight[...].astype(F32)
    lanes = weight.shape[0] // 2
    fill = jnp.zeros((even.shape[1] - lanes, weight.shape[1]), F32)
    upper = jnp.concatenate([weight[:lanes], fill], axis=0).astype(BF16)
    lower = jnp.concatenate([weight[lanes:], fill], axis=0).astype(BF16)
    values = dot(first, upper) + dot(second, lower) + pos[...]
    state[...] = values
    q[...], kv[...] = qkv_forward(values, mods, 0, qkv)


def block_body(
    state, q, kv, kvp, mods, proj, up, down, *rest,
):
    sources, rest = rest[:4], rest[4:]
    state1, q1, kv1, probs, attended, attn_out, middle, gp, act, branch = rest[:10]
    targets, sem = rest[10:14], rest[14]
    copies = [
        pltpu.make_async_copy(source.at[1], target, sem.at[i])
        for i, (source, target) in enumerate(zip(sources, targets))
    ]
    for copy in copies:
        copy.start()
    attend_forward(q, kv, kvp, probs, attended)
    m = mods
    attn = dot(attended[...], proj[...])
    attn_out[...] = attn.astype(BF16)
    mid = state[...] + m[0, 2:3] * attn
    middle[...] = mid
    out = mlp_forward(mid, m, 0, up, down, gp, act)
    branch[...] = out.astype(BF16)
    new = mid + m[0, 5:6] * out
    state1[...] = new
    copies[0].wait()
    q1[...], kv1[...] = qkv_forward(new, m, 1, targets[0])
    for copy in copies[1:]:
        copy.wait()


def turn_body(
    offsets, counts, state, q, kv, kvp, mods, cond, patches, final_weight, proj, up, down,
    probs, attended, attn_out, middle_grad, keep, send, preds,
    gp, act, table, low,
):
    z, _, _ = places()
    offset = offsets[z]
    live = (z < counts[0]).astype(F32)
    attend_forward(q, kv, kvp, probs, attended)
    m = mods
    attn = dot(attended[...], proj[...])
    attn_out[...] = attn.astype(BF16)
    middle = state[...] + m[1, 2:3] * attn
    branch = mlp_forward(middle, m, 1, up, down, gp, act)
    last = middle + m[1, 5:6] * branch
    normed, inverse = layer_norm(last)
    scale = 1.0 + m[2, 1:2]
    inner = (normed * scale + m[2, 0:1]).astype(BF16)
    weight = final_weight[...]
    lanes = weight.shape[1] // 2
    out = dot(inner, weight) * live
    preds[0], preds[1] = by_parity(out[:, :lanes], out[:, lanes:], offset)
    across = weight.astype(F32).T
    chosen = patches
    fill = jnp.zeros((chosen.shape[2] - lanes, across.shape[1]), F32)
    upper = jnp.concatenate([fill, across[:lanes]], axis=0).astype(BF16)
    lower = jnp.concatenate([fill, across[lanes:]], axis=0).astype(BF16)
    inner_grad = (dot(chosen[0], upper) + dot(chosen[1], lower)) * live
    table[...] = jnp.zeros_like(table)
    table[0:1, :] = token_sum(inner_grad)
    table[1:2, :] = token_sum(inner_grad * normed)
    table[5:10, :] = 0.5 * cond[0:5, :]
    skip = chosen.shape[2] - lanes
    for r in range(2):
        at = ROWS + r * lanes
        table[at : at + lanes, :] = (dot_tn(chosen[r], inner) * live)[skip:]
    grad = norm_back(inner_grad * scale, normed, inverse)
    size = 2 * (weight.shape[0] // 8)
    middle_grad[...] = mlp_backward(
        grad, middle, branch, m, 1, gp, act, up, down, keep, send, size, 0, table, 2, low
    )
    base = 4 * weight.shape[0]
    keep[base:] = table[...].astype(BF16)
    send[base:] = table[...].astype(BF16)


def attend_back_body(
    layer, q, kv, kvp, probs, attended, attn_out, middle_grad, mods, proj,
    dq, dkv, gproj, dkvs, rows,
):
    grad = middle_grad[...]
    attn_grad = (mods[layer, 2:3] * grad).astype(BF16)
    attended_grad = dot_nt(attn_grad, proj[...]).astype(BF16)
    masks = head_masks(BF16)
    width = q.shape[-1]
    for p in range(PAIRS):
        at = slice(p * LANES, (p + 1) * LANES)
        av = slice(width + p * LANES, width + (p + 1) * LANES)
        qp = q[:, at] * BF16(HEAD_DIM**-0.5)
        dop = attended_grad[:, at]
        ks, vs = (kv[:, at], kvp[:, at]), (kv[:, av], kvp[:, av])
        total = None
        parts = [[], [], [], []]
        q_t, do_t = qp.T, dop.T
        for h in range(2):
            doh = dop * masks[h]
            own = slice(h * HEAD_DIM, (h + 1) * HEAD_DIM)
            ps = [probs[2 * p + h, i] for i in range(2)]
            dps = [dot_nt(doh, vs[i]) for i in range(2)]
            pfs = [ps[i].astype(F32) for i in range(2)]
            inner = sum(jnp.sum(dps[i] * pfs[i], axis=-1, keepdims=True) for i in range(2))
            for i in range(2):
                ds = (pfs[i] * (dps[i] - inner)).astype(BF16)
                part = dot(ds, ks[i] * masks[h])
                total = part if total is None else total + part
                parts[2 * i].append(dot(q_t[own], ds))
                parts[2 * i + 1].append(dot(do_t[own], ps[i]))
        dq[:, at] = (total * HEAD_DIM**-0.5).astype(BF16)
        turned = [jnp.concatenate(part, axis=0).astype(BF16).T for part in parts]
        dkv[:, at] = turned[0]
        dkv[:, av] = turned[1]
        dkvs[:, at] = turned[2]
        dkvs[:, av] = turned[3]
    rows[...] = jnp.zeros_like(rows)
    rows[0:1, :] = token_sum(grad * attn_out[...].astype(F32))
    gproj[...] = dot_tn(attended[...], attn_grad).astype(BF16)


def middle_body(
    state1, middle_grad1, dq, dkv, dkvr, gproj, middle, branch, gp, act, mods, qkv, up, down,
    middle_grad, keep, send, rows, low,
):
    width = dq.shape[-1]
    block = width // 8
    size = 2 * block + 16
    rows[...] = jnp.zeros_like(rows)
    m = mods
    grad = qkv_backward(
        state1[...], middle_grad1[...], dq, dkv, dkvr, m, 1, qkv, gproj, keep, send,
        ((0, 16, unit_place, size, 2 * block), (16, block, chip_place, block - 16, 16 * size)), rows,
    )
    middle_grad[...] = mlp_backward(
        grad, middle[...], branch[...], m, 0, gp, act, up, down, keep, send, size, 0,
        rows, 2, low,
    )


def last_body(
    offsets, state0, middle_grad, dq, dkv, dkvr, gproj, mods, patches, patch_weight,
    rows_a1, rows_mid, rows_a0, qkv,
    keep, send, lgrads, rows, table,
):
    z, _, _ = places()
    offset = offsets[z]
    width = dq.shape[-1]
    block = width // 8
    grad = qkv_backward(
        state0[...], middle_grad[...], dq, dkv, dkvr, mods, 0, qkv, gproj, keep, send,
        ((0, block, lambda zz, ww, cc: unit_place(zz, ww, 1 - cc), block, 0),), rows,
    )
    embed_grad = grad.astype(BF16)
    chosen = patches
    gp0, gp1 = dot_tn(chosen[0], embed_grad), dot_tn(chosen[1], embed_grad)
    chans = patch_weight.shape[0] // 2
    window = dot_nt(embed_grad, patch_weight[...])
    lgrads[0], lgrads[1] = by_parity(window[:, :chans], window[:, chans:], offset)
    table[...] = jnp.zeros_like(table)
    table[0:2, :] = rows[0:2, :]
    table[2:3, :] = rows_a0[0:1, :]
    table[3:6, :] = rows_mid[2:5, :]
    table[6:8, :] = rows_mid[0:2, :]
    table[8:9, :] = rows_a1[0:1, :]
    table[ROWS : ROWS + chans, :] = gp0[:chans]
    table[ROWS + chans : ROWS + 2 * chans, :] = gp1[:chans]
    keep[16 * block :] = table[...].astype(BF16)
    send[16 * block :] = table[...].astype(BF16)


def second_body(keep, recv, keep_out, send_out):
    half = keep_out.shape[0]
    bit = wide_bits()[0]
    keep_out[...] = keep[rows_at(bit, half)] + recv[rows_at(bit, half)]
    send_out[...] = keep[rows_at(1 - bit, half)] + recv[rows_at(1 - bit, half)]


def beta_body(keep, recv, *chips):
    z, _, _ = places()
    size = chips[0].shape[0]
    base = keep.shape[0] - 4 * size
    for k, out in enumerate(chips):
        at = pl.ds(pl.multiple_of(base + (z ^ k) * size, 16), size)
        out[...] = keep[at] + recv[at]


def padded(*pieces):
    rows = jnp.concatenate(pieces, axis=0)
    fill = -rows.shape[0] % 16
    if fill:
        rows = jnp.concatenate([rows, jnp.zeros((fill, rows.shape[1]), F32)], axis=0)
    return rows.astype(BF16)


def paired(mine, other, sums):
    return padded(
        mine[:ROWS], other[:ROWS], mine[ROWS : ROWS + sums] + other[ROWS : ROWS + sums]
    )


def half_of_four(mine, other, sums, flip, four, total):
    _, c, w = places()
    first = jnp.where(c == flip, 1, 2)
    second = 3 - first
    spot = lax.rem(w, 4)
    four[spot] = mine[:ROWS]
    four[spot ^ first] = mine[ROWS : 2 * ROWS]
    four[spot ^ second] = other[:ROWS]
    four[spot ^ first ^ second] = other[ROWS : 2 * ROWS]
    at = slice(2 * ROWS, 2 * ROWS + sums)
    total[...] = mine[at] + other[at]
    half = sums // 2
    return padded(four[2 * c], four[2 * c + 1], total[pl.ds(pl.multiple_of(c * half, 8), half), :])


def first_body(keep, recv, keep_out, table, send):
    half = (keep.shape[0] - table.shape[0]) // 2
    bit = wide_bits()[0]
    keep_out[...] = keep[rows_at(bit, half)] + recv[rows_at(bit, half)]
    send[0:half] = keep[rows_at(1 - bit, half)] + recv[rows_at(1 - bit, half)]
    rows = keep[2 * half :] + recv[2 * half :]
    table[...] = rows
    send[half:] = rows


def first_pair_body(sums, keep, table, recv, keep_out, pair_out, send):
    size = keep.shape[0]
    half = size // 2
    bit = wide_bits()[1]
    keep_out[...] = keep[rows_at(bit, half)] + recv[rows_at(bit, half)]
    send[0:half] = keep[rows_at(1 - bit, half)] + recv[rows_at(1 - bit, half)]
    pair = paired(table[...].astype(F32), recv[size:].astype(F32), sums)
    pair_out[...] = pair
    send[half:] = pair


def first_chip_body(
    sums, keep, pair, recv, z0, z1, z2, z3, four, total
):
    z, _, _ = places()
    size = keep.shape[0]
    unit = size // 4
    rows = half_of_four(pair[...].astype(F32), recv[size:].astype(F32), sums, 0, four, total)
    for k, out in enumerate((z0, z1, z2, z3)):
        out[0:unit] = keep[rows_at(z ^ k, unit)] + recv[rows_at(z ^ k, unit)]
        out[unit:] = rows


def unit1_body(sums, o0, o1, o2, o3, unit, pack):
    ones = (o0, o1, o2, o3)
    unit[...] = chip_sum(ones, slice(0, unit.shape[0])).astype(BF16)
    chip_rows(sums, ones, unit.shape[0], pack)


def pack_body(preds, lgrads, tiles):
    z, _, _ = places()
    tok = preds.shape[1] // 4
    tiles[:, :, 256:] = jnp.zeros((4, 16, 128), BF16)
    for k in range(4):
        cut = pl.ds(pl.multiple_of((z ^ k) * tok, 8), tok)
        parts = [lgrads[0, cut, :], lgrads[1, cut, :]]
        leading = [part.astype(BF16).astype(F32) for part in parts]
        chans = lgrads.shape[2]
        latents = jnp.concatenate(
            [
                packed_tile(leading, chans, 8),
                packed_tile([a - b for a, b in zip(parts, leading)], chans, 8),
            ],
            axis=1,
        )
        predicted = packed_tile([preds[0, cut, :], preds[1, cut, :]], preds.shape[2], 8)
        tiles[k, :, 0:256] = jnp.concatenate([latents, predicted], axis=0).astype(BF16)


def chip_sum(parts, at):
    return sum(part[at].astype(F32) for part in parts)


def third_body(keep2, recv2, b0, b1, b2, b3, keep2_out, keepb, part, whole):
    half2, halfb = keep2.shape[0] // 2, keepb.shape[0]
    bit = wide_bits()[1]
    keep2_out[...] = keep2[rows_at(bit, half2)] + recv2[rows_at(bit, half2)]
    part[0:half2] = keep2[rows_at(1 - bit, half2)] + recv2[rows_at(1 - bit, half2)]
    whole[...] = chip_sum((b0, b1, b2, b3), slice(None)).astype(BF16)
    keepb[...] = whole[rows_at(bit, halfb)]
    part[half2:] = whole[rows_at(1 - bit, halfb)]


def third_send_body(keep3, recv3, part, keep3_out, table, send):
    size = part.shape[0]
    size3 = keep3.shape[0] - table.shape[0]
    half3 = size3 // 2
    bit = wide_bits()[1]
    send[0:size] = part[...]
    keep3_out[...] = keep3[rows_at(bit, half3)] + recv3[rows_at(bit, half3)]
    send[size : size + half3] = keep3[rows_at(1 - bit, half3)] + recv3[rows_at(1 - bit, half3)]
    rows = keep3[size3:] + recv3[size3:]
    table[...] = rows
    send[size + half3 :] = rows


def fourth_body(
    sums, keep2, keep3, keepb, table, recv, z0, z1, z2, z3, keep3_out, keepb_out, pair_out, send
):
    z, _, _ = places()
    size2, size3, sizeb = keep2.shape[0], keep3.shape[0], keepb.shape[0]
    half3, halfb = size3 // 2, sizeb // 2
    unit = size2 // 4
    for k, out in enumerate((z0, z1, z2, z3)):
        out[...] = keep2[rows_at(z ^ k, unit)] + recv[rows_at(z ^ k, unit)]
    bit = wide_bits()[0]

    def half(held, index, size, base):
        start = pl.multiple_of(index * size, 16)
        return held[pl.ds(start, size)] + recv[pl.ds(pl.multiple_of(start + base, 16), size)]

    keep3_out[...] = half(keep3, bit, half3, size2 + sizeb)
    send[0:half3] = half(keep3, 1 - bit, half3, size2 + sizeb)
    keepb_out[...] = half(keepb, bit, halfb, size2)
    send[half3 : half3 + halfb] = half(keepb, 1 - bit, halfb, size2)
    pair = paired(table[...].astype(F32), recv[size2 + size3 + sizeb :].astype(F32), sums)
    pair_out[...] = pair
    send[half3 + halfb :] = pair


def fifth_body(sums, keep3, keepb, pair, recv, tiles, z0, z1, z2, z3, unitb, four, total):
    z, _, _ = places()
    size3, sizeb = keep3.shape[0], keepb.shape[0]
    unit3 = size3 // 4
    other = recv[size3 + sizeb :].astype(F32)
    rows = half_of_four(pair[...].astype(F32), other, sums, 1, four, total)
    end = unit3 + rows.shape[0]
    for k, out in enumerate((z0, z1, z2, z3)):
        out[0:unit3] = keep3[rows_at(z ^ k, unit3)] + recv[rows_at(z ^ k, unit3)]
        out[unit3:end] = rows
        out[end:] = tiles[k]
    unitb[...] = keepb[...] + recv[size3 : size3 + sizeb]


def chip_rows(sums, parts, size, pack):
    rows = [part[size : size + 48 if sums > 8 else size + 32].astype(F32) for part in parts]
    total = sum(r[2 * ROWS : 2 * ROWS + sums] for r in rows)
    pack[...] = padded(*[r[: 2 * ROWS] for r in rows], total)


def unit12_body(unit1, t0, t1, t2, t3, unitb, unit):
    size, end2 = unit1.shape[0], t0.shape[0]
    unit[0:size] = unit1[...]
    unit[size : size + end2] = chip_sum((t0, t1, t2, t3), slice(None)).astype(BF16)
    unit[size + end2 :] = unitb[...]


def join_body(own, near, send):
    size = own.shape[0]
    send[0:size] = own[...]
    send[size:] = near[...]


def unit3_body(sums, z0, z1, z2, z3, unit, pack, tiles):
    parts = (z0, z1, z2, z3)
    size = unit.shape[0]
    unit[...] = chip_sum(parts, slice(0, size)).astype(BF16)
    chip_rows(sums, parts, size, pack)
    for k, part in enumerate(parts):
        tiles[k] = part[size + 32 :]


def silu_slope(values):
    sigmoid = jax.nn.sigmoid(values)
    return sigmoid * (1.0 + values * (1.0 - sigmoid))


def sample_table(table, pack, other):
    parts, half = table.shape[0], table.shape[1] // 2
    for side, held in enumerate((pack, other)):
        for i in range(parts):
            at = slice(128 * i, 128 * (i + 1))
            table[i, half * side : half * (side + 1)] = held[0:half, at].astype(F32)
    samples = table.shape[1] // ROWS

    def rows(r):
        return jnp.concatenate(
            [table[i, pl.ds(r, samples, stride=ROWS), :] for i in range(parts)], axis=-1
        )

    return rows


def join_sums(out, pack, other):
    c = lax.axis_index("cols")
    count = out.shape[0] // 2
    for side, held in enumerate((pack, other)):
        at = pl.ds(pl.multiple_of((c ^ side) * count, 8), count)
        out[at, :] = held[held.shape[0] - 16 :].astype(F32)[:count]


def early_sums_body(
    pack, other, final_mod,
    g_final_mod, g_final, shared_t, slopes, base, high, act_t, feat_t, hot, table,
):
    rows = sample_table(table, pack, other)
    join_sums(g_final, pack, other)
    fmods = jnp.concatenate([rows(0), rows(1)], axis=-1).astype(BF16)
    shared_t[...] = rows(ROW_SHARED).T
    g_final_mod[...] = dot(shared_t[...].astype(BF16), fmods)
    base[...] = dot_nt(fmods, final_mod[...])
    slopes[0] = silu_slope(rows(ROW_COND))
    slopes[1] = silu_slope(rows(ROW_HID))
    for k in range(3):
        high[k] = rows(2 + k)
    act_t[...] = rows(ROW_ACT).T.astype(BF16)
    feats = rows(ROW_FEAT)
    count = feat_t.shape[0]
    feat_t[...] = feats[:, :count].T.astype(BF16)
    label = (feats[:, count : count + 1] * 32.0 + feats[:, count + 1 : count + 2]).astype(jnp.int32)
    classes = hot.shape[0]
    lane = lax.broadcasted_iota(jnp.int32, (feats.shape[0], (classes + 127) // 128 * 128), 1)
    hot[...] = (lane == label).astype(F32).T[:classes].astype(BF16)


def sums_body(
    pack, other, modulation, time_out, shared_t, slopes, base, high, act_t, feat_t, hot,
    g_time_in, g_time_out, g_table, g_mod, g_patch, token,
    table, mod_v, table_v, time_out_v, time_in_v, sem,
):
    z, c, _ = places()
    token[...] = jnp.zeros_like(token)
    rows = sample_table(table, pack, other)
    mods = [
        jnp.concatenate([rows(k) for k in range(6)], axis=-1).astype(BF16),
        jnp.concatenate(
            [rows(k) for k in range(6, 9)] + [high[k] for k in range(3)], axis=-1
        ).astype(BF16),
    ]
    block = mod_v.shape[1]
    start = pl.multiple_of((z * 2 + c) * block, 8)
    mine = shared_t[pl.ds(start, block), :].astype(BF16)
    copies = []

    def leave(source, target):
        copies.append(pltpu.make_async_copy(source, target, sem.at[len(copies)]))
        copies[-1].start()

    for layer in range(2):
        mod_v[layer] = dot(mine, mods[layer])
    leave(mod_v, g_mod)
    shared_grad = base[...]
    for layer in range(2):
        shared_grad += dot_nt(mods[layer], modulation[layer])
    cond_grad = shared_grad * slopes[0]
    cond_low = cond_grad.astype(BF16)
    cond_rest = (cond_grad - cond_low.astype(F32)).astype(BF16)
    table_v[...] = dot(hot[...], cond_low) + dot(hot[...], cond_rest)
    leave(table_v, g_table)
    time_out_v[...] = dot(act_t[...], cond_low)
    leave(time_out_v, g_time_out)
    time_grad = dot_nt(cond_low, time_out[...]) * slopes[1]
    time_in_v[...] = dot(feat_t[...], time_grad.astype(BF16))
    leave(time_in_v, g_time_in)
    join_sums(g_patch, pack, other)
    for copy in copies:
        copy.wait()


def unpack_body(tiles, prediction, latent_grad, token):
    z, _, _ = places()
    token[...] = jnp.zeros_like(token)
    _, out_ch, height, wide = prediction.shape
    lat_ch = latent_grad.shape[1]
    for k in range(4):
        tile = tiles[k].astype(F32)
        image = unpacked_tile(tile[8:16, 0:256].astype(BF16), out_ch, height, wide)
        prediction[z ^ k] = image.astype(BF16).reshape(out_ch, height, wide)
        image = unpacked_tile(tile[0:8, 0:128].astype(BF16), lat_ch, height, wide)
        image = image + unpacked_tile(tile[0:8, 128:256].astype(BF16), lat_ch, height, wide)
        latent_grad[z ^ k] = image.reshape(lat_ch, height, wide)


def place_mlp(up, down, piece, unit):
    block, width = up.shape[0], down.shape[1]
    cols = pl.ds(pl.multiple_of(unit * width, 128), width)
    up[:, cols] = piece[0:block].astype(F32)
    down_rows = pl.ds(pl.multiple_of(unit * block, 8), block)
    down[down_rows, :] = piece[block : 2 * block].astype(F32)


def place_attn(qkv, proj, piece, unit):
    width = proj.shape[1]

    @pl.when(unit < 3)
    def _():
        cols = pl.ds(pl.multiple_of(unit * width, 128), width)
        qkv[:, cols] = piece.astype(F32)

    @pl.when(unit == 3)
    def _():
        proj[...] = piece.astype(F32)


def wide_spots():
    _, c, w = places()
    first = jnp.where(c == 0, 1, 2)
    spot = lax.rem(w, 4)
    return spot, spot ^ first, spot ^ first ^ 3, spot ^ 3


def leave_all(pairs, sem, copies):
    for source, target in pairs:
        copies.append(pltpu.make_async_copy(source, target, sem.at[len(copies)]))
        copies[-1].start()


def spread_body(own, near, far, g_qkv, g_proj, g_up, g_down, up, down, qkv, proj, sem):
    size2 = own.shape[0]
    block = proj.shape[0]
    size = 2 * block
    units = ((own, 0), (near, 0), (far, 0), (far, size2))
    copies = []
    for layer, start in ((1, 0), (0, size)):
        for (ref, base), unit in zip(units, wide_spots()):
            piece = ref[base + start : base + start + size]
            place_mlp(up.at[layer], down.at[layer], piece, unit)
        leave_all(
            ((up.at[layer], g_up.at[layer]), (down.at[layer], g_down.at[layer])), sem, copies
        )
    for (ref, base), unit in zip(units, wide_spots()):
        place_attn(qkv, proj, ref[base + 2 * size : base + size2], unit)
    leave_all(((qkv, g_qkv.at[1]), (proj, g_proj.at[1])), sem, copies)
    for copy in copies:
        copy.wait()


def last_spread_body(own, near, far, _q, _p, g_qkv, g_proj, qkv, proj, sem):
    size = own.shape[0]
    units = ((own, 0), (near, 0), (far, 0), (far, size))
    for (ref, base), unit in zip(units, wide_spots()):
        place_attn(qkv, proj, ref[base : base + size], unit)
    copies = []
    leave_all(((qkv, g_qkv.at[0]), (proj, g_proj.at[0])), sem, copies)
    for copy in copies:
        copy.wait()


def swap(value, axis, bit):
    count = lax.axis_size(axis)
    return lax.ppermute(value, axis, [(i, i ^ bit) for i in range(count)])


def swap_by_core(value, bits):
    wide, cores = lax.axis_size("wide"), lax.axis_size("cols")
    pairs = [
        (w * cores + c, (w ^ bits[c % 2]) * cores + c) for w in range(wide) for c in range(cores)
    ]
    return lax.ppermute(value, ("wide", "cols"), pairs)


FIRST, SECOND = (1, 2), (2, 1)


def rest_sum(value):
    bit = 4
    while bit < lax.axis_size("wide"):
        value = (value.astype(F32) + swap(value, "wide", bit).astype(F32)).astype(value.dtype)
        bit *= 2
    return value


def rest_gather(value):
    bit = 4
    while bit < lax.axis_size("wide"):
        value = jnp.concatenate([value, swap(value, "wide", bit)])
        bit *= 2
    return value


def position_tables(row_count, col_count, cores, width):
    quarter = width // 4
    omega = np.exp(-math.log(10000.0) * np.arange(quarter) / quarter)
    row_angle = np.arange(row_count)[:, None] * omega[None, :]
    col_angle = np.arange(col_count * cores)[:, None] * omega[None, :]
    row_part = np.concatenate([np.sin(row_angle), np.cos(row_angle)], axis=-1)
    col_part = np.concatenate([np.sin(col_angle), np.cos(col_angle)], axis=-1)
    col_part = col_part.reshape(cores, 1, col_count, width // 2)
    table = np.concatenate(
        [
            np.broadcast_to(row_part[None, :, None, :], (cores, row_count, col_count, width // 2)),
            np.broadcast_to(col_part, (cores, row_count, col_count, width // 2)),
        ],
        axis=-1,
    )
    return table.reshape(cores, row_count * col_count, width).astype(np.float32)


def shards(
    latent, pred_grad, timesteps, labels, offsets, counts, patch_weight, time_in, time_out,
    label_table, modulation, qkv_weight, proj_weight, up_weight, down_weight, final_mod, final_weight,
):
    slots, lat_ch, tile_h, tile_w = latent.shape
    out_ch = pred_grad.shape[1]
    width = patch_weight.shape[1]
    ff = up_weight.shape[2]
    n_rows, n_cols = lax.axis_size("rows"), lax.axis_size("cols")
    hp, wp = tile_h // 2, tile_w // 2
    tile_tok = hp * wp
    tokens = n_rows * tile_tok
    lanes = 2 * (lat_ch + out_ch)
    block = width // 8
    tok, wide_tok, double = (tokens, width), (tokens, ff), (tokens, 2 * width)

    tiles = kernel_call(
        tiles_body,
        [("h", latent), ("h", pred_grad)],
        [((2, tile_tok, lanes), BF16)] * n_rows,
        [
            pltpu.VMEM(latent.shape, BF16), pltpu.VMEM(pred_grad.shape, BF16),
            pltpu.SemaphoreType.DMA((2,)),
        ],
        us=1,
    )

    def along_z(parts):
        return [parts[0]] + [swap(parts[k], "rows", k) for k in range(1, n_rows)]

    def both_halves(pack):
        if lax.axis_size("wide") > 4:
            rows, sums = rest_gather(pack[: 8 * ROWS]), rest_sum(pack[8 * ROWS :])
            pack = jnp.concatenate([rows, sums])
        return pack, swap(pack, "cols", 1)

    tiles = along_z(tiles)
    half = time_in.shape[0] // 2
    freqs = np.exp(-math.log(10000.0) * np.arange(half, dtype=np.float32) / np.float32(half))
    positions = jnp.asarray(position_tables(n_rows * hp, wp, n_cols, width))
    blocks = (qkv_weight, proj_weight, up_weight, down_weight)
    weights = (time_out, modulation, final_mod) + blocks
    held = [(weight.shape[1:], BF16) for weight in blocks]
    (
        mods, cond, final_v, pos, time_out_v, modulation_v, final_mod_v, qkv0, proj0, up0, down0,
    ) = kernel_call(
        cond_body,
        [("s", timesteps), ("s", labels), ("v", jnp.asarray(freqs.astype(np.float32))[None])]
        + [("v", label_table), ("v", time_in), ("v", final_weight), ("h", positions)]
        + [("h", weight) for weight in weights],
        [((3, 8, width), F32), ((8, width), F32), (final_weight.shape, BF16), (tok, F32)]
        + [(weight.shape, BF16) for weight in weights[:3]]
        + held,
        [pltpu.SemaphoreType.DMA((len(weights) + 1,))],
        us=US["cond"],
    )
    probs_shape = (HEADS, 2, tokens, tokens)
    state0, q0, kv0, patches = kernel_call(
        embed_body,
        [("s", offsets)]
        + [("v", t) for t in tiles]
        + [("p", pos), ("p", mods), ("v", patch_weight), ("p", qkv0)],
        [(tok, F32), (tok, BF16), (double, BF16), ((2, tokens, lanes), BF16)],
        [pltpu.VMEM((n_rows, 2, tile_tok, lanes), BF16)],
        us=US["embed"],
    )
    kv0p = swap(kv0, "cols", 1)
    (
        state1, q1, kv1, probs0, attended0, attn_out0, middle0, gp0, act0, branch0, qkv1, proj1, up1, down1,
    ) = kernel_call(
        block_body,
        [("p", state0), ("p", q0), ("p", kv0), ("v", kv0p)]
        + [("p", a) for a in (mods, proj0, up0, down0)]
        + [("h", weight) for weight in blocks],
        [
            (tok, F32), (tok, BF16), (double, BF16), (probs_shape, BF16), (tok, BF16), (tok, BF16),
            (tok, F32), (wide_tok, BF16), (wide_tok, BF16), (tok, BF16),
        ]
        + held,
        [pltpu.SemaphoreType.DMA((4,))],
        us=US["block"],
    )
    kv1p = swap(kv1, "cols", 1)
    sums_a, sums_b = 4 * out_ch, 4 * lat_ch
    rows_1 = 16 * 2 * block + 48
    probs1, attended1, attn_out1, mgrad1, keep1, send1, preds = kernel_call(
        turn_body,
        [("s", offsets), ("s", counts), ("p", state1), ("p", q1), ("p", kv1), ("v", kv1p)]
        + [("p", a) for a in (mods, cond, patches, final_v, proj1, up1, down1)],
        [
            (probs_shape, BF16), (tok, BF16), (tok, BF16), (tok, F32), ((rows_1, width), BF16),
            ((rows_1, width), BF16), ((2, tokens, 2 * out_ch), F32),
        ],
        [
            pltpu.VMEM(wide_tok, BF16), pltpu.VMEM(wide_tok, BF16), pltpu.VMEM((48, width), F32),
            pltpu.VMEM(wide_tok, BF16),
        ],
        us=US["turn"],
    )
    recv1 = swap(send1, "cols", 1)

    def attend_back(layer, q, kv, kvp, *saved, after):
        return kernel_call(
            partial(attend_back_body, layer),
            [("p", q), ("p", kv), ("v", kvp)] + [("p", a) for a in saved[:-1] + (mods, saved[-1])],
            [
                (tok, BF16), (double, BF16), ((width, width), BF16), (double, BF16), ((8, width), F32),
            ],
            us=US["back"],
            after=after,
        )

    dq1, dkv1, gproj1, dkvs1, rows_a1 = attend_back(
        1, q1, kv1, kv1p, probs1, attended1, attn_out1, mgrad1, proj1, after=None
    )
    dkvr1 = swap(dkvs1, "cols", 1)
    keep1, table1, send1 = kernel_call(
        first_body,
        [("p", keep1), ("v", recv1)],
        [((8 * 2 * block, width), BF16), ((48, width), BF16), ((8 * 2 * block + 48, width), BF16)],
        us=US["A1"],
        after=rows_a1,
    )
    recv1 = swap_by_core(send1, FIRST)
    mgrad0, keep2, send2, rows_mid = kernel_call(
        middle_body,
        [("p", a) for a in (state1, mgrad1, dq1, dkv1)]
        + [("v", dkvr1)]
        + [("p", a) for a in (gproj1, middle0, branch0, gp0, act0, mods, qkv1, up0, down0)],
        [
            (tok, F32), ((16 * 3 * block, width), BF16), ((16 * 3 * block, width), BF16),
            ((8, width), F32),
        ],
        [pltpu.VMEM(wide_tok, BF16)],
        us=US["middle"],
        after=table1,
    )
    recv2 = swap(send2, "cols", 1)
    dq0, dkv0, gproj0, dkvs0, rows_a0 = attend_back(
        0, q0, kv0, kv0p, probs0, attended0, attn_out0, mgrad0, proj0, after=None
    )
    dkvr0 = swap(dkvs0, "cols", 1)
    keep1, pair1, send1 = kernel_call(
        partial(first_pair_body, sums_a),
        [("p", keep1), ("p", table1), ("v", recv1)],
        [((4 * 2 * block, width), BF16), ((64, width), BF16), ((4 * 2 * block + 64, width), BF16)],
        us=US["A2"],
        after=rows_a0,
    )
    recv1 = swap_by_core(send1, SECOND)
    alpha, beta = 2 * block + 16, block - 16
    send_rows = 4 * alpha + 2 * beta + 8 * block + 32
    whole_2, whole_r = keep2, recv2
    keep2, send2 = kernel_call(
        second_body,
        [("p", whole_2), ("v", whole_r)],
        [((8 * alpha, width), BF16)] * 2,
        us=US["A3"],
        after=pair1,
    )
    recv2 = swap_by_core(send2, FIRST)
    betas = kernel_call(
        beta_body,
        [("p", whole_2), ("v", whole_r)],
        [((4 * beta, width), BF16)] * 4,
        us=US["A3b"],
        after=keep2,
    )
    chips = betas[0]
    betas = along_z(betas)
    rows_3 = 16 * block + 32
    keep3, send3, lgrads = kernel_call(
        last_body,
        [("s", offsets), ("p", state0), ("p", mgrad0), ("p", dq0), ("p", dkv0), ("v", dkvr0)]
        + [("p", gproj0), ("p", mods), ("p", patches), ("v", patch_weight)]
        + [("p", a) for a in (rows_a1, rows_mid, rows_a0, qkv0)],
        [((rows_3, width), BF16), ((rows_3, width), BF16), ((2, tokens, 2 * lat_ch), F32)],
        [pltpu.VMEM((8, width), F32), pltpu.VMEM((32, width), F32)],
        us=US["last"],
        after=chips,
    )
    recv3 = swap(send3, "cols", 1)
    (tiles,) = kernel_call(
        pack_body, [("p", preds), ("p", lgrads)], [((4, 16, width), BF16)], us=US["pack"]
    )
    ones = kernel_call(
        partial(first_chip_body, sums_a),
        [("p", keep1), ("p", pair1), ("v", recv1)],
        [((2 * block + 48, width), BF16)] * 4,
        [pltpu.VMEM((4, ROWS, width), F32), pltpu.VMEM((sums_a, width), F32)],
        us=US["A2b"],
        after=tiles,
    )
    chips = ones[0]
    ones = along_z(ones)
    keep2, keepb, part = kernel_call(
        third_body,
        [("p", keep2), ("v", recv2), ("p", betas[0])] + [("v", beta) for beta in betas[1:]],
        [
            ((4 * alpha, width), BF16), ((2 * beta, width), BF16),
            ((4 * alpha + 2 * beta, width), BF16),
        ],
        [pltpu.VMEM((4 * beta, width), BF16)],
        us=US["A4"],
        after=chips,
    )
    keep3, table3, send = kernel_call(
        third_send_body,
        [("p", keep3), ("v", recv3), ("p", part)],
        [((8 * block, width), BF16), ((32, width), BF16), ((send_rows, width), BF16)],
        us=US["A4b"],
    )
    recv = swap_by_core(send, SECOND)
    *twos, keep3, keepb, pair3, send = kernel_call(
        partial(fourth_body, sums_b),
        [("p", keep2), ("p", keep3), ("p", keepb), ("p", table3), ("v", recv)],
        [((alpha, width), BF16)] * 4
        + [
            ((4 * block, width), BF16), ((beta, width), BF16), ((48, width), BF16),
            ((4 * block + beta + 48, width), BF16),
        ],
        us=US["A5"],
    )
    recv = swap_by_core(send, FIRST)
    twos = along_z(twos)
    pack = (8 * ROWS + 16, width)
    unit1, pack_a = kernel_call(
        partial(unit1_body, sums_a // 2),
        [("p", ones[0])] + [("v", one) for one in ones[1:]],
        [((2 * block, width), BF16), (pack, BF16)],
        us=US["U1"],
        after=pair3,
    )
    packs = both_halves(pack_a)
    *threes, unitb = kernel_call(
        partial(fifth_body, sums_b),
        [("p", keep3), ("p", keepb), ("p", pair3), ("v", recv), ("p", tiles)],
        [((block + 32 + 16, width), BF16)] * 4 + [((beta, width), BF16)],
        [pltpu.VMEM((4, ROWS, width), F32), pltpu.VMEM((sums_b, width), F32)],
        us=US["A6"],
        after=pack_a,
    )
    threes = along_z(threes)
    (unit2,) = kernel_call(
        unit12_body,
        [("p", unit1), ("p", twos[0])] + [("v", two) for two in twos[1:]] + [("p", unitb)],
        [((2 * block + alpha + beta, width), BF16)],
        us=US["U12"],
    )
    unit2 = rest_sum(unit2)
    near2 = swap_by_core(unit2, FIRST)
    samples = 2 * (packs[0].shape[0] - 16) // ROWS
    classes = label_table.shape[0]
    feat_count = time_in.shape[0]
    g_final_mod, g_final, *early = kernel_call(
        early_sums_body,
        [("p", packs[0]), ("v", packs[1]), ("p", final_mod_v)],
        [
            (final_mod.shape, F32, "any"), ((sums_a, width), F32, "any"), ((width, samples), F32),
            ((2, samples, width), F32), ((samples, width), F32), ((3, samples, width), F32),
            ((width, samples), BF16), ((feat_count, samples), BF16), ((classes, samples), BF16),
        ],
        [pltpu.VMEM((width // 128, samples * ROWS, 128), F32)],
        us=US["early"],
        after=unit2,
    )
    unit3, pack_b, tiles = kernel_call(
        partial(unit3_body, sums_b // 2),
        [("p", threes[0])] + [("v", three) for three in threes[1:]],
        [((block, width), BF16), (pack, BF16), ((4, 16, width), BF16)],
        us=US["U2"],
        after=early[0],
    )
    unit3 = rest_sum(unit3)
    near3 = swap_by_core(unit3, FIRST)
    (send2,) = kernel_call(
        join_body,
        [("p", unit2), ("v", near2)],
        [((2 * unit2.shape[0], width), BF16)],
        us=US["join"],
        after=tiles,
    )
    far2 = swap_by_core(send2, SECOND)
    packs = both_halves(pack_b)
    mod_shape = (2, block, 6 * width)
    g_time_in, g_time_out, g_table, g_mod, g_patch, token = kernel_call(
        sums_body,
        [("p", packs[0]), ("v", packs[1])]
        + [("p", a) for a in (modulation_v, time_out_v, *early)],
        [
            (time_in.shape, F32, "hbm"), (time_out.shape, F32, "hbm"), ((classes, width), F32, "hbm"),
            (mod_shape, F32, "hbm"), (patch_weight.shape, F32, "any"), ((8, 128), F32),
        ],
        [
            pltpu.VMEM((width // 128, samples * ROWS, 128), F32), pltpu.VMEM(mod_shape, F32),
            pltpu.VMEM((classes, width), F32), pltpu.VMEM(time_out.shape, F32),
            pltpu.VMEM(time_in.shape, F32), pltpu.SemaphoreType.DMA((4,)),
        ],
        us=US["sums"],
    )
    (send3,) = kernel_call(
        join_body,
        [("p", unit3), ("v", near3)],
        [((2 * block, width), BF16)],
        us=US["F3"],
        after=token,
    )
    far3 = swap_by_core(send3, SECOND)
    prediction, latent_grad, token = kernel_call(
        unpack_body,
        [("p", tiles)],
        [((slots, out_ch, tile_h, tile_w), BF16, "any"), (latent.shape, F32, "any"), ((8, 128), F32)],
        us=US["unpack"],
        after=send3,
    )
    up_shape, down_shape = (2, block, ff), (2, ff // 8, width)
    attn_scratch = [pltpu.VMEM((block, 3 * width), F32), pltpu.VMEM((block, width), F32)]
    attn_shapes = [((2, block, 3 * width), F32, "hbm"), ((2, block, width), F32, "hbm")]
    g_qkv, g_proj, g_up, g_down = kernel_call(
        spread_body,
        [("p", unit2), ("v", near2), ("v", far2)],
        attn_shapes + [(up_shape, F32, "hbm"), (down_shape, F32, "hbm")],
        [pltpu.VMEM(up_shape, F32), pltpu.VMEM(down_shape, F32)]
        + attn_scratch
        + [pltpu.SemaphoreType.DMA((6,))],
        us=US["spread"],
        after=token,
    )
    g_qkv, g_proj = kernel_call(
        last_spread_body,
        [("p", unit3), ("v", near3), ("v", far3), ("h", g_qkv), ("h", g_proj)],
        attn_shapes,
        attn_scratch + [pltpu.SemaphoreType.DMA((2,))],
        us=US["spread"],
        aliases=((3, 0), (4, 1)),
    )
    return (
        prediction, latent_grad, g_patch, g_time_in, g_time_out, g_table, g_mod, g_qkv, g_proj,
        g_up, g_down, g_final_mod, g_final.T,
    )


def solution(mesh):
    tiled, split = P("wide", None, "rows", "cols"), P(None, ("rows", "cols"), None)
    return jax.shard_map(
        shards,
        mesh=mesh,
        in_specs=(tiled, tiled, P("wide"), P("wide"), P("wide"), P("wide")) + (P(),) * 11,
        out_specs=(tiled, tiled, P(), P(), P(), P(), split, split, split, split, split, P(), P()),
        check_vma=False,
    )
```

```python
from functools import partial
import math

import jax
import jax.numpy as jnp
import numpy as np
from jax import lax
from jax.experimental import pallas as pl
from jax.experimental.pallas import tpu as pltpu
from jax.sharding import PartitionSpec as P

HEADS = 6
HEAD_DIM = 64
PAIRS = HEADS // 2
LANES = 2 * HEAD_DIM
EPS = 1e-06
F32 = jnp.float32
BF16 = jnp.bfloat16
ROWS = 12
ROW_SHARED, ROW_ACT, ROW_COND, ROW_HID, ROW_FEAT = 5, 6, 7, 8, 9
US = {
    "cond": 5, "embed": 2, "block": 6, "turn": 9, "back": 20, "middle": 4, "last": 4, "early": 0.05, "pack": 0.05, "join": 0.05, "U12": 0.05, "F3": 0.05, "unpack": 0.05, "sums": 5, "spread": 0.05,
    "A1": 0.05, "A2": 0.05, "A2b": 0.05, "A3": 0.05, "A3b": 0.05, "A4": 30, "A4b": 0.05, "A5": 0.05, "A6": 0.05, "S1": 0.05, "U2": 3,
    "U1": 1,
}


def dot(a, b):
    return jnp.dot(a, b, preferred_element_type=F32)


def dot_nt(a, b):
    return lax.dot_general(a, b, (((1,), (1,)), ((), ())), preferred_element_type=F32)


def dot_tn(a, b):
    return lax.dot_general(a, b, (((0,), (0,)), ((), ())), preferred_element_type=F32)


def sds(shape, dtype):
    return jax.ShapeDtypeStruct(shape, dtype)


def layer_norm(states):
    centred = states - jnp.mean(states, axis=-1, keepdims=True)
    inverse = lax.rsqrt(jnp.mean(centred * centred, axis=-1, keepdims=True) + EPS)
    return centred * inverse, inverse


def norm_back(grad, normed, inverse):
    mean_grad = jnp.mean(grad, axis=-1, keepdims=True)
    mean_cross = jnp.mean(grad * normed, axis=-1, keepdims=True)
    return inverse * (grad - mean_grad - normed * mean_cross)


def token_sum(values):
    return jnp.sum(values, axis=0, keepdims=True)


def head_masks(dtype):
    lane = lax.broadcasted_iota(jnp.int32, (1, LANES), 1)
    first = (lane < HEAD_DIM).astype(F32)
    return first.astype(dtype), (1.0 - first).astype(dtype)


def unit_place(zz, ww, cc):
    x, y = ww % 2, ww // 2
    return (x * 8 + y * 4 + zz) if cc == 0 else (y * 8 + x * 4 + zz)


def kernel_call(body, ins, outs, scratch=(), us=1.0, after=None, aliases=()):
    spaces = {"v": pltpu.VMEM, "p": pltpu.VMEM, "s": pltpu.SMEM, "h": pltpu.HBM}
    specs, arrays = [], []
    for kind, array in ins:
        specs.append(pl.BlockSpec(memory_space=spaces[kind]))
        if kind in "ph":
            array = pltpu.with_memory_space_constraint(array, spaces[kind])
        arrays.append(array)
    if after is not None:
        specs.append(pl.BlockSpec(memory_space=pl.ANY))
        arrays.append(after)

    def kernel(*refs):
        body(*refs[: len(ins)], *refs[len(arrays) :])

    return pl.pallas_call(
        kernel,
        in_specs=specs,
        out_specs=[
            pl.BlockSpec(memory_space=pltpu.HBM if "hbm" in o[2:] else pltpu.VMEM) for o in outs
        ],
        out_shape=[
            pltpu.VMEM(o[0], o[1]) if len(o) < 3 else sds(o[0], o[1]) if o[2] == "any" else pltpu.HBM(o[0], o[1])
            for o in outs
        ],
        input_output_aliases=dict(aliases),
        scratch_shapes=list(scratch),
        compiler_params=pltpu.CompilerParams(vmem_limit_bytes=24 * 1024 * 1024),
        cost_estimate=pl.CostEstimate(
            flops=int(us * 1.5e9), bytes_accessed=int(us * 1e6), transcendentals=0
        ),
    )(*arrays)


def one_hot(shape, test):
    first = lax.broadcasted_iota(jnp.int32, shape, 0)
    second = lax.broadcasted_iota(jnp.int32, shape, 1)
    return test(first, second).astype(F32).astype(BF16)


def places():
    return lax.axis_index("rows"), lax.axis_index("cols"), lax.axis_index("wide")


def chip_place(zz, ww, cc):
    x, y = ww % 2, ww // 2
    return zz * 4 + ((2 * y + x) if cc == 0 else (2 * x + y))


def wide_bits():
    _, c, w = places()
    x, y = lax.rem(w, 2), lax.rem(lax.div(w, 2), 2)
    return jnp.where(c == 0, x, y), jnp.where(c == 0, y, x)


def rows_at(index, count):
    return pl.ds(pl.multiple_of(index * count, 16), count)


def tiles_body(latent_h, pred_h, *rest):
    tiles, (latent, pred_grad, sem) = rest[:-3], rest[-3:]
    copies = [
        pltpu.make_async_copy(latent_h, latent, sem.at[0]),
        pltpu.make_async_copy(pred_h, pred_grad, sem.at[1]),
    ]
    for copy in copies:
        copy.start()
    z, _, _ = places()
    _, lat_ch, height, wide = latent.shape
    out_ch = pred_grad.shape[1]
    chans, tok = lat_ch + out_ch, height * wide // 4
    half = wide // 2
    lanes = 2 * chans
    spread = [one_hot((tok, wide), lambda t, v: v == 2 * (t % half) + u) for u in range(2)]
    inside = [
        one_hot((tok, chans * height), lambda t, v: v % height == 2 * (t // half) + par).astype(F32)
        for par in range(2)
    ]

    def lane_of(channel, u):
        return jnp.where(
            channel < lat_ch, u * lat_ch + channel, 2 * lat_ch + u * out_ch + channel - lat_ch
        )

    fold = [
        one_hot((chans * height, lanes), lambda v, lane: lane == lane_of(v // height, u))
        for u in range(2)
    ]
    for copy in copies:
        copy.wait()
    for k, tile in enumerate(tiles):
        image = jnp.concatenate(
            [
                latent[z ^ k].reshape(lat_ch * height, wide),
                pred_grad[z ^ k].reshape(out_ch * height, wide),
            ],
            axis=0,
        )
        wide_rows = [dot_nt(spread[u], image) for u in range(2)]
        for par in range(2):
            tile[par] = sum(
                dot((wide_rows[u] * inside[par]).astype(BF16), fold[u]) for u in range(2)
            ).astype(BF16)


def packed_tile(parities, lanes, order):
    tok = parities[0].shape[0]
    across = tok // order
    total = order * 2 * lanes
    block = 0.0
    for par in range(2):
        copy = one_hot((lanes, total), lambda a, b: b % (2 * lanes) == par * lanes + a)
        block = block + dot(parities[par].astype(BF16), copy)
    own = one_hot((tok, total), lambda t, b: b // (2 * lanes) == t // across).astype(F32)
    gather = one_hot((across, tok), lambda j, t: t % across == j)
    return dot(gather, (block * own).astype(BF16))


def unpacked_tile(block, chans, height, wide):
    lanes = 2 * chans
    half = wide // 2
    image = 0.0
    for u in range(2):
        chosen = one_hot(
            (chans * height, block.shape[1]),
            lambda v, b: b
            == (v % height) // 2 * 2 * lanes + v % 2 * lanes + u * chans + v // height,
        )
        column = dot_nt(chosen, block).astype(BF16)
        image = image + dot(column, one_hot((half, wide), lambda j, v: v == 2 * j + u))
    return image


def by_parity(first, second, offset):
    step = first.shape[0] // 32
    moved = jnp.concatenate([jnp.zeros((step, second.shape[1]), F32), second[:-step]], axis=0)
    return jnp.where(offset == 1, moved, first), jnp.where(offset == 1, first, second)


def cond_body(
    timesteps, labels, freqs, label_table, time_in, final_weight, positions, *rest,
):
    sources, (mods, cond, final_copy, pos), held = rest[:7], rest[7:11], rest[11:18]
    sem = rest[18]
    final_copy[...] = final_weight[...]
    sources = sources[:3] + tuple(source.at[0] for source in sources[3:])
    sources += (positions.at[lax.axis_index("cols")],)
    held = held + (pos,)
    copies = [
        pltpu.make_async_copy(source, target, sem.at[i])
        for i, (source, target) in enumerate(zip(sources, held))
    ]
    for copy in copies:
        copy.start()
    time_out, modulation, final_mod = held[:3]
    z, _, _ = places()
    label = labels[z]
    count, width = time_in.shape
    angles = jnp.full((8, count // 2), timesteps[z].astype(F32)) * freqs[...]
    feats = jnp.concatenate([jnp.cos(angles), jnp.sin(angles)], axis=-1).astype(BF16)
    hidden = dot(feats, time_in[...])
    act = (hidden * jax.nn.sigmoid(hidden)).astype(BF16)
    chosen = one_hot((8, label_table.shape[0]), lambda a, b: b == label)
    copies[0].wait()
    condition = dot(act, time_out[...]) + dot(chosen, label_table[...])
    shared = (condition * jax.nn.sigmoid(condition)).astype(BF16)
    mods[...] = jnp.zeros_like(mods)
    copies[1].wait()
    for layer in range(2):
        values = dot(shared, modulation[layer])
        for k in range(6):
            mods[layer, k : k + 1, :] = values[0:1, k * width : (k + 1) * width]
    copies[2].wait()
    values = dot(shared, final_mod[...])
    for k in range(2):
        mods[2, k : k + 1, :] = values[0:1, k * width : (k + 1) * width]
    lane = lax.broadcasted_iota(jnp.int32, (1, width - count), 1)
    marks = jnp.where(
        lane == 0, lax.div(label, 32), jnp.where(lane == 1, lax.rem(label, 32), 0)
    ).astype(F32)
    cond[...] = jnp.zeros_like(cond)
    cond[0:1, :] = shared[0:1].astype(F32)
    cond[1:2, :] = act[0:1].astype(F32)
    cond[2:3, :] = condition[0:1]
    cond[3:4, :] = hidden[0:1]
    cond[4:5, :] = jnp.concatenate([feats[0:1].astype(F32), marks], axis=-1)
    for copy in copies[3:]:
        copy.wait()


def qkv_forward(state, mods, layer, weight):
    width = state.shape[-1]
    normed, _ = layer_norm(state)
    inner = (normed * (1.0 + mods[layer, 1:2]) + mods[layer, 0:1]).astype(BF16)
    projected = dot(inner, weight[...]).astype(BF16)
    return projected[:, :width], projected[:, width:]


def attend_forward(q, kv, kvp, probs, attended):
    width = q.shape[-1]
    masks = head_masks(BF16)
    for p in range(PAIRS):
        at = slice(p * LANES, (p + 1) * LANES)
        av = slice(width + p * LANES, width + (p + 1) * LANES)
        qp = q[:, at] * BF16(HEAD_DIM**-0.5)
        k0, v0, k1, v1 = kv[:, at], kv[:, av], kvp[:, at], kvp[:, av]
        total = None
        for h in range(2):
            qh = qp * masks[h]
            s0, s1 = dot_nt(qh, k0), dot_nt(qh, k1)
            peak = jnp.maximum(
                jnp.max(s0, axis=-1, keepdims=True), jnp.max(s1, axis=-1, keepdims=True)
            )
            e0, e1 = jnp.exp(s0 - peak), jnp.exp(s1 - peak)
            scale = 1.0 / (
                jnp.sum(e0, axis=-1, keepdims=True) + jnp.sum(e1, axis=-1, keepdims=True)
            )
            p0, p1 = (e0 * scale).astype(BF16), (e1 * scale).astype(BF16)
            probs[2 * p + h, 0] = p0
            probs[2 * p + h, 1] = p1
            part = dot(p0, v0 * masks[h]) + dot(p1, v1 * masks[h])
            total = part if total is None else total + part
        attended[:, at] = total.astype(BF16)


CHUNK = 768


def mlp_forward(middle, mods, layer, up, down, gp, act):
    normed, _ = layer_norm(middle)
    inner = (normed * (1.0 + mods[layer, 4:5]) + mods[layer, 3:4]).astype(BF16)
    branch = None
    for start in range(0, up.shape[1], CHUNK):
        at = slice(start, start + CHUNK)
        hidden = dot(inner, up[:, at])
        square = hidden * hidden
        root = math.sqrt(2.0 / math.pi)
        bent = jnp.tanh(root * hidden * (1.0 + 0.044715 * square))
        half = 0.5 * (1.0 + bent)
        activated = (hidden * half).astype(BF16)
        act[:, at] = activated
        slope = half + 0.5 * hidden * (1.0 - bent * bent) * (root * (1.0 + 3 * 0.044715 * square))
        gp[:, at] = slope.astype(BF16)
        part = dot(activated, down[at, :])
        branch = part if branch is None else branch + part
    return branch


def put_units(keep, send, pair, place, size, at_row):
    first = lax.axis_index("cols") == 0
    block = pair[0].shape[0]
    own = jnp.where(first, place[0], place[1]) * size + at_row
    other = jnp.where(first, place[1], place[0]) * size + at_row
    keep[pl.ds(pl.multiple_of(own, 16), block), :] = jnp.where(first, pair[0], pair[1])
    send[pl.ds(pl.multiple_of(other, 16), block), :] = jnp.where(first, pair[1], pair[0])


def mlp_backward(
    grad, middle, branch, mods, layer, gp, act, up, down, keep, send, size, flip, rows, first, low
):
    width = middle.shape[-1]
    normed, inverse = layer_norm(middle)
    scale = 1.0 + mods[layer, 4:5]
    inner_t = (normed * scale + mods[layer, 3:4]).astype(BF16).T
    branch_grad = (mods[layer, 5:6] * grad).astype(BF16)
    inner_grad = None
    for start in range(0, up.shape[1], CHUNK):
        at = slice(start, start + CHUNK)
        act_grad = dot_nt(branch_grad, down[at, :])
        hidden_grad = (act_grad * gp[:, at].astype(F32)).astype(BF16)
        low[:, at] = hidden_grad
        part = dot_nt(hidden_grad, up[:, at])
        inner_grad = part if inner_grad is None else inner_grad + part
    block = width // 8
    for i in range(up.shape[1] // width):
        at = slice(i * width, (i + 1) * width)
        grad_up = dot(inner_t, low[:, at]).astype(BF16)
        for b in range(4):
            pair = [grad_up[(2 * b + cc) * block : (2 * b + cc + 1) * block] for cc in range(2)]
            place = [unit_place(b, i, cc ^ flip) for cc in range(2)]
            put_units(keep, send, pair, place, size, 0)
        grad_down = dot_tn(act[:, at], branch_grad).astype(BF16)
        for j in range(4):
            pair = [grad_down[(4 * cc + j) * block : (4 * cc + j + 1) * block] for cc in range(2)]
            place = [unit_place(i, j, cc ^ flip) for cc in range(2)]
            put_units(keep, send, pair, place, size, block)
    rows[first : first + 1, :] = token_sum(inner_grad)
    rows[first + 1 : first + 2, :] = token_sum(inner_grad * normed)
    rows[first + 2 : first + 3, :] = token_sum(grad * branch.astype(F32))
    return grad + norm_back(inner_grad * scale, normed, inverse)


def qkv_backward(
    state, middle_grad, dq, dkv, dkvr, mods, layer, weight, gproj, keep, send, shares, rows
):
    width = state.shape[-1]
    block = width // 8
    normed, inverse = layer_norm(state)
    scale = 1.0 + mods[layer, 1:2]
    inner_t = (normed * scale + mods[layer, 0:1]).astype(BF16).T
    dkv_sum = dkv[...] + dkvr[...]
    pieces = (dq[...], dkv_sum[:, :width], dkv_sum[:, width:])
    inner_grad = None

    def put(values, i):
        for b in range(4):
            pair = [values[(2 * b + cc) * block : (2 * b + cc + 1) * block] for cc in range(2)]
            for start, end, place_of, size, at_row in shares:
                place = [place_of(b, i, cc) for cc in range(2)]
                put_units(keep, send, [part[start:end] for part in pair], place, size, at_row)

    for i, piece in enumerate(pieces):
        part = dot_nt(piece, weight[:, i * width : (i + 1) * width])
        inner_grad = part if inner_grad is None else inner_grad + part
        put(dot(inner_t, piece).astype(BF16), i)
    put(gproj[...], 3)
    rows[0:1, :] = token_sum(inner_grad)
    rows[1:2, :] = token_sum(inner_grad * normed)
    return middle_grad + norm_back(inner_grad * scale, normed, inverse)


def embed_body(
    offsets, t0, t1, t2, t3, pos, mods, patch_weight, qkv,
    state, q, kv, patches, tiles,
):
    z, _, _ = places()
    offset = offsets[z]
    for k, tile in enumerate((t0, t1, t2, t3)):
        tiles[k] = tile[...]
    count = tiles.shape[0]
    even = jnp.concatenate([tiles[z ^ t, 0] for t in range(count)], axis=0).astype(F32)
    odd = jnp.concatenate([tiles[z ^ t, 1] for t in range(count)], axis=0).astype(F32)
    step = even.shape[0] // 32
    later = jnp.concatenate([even[step:], jnp.zeros((step, even.shape[1]), F32)], axis=0)
    first = jnp.where(offset == 1, odd, even).astype(BF16)
    second = jnp.where(offset == 1, later, odd).astype(BF16)
    patches[0] = first
    patches[1] = second
    weight = patch_weight[...].astype(F32)
    lanes = weight.shape[0] // 2
    fill = jnp.zeros((even.shape[1] - lanes, weight.shape[1]), F32)
    upper = jnp.concatenate([weight[:lanes], fill], axis=0).astype(BF16)
    lower = jnp.concatenate([weight[lanes:], fill], axis=0).astype(BF16)
    values = dot(first, upper) + dot(second, lower) + pos[...]
    state[...] = values
    q[...], kv[...] = qkv_forward(values, mods, 0, qkv)


def block_body(
    state, q, kv, kvp, mods, proj, up, down, *rest,
):
    sources, rest = rest[:4], rest[4:]
    state1, q1, kv1, probs, attended, attn_out, middle, gp, act, branch = rest[:10]
    targets, sem = rest[10:14], rest[14]
    copies = [
        pltpu.make_async_copy(source.at[1], target, sem.at[i])
        for i, (source, target) in enumerate(zip(sources, targets))
    ]
    for copy in copies:
        copy.start()
    attend_forward(q, kv, kvp, probs, attended)
    m = mods
    attn = dot(attended[...], proj[...])
    attn_out[...] = attn.astype(BF16)
    mid = state[...] + m[0, 2:3] * attn
    middle[...] = mid
    out = mlp_forward(mid, m, 0, up, down, gp, act)
    branch[...] = out.astype(BF16)
    new = mid + m[0, 5:6] * out
    state1[...] = new
    copies[0].wait()
    q1[...], kv1[...] = qkv_forward(new, m, 1, targets[0])
    for copy in copies[1:]:
        copy.wait()


def turn_body(
    offsets, counts, state, q, kv, kvp, mods, cond, patches, final_weight, proj, up, down,
    probs, attended, attn_out, middle_grad, keep, send, preds,
    gp, act, table, low,
):
    z, _, _ = places()
    offset = offsets[z]
    live = (z < counts[0]).astype(F32)
    attend_forward(q, kv, kvp, probs, attended)
    m = mods
    attn = dot(attended[...], proj[...])
    attn_out[...] = attn.astype(BF16)
    middle = state[...] + m[1, 2:3] * attn
    branch = mlp_forward(middle, m, 1, up, down, gp, act)
    last = middle + m[1, 5:6] * branch
    normed, inverse = layer_norm(last)
    scale = 1.0 + m[2, 1:2]
    inner = (normed * scale + m[2, 0:1]).astype(BF16)
    weight = final_weight[...]
    lanes = weight.shape[1] // 2
    out = dot(inner, weight) * live
    preds[0], preds[1] = by_parity(out[:, :lanes], out[:, lanes:], offset)
    across = weight.astype(F32).T
    chosen = patches
    fill = jnp.zeros((chosen.shape[2] - lanes, across.shape[1]), F32)
    upper = jnp.concatenate([fill, across[:lanes]], axis=0).astype(BF16)
    lower = jnp.concatenate([fill, across[lanes:]], axis=0).astype(BF16)
    inner_grad = (dot(chosen[0], upper) + dot(chosen[1], lower)) * live
    table[...] = jnp.zeros_like(table)
    table[0:1, :] = token_sum(inner_grad)
    table[1:2, :] = token_sum(inner_grad * normed)
    table[5:10, :] = 0.5 * cond[0:5, :]
    skip = chosen.shape[2] - lanes
    for r in range(2):
        at = ROWS + r * lanes
        table[at : at + lanes, :] = (dot_tn(chosen[r], inner) * live)[skip:]
    grad = norm_back(inner_grad * scale, normed, inverse)
    size = 2 * (weight.shape[0] // 8)
    middle_grad[...] = mlp_backward(
        grad, middle, branch, m, 1, gp, act, up, down, keep, send, size, 0, table, 2, low
    )
    base = 4 * weight.shape[0]
    keep[base:] = table[...].astype(BF16)
    send[base:] = table[...].astype(BF16)


def attend_back_body(
    layer, q, kv, kvp, probs, attended, attn_out, middle_grad, mods, proj,
    dq, dkv, gproj, dkvs, rows,
):
    grad = middle_grad[...]
    attn_grad = (mods[layer, 2:3] * grad).astype(BF16)
    attended_grad = dot_nt(attn_grad, proj[...]).astype(BF16)
    masks = head_masks(BF16)
    width = q.shape[-1]
    for p in range(PAIRS):
        at = slice(p * LANES, (p + 1) * LANES)
        av = slice(width + p * LANES, width + (p + 1) * LANES)
        qp = q[:, at] * BF16(HEAD_DIM**-0.5)
        dop = attended_grad[:, at]
        ks, vs = (kv[:, at], kvp[:, at]), (kv[:, av], kvp[:, av])
        total = None
        parts = [[], [], [], []]
        q_t, do_t = qp.T, dop.T
        for h in range(2):
            doh = dop * masks[h]
            own = slice(h * HEAD_DIM, (h + 1) * HEAD_DIM)
            ps = [probs[2 * p + h, i] for i in range(2)]
            dps = [dot_nt(doh, vs[i]) for i in range(2)]
            pfs = [ps[i].astype(F32) for i in range(2)]
            inner = sum(jnp.sum(dps[i] * pfs[i], axis=-1, keepdims=True) for i in range(2))
            for i in range(2):
                ds = (pfs[i] * (dps[i] - inner)).astype(BF16)
                part = dot(ds, ks[i] * masks[h])
                total = part if total is None else total + part
                parts[2 * i].append(dot(q_t[own], ds))
                parts[2 * i + 1].append(dot(do_t[own], ps[i]))
        dq[:, at] = (total * HEAD_DIM**-0.5).astype(BF16)
        turned = [jnp.concatenate(part, axis=0).astype(BF16).T for part in parts]
        dkv[:, at] = turned[0]
        dkv[:, av] = turned[1]
        dkvs[:, at] = turned[2]
        dkvs[:, av] = turned[3]
    rows[...] = jnp.zeros_like(rows)
    rows[0:1, :] = token_sum(grad * attn_out[...].astype(F32))
    gproj[...] = dot_tn(attended[...], attn_grad).astype(BF16)


def middle_body(
    state1, middle_grad1, dq, dkv, dkvr, gproj, middle, branch, gp, act, mods, qkv, up, down,
    middle_grad, keep, send, rows, low,
):
    width = dq.shape[-1]
    block = width // 8
    size = 2 * block + 16
    rows[...] = jnp.zeros_like(rows)
    m = mods
    grad = qkv_backward(
        state1[...], middle_grad1[...], dq, dkv, dkvr, m, 1, qkv, gproj, keep, send,
        ((0, 16, unit_place, size, 2 * block), (16, block, chip_place, block - 16, 16 * size)), rows,
    )
    middle_grad[...] = mlp_backward(
        grad, middle[...], branch[...], m, 0, gp, act, up, down, keep, send, size, 0,
        rows, 2, low,
    )


def last_body(
    offsets, state0, middle_grad, dq, dkv, dkvr, gproj, mods, patches, patch_weight,
    rows_a1, rows_mid, rows_a0, qkv,
    keep, send, lgrads, rows, table,
):
    z, _, _ = places()
    offset = offsets[z]
    width = dq.shape[-1]
    block = width // 8
    grad = qkv_backward(
        state0[...], middle_grad[...], dq, dkv, dkvr, mods, 0, qkv, gproj, keep, send,
        ((0, block, lambda zz, ww, cc: unit_place(zz, ww, 1 - cc), block, 0),), rows,
    )
    embed_grad = grad.astype(BF16)
    chosen = patches
    gp0, gp1 = dot_tn(chosen[0], embed_grad), dot_tn(chosen[1], embed_grad)
    chans = patch_weight.shape[0] // 2
    window = dot_nt(embed_grad, patch_weight[...])
    lgrads[0], lgrads[1] = by_parity(window[:, :chans], window[:, chans:], offset)
    table[...] = jnp.zeros_like(table)
    table[0:2, :] = rows[0:2, :]
    table[2:3, :] = rows_a0[0:1, :]
    table[3:6, :] = rows_mid[2:5, :]
    table[6:8, :] = rows_mid[0:2, :]
    table[8:9, :] = rows_a1[0:1, :]
    table[ROWS : ROWS + chans, :] = gp0[:chans]
    table[ROWS + chans : ROWS + 2 * chans, :] = gp1[:chans]
    keep[16 * block :] = table[...].astype(BF16)
    send[16 * block :] = table[...].astype(BF16)


def second_body(keep, recv, keep_out, send_out):
    half = keep_out.shape[0]
    bit = wide_bits()[0]
    keep_out[...] = keep[rows_at(bit, half)] + recv[rows_at(bit, half)]
    send_out[...] = keep[rows_at(1 - bit, half)] + recv[rows_at(1 - bit, half)]


def beta_body(keep, recv, *chips):
    z, _, _ = places()
    size = chips[0].shape[0]
    base = keep.shape[0] - 4 * size
    for k, out in enumerate(chips):
        at = pl.ds(pl.multiple_of(base + (z ^ k) * size, 16), size)
        out[...] = keep[at] + recv[at]


def padded(*pieces):
    rows = jnp.concatenate(pieces, axis=0)
    fill = -rows.shape[0] % 16
    if fill:
        rows = jnp.concatenate([rows, jnp.zeros((fill, rows.shape[1]), F32)], axis=0)
    return rows.astype(BF16)


def paired(mine, other, sums):
    return padded(
        mine[:ROWS], other[:ROWS], mine[ROWS : ROWS + sums] + other[ROWS : ROWS + sums]
    )


def half_of_four(mine, other, sums, flip, four, total):
    _, c, w = places()
    first = jnp.where(c == flip, 1, 2)
    second = 3 - first
    spot = lax.rem(w, 4)
    four[spot] = mine[:ROWS]
    four[spot ^ first] = mine[ROWS : 2 * ROWS]
    four[spot ^ second] = other[:ROWS]
    four[spot ^ first ^ second] = other[ROWS : 2 * ROWS]
    at = slice(2 * ROWS, 2 * ROWS + sums)
    total[...] = mine[at] + other[at]
    half = sums // 2
    return padded(four[2 * c], four[2 * c + 1], total[pl.ds(pl.multiple_of(c * half, 8), half), :])


def first_body(keep, recv, keep_out, table, send):
    half = (keep.shape[0] - table.shape[0]) // 2
    bit = wide_bits()[0]
    keep_out[...] = keep[rows_at(bit, half)] + recv[rows_at(bit, half)]
    send[0:half] = keep[rows_at(1 - bit, half)] + recv[rows_at(1 - bit, half)]
    rows = keep[2 * half :] + recv[2 * half :]
    table[...] = rows
    send[half:] = rows


def first_pair_body(sums, keep, table, recv, keep_out, pair_out, send):
    size = keep.shape[0]
    half = size // 2
    bit = wide_bits()[1]
    keep_out[...] = keep[rows_at(bit, half)] + recv[rows_at(bit, half)]
    send[0:half] = keep[rows_at(1 - bit, half)] + recv[rows_at(1 - bit, half)]
    pair = paired(table[...].astype(F32), recv[size:].astype(F32), sums)
    pair_out[...] = pair
    send[half:] = pair


def first_chip_body(
    sums, keep, pair, recv, z0, z1, z2, z3, four, total
):
    z, _, _ = places()
    size = keep.shape[0]
    unit = size // 4
    rows = half_of_four(pair[...].astype(F32), recv[size:].astype(F32), sums, 0, four, total)
    for k, out in enumerate((z0, z1, z2, z3)):
        out[0:unit] = keep[rows_at(z ^ k, unit)] + recv[rows_at(z ^ k, unit)]
        out[unit:] = rows


def unit1_body(sums, o0, o1, o2, o3, unit, pack):
    ones = (o0, o1, o2, o3)
    unit[...] = chip_sum(ones, slice(0, unit.shape[0])).astype(BF16)
    chip_rows(sums, ones, unit.shape[0], pack)


def pack_body(preds, lgrads, tiles):
    z, _, _ = places()
    tok = preds.shape[1] // 4
    tiles[:, :, 256:] = jnp.zeros((4, 16, 128), BF16)
    for k in range(4):
        cut = pl.ds(pl.multiple_of((z ^ k) * tok, 8), tok)
        parts = [lgrads[0, cut, :], lgrads[1, cut, :]]
        leading = [part.astype(BF16).astype(F32) for part in parts]
        chans = lgrads.shape[2]
        latents = jnp.concatenate(
            [
                packed_tile(leading, chans, 8),
                packed_tile([a - b for a, b in zip(parts, leading)], chans, 8),
            ],
            axis=1,
        )
        predicted = packed_tile([preds[0, cut, :], preds[1, cut, :]], preds.shape[2], 8)
        tiles[k, :, 0:256] = jnp.concatenate([latents, predicted], axis=0).astype(BF16)


def chip_sum(parts, at):
    return sum(part[at].astype(F32) for part in parts)


def third_body(keep2, recv2, b0, b1, b2, b3, keep2_out, keepb, part, whole):
    half2, halfb = keep2.shape[0] // 2, keepb.shape[0]
    bit = wide_bits()[1]
    keep2_out[...] = keep2[rows_at(bit, half2)] + recv2[rows_at(bit, half2)]
    part[0:half2] = keep2[rows_at(1 - bit, half2)] + recv2[rows_at(1 - bit, half2)]
    whole[...] = chip_sum((b0, b1, b2, b3), slice(None)).astype(BF16)
    keepb[...] = whole[rows_at(bit, halfb)]
    part[half2:] = whole[rows_at(1 - bit, halfb)]


def third_send_body(keep3, recv3, part, keep3_out, table, send):
    size = part.shape[0]
    size3 = keep3.shape[0] - table.shape[0]
    half3 = size3 // 2
    bit = wide_bits()[1]
    send[0:size] = part[...]
    keep3_out[...] = keep3[rows_at(bit, half3)] + recv3[rows_at(bit, half3)]
    send[size : size + half3] = keep3[rows_at(1 - bit, half3)] + recv3[rows_at(1 - bit, half3)]
    rows = keep3[size3:] + recv3[size3:]
    table[...] = rows
    send[size + half3 :] = rows


def fourth_body(
    sums, keep2, keep3, keepb, table, recv, z0, z1, z2, z3, keep3_out, keepb_out, pair_out, send
):
    z, _, _ = places()
    size2, size3, sizeb = keep2.shape[0], keep3.shape[0], keepb.shape[0]
    half3, halfb = size3 // 2, sizeb // 2
    unit = size2 // 4
    for k, out in enumerate((z0, z1, z2, z3)):
        out[...] = keep2[rows_at(z ^ k, unit)] + recv[rows_at(z ^ k, unit)]
    bit = wide_bits()[0]

    def half(held, index, size, base):
        start = pl.multiple_of(index * size, 16)
        return held[pl.ds(start, size)] + recv[pl.ds(pl.multiple_of(start + base, 16), size)]

    keep3_out[...] = half(keep3, bit, half3, size2 + sizeb)
    send[0:half3] = half(keep3, 1 - bit, half3, size2 + sizeb)
    keepb_out[...] = half(keepb, bit, halfb, size2)
    send[half3 : half3 + halfb] = half(keepb, 1 - bit, halfb, size2)
    pair = paired(table[...].astype(F32), recv[size2 + size3 + sizeb :].astype(F32), sums)
    pair_out[...] = pair
    send[half3 + halfb :] = pair


def fifth_body(sums, keep3, keepb, pair, recv, tiles, z0, z1, z2, z3, unitb, four, total):
    z, _, _ = places()
    size3, sizeb = keep3.shape[0], keepb.shape[0]
    unit3 = size3 // 4
    other = recv[size3 + sizeb :].astype(F32)
    rows = half_of_four(pair[...].astype(F32), other, sums, 1, four, total)
    end = unit3 + rows.shape[0]
    for k, out in enumerate((z0, z1, z2, z3)):
        out[0:unit3] = keep3[rows_at(z ^ k, unit3)] + recv[rows_at(z ^ k, unit3)]
        out[unit3:end] = rows
        out[end:] = tiles[k]
    unitb[...] = keepb[...] + recv[size3 : size3 + sizeb]


def chip_rows(sums, parts, size, pack):
    rows = [part[size : size + 48 if sums > 8 else size + 32].astype(F32) for part in parts]
    total = sum(r[2 * ROWS : 2 * ROWS + sums] for r in rows)
    pack[...] = padded(*[r[: 2 * ROWS] for r in rows], total)


def unit12_body(unit1, t0, t1, t2, t3, unitb, unit):
    size, end2 = unit1.shape[0], t0.shape[0]
    unit[0:size] = unit1[...]
    unit[size : size + end2] = chip_sum((t0, t1, t2, t3), slice(None)).astype(BF16)
    unit[size + end2 :] = unitb[...]


def join_body(own, near, send):
    size = own.shape[0]
    send[0:size] = own[...]
    send[size:] = near[...]


def unit3_body(sums, z0, z1, z2, z3, unit, pack, tiles):
    parts = (z0, z1, z2, z3)
    size = unit.shape[0]
    unit[...] = chip_sum(parts, slice(0, size)).astype(BF16)
    chip_rows(sums, parts, size, pack)
    for k, part in enumerate(parts):
        tiles[k] = part[size + 32 :]


def silu_slope(values):
    sigmoid = jax.nn.sigmoid(values)
    return sigmoid * (1.0 + values * (1.0 - sigmoid))


def sample_table(table, pack, other):
    parts, half = table.shape[0], table.shape[1] // 2
    for side, held in enumerate((pack, other)):
        for i in range(parts):
            at = slice(128 * i, 128 * (i + 1))
            table[i, half * side : half * (side + 1)] = held[0:half, at].astype(F32)
    samples = table.shape[1] // ROWS

    def rows(r):
        return jnp.concatenate(
            [table[i, pl.ds(r, samples, stride=ROWS), :] for i in range(parts)], axis=-1
        )

    return rows


def join_sums(out, pack, other):
    c = lax.axis_index("cols")
    count = out.shape[0] // 2
    for side, held in enumerate((pack, other)):
        at = pl.ds(pl.multiple_of((c ^ side) * count, 8), count)
        out[at, :] = held[held.shape[0] - 16 :].astype(F32)[:count]


def early_sums_body(
    pack, other, final_mod,
    g_final_mod, g_final, shared_t, slopes, base, high, act_t, feat_t, hot, table,
):
    rows = sample_table(table, pack, other)
    join_sums(g_final, pack, other)
    fmods = jnp.concatenate([rows(0), rows(1)], axis=-1).astype(BF16)
    shared_t[...] = rows(ROW_SHARED).T
    g_final_mod[...] = dot(shared_t[...].astype(BF16), fmods)
    base[...] = dot_nt(fmods, final_mod[...])
    slopes[0] = silu_slope(rows(ROW_COND))
    slopes[1] = silu_slope(rows(ROW_HID))
    for k in range(3):
        high[k] = rows(2 + k)
    act_t[...] = rows(ROW_ACT).T.astype(BF16)
    feats = rows(ROW_FEAT)
    count = feat_t.shape[0]
    feat_t[...] = feats[:, :count].T.astype(BF16)
    label = (feats[:, count : count + 1] * 32.0 + feats[:, count + 1 : count + 2]).astype(jnp.int32)
    classes = hot.shape[0]
    lane = lax.broadcasted_iota(jnp.int32, (feats.shape[0], (classes + 127) // 128 * 128), 1)
    hot[...] = (lane == label).astype(F32).T[:classes].astype(BF16)


def sums_body(
    pack, other, modulation, time_out, shared_t, slopes, base, high, act_t, feat_t, hot,
    time_in_v, time_out_v, table_v, mod_v, g_patch,
    table,
):
    z, c, _ = places()
    rows = sample_table(table, pack, other)
    mods = [
        jnp.concatenate([rows(k) for k in range(6)], axis=-1).astype(BF16),
        jnp.concatenate(
            [rows(k) for k in range(6, 9)] + [high[k] for k in range(3)], axis=-1
        ).astype(BF16),
    ]
    block = mod_v.shape[1]
    start = pl.multiple_of((z * 2 + c) * block, 8)
    mine = shared_t[pl.ds(start, block), :].astype(BF16)
    for layer in range(2):
        mod_v[layer] = dot(mine, mods[layer])
    shared_grad = base[...]
    for layer in range(2):
        shared_grad += dot_nt(mods[layer], modulation[layer])
    cond_grad = shared_grad * slopes[0]
    cond_low = cond_grad.astype(BF16)
    cond_rest = (cond_grad - cond_low.astype(F32)).astype(BF16)
    table_v[...] = dot(hot[...], cond_low) + dot(hot[...], cond_rest)
    time_out_v[...] = dot(act_t[...], cond_low)
    time_grad = dot_nt(cond_low, time_out[...]) * slopes[1]
    time_in_v[...] = dot(feat_t[...], time_grad.astype(BF16))
    join_sums(g_patch, pack, other)


def unpack_body(tiles, *refs):
    held, left, (prediction, latent_grad, token, sem) = refs[:5], refs[5:10], refs[10:]
    copies = []
    leave_all(tuple(zip(held, left)), sem, copies)
    z, _, _ = places()
    token[...] = jnp.zeros_like(token)
    _, out_ch, height, wide = prediction.shape
    lat_ch = latent_grad.shape[1]
    for k in range(4):
        tile = tiles[k].astype(F32)
        image = unpacked_tile(tile[8:16, 0:256].astype(BF16), out_ch, height, wide)
        prediction[z ^ k] = image.astype(BF16).reshape(out_ch, height, wide)
        image = unpacked_tile(tile[0:8, 0:128].astype(BF16), lat_ch, height, wide)
        image = image + unpacked_tile(tile[0:8, 128:256].astype(BF16), lat_ch, height, wide)
        latent_grad[z ^ k] = image.reshape(lat_ch, height, wide)
    for copy in copies:
        copy.wait()


def place_mlp(up, down, piece, unit):
    block, width = up.shape[0], down.shape[1]
    cols = pl.ds(pl.multiple_of(unit * width, 128), width)
    up[:, cols] = piece[0:block].astype(F32)
    down_rows = pl.ds(pl.multiple_of(unit * block, 8), block)
    down[down_rows, :] = piece[block : 2 * block].astype(F32)


def place_attn(qkv, proj, piece, unit):
    width = proj.shape[1]

    @pl.when(unit < 3)
    def _():
        cols = pl.ds(pl.multiple_of(unit * width, 128), width)
        qkv[:, cols] = piece.astype(F32)

    @pl.when(unit == 3)
    def _():
        proj[...] = piece.astype(F32)


def wide_spots():
    _, c, w = places()
    first = jnp.where(c == 0, 1, 2)
    spot = lax.rem(w, 4)
    return spot, spot ^ first, spot ^ first ^ 3, spot ^ 3


def leave_all(pairs, sem, copies):
    for source, target in pairs:
        copies.append(pltpu.make_async_copy(source, target, sem.at[len(copies)]))
        copies[-1].start()


def spread_body(own, near, far, g_qkv, g_proj, g_up, g_down, up, down, qkv, proj, sem):
    size2 = own.shape[0]
    block = proj.shape[0]
    size = 2 * block
    units = ((own, 0), (near, 0), (far, 0), (far, size2))
    copies = []
    for layer, start in ((1, 0), (0, size)):
        for (ref, base), unit in zip(units, wide_spots()):
            piece = ref[base + start : base + start + size]
            place_mlp(up.at[layer], down.at[layer], piece, unit)
        leave_all(
            ((up.at[layer], g_up.at[layer]), (down.at[layer], g_down.at[layer])), sem, copies
        )
    for (ref, base), unit in zip(units, wide_spots()):
        place_attn(qkv, proj, ref[base + 2 * size : base + size2], unit)
    leave_all(((qkv, g_qkv.at[1]), (proj, g_proj.at[1])), sem, copies)
    for copy in copies:
        copy.wait()


def last_spread_body(own, near, far, _q, _p, g_qkv, g_proj, qkv, proj, sem):
    size = own.shape[0]
    units = ((own, 0), (near, 0), (far, 0), (far, size))
    for (ref, base), unit in zip(units, wide_spots()):
        place_attn(qkv, proj, ref[base : base + size], unit)
    copies = []
    leave_all(((qkv, g_qkv.at[0]), (proj, g_proj.at[0])), sem, copies)
    for copy in copies:
        copy.wait()


def swap(value, axis, bit):
    count = lax.axis_size(axis)
    return lax.ppermute(value, axis, [(i, i ^ bit) for i in range(count)])


def swap_by_core(value, bits):
    wide, cores = lax.axis_size("wide"), lax.axis_size("cols")
    pairs = [
        (w * cores + c, (w ^ bits[c % 2]) * cores + c) for w in range(wide) for c in range(cores)
    ]
    return lax.ppermute(value, ("wide", "cols"), pairs)


FIRST, SECOND = (1, 2), (2, 1)


def rest_sum(value):
    bit = 4
    while bit < lax.axis_size("wide"):
        value = (value.astype(F32) + swap(value, "wide", bit).astype(F32)).astype(value.dtype)
        bit *= 2
    return value


def rest_gather(value):
    bit = 4
    while bit < lax.axis_size("wide"):
        value = jnp.concatenate([value, swap(value, "wide", bit)])
        bit *= 2
    return value


def position_tables(row_count, col_count, cores, width):
    quarter = width // 4
    omega = np.exp(-math.log(10000.0) * np.arange(quarter) / quarter)
    row_angle = np.arange(row_count)[:, None] * omega[None, :]
    col_angle = np.arange(col_count * cores)[:, None] * omega[None, :]
    row_part = np.concatenate([np.sin(row_angle), np.cos(row_angle)], axis=-1)
    col_part = np.concatenate([np.sin(col_angle), np.cos(col_angle)], axis=-1)
    col_part = col_part.reshape(cores, 1, col_count, width // 2)
    table = np.concatenate(
        [
            np.broadcast_to(row_part[None, :, None, :], (cores, row_count, col_count, width // 2)),
            np.broadcast_to(col_part, (cores, row_count, col_count, width // 2)),
        ],
        axis=-1,
    )
    return table.reshape(cores, row_count * col_count, width).astype(np.float32)


def shards(
    latent, pred_grad, timesteps, labels, offsets, counts, patch_weight, time_in, time_out,
    label_table, modulation, qkv_weight, proj_weight, up_weight, down_weight, final_mod, final_weight,
):
    slots, lat_ch, tile_h, tile_w = latent.shape
    out_ch = pred_grad.shape[1]
    width = patch_weight.shape[1]
    ff = up_weight.shape[2]
    n_rows, n_cols = lax.axis_size("rows"), lax.axis_size("cols")
    hp, wp = tile_h // 2, tile_w // 2
    tile_tok = hp * wp
    tokens = n_rows * tile_tok
    lanes = 2 * (lat_ch + out_ch)
    block = width // 8
    tok, wide_tok, double = (tokens, width), (tokens, ff), (tokens, 2 * width)

    tiles = kernel_call(
        tiles_body,
        [("h", latent), ("h", pred_grad)],
        [((2, tile_tok, lanes), BF16)] * n_rows,
        [
            pltpu.VMEM(latent.shape, BF16), pltpu.VMEM(pred_grad.shape, BF16),
            pltpu.SemaphoreType.DMA((2,)),
        ],
        us=1,
    )

    def along_z(parts):
        return [parts[0]] + [swap(parts[k], "rows", k) for k in range(1, n_rows)]

    def both_halves(pack):
        if lax.axis_size("wide") > 4:
            rows, sums = rest_gather(pack[: 8 * ROWS]), rest_sum(pack[8 * ROWS :])
            pack = jnp.concatenate([rows, sums])
        return pack, swap(pack, "cols", 1)

    tiles = along_z(tiles)
    half = time_in.shape[0] // 2
    freqs = np.exp(-math.log(10000.0) * np.arange(half, dtype=np.float32) / np.float32(half))
    positions = jnp.asarray(position_tables(n_rows * hp, wp, n_cols, width))
    blocks = (qkv_weight, proj_weight, up_weight, down_weight)
    weights = (time_out, modulation, final_mod) + blocks
    held = [(weight.shape[1:], BF16) for weight in blocks]
    (
        mods, cond, final_v, pos, time_out_v, modulation_v, final_mod_v, qkv0, proj0, up0, down0,
    ) = kernel_call(
        cond_body,
        [("s", timesteps), ("s", labels), ("v", jnp.asarray(freqs.astype(np.float32))[None])]
        + [("v", label_table), ("v", time_in), ("v", final_weight), ("h", positions)]
        + [("h", weight) for weight in weights],
        [((3, 8, width), F32), ((8, width), F32), (final_weight.shape, BF16), (tok, F32)]
        + [(weight.shape, BF16) for weight in weights[:3]]
        + held,
        [pltpu.SemaphoreType.DMA((len(weights) + 1,))],
        us=US["cond"],
    )
    probs_shape = (HEADS, 2, tokens, tokens)
    state0, q0, kv0, patches = kernel_call(
        embed_body,
        [("s", offsets)]
        + [("v", t) for t in tiles]
        + [("p", pos), ("p", mods), ("v", patch_weight), ("p", qkv0)],
        [(tok, F32), (tok, BF16), (double, BF16), ((2, tokens, lanes), BF16)],
        [pltpu.VMEM((n_rows, 2, tile_tok, lanes), BF16)],
        us=US["embed"],
    )
    kv0p = swap(kv0, "cols", 1)
    (
        state1, q1, kv1, probs0, attended0, attn_out0, middle0, gp0, act0, branch0, qkv1, proj1, up1, down1,
    ) = kernel_call(
        block_body,
        [("p", state0), ("p", q0), ("p", kv0), ("v", kv0p)]
        + [("p", a) for a in (mods, proj0, up0, down0)]
        + [("h", weight) for weight in blocks],
        [
            (tok, F32), (tok, BF16), (double, BF16), (probs_shape, BF16), (tok, BF16), (tok, BF16),
            (tok, F32), (wide_tok, BF16), (wide_tok, BF16), (tok, BF16),
        ]
        + held,
        [pltpu.SemaphoreType.DMA((4,))],
        us=US["block"],
    )
    kv1p = swap(kv1, "cols", 1)
    sums_a, sums_b = 4 * out_ch, 4 * lat_ch
    rows_1 = 16 * 2 * block + 48
    probs1, attended1, attn_out1, mgrad1, keep1, send1, preds = kernel_call(
        turn_body,
        [("s", offsets), ("s", counts), ("p", state1), ("p", q1), ("p", kv1), ("v", kv1p)]
        + [("p", a) for a in (mods, cond, patches, final_v, proj1, up1, down1)],
        [
            (probs_shape, BF16), (tok, BF16), (tok, BF16), (tok, F32), ((rows_1, width), BF16),
            ((rows_1, width), BF16), ((2, tokens, 2 * out_ch), F32),
        ],
        [
            pltpu.VMEM(wide_tok, BF16), pltpu.VMEM(wide_tok, BF16), pltpu.VMEM((48, width), F32),
            pltpu.VMEM(wide_tok, BF16),
        ],
        us=US["turn"],
    )
    recv1 = swap(send1, "cols", 1)

    def attend_back(layer, q, kv, kvp, *saved, after):
        return kernel_call(
            partial(attend_back_body, layer),
            [("p", q), ("p", kv), ("v", kvp)] + [("p", a) for a in saved[:-1] + (mods, saved[-1])],
            [
                (tok, BF16), (double, BF16), ((width, width), BF16), (double, BF16), ((8, width), F32),
            ],
            us=US["back"],
            after=after,
        )

    dq1, dkv1, gproj1, dkvs1, rows_a1 = attend_back(
        1, q1, kv1, kv1p, probs1, attended1, attn_out1, mgrad1, proj1, after=None
    )
    dkvr1 = swap(dkvs1, "cols", 1)
    keep1, table1, send1 = kernel_call(
        first_body,
        [("p", keep1), ("v", recv1)],
        [((8 * 2 * block, width), BF16), ((48, width), BF16), ((8 * 2 * block + 48, width), BF16)],
        us=US["A1"],
        after=rows_a1,
    )
    recv1 = swap_by_core(send1, FIRST)
    mgrad0, keep2, send2, rows_mid = kernel_call(
        middle_body,
        [("p", a) for a in (state1, mgrad1, dq1, dkv1)]
        + [("v", dkvr1)]
        + [("p", a) for a in (gproj1, middle0, branch0, gp0, act0, mods, qkv1, up0, down0)],
        [
            (tok, F32), ((16 * 3 * block, width), BF16), ((16 * 3 * block, width), BF16),
            ((8, width), F32),
        ],
        [pltpu.VMEM(wide_tok, BF16)],
        us=US["middle"],
        after=table1,
    )
    recv2 = swap(send2, "cols", 1)
    dq0, dkv0, gproj0, dkvs0, rows_a0 = attend_back(
        0, q0, kv0, kv0p, probs0, attended0, attn_out0, mgrad0, proj0, after=None
    )
    dkvr0 = swap(dkvs0, "cols", 1)
    alpha, beta = 2 * block + 16, block - 16
    send_rows = 4 * alpha + 2 * beta + 8 * block + 32
    whole_2, whole_r = keep2, recv2
    keep2, send2 = kernel_call(
        second_body,
        [("p", whole_2), ("v", whole_r)],
        [((8 * alpha, width), BF16)] * 2,
        us=US["A3"],
        after=rows_a0,
    )
    recv2 = swap_by_core(send2, FIRST)
    keep1, pair1, send1 = kernel_call(
        partial(first_pair_body, sums_a),
        [("p", keep1), ("p", table1), ("v", recv1)],
        [((4 * 2 * block, width), BF16), ((64, width), BF16), ((4 * 2 * block + 64, width), BF16)],
        us=US["A2"],
        after=keep2,
    )
    recv1 = swap_by_core(send1, SECOND)
    betas = kernel_call(
        beta_body,
        [("p", whole_2), ("v", whole_r)],
        [((4 * beta, width), BF16)] * 4,
        us=US["A3b"],
        after=pair1,
    )
    chips = betas[0]
    betas = along_z(betas)
    rows_3 = 16 * block + 32
    keep3, send3, lgrads = kernel_call(
        last_body,
        [("s", offsets), ("p", state0), ("p", mgrad0), ("p", dq0), ("p", dkv0), ("v", dkvr0)]
        + [("p", gproj0), ("p", mods), ("p", patches), ("v", patch_weight)]
        + [("p", a) for a in (rows_a1, rows_mid, rows_a0, qkv0)],
        [((rows_3, width), BF16), ((rows_3, width), BF16), ((2, tokens, 2 * lat_ch), F32)],
        [pltpu.VMEM((8, width), F32), pltpu.VMEM((32, width), F32)],
        us=US["last"],
        after=chips,
    )
    recv3 = swap(send3, "cols", 1)
    (tiles,) = kernel_call(
        pack_body, [("p", preds), ("p", lgrads)], [((4, 16, width), BF16)], us=US["pack"]
    )
    ones = kernel_call(
        partial(first_chip_body, sums_a),
        [("p", keep1), ("p", pair1), ("v", recv1)],
        [((2 * block + 48, width), BF16)] * 4,
        [pltpu.VMEM((4, ROWS, width), F32), pltpu.VMEM((sums_a, width), F32)],
        us=US["A2b"],
        after=tiles,
    )
    chips = ones[0]
    ones = along_z(ones)
    keep2, keepb, part = kernel_call(
        third_body,
        [("p", keep2), ("v", recv2), ("p", betas[0])] + [("v", beta) for beta in betas[1:]],
        [
            ((4 * alpha, width), BF16), ((2 * beta, width), BF16),
            ((4 * alpha + 2 * beta, width), BF16),
        ],
        [pltpu.VMEM((4 * beta, width), BF16)],
        us=US["A4"],
        after=chips,
    )
    keep3, table3, send = kernel_call(
        third_send_body,
        [("p", keep3), ("v", recv3), ("p", part)],
        [((8 * block, width), BF16), ((32, width), BF16), ((send_rows, width), BF16)],
        us=US["A4b"],
    )
    recv = swap_by_core(send, SECOND)
    *twos, keep3, keepb, pair3, send = kernel_call(
        partial(fourth_body, sums_b),
        [("p", keep2), ("p", keep3), ("p", keepb), ("p", table3), ("v", recv)],
        [((alpha, width), BF16)] * 4
        + [
            ((4 * block, width), BF16), ((beta, width), BF16), ((48, width), BF16),
            ((4 * block + beta + 48, width), BF16),
        ],
        us=US["A5"],
    )
    recv = swap_by_core(send, FIRST)
    twos = along_z(twos)
    pack = (8 * ROWS + 16, width)
    unit1, pack_a = kernel_call(
        partial(unit1_body, sums_a // 2),
        [("p", ones[0])] + [("v", one) for one in ones[1:]],
        [((2 * block, width), BF16), (pack, BF16)],
        us=US["U1"],
        after=pair3,
    )
    packs = both_halves(pack_a)
    *threes, unitb = kernel_call(
        partial(fifth_body, sums_b),
        [("p", keep3), ("p", keepb), ("p", pair3), ("v", recv), ("p", tiles)],
        [((block + 32 + 16, width), BF16)] * 4 + [((beta, width), BF16)],
        [pltpu.VMEM((4, ROWS, width), F32), pltpu.VMEM((sums_b, width), F32)],
        us=US["A6"],
        after=pack_a,
    )
    threes = along_z(threes)
    (unit2,) = kernel_call(
        unit12_body,
        [("p", unit1), ("p", twos[0])] + [("v", two) for two in twos[1:]] + [("p", unitb)],
        [((2 * block + alpha + beta, width), BF16)],
        us=US["U12"],
    )
    unit2 = rest_sum(unit2)
    near2 = swap_by_core(unit2, FIRST)
    samples = 2 * (packs[0].shape[0] - 16) // ROWS
    classes = label_table.shape[0]
    feat_count = time_in.shape[0]
    g_final_mod, g_final, *early = kernel_call(
        early_sums_body,
        [("p", packs[0]), ("v", packs[1]), ("p", final_mod_v)],
        [
            (final_mod.shape, F32, "any"), ((sums_a, width), F32, "any"), ((width, samples), F32),
            ((2, samples, width), F32), ((samples, width), F32), ((3, samples, width), F32),
            ((width, samples), BF16), ((feat_count, samples), BF16), ((classes, samples), BF16),
        ],
        [pltpu.VMEM((width // 128, samples * ROWS, 128), F32)],
        us=US["early"],
        after=unit2,
    )
    unit3, pack_b, tiles = kernel_call(
        partial(unit3_body, sums_b // 2),
        [("p", threes[0])] + [("v", three) for three in threes[1:]],
        [((block, width), BF16), (pack, BF16), ((4, 16, width), BF16)],
        us=US["U2"],
        after=early[0],
    )
    unit3 = rest_sum(unit3)
    near3 = swap_by_core(unit3, FIRST)
    (send2,) = kernel_call(
        join_body,
        [("p", unit2), ("v", near2)],
        [((2 * unit2.shape[0], width), BF16)],
        us=US["join"],
        after=tiles,
    )
    far2 = swap_by_core(send2, SECOND)
    packs = both_halves(pack_b)
    late_shapes = (
        time_in.shape, time_out.shape, (classes, width), (2, block, 6 * width), patch_weight.shape,
    )
    late = kernel_call(
        sums_body,
        [("p", packs[0]), ("v", packs[1])] + [("p", a) for a in (modulation_v, time_out_v, *early)],
        [(shape, F32) for shape in late_shapes],
        [pltpu.VMEM((width // 128, samples * ROWS, 128), F32)],
        us=US["sums"],
    )
    (send3,) = kernel_call(
        join_body,
        [("p", unit3), ("v", near3)],
        [((2 * block, width), BF16)],
        us=US["F3"],
        after=late[4],
    )
    far3 = swap_by_core(send3, SECOND)
    g_time_in, g_time_out, g_table, g_mod, g_patch, prediction, latent_grad, token = kernel_call(
        unpack_body,
        [("p", tiles)] + [("p", a) for a in late],
        [(shape, F32, "hbm") for shape in late_shapes]
        + [((slots, out_ch, tile_h, tile_w), BF16, "any"), (latent.shape, F32, "any"), ((8, 128), F32)],
        [pltpu.SemaphoreType.DMA((5,))],
        us=US["unpack"],
        after=send3,
    )
    up_shape, down_shape = (2, block, ff), (2, ff // 8, width)
    attn_scratch = [pltpu.VMEM((block, 3 * width), F32), pltpu.VMEM((block, width), F32)]
    attn_shapes = [((2, block, 3 * width), F32, "hbm"), ((2, block, width), F32, "hbm")]
    g_qkv, g_proj, g_up, g_down = kernel_call(
        spread_body,
        [("p", unit2), ("v", near2), ("v", far2)],
        attn_shapes + [(up_shape, F32, "hbm"), (down_shape, F32, "hbm")],
        [pltpu.VMEM(up_shape, F32), pltpu.VMEM(down_shape, F32)]
        + attn_scratch
        + [pltpu.SemaphoreType.DMA((6,))],
        us=US["spread"],
        after=token,
    )
    g_qkv, g_proj = kernel_call(
        last_spread_body,
        [("p", unit3), ("v", near3), ("v", far3), ("h", g_qkv), ("h", g_proj)],
        attn_shapes,
        attn_scratch + [pltpu.SemaphoreType.DMA((2,))],
        us=US["spread"],
        aliases=((3, 0), (4, 1)),
    )
    return (
        prediction, latent_grad, g_patch, g_time_in, g_time_out, g_table, g_mod, g_qkv, g_proj,
        g_up, g_down, g_final_mod, g_final.T,
    )


def solution(mesh):
    tiled, split = P("wide", None, "rows", "cols"), P(None, ("rows", "cols"), None)
    return jax.shard_map(
        shards,
        mesh=mesh,
        in_specs=(tiled, tiled, P("wide"), P("wide"), P("wide"), P("wide")) + (P(),) * 11,
        out_specs=(tiled, tiled, P(), P(), P(), P(), split, split, split, split, split, P(), P()),
        check_vma=False,
    )
```

```python
from functools import partial
import math

import jax
import jax.numpy as jnp
import numpy as np
from jax import lax
from jax.experimental import pallas as pl
from jax.experimental.pallas import tpu as pltpu
from jax.sharding import PartitionSpec as P

HEADS = 6
HEAD_DIM = 64
PAIRS = HEADS // 2
LANES = 2 * HEAD_DIM
EPS = 1e-06
F32 = jnp.float32
BF16 = jnp.bfloat16
ROWS = 12
ROW_SHARED, ROW_ACT, ROW_COND, ROW_HID, ROW_FEAT = 5, 6, 7, 8, 9
US = {
    "cond": 5, "embed": 2, "block": 6, "turn": 9, "back": 20, "middle": 4, "last": 4, "early": 0.05, "pack": 0.05, "join": 0.05, "U12": 0.05, "F3": 0.05, "unpack": 0.05, "relay": 0.05, "sums": 5, "spread": 0.05,
    "A1": 0.05, "A2": 0.05, "A2b": 0.05, "A3": 0.05, "A3b": 0.05, "A4": 30, "A4b": 0.05, "A5": 0.05, "A6": 0.05, "S1": 0.05, "U2": 3,
    "U1": 1,
}


def dot(a, b):
    return jnp.dot(a, b, preferred_element_type=F32)


def dot_nt(a, b):
    return lax.dot_general(a, b, (((1,), (1,)), ((), ())), preferred_element_type=F32)


def dot_tn(a, b):
    return lax.dot_general(a, b, (((0,), (0,)), ((), ())), preferred_element_type=F32)


def sds(shape, dtype):
    return jax.ShapeDtypeStruct(shape, dtype)


def layer_norm(states):
    centred = states - jnp.mean(states, axis=-1, keepdims=True)
    inverse = lax.rsqrt(jnp.mean(centred * centred, axis=-1, keepdims=True) + EPS)
    return centred * inverse, inverse


def norm_back(grad, normed, inverse):
    mean_grad = jnp.mean(grad, axis=-1, keepdims=True)
    mean_cross = jnp.mean(grad * normed, axis=-1, keepdims=True)
    return inverse * (grad - mean_grad - normed * mean_cross)


def token_sum(values):
    return jnp.sum(values, axis=0, keepdims=True)


def head_masks(dtype):
    lane = lax.broadcasted_iota(jnp.int32, (1, LANES), 1)
    first = (lane < HEAD_DIM).astype(F32)
    return first.astype(dtype), (1.0 - first).astype(dtype)


def unit_place(zz, ww, cc):
    x, y = ww % 2, ww // 2
    return (x * 8 + y * 4 + zz) if cc == 0 else (y * 8 + x * 4 + zz)


def kernel_call(body, ins, outs, scratch=(), us=1.0, after=None, aliases=()):
    spaces = {"v": pltpu.VMEM, "p": pltpu.VMEM, "s": pltpu.SMEM, "h": pltpu.HBM}
    specs, arrays = [], []
    for kind, array in ins:
        specs.append(pl.BlockSpec(memory_space=spaces[kind]))
        if kind in "ph":
            array = pltpu.with_memory_space_constraint(array, spaces[kind])
        arrays.append(array)
    if after is not None:
        specs.append(pl.BlockSpec(memory_space=pl.ANY))
        arrays.append(after)

    def kernel(*refs):
        body(*refs[: len(ins)], *refs[len(arrays) :])

    return pl.pallas_call(
        kernel,
        in_specs=specs,
        out_specs=[
            pl.BlockSpec(memory_space=pltpu.HBM if "hbm" in o[2:] else pltpu.VMEM) for o in outs
        ],
        out_shape=[
            pltpu.VMEM(o[0], o[1]) if len(o) < 3 else sds(o[0], o[1]) if o[2] == "any" else pltpu.HBM(o[0], o[1])
            for o in outs
        ],
        input_output_aliases=dict(aliases),
        scratch_shapes=list(scratch),
        compiler_params=pltpu.CompilerParams(vmem_limit_bytes=24 * 1024 * 1024),
        cost_estimate=pl.CostEstimate(
            flops=int(us * 1.5e9), bytes_accessed=int(us * 1e6), transcendentals=0
        ),
    )(*arrays)


def one_hot(shape, test):
    first = lax.broadcasted_iota(jnp.int32, shape, 0)
    second = lax.broadcasted_iota(jnp.int32, shape, 1)
    return test(first, second).astype(F32).astype(BF16)


def places():
    return lax.axis_index("rows"), lax.axis_index("cols"), lax.axis_index("wide")


def chip_place(zz, ww, cc):
    x, y = ww % 2, ww // 2
    return zz * 4 + ((2 * y + x) if cc == 0 else (2 * x + y))


def wide_bits():
    _, c, w = places()
    x, y = lax.rem(w, 2), lax.rem(lax.div(w, 2), 2)
    return jnp.where(c == 0, x, y), jnp.where(c == 0, y, x)


def rows_at(index, count):
    return pl.ds(pl.multiple_of(index * count, 16), count)


def tiles_body(latent_h, pred_h, *rest):
    tiles, (latent, pred_grad, sem) = rest[:-3], rest[-3:]
    copies = [
        pltpu.make_async_copy(latent_h, latent, sem.at[0]),
        pltpu.make_async_copy(pred_h, pred_grad, sem.at[1]),
    ]
    for copy in copies:
        copy.start()
    z, _, _ = places()
    _, lat_ch, height, wide = latent.shape
    out_ch = pred_grad.shape[1]
    chans, tok = lat_ch + out_ch, height * wide // 4
    half = wide // 2
    lanes = 2 * chans
    spread = [one_hot((tok, wide), lambda t, v: v == 2 * (t % half) + u) for u in range(2)]
    inside = [
        one_hot((tok, chans * height), lambda t, v: v % height == 2 * (t // half) + par).astype(F32)
        for par in range(2)
    ]

    def lane_of(channel, u):
        return jnp.where(
            channel < lat_ch, u * lat_ch + channel, 2 * lat_ch + u * out_ch + channel - lat_ch
        )

    fold = [
        one_hot((chans * height, lanes), lambda v, lane: lane == lane_of(v // height, u))
        for u in range(2)
    ]
    for copy in copies:
        copy.wait()
    for k, tile in enumerate(tiles):
        image = jnp.concatenate(
            [
                latent[z ^ k].reshape(lat_ch * height, wide),
                pred_grad[z ^ k].reshape(out_ch * height, wide),
            ],
            axis=0,
        )
        wide_rows = [dot_nt(spread[u], image) for u in range(2)]
        for par in range(2):
            tile[par] = sum(
                dot((wide_rows[u] * inside[par]).astype(BF16), fold[u]) for u in range(2)
            ).astype(BF16)


def packed_tile(parities, lanes, order):
    tok = parities[0].shape[0]
    across = tok // order
    total = order * 2 * lanes
    block = 0.0
    for par in range(2):
        copy = one_hot((lanes, total), lambda a, b: b % (2 * lanes) == par * lanes + a)
        block = block + dot(parities[par].astype(BF16), copy)
    own = one_hot((tok, total), lambda t, b: b // (2 * lanes) == t // across).astype(F32)
    gather = one_hot((across, tok), lambda j, t: t % across == j)
    return dot(gather, (block * own).astype(BF16))


def unpacked_tile(block, chans, height, wide):
    lanes = 2 * chans
    half = wide // 2
    image = 0.0
    for u in range(2):
        chosen = one_hot(
            (chans * height, block.shape[1]),
            lambda v, b: b
            == (v % height) // 2 * 2 * lanes + v % 2 * lanes + u * chans + v // height,
        )
        column = dot_nt(chosen, block).astype(BF16)
        image = image + dot(column, one_hot((half, wide), lambda j, v: v == 2 * j + u))
    return image


def by_parity(first, second, offset):
    step = first.shape[0] // 32
    moved = jnp.concatenate([jnp.zeros((step, second.shape[1]), F32), second[:-step]], axis=0)
    return jnp.where(offset == 1, moved, first), jnp.where(offset == 1, first, second)


def cond_body(
    timesteps, labels, freqs, label_table, time_in, final_weight, positions, *rest,
):
    sources, (mods, cond, final_copy, pos), held = rest[:7], rest[7:11], rest[11:18]
    sem = rest[18]
    final_copy[...] = final_weight[...]
    sources = sources[:3] + tuple(source.at[0] for source in sources[3:])
    sources += (positions.at[lax.axis_index("cols")],)
    held = held + (pos,)
    copies = [
        pltpu.make_async_copy(source, target, sem.at[i])
        for i, (source, target) in enumerate(zip(sources, held))
    ]
    for copy in copies:
        copy.start()
    time_out, modulation, final_mod = held[:3]
    z, _, _ = places()
    label = labels[z]
    count, width = time_in.shape
    angles = jnp.full((8, count // 2), timesteps[z].astype(F32)) * freqs[...]
    feats = jnp.concatenate([jnp.cos(angles), jnp.sin(angles)], axis=-1).astype(BF16)
    hidden = dot(feats, time_in[...])
    act = (hidden * jax.nn.sigmoid(hidden)).astype(BF16)
    chosen = one_hot((8, label_table.shape[0]), lambda a, b: b == label)
    copies[0].wait()
    condition = dot(act, time_out[...]) + dot(chosen, label_table[...])
    shared = (condition * jax.nn.sigmoid(condition)).astype(BF16)
    mods[...] = jnp.zeros_like(mods)
    copies[1].wait()
    for layer in range(2):
        values = dot(shared, modulation[layer])
        for k in range(6):
            mods[layer, k : k + 1, :] = values[0:1, k * width : (k + 1) * width]
    copies[2].wait()
    values = dot(shared, final_mod[...])
    for k in range(2):
        mods[2, k : k + 1, :] = values[0:1, k * width : (k + 1) * width]
    lane = lax.broadcasted_iota(jnp.int32, (1, width - count), 1)
    marks = jnp.where(
        lane == 0, lax.div(label, 32), jnp.where(lane == 1, lax.rem(label, 32), 0)
    ).astype(F32)
    cond[...] = jnp.zeros_like(cond)
    cond[0:1, :] = shared[0:1].astype(F32)
    cond[1:2, :] = act[0:1].astype(F32)
    cond[2:3, :] = condition[0:1]
    cond[3:4, :] = hidden[0:1]
    cond[4:5, :] = jnp.concatenate([feats[0:1].astype(F32), marks], axis=-1)
    for copy in copies[3:]:
        copy.wait()


def qkv_forward(state, mods, layer, weight):
    width = state.shape[-1]
    normed, _ = layer_norm(state)
    inner = (normed * (1.0 + mods[layer, 1:2]) + mods[layer, 0:1]).astype(BF16)
    projected = dot(inner, weight[...]).astype(BF16)
    return projected[:, :width], projected[:, width:]


def attend_forward(q, kv, kvp, probs, attended):
    width = q.shape[-1]
    masks = head_masks(BF16)
    for p in range(PAIRS):
        at = slice(p * LANES, (p + 1) * LANES)
        av = slice(width + p * LANES, width + (p + 1) * LANES)
        qp = q[:, at] * BF16(HEAD_DIM**-0.5)
        k0, v0, k1, v1 = kv[:, at], kv[:, av], kvp[:, at], kvp[:, av]
        total = None
        for h in range(2):
            qh = qp * masks[h]
            s0, s1 = dot_nt(qh, k0), dot_nt(qh, k1)
            peak = jnp.maximum(
                jnp.max(s0, axis=-1, keepdims=True), jnp.max(s1, axis=-1, keepdims=True)
            )
            e0, e1 = jnp.exp(s0 - peak), jnp.exp(s1 - peak)
            scale = 1.0 / (
                jnp.sum(e0, axis=-1, keepdims=True) + jnp.sum(e1, axis=-1, keepdims=True)
            )
            p0, p1 = (e0 * scale).astype(BF16), (e1 * scale).astype(BF16)
            probs[2 * p + h, 0] = p0
            probs[2 * p + h, 1] = p1
            part = dot(p0, v0 * masks[h]) + dot(p1, v1 * masks[h])
            total = part if total is None else total + part
        attended[:, at] = total.astype(BF16)


CHUNK = 768


def mlp_forward(middle, mods, layer, up, down, gp, act):
    normed, _ = layer_norm(middle)
    inner = (normed * (1.0 + mods[layer, 4:5]) + mods[layer, 3:4]).astype(BF16)
    branch = None
    for start in range(0, up.shape[1], CHUNK):
        at = slice(start, start + CHUNK)
        hidden = dot(inner, up[:, at])
        square = hidden * hidden
        root = math.sqrt(2.0 / math.pi)
        bent = jnp.tanh(root * hidden * (1.0 + 0.044715 * square))
        half = 0.5 * (1.0 + bent)
        activated = (hidden * half).astype(BF16)
        act[:, at] = activated
        slope = half + 0.5 * hidden * (1.0 - bent * bent) * (root * (1.0 + 3 * 0.044715 * square))
        gp[:, at] = slope.astype(BF16)
        part = dot(activated, down[at, :])
        branch = part if branch is None else branch + part
    return branch


def put_units(keep, send, pair, place, size, at_row):
    first = lax.axis_index("cols") == 0
    block = pair[0].shape[0]
    own = jnp.where(first, place[0], place[1]) * size + at_row
    other = jnp.where(first, place[1], place[0]) * size + at_row
    keep[pl.ds(pl.multiple_of(own, 16), block), :] = jnp.where(first, pair[0], pair[1])
    send[pl.ds(pl.multiple_of(other, 16), block), :] = jnp.where(first, pair[1], pair[0])


def mlp_backward(
    grad, middle, branch, mods, layer, gp, act, up, down, keep, send, size, flip, rows, first, low
):
    width = middle.shape[-1]
    normed, inverse = layer_norm(middle)
    scale = 1.0 + mods[layer, 4:5]
    inner_t = (normed * scale + mods[layer, 3:4]).astype(BF16).T
    branch_grad = (mods[layer, 5:6] * grad).astype(BF16)
    inner_grad = None
    for start in range(0, up.shape[1], CHUNK):
        at = slice(start, start + CHUNK)
        act_grad = dot_nt(branch_grad, down[at, :])
        hidden_grad = (act_grad * gp[:, at].astype(F32)).astype(BF16)
        low[:, at] = hidden_grad
        part = dot_nt(hidden_grad, up[:, at])
        inner_grad = part if inner_grad is None else inner_grad + part
    block = width // 8
    for i in range(up.shape[1] // width):
        at = slice(i * width, (i + 1) * width)
        grad_up = dot(inner_t, low[:, at]).astype(BF16)
        for b in range(4):
            pair = [grad_up[(2 * b + cc) * block : (2 * b + cc + 1) * block] for cc in range(2)]
            place = [unit_place(b, i, cc ^ flip) for cc in range(2)]
            put_units(keep, send, pair, place, size, 0)
        grad_down = dot_tn(act[:, at], branch_grad).astype(BF16)
        for j in range(4):
            pair = [grad_down[(4 * cc + j) * block : (4 * cc + j + 1) * block] for cc in range(2)]
            place = [unit_place(i, j, cc ^ flip) for cc in range(2)]
            put_units(keep, send, pair, place, size, block)
    rows[first : first + 1, :] = token_sum(inner_grad)
    rows[first + 1 : first + 2, :] = token_sum(inner_grad * normed)
    rows[first + 2 : first + 3, :] = token_sum(grad * branch.astype(F32))
    return grad + norm_back(inner_grad * scale, normed, inverse)


def qkv_backward(
    state, middle_grad, dq, dkv, dkvr, mods, layer, weight, gproj, keep, send, shares, rows
):
    width = state.shape[-1]
    block = width // 8
    normed, inverse = layer_norm(state)
    scale = 1.0 + mods[layer, 1:2]
    inner_t = (normed * scale + mods[layer, 0:1]).astype(BF16).T
    dkv_sum = dkv[...] + dkvr[...]
    pieces = (dq[...], dkv_sum[:, :width], dkv_sum[:, width:])
    inner_grad = None

    def put(values, i):
        for b in range(4):
            pair = [values[(2 * b + cc) * block : (2 * b + cc + 1) * block] for cc in range(2)]
            for start, end, place_of, size, at_row in shares:
                place = [place_of(b, i, cc) for cc in range(2)]
                put_units(keep, send, [part[start:end] for part in pair], place, size, at_row)

    for i, piece in enumerate(pieces):
        part = dot_nt(piece, weight[:, i * width : (i + 1) * width])
        inner_grad = part if inner_grad is None else inner_grad + part
        put(dot(inner_t, piece).astype(BF16), i)
    put(gproj[...], 3)
    rows[0:1, :] = token_sum(inner_grad)
    rows[1:2, :] = token_sum(inner_grad * normed)
    return middle_grad + norm_back(inner_grad * scale, normed, inverse)


def embed_body(
    offsets, t0, t1, t2, t3, pos, mods, patch_weight, qkv,
    state, q, kv, patches, tiles,
):
    z, _, _ = places()
    offset = offsets[z]
    for i, tile in enumerate((t0, t1, t2, t3)):
        tiles[-i % 4] = tile[...]
    count = tiles.shape[0]
    even = jnp.concatenate([tiles[z ^ t, 0] for t in range(count)], axis=0).astype(F32)
    odd = jnp.concatenate([tiles[z ^ t, 1] for t in range(count)], axis=0).astype(F32)
    step = even.shape[0] // 32
    later = jnp.concatenate([even[step:], jnp.zeros((step, even.shape[1]), F32)], axis=0)
    first = jnp.where(offset == 1, odd, even).astype(BF16)
    second = jnp.where(offset == 1, later, odd).astype(BF16)
    patches[0] = first
    patches[1] = second
    weight = patch_weight[...].astype(F32)
    lanes = weight.shape[0] // 2
    fill = jnp.zeros((even.shape[1] - lanes, weight.shape[1]), F32)
    upper = jnp.concatenate([weight[:lanes], fill], axis=0).astype(BF16)
    lower = jnp.concatenate([weight[lanes:], fill], axis=0).astype(BF16)
    values = dot(first, upper) + dot(second, lower) + pos[...]
    state[...] = values
    q[...], kv[...] = qkv_forward(values, mods, 0, qkv)


def block_body(
    state, q, kv, kvp, mods, proj, up, down, *rest,
):
    sources, rest = rest[:4], rest[4:]
    state1, q1, kv1, probs, attended, attn_out, middle, gp, act, branch = rest[:10]
    targets, sem = rest[10:14], rest[14]
    copies = [
        pltpu.make_async_copy(source.at[1], target, sem.at[i])
        for i, (source, target) in enumerate(zip(sources, targets))
    ]
    for copy in copies:
        copy.start()
    attend_forward(q, kv, kvp, probs, attended)
    m = mods
    attn = dot(attended[...], proj[...])
    attn_out[...] = attn.astype(BF16)
    mid = state[...] + m[0, 2:3] * attn
    middle[...] = mid
    out = mlp_forward(mid, m, 0, up, down, gp, act)
    branch[...] = out.astype(BF16)
    new = mid + m[0, 5:6] * out
    state1[...] = new
    copies[0].wait()
    q1[...], kv1[...] = qkv_forward(new, m, 1, targets[0])
    for copy in copies[1:]:
        copy.wait()


def turn_body(
    offsets, counts, state, q, kv, kvp, mods, cond, patches, final_weight, proj, up, down,
    probs, attended, attn_out, middle_grad, keep, send, preds,
    gp, act, table, low,
):
    z, _, _ = places()
    offset = offsets[z]
    live = (z < counts[0]).astype(F32)
    attend_forward(q, kv, kvp, probs, attended)
    m = mods
    attn = dot(attended[...], proj[...])
    attn_out[...] = attn.astype(BF16)
    middle = state[...] + m[1, 2:3] * attn
    branch = mlp_forward(middle, m, 1, up, down, gp, act)
    last = middle + m[1, 5:6] * branch
    normed, inverse = layer_norm(last)
    scale = 1.0 + m[2, 1:2]
    inner = (normed * scale + m[2, 0:1]).astype(BF16)
    weight = final_weight[...]
    lanes = weight.shape[1] // 2
    out = dot(inner, weight) * live
    preds[0], preds[1] = by_parity(out[:, :lanes], out[:, lanes:], offset)
    across = weight.astype(F32).T
    chosen = patches
    fill = jnp.zeros((chosen.shape[2] - lanes, across.shape[1]), F32)
    upper = jnp.concatenate([fill, across[:lanes]], axis=0).astype(BF16)
    lower = jnp.concatenate([fill, across[lanes:]], axis=0).astype(BF16)
    inner_grad = (dot(chosen[0], upper) + dot(chosen[1], lower)) * live
    table[...] = jnp.zeros_like(table)
    table[0:1, :] = token_sum(inner_grad)
    table[1:2, :] = token_sum(inner_grad * normed)
    table[5:10, :] = 0.5 * cond[0:5, :]
    skip = chosen.shape[2] - lanes
    for r in range(2):
        at = ROWS + r * lanes
        table[at : at + lanes, :] = (dot_tn(chosen[r], inner) * live)[skip:]
    grad = norm_back(inner_grad * scale, normed, inverse)
    size = 2 * (weight.shape[0] // 8)
    middle_grad[...] = mlp_backward(
        grad, middle, branch, m, 1, gp, act, up, down, keep, send, size, 0, table, 2, low
    )
    base = 4 * weight.shape[0]
    keep[base:] = table[...].astype(BF16)
    send[base:] = table[...].astype(BF16)


def attend_back_body(
    layer, q, kv, kvp, probs, attended, attn_out, middle_grad, mods, proj,
    dq, dkv, gproj, dkvs, rows,
):
    grad = middle_grad[...]
    attn_grad = (mods[layer, 2:3] * grad).astype(BF16)
    attended_grad = dot_nt(attn_grad, proj[...]).astype(BF16)
    masks = head_masks(BF16)
    width = q.shape[-1]
    for p in range(PAIRS):
        at = slice(p * LANES, (p + 1) * LANES)
        av = slice(width + p * LANES, width + (p + 1) * LANES)
        qp = q[:, at] * BF16(HEAD_DIM**-0.5)
        dop = attended_grad[:, at]
        ks, vs = (kv[:, at], kvp[:, at]), (kv[:, av], kvp[:, av])
        total = None
        parts = [[], [], [], []]
        q_t, do_t = qp.T, dop.T
        for h in range(2):
            doh = dop * masks[h]
            own = slice(h * HEAD_DIM, (h + 1) * HEAD_DIM)
            ps = [probs[2 * p + h, i] for i in range(2)]
            dps = [dot_nt(doh, vs[i]) for i in range(2)]
            pfs = [ps[i].astype(F32) for i in range(2)]
            inner = sum(jnp.sum(dps[i] * pfs[i], axis=-1, keepdims=True) for i in range(2))
            for i in range(2):
                ds = (pfs[i] * (dps[i] - inner)).astype(BF16)
                part = dot(ds, ks[i] * masks[h])
                total = part if total is None else total + part
                parts[2 * i].append(dot(q_t[own], ds))
                parts[2 * i + 1].append(dot(do_t[own], ps[i]))
        dq[:, at] = (total * HEAD_DIM**-0.5).astype(BF16)
        turned = [jnp.concatenate(part, axis=0).astype(BF16).T for part in parts]
        dkv[:, at] = turned[0]
        dkv[:, av] = turned[1]
        dkvs[:, at] = turned[2]
        dkvs[:, av] = turned[3]
    rows[...] = jnp.zeros_like(rows)
    rows[0:1, :] = token_sum(grad * attn_out[...].astype(F32))
    gproj[...] = dot_tn(attended[...], attn_grad).astype(BF16)


def middle_body(
    state1, middle_grad1, dq, dkv, dkvr, gproj, middle, branch, gp, act, mods, qkv, up, down,
    middle_grad, keep, send, rows, low,
):
    width = dq.shape[-1]
    block = width // 8
    size = 2 * block
    rows[...] = jnp.zeros_like(rows)
    m = mods
    grad = qkv_backward(
        state1[...], middle_grad1[...], dq, dkv, dkvr, m, 1, qkv, gproj, keep, send,
        ((0, block, chip_place, block, 16 * size),), rows,
    )
    middle_grad[...] = mlp_backward(
        grad, middle[...], branch[...], m, 0, gp, act, up, down, keep, send, size, 0,
        rows, 2, low,
    )


def last_body(
    offsets, state0, middle_grad, dq, dkv, dkvr, gproj, mods, patches, patch_weight,
    rows_a1, rows_mid, rows_a0, qkv,
    keep, send, lgrads, rows, table,
):
    z, _, _ = places()
    offset = offsets[z]
    width = dq.shape[-1]
    block = width // 8
    grad = qkv_backward(
        state0[...], middle_grad[...], dq, dkv, dkvr, mods, 0, qkv, gproj, keep, send,
        ((0, block, lambda zz, ww, cc: unit_place(zz, ww, 1 - cc), block, 0),), rows,
    )
    embed_grad = grad.astype(BF16)
    chosen = patches
    gp0, gp1 = dot_tn(chosen[0], embed_grad), dot_tn(chosen[1], embed_grad)
    chans = patch_weight.shape[0] // 2
    window = dot_nt(embed_grad, patch_weight[...])
    lgrads[0], lgrads[1] = by_parity(window[:, :chans], window[:, chans:], offset)
    table[...] = jnp.zeros_like(table)
    table[0:2, :] = rows[0:2, :]
    table[2:3, :] = rows_a0[0:1, :]
    table[3:6, :] = rows_mid[2:5, :]
    table[6:8, :] = rows_mid[0:2, :]
    table[8:9, :] = rows_a1[0:1, :]
    table[ROWS : ROWS + chans, :] = gp0[:chans]
    table[ROWS + chans : ROWS + 2 * chans, :] = gp1[:chans]
    keep[16 * block :] = table[...].astype(BF16)
    send[16 * block :] = table[...].astype(BF16)


def second_body(keep, recv, keep_out, send_out):
    half = keep_out.shape[0]
    bit = wide_bits()[0]
    keep_out[...] = keep[rows_at(bit, half)] + recv[rows_at(bit, half)]
    send_out[...] = keep[rows_at(1 - bit, half)] + recv[rows_at(1 - bit, half)]


def beta_body(keep, recv, *chips):
    z, _, _ = places()
    size = chips[0].shape[0]
    base = keep.shape[0] - 4 * size
    for k, out in enumerate(chips):
        at = pl.ds(pl.multiple_of(base + (z ^ k) * size, 16), size)
        out[...] = keep[at] + recv[at]


def padded(*pieces):
    rows = jnp.concatenate(pieces, axis=0)
    fill = -rows.shape[0] % 16
    if fill:
        rows = jnp.concatenate([rows, jnp.zeros((fill, rows.shape[1]), F32)], axis=0)
    return rows.astype(BF16)


def paired(mine, other, sums):
    return padded(
        mine[:ROWS], other[:ROWS], mine[ROWS : ROWS + sums] + other[ROWS : ROWS + sums]
    )


def half_of_four(mine, other, sums, flip, four, total):
    _, c, w = places()
    first = jnp.where(c == flip, 1, 2)
    second = 3 - first
    spot = lax.rem(w, 4)
    four[spot] = mine[:ROWS]
    four[spot ^ first] = mine[ROWS : 2 * ROWS]
    four[spot ^ second] = other[:ROWS]
    four[spot ^ first ^ second] = other[ROWS : 2 * ROWS]
    at = slice(2 * ROWS, 2 * ROWS + sums)
    total[...] = mine[at] + other[at]
    half = sums // 2
    return four[2 * c], four[2 * c + 1], total[pl.ds(pl.multiple_of(c * half, 8), half), :]


def first_body(keep, recv, keep_out, table, send):
    half = (keep.shape[0] - table.shape[0]) // 2
    bit = wide_bits()[0]
    keep_out[...] = keep[rows_at(bit, half)] + recv[rows_at(bit, half)]
    send[0:half] = keep[rows_at(1 - bit, half)] + recv[rows_at(1 - bit, half)]
    rows = keep[2 * half :] + recv[2 * half :]
    table[...] = rows
    send[half:] = rows


def first_pair_body(sums, keep, table, recv, keep_out, pair_out, send):
    size = keep.shape[0]
    half = size // 2
    bit = wide_bits()[1]
    keep_out[...] = keep[rows_at(bit, half)] + recv[rows_at(bit, half)]
    send[0:half] = keep[rows_at(1 - bit, half)] + recv[rows_at(1 - bit, half)]
    pair = paired(table[...].astype(F32), recv[size:].astype(F32), sums)
    pair_out[...] = pair
    send[half:] = pair


def first_chip_body(
    sums, keep, pair, recv, tiles, z0, z1, z2, z3, four, total
):
    z, _, _ = places()
    size = keep.shape[0]
    unit = size // 4
    rows = half_of_four(pair[...].astype(F32), recv[size:].astype(F32), sums, 0, four, total)
    for k, out in enumerate((z0, z1, z2, z3)):
        out[0:unit] = keep[rows_at(z ^ k, unit)] + recv[rows_at(z ^ k, unit)]
        out[unit:] = padded(*rows, tiles[k])


def unit1_body(sums, o0, o1, o2, o3, unit, pack, tiles):
    ones = (o0, o1, o2, o3)
    unit[...] = chip_sum(ones, slice(0, unit.shape[0])).astype(BF16)
    chip_rows(sums, ones, unit.shape[0], pack)
    for i, one in enumerate(ones):
        tiles[-i % 4] = one[unit.shape[0] + 32 :].astype(F32)[8:]


def pack_body(preds, lgrads, tiles):
    z, _, _ = places()
    tok = preds.shape[1] // 4
    for k in range(4):
        cut = pl.ds(pl.multiple_of((z ^ k) * tok, 8), tok)
        latents = packed_tile([lgrads[0, cut, :], lgrads[1, cut, :]], lgrads.shape[2], 8)
        predicted = packed_tile([preds[0, cut, :], preds[1, cut, :]], preds.shape[2], 8)
        tiles[k] = jnp.concatenate([latents, predicted], axis=1)


def chip_sum(parts, at):
    return sum(part[at].astype(F32) for part in parts)


def third_body(keep2, recv2, b0, b1, b2, b3, keep2_out, keepb, part, whole):
    half2, halfb = keep2.shape[0] // 2, keepb.shape[0]
    bit = wide_bits()[1]
    keep2_out[...] = keep2[rows_at(bit, half2)] + recv2[rows_at(bit, half2)]
    part[0:half2] = keep2[rows_at(1 - bit, half2)] + recv2[rows_at(1 - bit, half2)]
    whole[...] = chip_sum((b0, b1, b2, b3), slice(None)).astype(BF16)
    keepb[...] = whole[rows_at(bit, halfb)]
    part[half2:] = whole[rows_at(1 - bit, halfb)]


def third_send_body(keep3, recv3, part, keep3_out, table, send):
    size = part.shape[0]
    size3 = keep3.shape[0] - table.shape[0]
    half3 = size3 // 2
    bit = wide_bits()[1]
    send[0:size] = part[...]
    keep3_out[...] = keep3[rows_at(bit, half3)] + recv3[rows_at(bit, half3)]
    send[size : size + half3] = keep3[rows_at(1 - bit, half3)] + recv3[rows_at(1 - bit, half3)]
    rows = keep3[size3:] + recv3[size3:]
    table[...] = rows
    send[size + half3 :] = rows


def fourth_body(
    sums, keep2, keep3, keepb, table, recv, z0, z1, z2, z3, keep3_out, keepb_out, pair_out, send
):
    z, _, _ = places()
    size2, size3, sizeb = keep2.shape[0], keep3.shape[0], keepb.shape[0]
    half3, halfb = size3 // 2, sizeb // 2
    unit = size2 // 4
    for k, out in enumerate((z0, z1, z2, z3)):
        out[...] = keep2[rows_at(z ^ k, unit)] + recv[rows_at(z ^ k, unit)]
    bit = wide_bits()[0]

    def half(held, index, size, base):
        start = pl.multiple_of(index * size, 16)
        return held[pl.ds(start, size)] + recv[pl.ds(pl.multiple_of(start + base, 16), size)]

    keep3_out[...] = half(keep3, bit, half3, size2 + sizeb)
    send[0:half3] = half(keep3, 1 - bit, half3, size2 + sizeb)
    keepb_out[...] = half(keepb, bit, halfb, size2)
    send[half3 : half3 + halfb] = half(keepb, 1 - bit, halfb, size2)
    pair = paired(table[...].astype(F32), recv[size2 + size3 + sizeb :].astype(F32), sums)
    pair_out[...] = pair
    send[half3 + halfb :] = pair


def fifth_body(sums, keep3, keepb, pair, recv, z0, z1, z2, z3, unitb, four, total):
    z, _, _ = places()
    size3, sizeb = keep3.shape[0], keepb.shape[0]
    unit3 = size3 // 4
    other = recv[size3 + sizeb :].astype(F32)
    rows = padded(*half_of_four(pair[...].astype(F32), other, sums, 1, four, total))
    for k, out in enumerate((z0, z1, z2, z3)):
        out[0:unit3] = keep3[rows_at(z ^ k, unit3)] + recv[rows_at(z ^ k, unit3)]
        out[unit3:] = rows
    unitb[...] = keepb[...] + recv[size3 : size3 + sizeb]


def chip_rows(sums, parts, size, pack):
    rows = [part[size : size + 48 if sums > 8 else size + 32].astype(F32) for part in parts]
    total = sum(r[2 * ROWS : 2 * ROWS + sums] for r in rows)
    pack[...] = padded(*[r[: 2 * ROWS] for r in rows], total)


def unit12_body(unit1, t0, t1, t2, t3, unitb, unit):
    size, end2 = unit1.shape[0], t0.shape[0]
    unit[0:size] = unit1[...]
    unit[size : size + end2] = chip_sum((t0, t1, t2, t3), slice(None)).astype(BF16)
    unit[size + end2 :] = unitb[...]


def join_body(own, near, send):
    size = own.shape[0]
    send[0:size] = own[...]
    send[size:] = near[...]


def unit3_body(sums, z0, z1, z2, z3, unit, pack):
    parts = (z0, z1, z2, z3)
    size = unit.shape[0]
    unit[...] = chip_sum(parts, slice(0, size)).astype(BF16)
    chip_rows(sums, parts, size, pack)


def silu_slope(values):
    sigmoid = jax.nn.sigmoid(values)
    return sigmoid * (1.0 + values * (1.0 - sigmoid))


def sample_table(table, pack, other):
    parts, half = table.shape[0], table.shape[1] // 2
    for side, held in enumerate((pack, other)):
        for i in range(parts):
            at = slice(128 * i, 128 * (i + 1))
            table[i, half * side : half * (side + 1)] = held[0:half, at].astype(F32)
    samples = table.shape[1] // ROWS

    def rows(r):
        return jnp.concatenate(
            [table[i, pl.ds(r, samples, stride=ROWS), :] for i in range(parts)], axis=-1
        )

    return rows


def join_sums(out, pack, other):
    c = lax.axis_index("cols")
    count = out.shape[0] // 2
    for side, held in enumerate((pack, other)):
        at = pl.ds(pl.multiple_of((c ^ side) * count, 8), count)
        out[at, :] = held[held.shape[0] - 16 :].astype(F32)[:count]


def early_sums_body(
    pack, other, final_mod,
    g_final_mod, g_final, shared_t, slopes, base, high, act_t, feat_t, hot, table,
):
    rows = sample_table(table, pack, other)
    join_sums(g_final, pack, other)
    fmods = jnp.concatenate([rows(0), rows(1)], axis=-1).astype(BF16)
    shared_t[...] = rows(ROW_SHARED).T
    g_final_mod[...] = dot(shared_t[...].astype(BF16), fmods)
    base[...] = dot_nt(fmods, final_mod[...])
    slopes[0] = silu_slope(rows(ROW_COND))
    slopes[1] = silu_slope(rows(ROW_HID))
    for k in range(3):
        high[k] = rows(2 + k)
    act_t[...] = rows(ROW_ACT).T.astype(BF16)
    feats = rows(ROW_FEAT)
    count = feat_t.shape[0]
    feat_t[...] = feats[:, :count].T.astype(BF16)
    label = (feats[:, count : count + 1] * 32.0 + feats[:, count + 1 : count + 2]).astype(jnp.int32)
    classes = hot.shape[0]
    lane = lax.broadcasted_iota(jnp.int32, (feats.shape[0], (classes + 127) // 128 * 128), 1)
    hot[...] = (lane == label).astype(F32).T[:classes].astype(BF16)


def sums_body(
    pack, other, modulation, time_out, shared_t, slopes, base, high, act_t, feat_t, hot,
    time_in_v, time_out_v, table_v, mod_v, g_patch,
    table,
):
    z, c, _ = places()
    rows = sample_table(table, pack, other)
    mods = [
        jnp.concatenate([rows(k) for k in range(6)], axis=-1).astype(BF16),
        jnp.concatenate(
            [rows(k) for k in range(6, 9)] + [high[k] for k in range(3)], axis=-1
        ).astype(BF16),
    ]
    block = mod_v.shape[1]
    start = pl.multiple_of((z * 2 + c) * block, 8)
    mine = shared_t[pl.ds(start, block), :].astype(BF16)
    for layer in range(2):
        mod_v[layer] = dot(mine, mods[layer])
    shared_grad = base[...]
    for layer in range(2):
        shared_grad += dot_nt(mods[layer], modulation[layer])
    cond_grad = shared_grad * slopes[0]
    cond_low = cond_grad.astype(BF16)
    cond_rest = (cond_grad - cond_low.astype(F32)).astype(BF16)
    table_v[...] = dot(hot[...], cond_low) + dot(hot[...], cond_rest)
    time_out_v[...] = dot(act_t[...], cond_low)
    time_grad = dot_nt(cond_low, time_out[...]) * slopes[1]
    time_in_v[...] = dot(feat_t[...], time_grad.astype(BF16))
    join_sums(g_patch, pack, other)


def unpack_body(tiles, *refs):
    held, left, (prediction, latent_grad, token, sem) = refs[:5], refs[5:10], refs[10:]
    copies = []
    leave_all(tuple(zip(held, left)), sem, copies)
    z, _, _ = places()
    token[...] = jnp.zeros_like(token)
    _, out_ch, height, wide = prediction.shape
    lat_ch = latent_grad.shape[1]
    for k in range(4):
        split = tiles.shape[2] // 3
        image = unpacked_tile(tiles[k, :, split:].astype(BF16), out_ch, height, wide)
        prediction[z ^ k] = image.astype(BF16).reshape(out_ch, height, wide)
        image = unpacked_tile(tiles[k, :, :split].astype(BF16), lat_ch, height, wide)
        latent_grad[z ^ k] = image.reshape(lat_ch, height, wide)
    for copy in copies:
        copy.wait()


def place_mlp(up, down, piece, unit):
    block, width = up.shape[0], down.shape[1]
    cols = pl.ds(pl.multiple_of(unit * width, 128), width)
    up[:, cols] = piece[0:block].astype(F32)
    down_rows = pl.ds(pl.multiple_of(unit * block, 8), block)
    down[down_rows, :] = piece[block : 2 * block].astype(F32)


def place_attn(qkv, proj, piece, unit):
    width = proj.shape[1]

    @pl.when(unit < 3)
    def _():
        cols = pl.ds(pl.multiple_of(unit * width, 128), width)
        qkv[:, cols] = piece.astype(F32)

    @pl.when(unit == 3)
    def _():
        proj[...] = piece.astype(F32)


def wide_spots():
    _, c, w = places()
    first = jnp.where(c == 0, 1, 2)
    spot = lax.rem(w, 4)
    return spot, spot ^ first, spot ^ first ^ 3, spot ^ 3


def leave_all(pairs, sem, copies):
    for source, target in pairs:
        copies.append(pltpu.make_async_copy(source, target, sem.at[len(copies)]))
        copies[-1].start()


def spread_body(own, near, far, g_qkv, g_proj, g_up, g_down, up, down, qkv, proj, sem):
    size2 = own.shape[0]
    block = proj.shape[0]
    size = 2 * block
    units = ((own, 0), (near, 0), (far, 0), (far, size2))
    copies = []
    for layer, start in ((1, 0), (0, size)):
        for (ref, base), unit in zip(units, wide_spots()):
            piece = ref[base + start : base + start + size]
            place_mlp(up.at[layer], down.at[layer], piece, unit)
        leave_all(
            ((up.at[layer], g_up.at[layer]), (down.at[layer], g_down.at[layer])), sem, copies
        )
    for (ref, base), unit in zip(units, wide_spots()):
        place_attn(qkv, proj, ref[base + 2 * size : base + size2], unit)
    leave_all(((qkv, g_qkv.at[1]), (proj, g_proj.at[1])), sem, copies)
    for copy in copies:
        copy.wait()


def last_spread_body(own, near, far, _q, _p, g_qkv, g_proj, qkv, proj, sem):
    size = own.shape[0]
    units = ((own, 0), (near, 0), (far, 0), (far, size))
    for (ref, base), unit in zip(units, wide_spots()):
        place_attn(qkv, proj, ref[base : base + size], unit)
    copies = []
    leave_all(((qkv, g_qkv.at[0]), (proj, g_proj.at[0])), sem, copies)
    for copy in copies:
        copy.wait()


def swap(value, axis, bit):
    count = lax.axis_size(axis)
    return lax.ppermute(value, axis, [(i, i ^ bit) for i in range(count)])


def swap_by_core(value, bits):
    wide, cores = lax.axis_size("wide"), lax.axis_size("cols")
    pairs = [
        (w * cores + c, (w ^ bits[c % 2]) * cores + c) for w in range(wide) for c in range(cores)
    ]
    return lax.ppermute(value, ("wide", "cols"), pairs)


FIRST, SECOND = (1, 2), (2, 1)


def rest_sum(value):
    bit = 4
    while bit < lax.axis_size("wide"):
        value = (value.astype(F32) + swap(value, "wide", bit).astype(F32)).astype(value.dtype)
        bit *= 2
    return value


def rest_gather(value):
    bit = 4
    while bit < lax.axis_size("wide"):
        value = jnp.concatenate([value, swap(value, "wide", bit)])
        bit *= 2
    return value


def position_tables(row_count, col_count, cores, width):
    quarter = width // 4
    omega = np.exp(-math.log(10000.0) * np.arange(quarter) / quarter)
    row_angle = np.arange(row_count)[:, None] * omega[None, :]
    col_angle = np.arange(col_count * cores)[:, None] * omega[None, :]
    row_part = np.concatenate([np.sin(row_angle), np.cos(row_angle)], axis=-1)
    col_part = np.concatenate([np.sin(col_angle), np.cos(col_angle)], axis=-1)
    col_part = col_part.reshape(cores, 1, col_count, width // 2)
    table = np.concatenate(
        [
            np.broadcast_to(row_part[None, :, None, :], (cores, row_count, col_count, width // 2)),
            np.broadcast_to(col_part, (cores, row_count, col_count, width // 2)),
        ],
        axis=-1,
    )
    return table.reshape(cores, row_count * col_count, width).astype(np.float32)


def shards(
    latent, pred_grad, timesteps, labels, offsets, counts, patch_weight, time_in, time_out,
    label_table, modulation, qkv_weight, proj_weight, up_weight, down_weight, final_mod, final_weight,
):
    slots, lat_ch, tile_h, tile_w = latent.shape
    out_ch = pred_grad.shape[1]
    width = patch_weight.shape[1]
    ff = up_weight.shape[2]
    n_rows, n_cols = lax.axis_size("rows"), lax.axis_size("cols")
    hp, wp = tile_h // 2, tile_w // 2
    tile_tok = hp * wp
    tokens = n_rows * tile_tok
    lanes = 2 * (lat_ch + out_ch)
    block = width // 8
    tok, wide_tok, double = (tokens, width), (tokens, ff), (tokens, 2 * width)

    tiles = kernel_call(
        tiles_body,
        [("h", latent), ("h", pred_grad)],
        [((2, tile_tok, lanes), BF16)] * n_rows,
        [
            pltpu.VMEM(latent.shape, BF16), pltpu.VMEM(pred_grad.shape, BF16),
            pltpu.SemaphoreType.DMA((2,)),
        ],
        us=1,
    )

    def along_z(parts):
        return [parts[0]] + [swap(parts[k], "rows", k) for k in reversed(range(1, n_rows))]

    def both_halves(pack):
        if lax.axis_size("wide") > 4:
            rows, sums = rest_gather(pack[: 8 * ROWS]), rest_sum(pack[8 * ROWS :])
            pack = jnp.concatenate([rows, sums])
        return pack, swap(pack, "cols", 1)

    tiles = along_z(tiles)
    half = time_in.shape[0] // 2
    freqs = np.exp(-math.log(10000.0) * np.arange(half, dtype=np.float32) / np.float32(half))
    positions = jnp.asarray(position_tables(n_rows * hp, wp, n_cols, width))
    blocks = (qkv_weight, proj_weight, up_weight, down_weight)
    weights = (time_out, modulation, final_mod) + blocks
    held = [(weight.shape[1:], BF16) for weight in blocks]
    (
        mods, cond, final_v, pos, time_out_v, modulation_v, final_mod_v, qkv0, proj0, up0, down0,
    ) = kernel_call(
        cond_body,
        [("s", timesteps), ("s", labels), ("v", jnp.asarray(freqs.astype(np.float32))[None])]
        + [("v", label_table), ("v", time_in), ("v", final_weight), ("h", positions)]
        + [("h", weight) for weight in weights],
        [((3, 8, width), F32), ((8, width), F32), (final_weight.shape, BF16), (tok, F32)]
        + [(weight.shape, BF16) for weight in weights[:3]]
        + held,
        [pltpu.SemaphoreType.DMA((len(weights) + 1,))],
        us=US["cond"],
    )
    probs_shape = (HEADS, 2, tokens, tokens)
    state0, q0, kv0, patches = kernel_call(
        embed_body,
        [("s", offsets)]
        + [("v", t) for t in tiles]
        + [("p", pos), ("p", mods), ("v", patch_weight), ("p", qkv0)],
        [(tok, F32), (tok, BF16), (double, BF16), ((2, tokens, lanes), BF16)],
        [pltpu.VMEM((n_rows, 2, tile_tok, lanes), BF16)],
        us=US["embed"],
    )
    kv0p = swap(kv0, "cols", 1)
    (
        state1, q1, kv1, probs0, attended0, attn_out0, middle0, gp0, act0, branch0, qkv1, proj1, up1, down1,
    ) = kernel_call(
        block_body,
        [("p", state0), ("p", q0), ("p", kv0), ("v", kv0p)]
        + [("p", a) for a in (mods, proj0, up0, down0)]
        + [("h", weight) for weight in blocks],
        [
            (tok, F32), (tok, BF16), (double, BF16), (probs_shape, BF16), (tok, BF16), (tok, BF16),
            (tok, F32), (wide_tok, BF16), (wide_tok, BF16), (tok, BF16),
        ]
        + held,
        [pltpu.SemaphoreType.DMA((4,))],
        us=US["block"],
    )
    kv1p = swap(kv1, "cols", 1)
    sums_a, sums_b = 4 * out_ch, 4 * lat_ch
    rows_1 = 16 * 2 * block + 48
    probs1, attended1, attn_out1, mgrad1, keep1, send1, preds = kernel_call(
        turn_body,
        [("s", offsets), ("s", counts), ("p", state1), ("p", q1), ("p", kv1), ("v", kv1p)]
        + [("p", a) for a in (mods, cond, patches, final_v, proj1, up1, down1)],
        [
            (probs_shape, BF16), (tok, BF16), (tok, BF16), (tok, F32), ((rows_1, width), BF16),
            ((rows_1, width), BF16), ((2, tokens, 2 * out_ch), F32),
        ],
        [
            pltpu.VMEM(wide_tok, BF16), pltpu.VMEM(wide_tok, BF16), pltpu.VMEM((48, width), F32),
            pltpu.VMEM(wide_tok, BF16),
        ],
        us=US["turn"],
    )
    recv1 = swap(send1, "cols", 1)

    def attend_back(layer, q, kv, kvp, *saved, after):
        return kernel_call(
            partial(attend_back_body, layer),
            [("p", q), ("p", kv), ("v", kvp)] + [("p", a) for a in saved[:-1] + (mods, saved[-1])],
            [
                (tok, BF16), (double, BF16), ((width, width), BF16), (double, BF16), ((8, width), F32),
            ],
            us=US["back"],
            after=after,
        )

    dq1, dkv1, gproj1, dkvs1, rows_a1 = attend_back(
        1, q1, kv1, kv1p, probs1, attended1, attn_out1, mgrad1, proj1, after=None
    )
    dkvr1 = swap(dkvs1, "cols", 1)
    keep1, table1, send1 = kernel_call(
        first_body,
        [("p", keep1), ("v", recv1)],
        [((8 * 2 * block, width), BF16), ((48, width), BF16), ((8 * 2 * block + 48, width), BF16)],
        us=US["A1"],
        after=rows_a1,
    )
    recv1 = swap_by_core(send1, FIRST)
    mgrad0, keep2, send2, rows_mid = kernel_call(
        middle_body,
        [("p", a) for a in (state1, mgrad1, dq1, dkv1)]
        + [("v", dkvr1)]
        + [("p", a) for a in (gproj1, middle0, branch0, gp0, act0, mods, qkv1, up0, down0)],
        [
            (tok, F32), ((16 * 3 * block, width), BF16), ((16 * 3 * block, width), BF16),
            ((8, width), F32),
        ],
        [pltpu.VMEM(wide_tok, BF16)],
        us=US["middle"],
        after=table1,
    )
    recv2 = swap(send2, "cols", 1)
    dq0, dkv0, gproj0, dkvs0, rows_a0 = attend_back(
        0, q0, kv0, kv0p, probs0, attended0, attn_out0, mgrad0, proj0, after=None
    )
    dkvr0 = swap(dkvs0, "cols", 1)
    alpha, beta = 2 * block, block
    send_rows = 4 * alpha + 2 * beta + 8 * block + 32
    whole_2, whole_r = keep2, recv2
    keep2, send2 = kernel_call(
        second_body,
        [("p", whole_2), ("v", whole_r)],
        [((8 * alpha, width), BF16)] * 2,
        us=US["A3"],
        after=rows_a0,
    )
    recv2 = swap_by_core(send2, FIRST)
    keep1, pair1, send1 = kernel_call(
        partial(first_pair_body, sums_a),
        [("p", keep1), ("p", table1), ("v", recv1)],
        [((4 * 2 * block, width), BF16), ((64, width), BF16), ((4 * 2 * block + 64, width), BF16)],
        us=US["A2"],
        after=keep2,
    )
    recv1 = swap_by_core(send1, SECOND)
    betas = kernel_call(
        beta_body,
        [("p", whole_2), ("v", whole_r)],
        [((4 * beta, width), BF16)] * 4,
        us=US["A3b"],
        after=pair1,
    )
    chips = betas[0]
    betas = along_z(betas)
    rows_3 = 16 * block + 32
    keep3, send3, lgrads = kernel_call(
        last_body,
        [("s", offsets), ("p", state0), ("p", mgrad0), ("p", dq0), ("p", dkv0), ("v", dkvr0)]
        + [("p", gproj0), ("p", mods), ("p", patches), ("v", patch_weight)]
        + [("p", a) for a in (rows_a1, rows_mid, rows_a0, qkv0)],
        [((rows_3, width), BF16), ((rows_3, width), BF16), ((2, tokens, 2 * lat_ch), F32)],
        [pltpu.VMEM((8, width), F32), pltpu.VMEM((32, width), F32)],
        us=US["last"],
        after=chips,
    )
    recv3 = swap(send3, "cols", 1)
    (tiles,) = kernel_call(
        pack_body, [("p", preds), ("p", lgrads)], [((4, 8, width), F32)], us=US["pack"]
    )
    ones = kernel_call(
        partial(first_chip_body, sums_a),
        [("p", keep1), ("p", pair1), ("v", recv1), ("p", tiles)],
        [((2 * block + 48, width), BF16)] * 4,
        [pltpu.VMEM((4, ROWS, width), F32), pltpu.VMEM((sums_a, width), F32)],
        us=US["A2b"],
    )
    chips = ones[0]
    ones = along_z(ones)
    keep2, keepb, part = kernel_call(
        third_body,
        [("p", keep2), ("v", recv2), ("p", betas[0])] + [("v", beta) for beta in betas[1:]],
        [
            ((4 * alpha, width), BF16), ((2 * beta, width), BF16),
            ((4 * alpha + 2 * beta, width), BF16),
        ],
        [pltpu.VMEM((4 * beta, width), BF16)],
        us=US["A4"],
        after=chips,
    )
    keep3, table3, send = kernel_call(
        third_send_body,
        [("p", keep3), ("v", recv3), ("p", part)],
        [((8 * block, width), BF16), ((32, width), BF16), ((send_rows, width), BF16)],
        us=US["A4b"],
    )
    recv = swap_by_core(send, SECOND)
    *twos, keep3, keepb, pair3, send = kernel_call(
        partial(fourth_body, sums_b),
        [("p", keep2), ("p", keep3), ("p", keepb), ("p", table3), ("v", recv)],
        [((alpha, width), BF16)] * 4
        + [
            ((4 * block, width), BF16), ((beta, width), BF16), ((48, width), BF16),
            ((4 * block + beta + 48, width), BF16),
        ],
        us=US["A5"],
    )
    recv = swap_by_core(send, FIRST)
    twos = along_z(twos)
    pack = (8 * ROWS + 16, width)
    unit1, pack_a, tiles = kernel_call(
        partial(unit1_body, sums_a // 2),
        [("p", ones[0])] + [("v", one) for one in ones[1:]],
        [((2 * block, width), BF16), (pack, BF16), ((4, 8, width), F32)],
        us=US["U1"],
        after=pair3,
    )
    packs = both_halves(pack_a)
    *threes, unitb = kernel_call(
        partial(fifth_body, sums_b),
        [("p", keep3), ("p", keepb), ("p", pair3), ("v", recv)],
        [((block + 32, width), BF16)] * 4 + [((beta, width), BF16)],
        [pltpu.VMEM((4, ROWS, width), F32), pltpu.VMEM((sums_b, width), F32)],
        us=US["A6"],
        after=pack_a,
    )
    threes = along_z(threes)
    (unit2,) = kernel_call(
        unit12_body,
        [("p", unit1), ("p", twos[0])] + [("v", two) for two in twos[1:]] + [("p", unitb)],
        [((2 * block + alpha + beta, width), BF16)],
        us=US["U12"],
    )
    unit2 = rest_sum(unit2)
    near2 = swap_by_core(unit2, FIRST)
    samples = 2 * (packs[0].shape[0] - 16) // ROWS
    classes = label_table.shape[0]
    feat_count = time_in.shape[0]
    g_final_mod, g_final, *early = kernel_call(
        early_sums_body,
        [("p", packs[0]), ("v", packs[1]), ("p", final_mod_v)],
        [
            (final_mod.shape, F32, "any"), ((sums_a, width), F32, "any"), ((width, samples), F32),
            ((2, samples, width), F32), ((samples, width), F32), ((3, samples, width), F32),
            ((width, samples), BF16), ((feat_count, samples), BF16), ((classes, samples), BF16),
        ],
        [pltpu.VMEM((width // 128, samples * ROWS, 128), F32)],
        us=US["early"],
        after=unit2,
    )
    unit3, pack_b = kernel_call(
        partial(unit3_body, sums_b // 2),
        [("p", threes[0])] + [("v", three) for three in threes[1:]],
        [((block, width), BF16), (pack, BF16)],
        us=US["U2"],
        after=early[0],
    )
    unit3 = rest_sum(unit3)
    near3 = swap_by_core(unit3, FIRST)
    (send2,) = kernel_call(
        join_body,
        [("p", unit2), ("v", near2)],
        [((2 * unit2.shape[0], width), BF16)],
        us=US["join"],
        after=pack_b,
    )
    far2 = swap_by_core(send2, SECOND)
    packs = both_halves(pack_b)
    late_shapes = (
        time_in.shape, time_out.shape, (classes, width), (2, block, 6 * width), patch_weight.shape,
    )
    late = kernel_call(
        sums_body,
        [("p", packs[0]), ("v", packs[1])] + [("p", a) for a in (modulation_v, time_out_v, *early)],
        [(shape, F32) for shape in late_shapes],
        [pltpu.VMEM((width // 128, samples * ROWS, 128), F32)],
        us=US["sums"],
    )
    (send3,) = kernel_call(
        join_body,
        [("p", unit3), ("v", near3)],
        [((2 * block, width), BF16)],
        us=US["F3"],
        after=late[4],
    )
    far3 = swap_by_core(send3, SECOND)
    g_time_in, g_time_out, g_table, g_mod, g_patch, prediction, latent_grad, token = kernel_call(
        unpack_body,
        [("p", tiles)] + [("p", a) for a in late],
        [(shape, F32, "hbm") for shape in late_shapes]
        + [((slots, out_ch, tile_h, tile_w), BF16, "any"), (latent.shape, F32, "any"), ((8, 128), F32)],
        [pltpu.SemaphoreType.DMA((5,))],
        us=US["unpack"],
        after=send3,
    )
    up_shape, down_shape = (2, block, ff), (2, ff // 8, width)
    attn_scratch = [pltpu.VMEM((block, 3 * width), F32), pltpu.VMEM((block, width), F32)]
    attn_shapes = [((2, block, 3 * width), F32, "hbm"), ((2, block, width), F32, "hbm")]
    g_qkv, g_proj, g_up, g_down = kernel_call(
        spread_body,
        [("p", unit2), ("v", near2), ("v", far2)],
        attn_shapes + [(up_shape, F32, "hbm"), (down_shape, F32, "hbm")],
        [pltpu.VMEM(up_shape, F32), pltpu.VMEM(down_shape, F32)]
        + attn_scratch
        + [pltpu.SemaphoreType.DMA((6,))],
        us=US["spread"],
        after=token,
    )
    g_qkv, g_proj = kernel_call(
        last_spread_body,
        [("p", unit3), ("v", near3), ("v", far3), ("h", g_qkv), ("h", g_proj)],
        attn_shapes,
        attn_scratch + [pltpu.SemaphoreType.DMA((2,))],
        us=US["spread"],
        aliases=((3, 0), (4, 1)),
    )
    return (
        prediction, latent_grad, g_patch, g_time_in, g_time_out, g_table, g_mod, g_qkv, g_proj,
        g_up, g_down, g_final_mod, g_final.T,
    )


def solution(mesh):
    tiled, split = P("wide", None, "rows", "cols"), P(None, ("rows", "cols"), None)
    return jax.shard_map(
        shards,
        mesh=mesh,
        in_specs=(tiled, tiled, P("wide"), P("wide"), P("wide"), P("wide")) + (P(),) * 11,
        out_specs=(tiled, tiled, P(), P(), P(), P(), split, split, split, split, split, P(), P()),
        check_vma=False,
    )
```

```python
from functools import partial
import math

import jax
import jax.numpy as jnp
import numpy as np
from jax import lax
from jax.experimental import pallas as pl
from jax.experimental.pallas import tpu as pltpu
from jax.sharding import PartitionSpec as P

HEADS = 6
HEAD_DIM = 64
PAIRS = HEADS // 2
LANES = 2 * HEAD_DIM
EPS = 1e-06
F32 = jnp.float32
BF16 = jnp.bfloat16
ROWS = 12
ROW_SHARED, ROW_ACT, ROW_COND, ROW_HID, ROW_FEAT = 5, 6, 7, 8, 9
US = {
    "cond": 5, "embed": 2, "block": 6, "turn": 9, "back": 20, "middle": 4, "last": 4, "early": 0.05, "pack": 0.05, "join": 0.05, "U12": 0.05, "F3": 0.05, "unpack": 0.05, "relay": 0.05, "sums": 5, "spread": 0.05,
    "A1": 0.05, "A2": 0.05, "A2b": 0.05, "A3": 0.05, "A3b": 0.05, "A4": 30, "A4b": 0.05, "A5": 0.05, "A6": 0.05, "S1": 0.05, "U2": 3,
    "U1": 1,
}


def dot(a, b):
    return jnp.dot(a, b, preferred_element_type=F32)


def dot_nt(a, b):
    return lax.dot_general(a, b, (((1,), (1,)), ((), ())), preferred_element_type=F32)


def dot_tn(a, b):
    return lax.dot_general(a, b, (((0,), (0,)), ((), ())), preferred_element_type=F32)


def sds(shape, dtype):
    return jax.ShapeDtypeStruct(shape, dtype)


def layer_norm(states):
    centred = states - jnp.mean(states, axis=-1, keepdims=True)
    inverse = lax.rsqrt(jnp.mean(centred * centred, axis=-1, keepdims=True) + EPS)
    return centred * inverse, inverse


def norm_back(grad, normed, inverse):
    mean_grad = jnp.mean(grad, axis=-1, keepdims=True)
    mean_cross = jnp.mean(grad * normed, axis=-1, keepdims=True)
    return inverse * (grad - mean_grad - normed * mean_cross)


def token_sum(values):
    return jnp.sum(values, axis=0, keepdims=True)


def head_masks(dtype):
    lane = lax.broadcasted_iota(jnp.int32, (1, LANES), 1)
    first = (lane < HEAD_DIM).astype(F32)
    return first.astype(dtype), (1.0 - first).astype(dtype)


def unit_place(zz, ww, cc):
    x, y = ww % 2, ww // 2
    return (x * 8 + y * 4 + zz) if cc == 0 else (y * 8 + x * 4 + zz)


def kernel_call(body, ins, outs, scratch=(), us=1.0, after=None, aliases=()):
    spaces = {"v": pltpu.VMEM, "p": pltpu.VMEM, "s": pltpu.SMEM, "h": pltpu.HBM}
    specs, arrays = [], []
    for kind, array in ins:
        specs.append(pl.BlockSpec(memory_space=spaces[kind]))
        if kind in "ph":
            array = pltpu.with_memory_space_constraint(array, spaces[kind])
        arrays.append(array)
    if after is not None:
        specs.append(pl.BlockSpec(memory_space=pl.ANY))
        arrays.append(after)

    def kernel(*refs):
        body(*refs[: len(ins)], *refs[len(arrays) :])

    return pl.pallas_call(
        kernel,
        in_specs=specs,
        out_specs=[
            pl.BlockSpec(memory_space=pltpu.HBM if "hbm" in o[2:] else pltpu.VMEM) for o in outs
        ],
        out_shape=[
            pltpu.VMEM(o[0], o[1]) if len(o) < 3 else sds(o[0], o[1]) if o[2] == "any" else pltpu.HBM(o[0], o[1])
            for o in outs
        ],
        input_output_aliases=dict(aliases),
        scratch_shapes=list(scratch),
        compiler_params=pltpu.CompilerParams(vmem_limit_bytes=24 * 1024 * 1024),
        cost_estimate=pl.CostEstimate(
            flops=int(us * 1.5e9), bytes_accessed=int(us * 1e6), transcendentals=0
        ),
    )(*arrays)


def one_hot(shape, test):
    first = lax.broadcasted_iota(jnp.int32, shape, 0)
    second = lax.broadcasted_iota(jnp.int32, shape, 1)
    return test(first, second).astype(F32).astype(BF16)


def places():
    return lax.axis_index("rows"), lax.axis_index("cols"), lax.axis_index("wide")


def chip_place(zz, ww, cc):
    x, y = ww % 2, ww // 2
    return zz * 4 + ((2 * y + x) if cc == 0 else (2 * x + y))


def wide_bits():
    _, c, w = places()
    x, y = lax.rem(w, 2), lax.rem(lax.div(w, 2), 2)
    return jnp.where(c == 0, x, y), jnp.where(c == 0, y, x)


def rows_at(index, count):
    return pl.ds(pl.multiple_of(index * count, 16), count)


def tiles_body(latent_h, pred_h, *rest):
    tiles, (latent, pred_grad, sem) = rest[:-3], rest[-3:]
    copies = [
        pltpu.make_async_copy(latent_h, latent, sem.at[0]),
        pltpu.make_async_copy(pred_h, pred_grad, sem.at[1]),
    ]
    for copy in copies:
        copy.start()
    z, _, _ = places()
    _, lat_ch, height, wide = latent.shape
    out_ch = pred_grad.shape[1]
    chans, tok = lat_ch + out_ch, height * wide // 4
    half = wide // 2
    lanes = 2 * chans
    spread = [one_hot((tok, wide), lambda t, v: v == 2 * (t % half) + u) for u in range(2)]
    inside = [
        one_hot((tok, chans * height), lambda t, v: v % height == 2 * (t // half) + par).astype(F32)
        for par in range(2)
    ]

    def lane_of(channel, u):
        return jnp.where(
            channel < lat_ch, u * lat_ch + channel, 2 * lat_ch + u * out_ch + channel - lat_ch
        )

    fold = [
        one_hot((chans * height, lanes), lambda v, lane: lane == lane_of(v // height, u))
        for u in range(2)
    ]
    for copy in copies:
        copy.wait()
    for k, tile in enumerate(tiles):
        image = jnp.concatenate(
            [
                latent[z ^ k].reshape(lat_ch * height, wide),
                pred_grad[z ^ k].reshape(out_ch * height, wide),
            ],
            axis=0,
        )
        wide_rows = [dot_nt(spread[u], image) for u in range(2)]
        for par in range(2):
            tile[par] = sum(
                dot((wide_rows[u] * inside[par]).astype(BF16), fold[u]) for u in range(2)
            ).astype(BF16)


def packed_tile(parities, lanes, order):
    tok = parities[0].shape[0]
    across = tok // order
    total = order * 2 * lanes
    block = 0.0
    for par in range(2):
        copy = one_hot((lanes, total), lambda a, b: b % (2 * lanes) == par * lanes + a)
        block = block + dot(parities[par].astype(BF16), copy)
    own = one_hot((tok, total), lambda t, b: b // (2 * lanes) == t // across).astype(F32)
    gather = one_hot((across, tok), lambda j, t: t % across == j)
    return dot(gather, (block * own).astype(BF16))


def unpacked_tile(block, chans, height, wide):
    lanes = 2 * chans
    half = wide // 2
    image = 0.0
    for u in range(2):
        chosen = one_hot(
            (chans * height, block.shape[1]),
            lambda v, b: b
            == (v % height) // 2 * 2 * lanes + v % 2 * lanes + u * chans + v // height,
        )
        column = dot_nt(chosen, block).astype(BF16)
        image = image + dot(column, one_hot((half, wide), lambda j, v: v == 2 * j + u))
    return image


def by_parity(first, second, offset):
    step = first.shape[0] // 32
    moved = jnp.concatenate([jnp.zeros((step, second.shape[1]), F32), second[:-step]], axis=0)
    return jnp.where(offset == 1, moved, first), jnp.where(offset == 1, first, second)


def cond_body(
    timesteps, labels, freqs, label_table, time_in, final_weight, positions, *rest,
):
    sources, (mods, cond, final_copy, pos), held = rest[:7], rest[7:11], rest[11:18]
    sem = rest[18]
    final_copy[...] = final_weight[...]
    sources = sources[:3] + tuple(source.at[0] for source in sources[3:])
    sources += (positions.at[lax.axis_index("cols")],)
    held = held + (pos,)
    copies = [
        pltpu.make_async_copy(source, target, sem.at[i])
        for i, (source, target) in enumerate(zip(sources, held))
    ]
    for copy in copies:
        copy.start()
    time_out, modulation, final_mod = held[:3]
    z, _, _ = places()
    label = labels[z]
    count, width = time_in.shape
    angles = jnp.full((8, count // 2), timesteps[z].astype(F32)) * freqs[...]
    feats = jnp.concatenate([jnp.cos(angles), jnp.sin(angles)], axis=-1).astype(BF16)
    hidden = dot(feats, time_in[...])
    act = (hidden * jax.nn.sigmoid(hidden)).astype(BF16)
    chosen = one_hot((8, label_table.shape[0]), lambda a, b: b == label)
    copies[0].wait()
    condition = dot(act, time_out[...]) + dot(chosen, label_table[...])
    shared = (condition * jax.nn.sigmoid(condition)).astype(BF16)
    mods[...] = jnp.zeros_like(mods)
    copies[1].wait()
    for layer in range(2):
        values = dot(shared, modulation[layer])
        for k in range(6):
            mods[layer, k : k + 1, :] = values[0:1, k * width : (k + 1) * width]
    copies[2].wait()
    values = dot(shared, final_mod[...])
    for k in range(2):
        mods[2, k : k + 1, :] = values[0:1, k * width : (k + 1) * width]
    lane = lax.broadcasted_iota(jnp.int32, (1, width - count), 1)
    marks = jnp.where(
        lane == 0, lax.div(label, 32), jnp.where(lane == 1, lax.rem(label, 32), 0)
    ).astype(F32)
    cond[...] = jnp.zeros_like(cond)
    cond[0:1, :] = shared[0:1].astype(F32)
    cond[1:2, :] = act[0:1].astype(F32)
    cond[2:3, :] = condition[0:1]
    cond[3:4, :] = hidden[0:1]
    cond[4:5, :] = jnp.concatenate([feats[0:1].astype(F32), marks], axis=-1)
    for copy in copies[3:]:
        copy.wait()


def qkv_forward(state, mods, layer, weight):
    width = state.shape[-1]
    normed, _ = layer_norm(state)
    inner = (normed * (1.0 + mods[layer, 1:2]) + mods[layer, 0:1]).astype(BF16)
    projected = dot(inner, weight[...]).astype(BF16)
    return projected[:, :width], projected[:, width:]


def attend_forward(q, kv, kvp, probs, attended):
    width = q.shape[-1]
    masks = head_masks(BF16)
    for p in range(PAIRS):
        at = slice(p * LANES, (p + 1) * LANES)
        av = slice(width + p * LANES, width + (p + 1) * LANES)
        qp = q[:, at] * BF16(HEAD_DIM**-0.5)
        k0, v0, k1, v1 = kv[:, at], kv[:, av], kvp[:, at], kvp[:, av]
        total = None
        for h in range(2):
            qh = qp * masks[h]
            s0, s1 = dot_nt(qh, k0), dot_nt(qh, k1)
            peak = jnp.maximum(
                jnp.max(s0, axis=-1, keepdims=True), jnp.max(s1, axis=-1, keepdims=True)
            )
            e0, e1 = jnp.exp(s0 - peak), jnp.exp(s1 - peak)
            scale = 1.0 / (
                jnp.sum(e0, axis=-1, keepdims=True) + jnp.sum(e1, axis=-1, keepdims=True)
            )
            p0, p1 = (e0 * scale).astype(BF16), (e1 * scale).astype(BF16)
            probs[2 * p + h, 0] = p0
            probs[2 * p + h, 1] = p1
            part = dot(p0, v0 * masks[h]) + dot(p1, v1 * masks[h])
            total = part if total is None else total + part
        attended[:, at] = total.astype(BF16)


CHUNK = 768
BACK_CHUNK = 1536


def mlp_forward(middle, mods, layer, up, down, gp, act):
    normed, _ = layer_norm(middle)
    inner = (normed * (1.0 + mods[layer, 4:5]) + mods[layer, 3:4]).astype(BF16)
    branch = None
    for start in range(0, up.shape[1], CHUNK):
        at = slice(start, start + CHUNK)
        hidden = dot(inner, up[:, at])
        square = hidden * hidden
        root = math.sqrt(2.0 / math.pi)
        bent = jnp.tanh(root * hidden * (1.0 + 0.044715 * square))
        half = 0.5 * (1.0 + bent)
        activated = (hidden * half).astype(BF16)
        act[:, at] = activated
        slope = half + 0.5 * hidden * (1.0 - bent * bent) * (root * (1.0 + 3 * 0.044715 * square))
        gp[:, at] = slope.astype(BF16)
        part = dot(activated, down[at, :])
        branch = part if branch is None else branch + part
    return branch


def put_units(keep, send, pair, place, size, at_row):
    first = lax.axis_index("cols") == 0
    block = pair[0].shape[0]
    own = jnp.where(first, place[0], place[1]) * size + at_row
    other = jnp.where(first, place[1], place[0]) * size + at_row
    keep[pl.ds(pl.multiple_of(own, 16), block), :] = jnp.where(first, pair[0], pair[1])
    send[pl.ds(pl.multiple_of(other, 16), block), :] = jnp.where(first, pair[1], pair[0])


def mlp_backward(
    grad, middle, branch, mods, layer, gp, act, up, down, keep, send, size, flip, rows, first, low
):
    width = middle.shape[-1]
    normed, inverse = layer_norm(middle)
    scale = 1.0 + mods[layer, 4:5]
    inner_t = (normed * scale + mods[layer, 3:4]).astype(BF16).T
    branch_grad = (mods[layer, 5:6] * grad).astype(BF16)
    inner_grad = None
    for start in range(0, up.shape[1], BACK_CHUNK):
        at = slice(start, start + BACK_CHUNK)
        act_grad = dot_nt(branch_grad, down[at, :])
        hidden_grad = (act_grad * gp[:, at].astype(F32)).astype(BF16)
        low[:, at] = hidden_grad
        part = dot_nt(hidden_grad, up[:, at])
        inner_grad = part if inner_grad is None else inner_grad + part
    block = width // 8
    for i in range(up.shape[1] // width):
        at = slice(i * width, (i + 1) * width)
        grad_up = dot(inner_t, low[:, at]).astype(BF16)
        for b in range(4):
            pair = [grad_up[(2 * b + cc) * block : (2 * b + cc + 1) * block] for cc in range(2)]
            place = [unit_place(b, i, cc ^ flip) for cc in range(2)]
            put_units(keep, send, pair, place, size, 0)
        grad_down = dot_tn(act[:, at], branch_grad).astype(BF16)
        for j in range(4):
            pair = [grad_down[(4 * cc + j) * block : (4 * cc + j + 1) * block] for cc in range(2)]
            place = [unit_place(i, j, cc ^ flip) for cc in range(2)]
            put_units(keep, send, pair, place, size, block)
    rows[first : first + 1, :] = token_sum(inner_grad)
    rows[first + 1 : first + 2, :] = token_sum(inner_grad * normed)
    rows[first + 2 : first + 3, :] = token_sum(grad * branch.astype(F32))
    return grad + norm_back(inner_grad * scale, normed, inverse)


def qkv_backward(
    state, middle_grad, dq, dkv, dkvr, mods, layer, weight, gproj, keep, send, shares, rows
):
    width = state.shape[-1]
    block = width // 8
    normed, inverse = layer_norm(state)
    scale = 1.0 + mods[layer, 1:2]
    inner_t = (normed * scale + mods[layer, 0:1]).astype(BF16).T
    dkv_sum = dkv[...] + dkvr[...]
    pieces = (dq[...], dkv_sum[:, :width], dkv_sum[:, width:])
    inner_grad = None

    def put(values, i):
        for b in range(4):
            pair = [values[(2 * b + cc) * block : (2 * b + cc + 1) * block] for cc in range(2)]
            for start, end, place_of, size, at_row in shares:
                place = [place_of(b, i, cc) for cc in range(2)]
                put_units(keep, send, [part[start:end] for part in pair], place, size, at_row)

    for i, piece in enumerate(pieces):
        part = dot_nt(piece, weight[:, i * width : (i + 1) * width])
        inner_grad = part if inner_grad is None else inner_grad + part
        put(dot(inner_t, piece).astype(BF16), i)
    put(gproj[...], 3)
    rows[0:1, :] = token_sum(inner_grad)
    rows[1:2, :] = token_sum(inner_grad * normed)
    return middle_grad + norm_back(inner_grad * scale, normed, inverse)


def embed_body(
    offsets, t0, t1, t2, t3, pos, mods, patch_weight, qkv,
    state, q, kv, patches, tiles,
):
    z, _, _ = places()
    offset = offsets[z]
    for i, tile in enumerate((t0, t1, t2, t3)):
        tiles[-i % 4] = tile[...]
    count = tiles.shape[0]
    even = jnp.concatenate([tiles[z ^ t, 0] for t in range(count)], axis=0).astype(F32)
    odd = jnp.concatenate([tiles[z ^ t, 1] for t in range(count)], axis=0).astype(F32)
    step = even.shape[0] // 32
    later = jnp.concatenate([even[step:], jnp.zeros((step, even.shape[1]), F32)], axis=0)
    first = jnp.where(offset == 1, odd, even).astype(BF16)
    second = jnp.where(offset == 1, later, odd).astype(BF16)
    patches[0] = first
    patches[1] = second
    weight = patch_weight[...].astype(F32)
    lanes = weight.shape[0] // 2
    fill = jnp.zeros((even.shape[1] - lanes, weight.shape[1]), F32)
    upper = jnp.concatenate([weight[:lanes], fill], axis=0).astype(BF16)
    lower = jnp.concatenate([weight[lanes:], fill], axis=0).astype(BF16)
    values = dot(first, upper) + dot(second, lower) + pos[...]
    state[...] = values
    q[...], kv[...] = qkv_forward(values, mods, 0, qkv)


def block_body(
    state, q, kv, kvp, mods, proj, up, down, *rest,
):
    sources, rest = rest[:4], rest[4:]
    state1, q1, kv1, probs, attended, attn_out, middle, gp, act, branch = rest[:10]
    targets, sem = rest[10:14], rest[14]
    copies = [
        pltpu.make_async_copy(source.at[1], target, sem.at[i])
        for i, (source, target) in enumerate(zip(sources, targets))
    ]
    for copy in copies:
        copy.start()
    attend_forward(q, kv, kvp, probs, attended)
    m = mods
    attn = dot(attended[...], proj[...])
    attn_out[...] = attn.astype(BF16)
    mid = state[...] + m[0, 2:3] * attn
    middle[...] = mid
    out = mlp_forward(mid, m, 0, up, down, gp, act)
    branch[...] = out.astype(BF16)
    new = mid + m[0, 5:6] * out
    state1[...] = new
    copies[0].wait()
    q1[...], kv1[...] = qkv_forward(new, m, 1, targets[0])
    for copy in copies[1:]:
        copy.wait()


def turn_body(
    offsets, counts, state, q, kv, kvp, mods, cond, patches, final_weight, proj, up, down,
    probs, attended, attn_out, middle_grad, keep, send, preds,
    gp, act, table, low,
):
    z, _, _ = places()
    offset = offsets[z]
    live = (z < counts[0]).astype(F32)
    attend_forward(q, kv, kvp, probs, attended)
    m = mods
    attn = dot(attended[...], proj[...])
    attn_out[...] = attn.astype(BF16)
    middle = state[...] + m[1, 2:3] * attn
    branch = mlp_forward(middle, m, 1, up, down, gp, act)
    last = middle + m[1, 5:6] * branch
    normed, inverse = layer_norm(last)
    scale = 1.0 + m[2, 1:2]
    inner = (normed * scale + m[2, 0:1]).astype(BF16)
    weight = final_weight[...]
    lanes = weight.shape[1] // 2
    out = dot(inner, weight) * live
    preds[0], preds[1] = by_parity(out[:, :lanes], out[:, lanes:], offset)
    across = weight.astype(F32).T
    chosen = patches
    fill = jnp.zeros((chosen.shape[2] - lanes, across.shape[1]), F32)
    upper = jnp.concatenate([fill, across[:lanes]], axis=0).astype(BF16)
    lower = jnp.concatenate([fill, across[lanes:]], axis=0).astype(BF16)
    inner_grad = (dot(chosen[0], upper) + dot(chosen[1], lower)) * live
    table[...] = jnp.zeros_like(table)
    table[0:1, :] = token_sum(inner_grad)
    table[1:2, :] = token_sum(inner_grad * normed)
    table[5:10, :] = 0.5 * cond[0:5, :]
    skip = chosen.shape[2] - lanes
    for r in range(2):
        at = ROWS + r * lanes
        table[at : at + lanes, :] = (dot_tn(chosen[r], inner) * live)[skip:]
    grad = norm_back(inner_grad * scale, normed, inverse)
    size = 2 * (weight.shape[0] // 8)
    middle_grad[...] = mlp_backward(
        grad, middle, branch, m, 1, gp, act, up, down, keep, send, size, 0, table, 2, low
    )
    base = 4 * weight.shape[0]
    keep[base:] = table[...].astype(BF16)
    send[base:] = table[...].astype(BF16)


def attend_back_body(
    layer, q, kv, kvp, probs, attended, attn_out, middle_grad, mods, proj,
    dq, dkv, gproj, dkvs, rows,
):
    grad = middle_grad[...]
    attn_grad = (mods[layer, 2:3] * grad).astype(BF16)
    attended_grad = dot_nt(attn_grad, proj[...]).astype(BF16)
    masks = head_masks(BF16)
    width = q.shape[-1]
    for p in range(PAIRS):
        at = slice(p * LANES, (p + 1) * LANES)
        av = slice(width + p * LANES, width + (p + 1) * LANES)
        qp = q[:, at] * BF16(HEAD_DIM**-0.5)
        dop = attended_grad[:, at]
        ks, vs = (kv[:, at], kvp[:, at]), (kv[:, av], kvp[:, av])
        total = None
        parts = [[], [], [], []]
        q_t, do_t = qp.T, dop.T
        for h in range(2):
            doh = dop * masks[h]
            own = slice(h * HEAD_DIM, (h + 1) * HEAD_DIM)
            ps = [probs[2 * p + h, i] for i in range(2)]
            dps = [dot_nt(doh, vs[i]) for i in range(2)]
            pfs = [ps[i].astype(F32) for i in range(2)]
            inner = sum(jnp.sum(dps[i] * pfs[i], axis=-1, keepdims=True) for i in range(2))
            for i in range(2):
                ds = (pfs[i] * (dps[i] - inner)).astype(BF16)
                part = dot(ds, ks[i] * masks[h])
                total = part if total is None else total + part
                parts[2 * i].append(dot(q_t[own], ds))
                parts[2 * i + 1].append(dot(do_t[own], ps[i]))
        dq[:, at] = (total * HEAD_DIM**-0.5).astype(BF16)
        turned = [jnp.concatenate(part, axis=0).astype(BF16).T for part in parts]
        dkv[:, at] = turned[0]
        dkv[:, av] = turned[1]
        dkvs[:, at] = turned[2]
        dkvs[:, av] = turned[3]
    rows[...] = jnp.zeros_like(rows)
    rows[0:1, :] = token_sum(grad * attn_out[...].astype(F32))
    gproj[...] = dot_tn(attended[...], attn_grad).astype(BF16)


def middle_body(
    state1, middle_grad1, dq, dkv, dkvr, gproj, middle, branch, gp, act, mods, qkv, up, down,
    middle_grad, keep, send, rows, low,
):
    width = dq.shape[-1]
    block = width // 8
    size = 2 * block
    rows[...] = jnp.zeros_like(rows)
    m = mods
    grad = qkv_backward(
        state1[...], middle_grad1[...], dq, dkv, dkvr, m, 1, qkv, gproj, keep, send,
        ((0, block, chip_place, block, 16 * size),), rows,
    )
    middle_grad[...] = mlp_backward(
        grad, middle[...], branch[...], m, 0, gp, act, up, down, keep, send, size, 0,
        rows, 2, low,
    )


def last_body(
    offsets, state0, middle_grad, dq, dkv, dkvr, gproj, mods, patches, patch_weight,
    rows_a1, rows_mid, rows_a0, qkv,
    keep, send, lgrads, rows, table,
):
    z, _, _ = places()
    offset = offsets[z]
    width = dq.shape[-1]
    block = width // 8
    grad = qkv_backward(
        state0[...], middle_grad[...], dq, dkv, dkvr, mods, 0, qkv, gproj, keep, send,
        ((0, block, lambda zz, ww, cc: unit_place(zz, ww, 1 - cc), block, 0),), rows,
    )
    embed_grad = grad.astype(BF16)
    chosen = patches
    gp0, gp1 = dot_tn(chosen[0], embed_grad), dot_tn(chosen[1], embed_grad)
    chans = patch_weight.shape[0] // 2
    window = dot_nt(embed_grad, patch_weight[...])
    lgrads[0], lgrads[1] = by_parity(window[:, :chans], window[:, chans:], offset)
    table[...] = jnp.zeros_like(table)
    table[0:2, :] = rows[0:2, :]
    table[2:3, :] = rows_a0[0:1, :]
    table[3:6, :] = rows_mid[2:5, :]
    table[6:8, :] = rows_mid[0:2, :]
    table[8:9, :] = rows_a1[0:1, :]
    table[ROWS : ROWS + chans, :] = gp0[:chans]
    table[ROWS + chans : ROWS + 2 * chans, :] = gp1[:chans]
    keep[16 * block :] = table[...].astype(BF16)
    send[16 * block :] = table[...].astype(BF16)


def second_body(keep, recv, keep_out, send_out):
    half = keep_out.shape[0]
    bit = wide_bits()[0]
    keep_out[...] = keep[rows_at(bit, half)] + recv[rows_at(bit, half)]
    send_out[...] = keep[rows_at(1 - bit, half)] + recv[rows_at(1 - bit, half)]


def beta_body(keep, recv, *chips):
    z, _, _ = places()
    size = chips[0].shape[0]
    base = keep.shape[0] - 4 * size
    for k, out in enumerate(chips):
        at = pl.ds(pl.multiple_of(base + (z ^ k) * size, 16), size)
        out[...] = keep[at] + recv[at]


def padded(*pieces):
    rows = jnp.concatenate(pieces, axis=0)
    fill = -rows.shape[0] % 16
    if fill:
        rows = jnp.concatenate([rows, jnp.zeros((fill, rows.shape[1]), F32)], axis=0)
    return rows.astype(BF16)


def paired(mine, other, sums):
    return padded(
        mine[:ROWS], other[:ROWS], mine[ROWS : ROWS + sums] + other[ROWS : ROWS + sums]
    )


def half_of_four(mine, other, sums, flip, four, total):
    _, c, w = places()
    first = jnp.where(c == flip, 1, 2)
    second = 3 - first
    spot = lax.rem(w, 4)
    four[spot] = mine[:ROWS]
    four[spot ^ first] = mine[ROWS : 2 * ROWS]
    four[spot ^ second] = other[:ROWS]
    four[spot ^ first ^ second] = other[ROWS : 2 * ROWS]
    at = slice(2 * ROWS, 2 * ROWS + sums)
    total[...] = mine[at] + other[at]
    half = sums // 2
    return four[2 * c], four[2 * c + 1], total[pl.ds(pl.multiple_of(c * half, 8), half), :]


def first_body(keep, recv, keep_out, table, send):
    half = (keep.shape[0] - table.shape[0]) // 2
    bit = wide_bits()[0]
    keep_out[...] = keep[rows_at(bit, half)] + recv[rows_at(bit, half)]
    send[0:half] = keep[rows_at(1 - bit, half)] + recv[rows_at(1 - bit, half)]
    rows = keep[2 * half :] + recv[2 * half :]
    table[...] = rows
    send[half:] = rows


def first_pair_body(sums, keep, table, recv, keep_out, pair_out, send):
    size = keep.shape[0]
    half = size // 2
    bit = wide_bits()[1]
    keep_out[...] = keep[rows_at(bit, half)] + recv[rows_at(bit, half)]
    send[0:half] = keep[rows_at(1 - bit, half)] + recv[rows_at(1 - bit, half)]
    pair = paired(table[...].astype(F32), recv[size:].astype(F32), sums)
    pair_out[...] = pair
    send[half:] = pair


def first_chip_body(
    sums, keep, pair, recv, tiles, z0, z1, z2, z3, four, total
):
    z, _, _ = places()
    size = keep.shape[0]
    unit = size // 4
    rows = half_of_four(pair[...].astype(F32), recv[size:].astype(F32), sums, 0, four, total)
    for k, out in enumerate((z0, z1, z2, z3)):
        out[0:unit] = keep[rows_at(z ^ k, unit)] + recv[rows_at(z ^ k, unit)]
        out[unit:] = padded(*rows, tiles[k])


def unit1_body(sums, o0, o1, o2, o3, unit, pack, tiles):
    ones = (o0, o1, o2, o3)
    unit[...] = chip_sum(ones, slice(0, unit.shape[0])).astype(BF16)
    chip_rows(sums, ones, unit.shape[0], pack)
    for i, one in enumerate(ones):
        tiles[-i % 4] = one[unit.shape[0] + 32 :].astype(F32)[8:]


def pack_body(preds, lgrads, tiles):
    z, _, _ = places()
    tok = preds.shape[1] // 4
    for k in range(4):
        cut = pl.ds(pl.multiple_of((z ^ k) * tok, 8), tok)
        latents = packed_tile([lgrads[0, cut, :], lgrads[1, cut, :]], lgrads.shape[2], 8)
        predicted = packed_tile([preds[0, cut, :], preds[1, cut, :]], preds.shape[2], 8)
        tiles[k] = jnp.concatenate([latents, predicted], axis=1)


def chip_sum(parts, at):
    return sum(part[at].astype(F32) for part in parts)


def third_body(keep2, recv2, b0, b1, b2, b3, keep2_out, keepb, part, whole):
    half2, halfb = keep2.shape[0] // 2, keepb.shape[0]
    bit = wide_bits()[1]
    keep2_out[...] = keep2[rows_at(bit, half2)] + recv2[rows_at(bit, half2)]
    part[0:half2] = keep2[rows_at(1 - bit, half2)] + recv2[rows_at(1 - bit, half2)]
    whole[...] = chip_sum((b0, b1, b2, b3), slice(None)).astype(BF16)
    keepb[...] = whole[rows_at(bit, halfb)]
    part[half2:] = whole[rows_at(1 - bit, halfb)]


def third_send_body(keep3, recv3, part, keep3_out, table, send):
    size = part.shape[0]
    size3 = keep3.shape[0] - table.shape[0]
    half3 = size3 // 2
    bit = wide_bits()[1]
    send[0:size] = part[...]
    keep3_out[...] = keep3[rows_at(bit, half3)] + recv3[rows_at(bit, half3)]
    send[size : size + half3] = keep3[rows_at(1 - bit, half3)] + recv3[rows_at(1 - bit, half3)]
    rows = keep3[size3:] + recv3[size3:]
    table[...] = rows
    send[size + half3 :] = rows


def fourth_body(
    sums, keep2, keep3, keepb, table, recv, z0, z1, z2, z3, keep3_out, keepb_out, pair_out, send
):
    z, _, _ = places()
    size2, size3, sizeb = keep2.shape[0], keep3.shape[0], keepb.shape[0]
    half3, halfb = size3 // 2, sizeb // 2
    unit = size2 // 4
    for k, out in enumerate((z0, z1, z2, z3)):
        out[...] = keep2[rows_at(z ^ k, unit)] + recv[rows_at(z ^ k, unit)]
    bit = wide_bits()[0]

    def half(held, index, size, base):
        start = pl.multiple_of(index * size, 16)
        return held[pl.ds(start, size)] + recv[pl.ds(pl.multiple_of(start + base, 16), size)]

    keep3_out[...] = half(keep3, bit, half3, size2 + sizeb)
    send[0:half3] = half(keep3, 1 - bit, half3, size2 + sizeb)
    keepb_out[...] = half(keepb, bit, halfb, size2)
    send[half3 : half3 + halfb] = half(keepb, 1 - bit, halfb, size2)
    pair = paired(table[...].astype(F32), recv[size2 + size3 + sizeb :].astype(F32), sums)
    pair_out[...] = pair
    send[half3 + halfb :] = pair


def fifth_body(sums, keep3, keepb, pair, recv, z0, z1, z2, z3, unitb, four, total):
    z, _, _ = places()
    size3, sizeb = keep3.shape[0], keepb.shape[0]
    unit3 = size3 // 4
    other = recv[size3 + sizeb :].astype(F32)
    rows = padded(*half_of_four(pair[...].astype(F32), other, sums, 1, four, total))
    for k, out in enumerate((z0, z1, z2, z3)):
        out[0:unit3] = keep3[rows_at(z ^ k, unit3)] + recv[rows_at(z ^ k, unit3)]
        out[unit3:] = rows
    unitb[...] = keepb[...] + recv[size3 : size3 + sizeb]


def chip_rows(sums, parts, size, pack):
    rows = [part[size : size + 48 if sums > 8 else size + 32].astype(F32) for part in parts]
    total = sum(r[2 * ROWS : 2 * ROWS + sums] for r in rows)
    pack[...] = padded(*[r[: 2 * ROWS] for r in rows], total)


def unit12_body(unit1, t0, t1, t2, t3, unitb, unit):
    size, end2 = unit1.shape[0], t0.shape[0]
    unit[0:size] = unit1[...]
    unit[size : size + end2] = chip_sum((t0, t1, t2, t3), slice(None)).astype(BF16)
    unit[size + end2 :] = unitb[...]


def join_body(own, near, send):
    size = own.shape[0]
    send[0:size] = own[...]
    send[size:] = near[...]


def unit3_body(sums, z0, z1, z2, z3, unit, pack):
    parts = (z0, z1, z2, z3)
    size = unit.shape[0]
    unit[...] = chip_sum(parts, slice(0, size)).astype(BF16)
    chip_rows(sums, parts, size, pack)


def silu_slope(values):
    sigmoid = jax.nn.sigmoid(values)
    return sigmoid * (1.0 + values * (1.0 - sigmoid))


def sample_table(table, pack, other):
    parts, half = table.shape[0], table.shape[1] // 2
    for side, held in enumerate((pack, other)):
        for i in range(parts):
            at = slice(128 * i, 128 * (i + 1))
            table[i, half * side : half * (side + 1)] = held[0:half, at].astype(F32)
    samples = table.shape[1] // ROWS

    def rows(r):
        return jnp.concatenate(
            [table[i, pl.ds(r, samples, stride=ROWS), :] for i in range(parts)], axis=-1
        )

    return rows


def join_sums(out, pack, other):
    c = lax.axis_index("cols")
    count = out.shape[0] // 2
    for side, held in enumerate((pack, other)):
        at = pl.ds(pl.multiple_of((c ^ side) * count, 8), count)
        out[at, :] = held[held.shape[0] - 16 :].astype(F32)[:count]


def early_sums_body(
    pack, other, final_mod,
    g_final_mod, g_final, shared_t, slopes, base, high, act_t, feat_t, hot, table,
):
    rows = sample_table(table, pack, other)
    join_sums(g_final, pack, other)
    fmods = jnp.concatenate([rows(0), rows(1)], axis=-1).astype(BF16)
    shared_t[...] = rows(ROW_SHARED).T
    g_final_mod[...] = dot(shared_t[...].astype(BF16), fmods)
    base[...] = dot_nt(fmods, final_mod[...])
    slopes[0] = silu_slope(rows(ROW_COND))
    slopes[1] = silu_slope(rows(ROW_HID))
    for k in range(3):
        high[k] = rows(2 + k)
    act_t[...] = rows(ROW_ACT).T.astype(BF16)
    feats = rows(ROW_FEAT)
    count = feat_t.shape[0]
    feat_t[...] = feats[:, :count].T.astype(BF16)
    label = (feats[:, count : count + 1] * 32.0 + feats[:, count + 1 : count + 2]).astype(jnp.int32)
    classes = hot.shape[0]
    lane = lax.broadcasted_iota(jnp.int32, (feats.shape[0], (classes + 127) // 128 * 128), 1)
    hot[...] = (lane == label).astype(F32).T[:classes].astype(BF16)


def sums_body(
    pack, other, modulation, time_out, shared_t, slopes, base, high, act_t, feat_t, hot,
    time_in_v, time_out_v, table_v, mod_v, g_patch,
    table,
):
    z, c, _ = places()
    rows = sample_table(table, pack, other)
    mods = [
        jnp.concatenate([rows(k) for k in range(6)], axis=-1).astype(BF16),
        jnp.concatenate(
            [rows(k) for k in range(6, 9)] + [high[k] for k in range(3)], axis=-1
        ).astype(BF16),
    ]
    block = mod_v.shape[1]
    start = pl.multiple_of((z * 2 + c) * block, 8)
    mine = shared_t[pl.ds(start, block), :].astype(BF16)
    for layer in range(2):
        mod_v[layer] = dot(mine, mods[layer])
    shared_grad = base[...]
    for layer in range(2):
        shared_grad += dot_nt(mods[layer], modulation[layer])
    cond_grad = shared_grad * slopes[0]
    cond_low = cond_grad.astype(BF16)
    cond_rest = (cond_grad - cond_low.astype(F32)).astype(BF16)
    table_v[...] = dot(hot[...], cond_low) + dot(hot[...], cond_rest)
    time_out_v[...] = dot(act_t[...], cond_low)
    time_grad = dot_nt(cond_low, time_out[...]) * slopes[1]
    time_in_v[...] = dot(feat_t[...], time_grad.astype(BF16))
    join_sums(g_patch, pack, other)


def unpack_body(tiles, *refs):
    held, left, (prediction, latent_grad, token, sem) = refs[:5], refs[5:10], refs[10:]
    copies = []
    leave_all(tuple(zip(held, left)), sem, copies)
    z, _, _ = places()
    token[...] = jnp.zeros_like(token)
    _, out_ch, height, wide = prediction.shape
    lat_ch = latent_grad.shape[1]
    for k in range(4):
        split = tiles.shape[2] // 3
        image = unpacked_tile(tiles[k, :, split:].astype(BF16), out_ch, height, wide)
        prediction[z ^ k] = image.astype(BF16).reshape(out_ch, height, wide)
        image = unpacked_tile(tiles[k, :, :split].astype(BF16), lat_ch, height, wide)
        latent_grad[z ^ k] = image.reshape(lat_ch, height, wide)
    for copy in copies:
        copy.wait()


def place_mlp(up, down, piece, unit):
    block, width = up.shape[0], down.shape[1]
    cols = pl.ds(pl.multiple_of(unit * width, 128), width)
    up[:, cols] = piece[0:block].astype(F32)
    down_rows = pl.ds(pl.multiple_of(unit * block, 8), block)
    down[down_rows, :] = piece[block : 2 * block].astype(F32)


def place_attn(qkv, proj, piece, unit):
    width = proj.shape[1]

    @pl.when(unit < 3)
    def _():
        cols = pl.ds(pl.multiple_of(unit * width, 128), width)
        qkv[:, cols] = piece.astype(F32)

    @pl.when(unit == 3)
    def _():
        proj[...] = piece.astype(F32)


def wide_spots():
    _, c, w = places()
    first = jnp.where(c == 0, 1, 2)
    spot = lax.rem(w, 4)
    return spot, spot ^ first, spot ^ first ^ 3, spot ^ 3


def leave_all(pairs, sem, copies):
    for source, target in pairs:
        copies.append(pltpu.make_async_copy(source, target, sem.at[len(copies)]))
        copies[-1].start()


def spread_body(own, near, far, g_qkv, g_proj, g_up, g_down, up, down, qkv, proj, sem):
    size2 = own.shape[0]
    block = proj.shape[0]
    size = 2 * block
    units = ((own, 0), (near, 0), (far, 0), (far, size2))
    copies = []
    for layer, start in ((1, 0), (0, size)):
        for (ref, base), unit in zip(units, wide_spots()):
            piece = ref[base + start : base + start + size]
            place_mlp(up.at[layer], down.at[layer], piece, unit)
        leave_all(
            ((up.at[layer], g_up.at[layer]), (down.at[layer], g_down.at[layer])), sem, copies
        )
    for (ref, base), unit in zip(units, wide_spots()):
        place_attn(qkv, proj, ref[base + 2 * size : base + size2], unit)
    leave_all(((qkv, g_qkv.at[1]), (proj, g_proj.at[1])), sem, copies)
    for copy in copies:
        copy.wait()


def last_spread_body(own, near, far, _q, _p, g_qkv, g_proj, qkv, proj, sem):
    size = own.shape[0]
    units = ((own, 0), (near, 0), (far, 0), (far, size))
    for (ref, base), unit in zip(units, wide_spots()):
        place_attn(qkv, proj, ref[base : base + size], unit)
    copies = []
    leave_all(((qkv, g_qkv.at[0]), (proj, g_proj.at[0])), sem, copies)
    for copy in copies:
        copy.wait()


def swap(value, axis, bit):
    count = lax.axis_size(axis)
    return lax.ppermute(value, axis, [(i, i ^ bit) for i in range(count)])


def swap_by_core(value, bits):
    wide, cores = lax.axis_size("wide"), lax.axis_size("cols")
    pairs = [
        (w * cores + c, (w ^ bits[c % 2]) * cores + c) for w in range(wide) for c in range(cores)
    ]
    return lax.ppermute(value, ("wide", "cols"), pairs)


FIRST, SECOND = (1, 2), (2, 1)


def rest_sum(value):
    bit = 4
    while bit < lax.axis_size("wide"):
        value = (value.astype(F32) + swap(value, "wide", bit).astype(F32)).astype(value.dtype)
        bit *= 2
    return value


def rest_gather(value):
    bit = 4
    while bit < lax.axis_size("wide"):
        value = jnp.concatenate([value, swap(value, "wide", bit)])
        bit *= 2
    return value


def position_tables(row_count, col_count, cores, width):
    quarter = width // 4
    omega = np.exp(-math.log(10000.0) * np.arange(quarter) / quarter)
    row_angle = np.arange(row_count)[:, None] * omega[None, :]
    col_angle = np.arange(col_count * cores)[:, None] * omega[None, :]
    row_part = np.concatenate([np.sin(row_angle), np.cos(row_angle)], axis=-1)
    col_part = np.concatenate([np.sin(col_angle), np.cos(col_angle)], axis=-1)
    col_part = col_part.reshape(cores, 1, col_count, width // 2)
    table = np.concatenate(
        [
            np.broadcast_to(row_part[None, :, None, :], (cores, row_count, col_count, width // 2)),
            np.broadcast_to(col_part, (cores, row_count, col_count, width // 2)),
        ],
        axis=-1,
    )
    return table.reshape(cores, row_count * col_count, width).astype(np.float32)


def shards(
    latent, pred_grad, timesteps, labels, offsets, counts, patch_weight, time_in, time_out,
    label_table, modulation, qkv_weight, proj_weight, up_weight, down_weight, final_mod, final_weight,
):
    slots, lat_ch, tile_h, tile_w = latent.shape
    out_ch = pred_grad.shape[1]
    width = patch_weight.shape[1]
    ff = up_weight.shape[2]
    n_rows, n_cols = lax.axis_size("rows"), lax.axis_size("cols")
    hp, wp = tile_h // 2, tile_w // 2
    tile_tok = hp * wp
    tokens = n_rows * tile_tok
    lanes = 2 * (lat_ch + out_ch)
    block = width // 8
    tok, wide_tok, double = (tokens, width), (tokens, ff), (tokens, 2 * width)

    tiles = kernel_call(
        tiles_body,
        [("h", latent), ("h", pred_grad)],
        [((2, tile_tok, lanes), BF16)] * n_rows,
        [
            pltpu.VMEM(latent.shape, BF16), pltpu.VMEM(pred_grad.shape, BF16),
            pltpu.SemaphoreType.DMA((2,)),
        ],
        us=1,
    )

    def along_z(parts):
        return [parts[0]] + [swap(parts[k], "rows", k) for k in reversed(range(1, n_rows))]

    def both_halves(pack):
        if lax.axis_size("wide") > 4:
            rows, sums = rest_gather(pack[: 8 * ROWS]), rest_sum(pack[8 * ROWS :])
            pack = jnp.concatenate([rows, sums])
        return pack, swap(pack, "cols", 1)

    tiles = along_z(tiles)
    half = time_in.shape[0] // 2
    freqs = np.exp(-math.log(10000.0) * np.arange(half, dtype=np.float32) / np.float32(half))
    positions = jnp.asarray(position_tables(n_rows * hp, wp, n_cols, width))
    blocks = (qkv_weight, proj_weight, up_weight, down_weight)
    weights = (time_out, modulation, final_mod) + blocks
    held = [(weight.shape[1:], BF16) for weight in blocks]
    (
        mods, cond, final_v, pos, time_out_v, modulation_v, final_mod_v, qkv0, proj0, up0, down0,
    ) = kernel_call(
        cond_body,
        [("s", timesteps), ("s", labels), ("v", jnp.asarray(freqs.astype(np.float32))[None])]
        + [("v", label_table), ("v", time_in), ("v", final_weight), ("h", positions)]
        + [("h", weight) for weight in weights],
        [((3, 8, width), F32), ((8, width), F32), (final_weight.shape, BF16), (tok, F32)]
        + [(weight.shape, BF16) for weight in weights[:3]]
        + held,
        [pltpu.SemaphoreType.DMA((len(weights) + 1,))],
        us=US["cond"],
    )
    probs_shape = (HEADS, 2, tokens, tokens)
    state0, q0, kv0, patches = kernel_call(
        embed_body,
        [("s", offsets)]
        + [("v", t) for t in tiles]
        + [("p", pos), ("p", mods), ("v", patch_weight), ("p", qkv0)],
        [(tok, F32), (tok, BF16), (double, BF16), ((2, tokens, lanes), BF16)],
        [pltpu.VMEM((n_rows, 2, tile_tok, lanes), BF16)],
        us=US["embed"],
    )
    kv0p = swap(kv0, "cols", 1)
    (
        state1, q1, kv1, probs0, attended0, attn_out0, middle0, gp0, act0, branch0, qkv1, proj1, up1, down1,
    ) = kernel_call(
        block_body,
        [("p", state0), ("p", q0), ("p", kv0), ("v", kv0p)]
        + [("p", a) for a in (mods, proj0, up0, down0)]
        + [("h", weight) for weight in blocks],
        [
            (tok, F32), (tok, BF16), (double, BF16), (probs_shape, BF16), (tok, BF16), (tok, BF16),
            (tok, F32), (wide_tok, BF16), (wide_tok, BF16), (tok, BF16),
        ]
        + held,
        [pltpu.SemaphoreType.DMA((4,))],
        us=US["block"],
    )
    kv1p = swap(kv1, "cols", 1)
    sums_a, sums_b = 4 * out_ch, 4 * lat_ch
    rows_1 = 16 * 2 * block + 48
    probs1, attended1, attn_out1, mgrad1, keep1, send1, preds = kernel_call(
        turn_body,
        [("s", offsets), ("s", counts), ("p", state1), ("p", q1), ("p", kv1), ("v", kv1p)]
        + [("p", a) for a in (mods, cond, patches, final_v, proj1, up1, down1)],
        [
            (probs_shape, BF16), (tok, BF16), (tok, BF16), (tok, F32), ((rows_1, width), BF16),
            ((rows_1, width), BF16), ((2, tokens, 2 * out_ch), F32),
        ],
        [
            pltpu.VMEM(wide_tok, BF16), pltpu.VMEM(wide_tok, BF16), pltpu.VMEM((48, width), F32),
            pltpu.VMEM(wide_tok, BF16),
        ],
        us=US["turn"],
    )
    recv1 = swap(send1, "cols", 1)

    def attend_back(layer, q, kv, kvp, *saved, after):
        return kernel_call(
            partial(attend_back_body, layer),
            [("p", q), ("p", kv), ("v", kvp)] + [("p", a) for a in saved[:-1] + (mods, saved[-1])],
            [
                (tok, BF16), (double, BF16), ((width, width), BF16), (double, BF16), ((8, width), F32),
            ],
            us=US["back"],
            after=after,
        )

    dq1, dkv1, gproj1, dkvs1, rows_a1 = attend_back(
        1, q1, kv1, kv1p, probs1, attended1, attn_out1, mgrad1, proj1, after=None
    )
    dkvr1 = swap(dkvs1, "cols", 1)
    keep1, table1, send1 = kernel_call(
        first_body,
        [("p", keep1), ("v", recv1)],
        [((8 * 2 * block, width), BF16), ((48, width), BF16), ((8 * 2 * block + 48, width), BF16)],
        us=US["A1"],
        after=rows_a1,
    )
    recv1 = swap_by_core(send1, FIRST)
    mgrad0, keep2, send2, rows_mid = kernel_call(
        middle_body,
        [("p", a) for a in (state1, mgrad1, dq1, dkv1)]
        + [("v", dkvr1)]
        + [("p", a) for a in (gproj1, middle0, branch0, gp0, act0, mods, qkv1, up0, down0)],
        [
            (tok, F32), ((16 * 3 * block, width), BF16), ((16 * 3 * block, width), BF16),
            ((8, width), F32),
        ],
        [pltpu.VMEM(wide_tok, BF16)],
        us=US["middle"],
        after=table1,
    )
    recv2 = swap(send2, "cols", 1)
    dq0, dkv0, gproj0, dkvs0, rows_a0 = attend_back(
        0, q0, kv0, kv0p, probs0, attended0, attn_out0, mgrad0, proj0, after=None
    )
    dkvr0 = swap(dkvs0, "cols", 1)
    alpha, beta = 2 * block, block
    send_rows = 4 * alpha + 2 * beta + 8 * block + 32
    whole_2, whole_r = keep2, recv2
    keep2, send2 = kernel_call(
        second_body,
        [("p", whole_2), ("v", whole_r)],
        [((8 * alpha, width), BF16)] * 2,
        us=US["A3"],
        after=rows_a0,
    )
    recv2 = swap_by_core(send2, FIRST)
    keep1, pair1, send1 = kernel_call(
        partial(first_pair_body, sums_a),
        [("p", keep1), ("p", table1), ("v", recv1)],
        [((4 * 2 * block, width), BF16), ((64, width), BF16), ((4 * 2 * block + 64, width), BF16)],
        us=US["A2"],
        after=keep2,
    )
    recv1 = swap_by_core(send1, SECOND)
    betas = kernel_call(
        beta_body,
        [("p", whole_2), ("v", whole_r)],
        [((4 * beta, width), BF16)] * 4,
        us=US["A3b"],
        after=pair1,
    )
    chips = betas[0]
    betas = along_z(betas)
    rows_3 = 16 * block + 32
    keep3, send3, lgrads = kernel_call(
        last_body,
        [("s", offsets), ("p", state0), ("p", mgrad0), ("p", dq0), ("p", dkv0), ("v", dkvr0)]
        + [("p", gproj0), ("p", mods), ("p", patches), ("v", patch_weight)]
        + [("p", a) for a in (rows_a1, rows_mid, rows_a0, qkv0)],
        [((rows_3, width), BF16), ((rows_3, width), BF16), ((2, tokens, 2 * lat_ch), F32)],
        [pltpu.VMEM((8, width), F32), pltpu.VMEM((32, width), F32)],
        us=US["last"],
        after=chips,
    )
    recv3 = swap(send3, "cols", 1)
    (tiles,) = kernel_call(
        pack_body, [("p", preds), ("p", lgrads)], [((4, 8, width), F32)], us=US["pack"]
    )
    ones = kernel_call(
        partial(first_chip_body, sums_a),
        [("p", keep1), ("p", pair1), ("v", recv1), ("p", tiles)],
        [((2 * block + 48, width), BF16)] * 4,
        [pltpu.VMEM((4, ROWS, width), F32), pltpu.VMEM((sums_a, width), F32)],
        us=US["A2b"],
    )
    chips = ones[0]
    ones = along_z(ones)
    keep2, keepb, part = kernel_call(
        third_body,
        [("p", keep2), ("v", recv2), ("p", betas[0])] + [("v", beta) for beta in betas[1:]],
        [
            ((4 * alpha, width), BF16), ((2 * beta, width), BF16),
            ((4 * alpha + 2 * beta, width), BF16),
        ],
        [pltpu.VMEM((4 * beta, width), BF16)],
        us=US["A4"],
        after=chips,
    )
    keep3, table3, send = kernel_call(
        third_send_body,
        [("p", keep3), ("v", recv3), ("p", part)],
        [((8 * block, width), BF16), ((32, width), BF16), ((send_rows, width), BF16)],
        us=US["A4b"],
    )
    recv = swap_by_core(send, SECOND)
    *twos, keep3, keepb, pair3, send = kernel_call(
        partial(fourth_body, sums_b),
        [("p", keep2), ("p", keep3), ("p", keepb), ("p", table3), ("v", recv)],
        [((alpha, width), BF16)] * 4
        + [
            ((4 * block, width), BF16), ((beta, width), BF16), ((48, width), BF16),
            ((4 * block + beta + 48, width), BF16),
        ],
        us=US["A5"],
    )
    recv = swap_by_core(send, FIRST)
    twos = along_z(twos)
    pack = (8 * ROWS + 16, width)
    unit1, pack_a, tiles = kernel_call(
        partial(unit1_body, sums_a // 2),
        [("p", ones[0])] + [("v", one) for one in ones[1:]],
        [((2 * block, width), BF16), (pack, BF16), ((4, 8, width), F32)],
        us=US["U1"],
        after=pair3,
    )
    packs = both_halves(pack_a)
    *threes, unitb = kernel_call(
        partial(fifth_body, sums_b),
        [("p", keep3), ("p", keepb), ("p", pair3), ("v", recv)],
        [((block + 32, width), BF16)] * 4 + [((beta, width), BF16)],
        [pltpu.VMEM((4, ROWS, width), F32), pltpu.VMEM((sums_b, width), F32)],
        us=US["A6"],
        after=pack_a,
    )
    threes = along_z(threes)
    (unit2,) = kernel_call(
        unit12_body,
        [("p", unit1), ("p", twos[0])] + [("v", two) for two in twos[1:]] + [("p", unitb)],
        [((2 * block + alpha + beta, width), BF16)],
        us=US["U12"],
    )
    unit2 = rest_sum(unit2)
    near2 = swap_by_core(unit2, FIRST)
    samples = 2 * (packs[0].shape[0] - 16) // ROWS
    classes = label_table.shape[0]
    feat_count = time_in.shape[0]
    g_final_mod, g_final, *early = kernel_call(
        early_sums_body,
        [("p", packs[0]), ("v", packs[1]), ("p", final_mod_v)],
        [
            (final_mod.shape, F32, "any"), ((sums_a, width), F32, "any"), ((width, samples), F32),
            ((2, samples, width), F32), ((samples, width), F32), ((3, samples, width), F32),
            ((width, samples), BF16), ((feat_count, samples), BF16), ((classes, samples), BF16),
        ],
        [pltpu.VMEM((width // 128, samples * ROWS, 128), F32)],
        us=US["early"],
        after=unit2,
    )
    unit3, pack_b = kernel_call(
        partial(unit3_body, sums_b // 2),
        [("p", threes[0])] + [("v", three) for three in threes[1:]],
        [((block, width), BF16), (pack, BF16)],
        us=US["U2"],
        after=early[0],
    )
    unit3 = rest_sum(unit3)
    near3 = swap_by_core(unit3, FIRST)
    (send2,) = kernel_call(
        join_body,
        [("p", unit2), ("v", near2)],
        [((2 * unit2.shape[0], width), BF16)],
        us=US["join"],
        after=pack_b,
    )
    far2 = swap_by_core(send2, SECOND)
    packs = both_halves(pack_b)
    late_shapes = (
        time_in.shape, time_out.shape, (classes, width), (2, block, 6 * width), patch_weight.shape,
    )
    late = kernel_call(
        sums_body,
        [("p", packs[0]), ("v", packs[1])] + [("p", a) for a in (modulation_v, time_out_v, *early)],
        [(shape, F32) for shape in late_shapes],
        [pltpu.VMEM((width // 128, samples * ROWS, 128), F32)],
        us=US["sums"],
    )
    (send3,) = kernel_call(
        join_body,
        [("p", unit3), ("v", near3)],
        [((2 * block, width), BF16)],
        us=US["F3"],
        after=late[4],
    )
    far3 = swap_by_core(send3, SECOND)
    g_time_in, g_time_out, g_table, g_mod, g_patch, prediction, latent_grad, token = kernel_call(
        unpack_body,
        [("p", tiles)] + [("p", a) for a in late],
        [(shape, F32, "hbm") for shape in late_shapes]
        + [((slots, out_ch, tile_h, tile_w), BF16, "any"), (latent.shape, F32, "any"), ((8, 128), F32)],
        [pltpu.SemaphoreType.DMA((5,))],
        us=US["unpack"],
        after=send3,
    )
    up_shape, down_shape = (2, block, ff), (2, ff // 8, width)
    attn_scratch = [pltpu.VMEM((block, 3 * width), F32), pltpu.VMEM((block, width), F32)]
    attn_shapes = [((2, block, 3 * width), F32, "hbm"), ((2, block, width), F32, "hbm")]
    g_qkv, g_proj, g_up, g_down = kernel_call(
        spread_body,
        [("p", unit2), ("v", near2), ("v", far2)],
        attn_shapes + [(up_shape, F32, "hbm"), (down_shape, F32, "hbm")],
        [pltpu.VMEM(up_shape, F32), pltpu.VMEM(down_shape, F32)]
        + attn_scratch
        + [pltpu.SemaphoreType.DMA((6,))],
        us=US["spread"],
        after=token,
    )
    g_qkv, g_proj = kernel_call(
        last_spread_body,
        [("p", unit3), ("v", near3), ("v", far3), ("h", g_qkv), ("h", g_proj)],
        attn_shapes,
        attn_scratch + [pltpu.SemaphoreType.DMA((2,))],
        us=US["spread"],
        aliases=((3, 0), (4, 1)),
    )
    return (
        prediction, latent_grad, g_patch, g_time_in, g_time_out, g_table, g_mod, g_qkv, g_proj,
        g_up, g_down, g_final_mod, g_final.T,
    )


def solution(mesh):
    tiled, split = P("wide", None, "rows", "cols"), P(None, ("rows", "cols"), None)
    return jax.shard_map(
        shards,
        mesh=mesh,
        in_specs=(tiled, tiled, P("wide"), P("wide"), P("wide"), P("wide")) + (P(),) * 11,
        out_specs=(tiled, tiled, P(), P(), P(), P(), split, split, split, split, split, P(), P()),
        check_vma=False,
    )
```
